32 devices in a mesh: row: 8 (over z, y), col: 4 (over x, core).
Axes of the slice: x: 2, y: 2, z: 4, core: 2. Of those that a mesh axis runs over, the one named last changes fastest.
Arguments:
- image_batch: bfloat16 [16, 64, 128, 2], P(None, 'row', 'col'), may hold values from -12 to 12
- valid_mask: int32 [16, 64, 128], P(None, 'row', 'col'), may hold values from 0 to 1, as said below
- flow_target: int32 [16, 64, 128, 2], P(None, 'row', 'col'), may hold values from -80 to 80
- cell_labels: int32 [16, 64, 128], P(None, 'row', 'col'), may hold values 0 or 1
- w_first: float32 [10, 2, 32], replicated, may hold values from -1.5 to 1.5
- w_convs: float32 [3, 9, 32, 32], replicated, may hold values from -0.375 to 0.375
- w_style: float32 [2, 32, 32], replicated, may hold values from -1 to 1
- w_head: float32 [33, 3], replicated, may hold values from -1 to 1
- batch_norm_table: float32 [2, 4, 32], replicated, may hold values from -0.6 to 1.5
- mom_first: float32 [10, 2, 32], replicated, may hold values from -0.022097087 to 0.022097087
- mom_convs: float32 [3, 9, 32, 32], replicated, may hold values from -0.022097087 to 0.022097087
- mom_style: float32 [2, 32, 32], replicated, may hold values from -0.022097087 to 0.022097087
- mom_head: float32 [33, 3], replicated, may hold values from -0.022097087 to 0.022097087
- mom_norms: float32 [2, 4, 32], replicated, may hold values from -0.022097087 to 0.022097087
- sqr_first: float32 [10, 2, 32], replicated, may hold values from 3.0517578e-05 to 0.00012207031
- sqr_convs: float32 [3, 9, 32, 32], replicated, may hold values from 3.0517578e-05 to 0.00012207031
- sqr_style: float32 [2, 32, 32], replicated, may hold values from 3.0517578e-05 to 0.00012207031
- sqr_head: float32 [33, 3], replicated, may hold values from 3.0517578e-05 to 0.00012207031
- sqr_norms: float32 [2, 4, 32], replicated, may hold values from 3.0517578e-05 to 0.00012207031
Outputs:
- loss_total: float32 [], replicated
- valid_count: float32 [], replicated
- first_master: float32 [10, 2, 32], replicated
- first_moment: float32 [10, 2, 32], replicated
- first_square: float32 [10, 2, 32], replicated
- first_copy: bfloat16 [10, 2, 32], replicated
- convs_master: float32 [3, 9, 32, 32], replicated
- convs_moment: float32 [3, 9, 32, 32], replicated
- convs_square: float32 [3, 9, 32, 32], replicated
- convs_copy: bfloat16 [3, 9, 32, 32], replicated
- style_master: float32 [2, 32, 32], replicated
- style_moment: float32 [2, 32, 32], replicated
- style_square: float32 [2, 32, 32], replicated
- head_master: float32 [33, 3], replicated
- head_moment: float32 [33, 3], replicated
- head_square: float32 [33, 3], replicated
- head_copy: bfloat16 [33, 3], replicated
- norms_master: float32 [2, 4, 32], replicated
- norms_moment: float32 [2, 4, 32], replicated
- norms_square: float32 [2, 4, 32], replicated
The draws below stay inside these ranges and needn't reach their ends.
Inputs may be any that keep to these rules, and one draw needn't show every extreme that they name: `valid_mask`: each image's pixel at row 0, column 0 is 1.
All inputs are finite; a program needn't handle non-finite values. No bound on the sum of `cell_labels` on one device may be relied on, other than what follows from the above.
Results may differ from the reference program's by a relative error of at most 0.0087.
The reference program's roundings to bfloat16 on the way count: a program that leaves them out, or rounds other values in their place, can miss the bound.
Values may be sent and summed in bfloat16 or wider, within the bound.
No kernel may reach another device: no remote copies, remote signals or barrier semaphores. Data moves between devices by JAX's collectives and lax.ppermute only.
A program may use at most 128 MiB of HBM per device.

```python
import math
import jax
import jax.numpy as jnp
from jax import lax

CHANNELS = 32
IN_CH = 2
IMAGES = 16
STEP = 5
H = 64
W = 128


def draw_image_batch(key, part):
    key = jax.random.fold_in(key, 11)
    noise_key, scale_key, offset_key = jax.random.split(key, 3)
    rows = jnp.arange(H, dtype=jnp.float32) / max(H - 1, 1)
    cols = jnp.arange(W, dtype=jnp.float32) / max(W - 1, 1)
    noise = jnp.clip(jax.random.normal(noise_key, (IMAGES, H, W, IN_CH), jnp.float32), -4.0, 4.0)
    rising = 2.0
    ramp = jnp.sqrt((1.0 + rising * rows)[:, None] * (1.0 + rising * cols)[None, :] / (1.0 + rising))
    scales = jnp.exp(jax.random.uniform(scale_key, (IMAGES, 1, 1, 1), jnp.float32, -0.5, 0.47))
    shift_values = jnp.clip(0.3 * jax.random.normal(offset_key, (IMAGES, 1, 1, IN_CH), jnp.float32), -0.9, 0.9)
    return (noise * ramp[None, :, :, None] * scales + shift_values).astype(jnp.bfloat16)


def draw_valid_mask(key, part):
    key = jax.random.fold_in(key, 7)
    rows = jnp.arange(H, dtype=jnp.int32)
    cols = jnp.arange(W, dtype=jnp.int32)
    row_weight = 300 + 600 * rows // max(H - 1, 1)
    col_weight = 333 + 667 * cols // max(W - 1, 1)
    threshold = row_weight[:, None] * col_weight[None, :] // 1000
    draws = jax.random.randint(key, (IMAGES, H, W), 0, 1000, dtype=jnp.int32)
    valid = (draws < threshold[None]).astype(jnp.int32)
    return valid.at[:, 0, 0].set(1)


def draw_batch_norm_table(key, part):
    key = jax.random.fold_in(key, 5)
    gain_key, bias_key = jax.random.split(key)
    gains = jax.random.uniform(gain_key, (4, CHANNELS), jnp.float32, 0.7, 1.4)
    biases = jnp.clip(0.2 * jax.random.normal(bias_key, (4, CHANNELS), jnp.float32), -0.6, 0.6)
    return jnp.stack([gains, biases])


def plant(values, stream_key, least, top_value):
    extent = values.shape
    spot = [jax.random.randint(jax.random.fold_in(stream_key, axis), (), 0, extent[axis]) for axis in range(len(extent))]
    values = values.at[tuple(spot)].set(least)
    longest = extent.index(max(extent))
    spot[longest] = (spot[longest] + 1) % extent[longest]
    return values.at[tuple(spot)].set(top_value)


def scatter_about(stream_key, shape, width, limit, held_as=jnp.bfloat16):
    entries = width * jax.random.normal(stream_key, shape, jnp.float32)
    return jnp.clip(entries, min=-limit, max=limit).astype(held_as)


def setup_inputs(seed: int = 0) -> dict:
    key_list = jax.random.split(jax.random.key(seed), 20)
    return {
        "image_batch": draw_image_batch(jax.random.fold_in(key_list[19], 71), 0),
        "valid_mask": draw_valid_mask(jax.random.fold_in(key_list[19], 71), 0),
        "flow_target": plant(jax.random.randint(key_list[2], (IMAGES, H, W, 2), -80, 81), jax.random.fold_in(key_list[2], 1), -80, 80).astype(jnp.int32),
        "cell_labels": plant((jax.random.randint(key_list[3], (IMAGES, H, W), 0, 2) < 1).astype(jnp.int32), jax.random.fold_in(key_list[3], 1), 0, 1),
        "w_first": scatter_about(key_list[4], (10, IN_CH, CHANNELS), (9 * IN_CH) ** -0.5, 1.5, jnp.float32),
        "w_convs": scatter_about(key_list[5], (3, 9, CHANNELS, CHANNELS), (9 * CHANNELS) ** -0.5, 0.375, jnp.float32),
        "w_style": scatter_about(key_list[6], (2, CHANNELS, CHANNELS), CHANNELS ** -0.5, 1.0, jnp.float32),
        "w_head": scatter_about(key_list[7], (CHANNELS + 1, 3), CHANNELS ** -0.5, 1.0, jnp.float32),
        "batch_norm_table": draw_batch_norm_table(jax.random.fold_in(key_list[19], 71), 0),
        "mom_first": scatter_about(key_list[9], (10, IN_CH, CHANNELS), (2.0 / (IMAGES * H * W) ** 0.5), 0.022097087, jnp.float32),
        "mom_convs": scatter_about(key_list[10], (3, 9, CHANNELS, CHANNELS), (2.0 / (IMAGES * H * W) ** 0.5), 0.022097087, jnp.float32),
        "mom_style": scatter_about(key_list[11], (2, CHANNELS, CHANNELS), (2.0 / (IMAGES * H * W) ** 0.5), 0.022097087, jnp.float32),
        "mom_head": scatter_about(key_list[12], (CHANNELS + 1, 3), (2.0 / (IMAGES * H * W) ** 0.5), 0.022097087, jnp.float32),
        "mom_norms": scatter_about(key_list[13], (2, 4, CHANNELS), (2.0 / (IMAGES * H * W) ** 0.5), 0.022097087, jnp.float32),
        "sqr_first": jnp.clip(jnp.exp(jax.random.uniform(key_list[14], (10, IN_CH, CHANNELS), jnp.float32, math.log(3.0517578125e-05), math.log(0.00012207031))), 3.0517578125e-05, 0.00012207031),
        "sqr_convs": jnp.clip(jnp.exp(jax.random.uniform(key_list[15], (3, 9, CHANNELS, CHANNELS), jnp.float32, math.log(3.0517578125e-05), math.log(0.00012207031))), 3.0517578125e-05, 0.00012207031),
        "sqr_style": jnp.clip(jnp.exp(jax.random.uniform(key_list[16], (2, CHANNELS, CHANNELS), jnp.float32, math.log(3.0517578125e-05), math.log(0.00012207031))), 3.0517578125e-05, 0.00012207031),
        "sqr_head": jnp.clip(jnp.exp(jax.random.uniform(key_list[17], (CHANNELS + 1, 3), jnp.float32, math.log(3.0517578125e-05), math.log(0.00012207031))), 3.0517578125e-05, 0.00012207031),
        "sqr_norms": jnp.clip(jnp.exp(jax.random.uniform(key_list[18], (2, 4, CHANNELS), jnp.float32, math.log(3.0517578125e-05), math.log(0.00012207031))), 3.0517578125e-05, 0.00012207031),
    }


@jax.custom_vjp
def low(v):
    return lax.optimization_barrier(v.astype(jnp.bfloat16)).astype(jnp.float32)

@jax.custom_vjp
def low_back(v):
    return v

def low_keep(v):
    return (low(v), None)

def low_pass(kept, grad):
    return (grad,)

def back_keep(v):
    return (v, None)

def back_low(kept, grad):
    return (low(grad),)
low.defvjp(low_keep, low_pass)
low_back.defvjp(back_keep, back_low)
highest = lax.Precision.HIGHEST
norm_eps = 1e-05
flow_scale = 32.0
adam_eps = 1e-08
weight_decay = 0.01
beta_one = 0.5
beta_two = 0.5
rate_table = (0.2, 0.05, 0.15, 0.15, 0.2)

def conv_same(tensor, kernel):
    shaped = kernel.reshape(3, 3, kernel.shape[1], kernel.shape[2])
    return lax.conv_general_dilated(tensor, shaped, (1, 1), ((1, 1), (1, 1)), dimension_numbers=('NHWC', 'HWIO', 'NHWC'), precision=highest)

def batch_norm(tensor, scaling, offset):
    average = lax.optimization_barrier(jnp.mean(tensor, axis=(0, 1, 2)))
    spread = lax.optimization_barrier(jnp.mean(jnp.square(tensor - average), axis=(0, 1, 2)))
    return (tensor - average) * lax.rsqrt(spread + norm_eps) * scaling + offset

def smooth_pool(tensor):
    images, row_count, col_count, chan_count = tensor.shape
    blocks = tensor.reshape(images, row_count // 2, 2, col_count // 2, 2, chan_count)
    return jax.nn.logsumexp(blocks, axis=(2, 4))

def expand(tensor):
    return jnp.repeat(jnp.repeat(tensor, 2, axis=1), 2, axis=2)

def forward(params, image_batch, valid_mask, flow_target, cell_labels):
    w_first, w_convs, w_style, w_head, batch_norm_table = params
    first_low = low(w_first)
    convs_low = low(w_convs)
    head_low = low(w_head)
    pre_first = low_back(conv_same(image_batch, first_low[:9]))
    skip_proj = jnp.einsum('bhwc,cd->bhwd', image_batch, first_low[9], precision=highest)
    hidden_one = low(jax.nn.silu(batch_norm(pre_first, batch_norm_table[0, 0], batch_norm_table[1, 0])))
    summed_two = low_back(conv_same(hidden_one, convs_low[0]) + skip_proj)
    encoded = jax.nn.silu(batch_norm(summed_two, batch_norm_table[0, 1], batch_norm_table[1, 1]))
    pooled = smooth_pool(encoded)
    style = lax.optimization_barrier(jnp.mean(pooled, axis=(1, 2)))
    merged = low(expand(pooled) + encoded)
    style_one = jnp.dot(style, w_style[0], precision=highest)[:, None, None, :]
    decode_one = low_back(conv_same(merged, convs_low[1]) + style_one)
    hidden_three = low(jax.nn.silu(batch_norm(decode_one, batch_norm_table[0, 2], batch_norm_table[1, 2])))
    style_two = jnp.dot(style, w_style[1], precision=highest)[:, None, None, :]
    decode_two = low_back(conv_same(hidden_three, convs_low[2]) + style_two)
    decoded = low(jax.nn.silu(batch_norm(decode_two + merged, batch_norm_table[0, 3], batch_norm_table[1, 3])))
    head_out = low_back(jnp.einsum('bhwc,ck->bhwk', decoded, head_low[:-1], precision=highest) + head_low[-1])
    flows = head_out[..., :2]
    logits = head_out[..., 2]
    weights = valid_mask.astype(jnp.float32)
    targets = flow_target.astype(jnp.float32) / flow_scale
    labels = cell_labels.astype(jnp.float32)
    per_pixel = lax.optimization_barrier(jnp.sum(jnp.square(flows - targets), axis=-1)) + jax.nn.softplus(logits) - labels * logits
    loss_total = jnp.sum(weights * per_pixel)
    valid_count = jnp.sum(weights)
    return (loss_total / valid_count, (loss_total, valid_count))

def adamw(master, moment, square, grad, rate):
    new_moment = beta_one * moment + (1.0 - beta_one) * grad
    new_square = beta_two * square + (1.0 - beta_two) * grad * grad
    moment_hat = new_moment / (1.0 - beta_one ** STEP)
    square_hat = new_square / (1.0 - beta_two ** STEP)
    new_master = master - rate * (moment_hat / (jnp.sqrt(square_hat) + adam_eps) + weight_decay * master)
    return (new_master, new_moment, new_square)

def reference(image_batch, valid_mask, flow_target, cell_labels, w_first, w_convs, w_style, w_head, batch_norm_table, mom_first, mom_convs, mom_style, mom_head, mom_norms, sqr_first, sqr_convs, sqr_style, sqr_head, sqr_norms):
    params = (w_first, w_convs, w_style, w_head, batch_norm_table)
    moments = (mom_first, mom_convs, mom_style, mom_head, mom_norms)
    squares = (sqr_first, sqr_convs, sqr_style, sqr_head, sqr_norms)
    floats = image_batch.astype(jnp.float32)

    def loss_of(values):
        return forward(values, floats, valid_mask, flow_target, cell_labels)
    loss_value, pullback, sums = jax.vjp(loss_of, params, has_aux=True)
    grads = pullback(jnp.ones((), loss_value.dtype))[0]
    updated = [adamw(params[index], moments[index], squares[index], grads[index], rate_table[index]) for index in range(5)]
    return (sums[0], sums[1], updated[0][0], updated[0][1], updated[0][2], updated[0][0].astype(jnp.bfloat16), updated[1][0], updated[1][1], updated[1][2], updated[1][0].astype(jnp.bfloat16), updated[2][0], updated[2][1], updated[2][2], updated[3][0], updated[3][1], updated[3][2], updated[3][0].astype(jnp.bfloat16), updated[4][0], updated[4][1], updated[4][2])
```

```python
import jax
import jax.numpy as jnp
from jax import lax
from jax.sharding import PartitionSpec as P

STEP = 5


highest = lax.Precision.HIGHEST
norm_eps = 1e-05
flow_scale = 32.0
adam_eps = 1e-08
weight_decay = 0.01
beta_one = 0.5
beta_two = 0.5
rate_table = (0.2, 0.05, 0.15, 0.15, 0.2)


def with_halo(block, sides, width):
    for axis, dim in sides:
        count = lax.axis_size(axis)
        forward = [(i, i + 1) for i in range(count - 1)]
        backward = [(target, source) for source, target in forward]
        low = lax.ppermute(
            lax.slice_in_dim(block, block.shape[dim] - width, None, axis=dim), axis, forward
        )
        high = lax.ppermute(lax.slice_in_dim(block, 0, width, axis=dim), axis, backward)
        block = jnp.concatenate([low, block, high], axis=dim)
    return block


def widen(tensor):
    return with_halo(tensor, (("row", 1), ("col", 2)), 1)


def conv_valid(padded, kernel):
    shaped = kernel.reshape(3, 3, kernel.shape[1], kernel.shape[2])
    return lax.conv_general_dilated(
        padded,
        shaped,
        (1, 1),
        ((0, 0), (0, 0)),
        dimension_numbers=("NHWC", "HWIO", "NHWC"),
        preferred_element_type=jnp.float32,
    )


def flipped(kernel):
    shaped = kernel.reshape(3, 3, kernel.shape[1], kernel.shape[2])[::-1, ::-1]
    return jnp.swapaxes(shaped, 2, 3).reshape(9, kernel.shape[2], kernel.shape[1])


def conv_input_grad(grad_low, kernel):
    spread_out = conv_valid(jnp.pad(grad_low, ((0, 0), (2, 2), (2, 2), (0, 0))), flipped(kernel))
    row_edges = jnp.concatenate([spread_out[:, :1], spread_out[:, -1:]], axis=1)
    row_parts = with_halo(row_edges.astype(jnp.bfloat16), (("row", 1),), 1).astype(row_edges.dtype)
    inner = spread_out[:, 1:-1]
    inner = inner.at[:, 0].add(row_parts[:, 0]).at[:, -1].add(row_parts[:, 3])
    col_edges = jnp.concatenate([inner[:, :, :1], inner[:, :, -1:]], axis=2)
    col_parts = with_halo(col_edges.astype(jnp.bfloat16), (("col", 2),), 1).astype(col_edges.dtype)
    result = inner[:, :, 1:-1]
    return result.at[:, :, 0].add(col_parts[:, :, 0]).at[:, :, -1].add(col_parts[:, :, 3])


def tap_grads(padded, grad_low):
    row_count = grad_low.shape[1]
    col_count = grad_low.shape[2]
    return jnp.stack(
        [
            jnp.einsum(
                "bhwc,bhwd->cd",
                padded[:, tap_row : tap_row + row_count, tap_col : tap_col + col_count],
                grad_low,
                preferred_element_type=jnp.float32,
            )
            for tap_row in range(3)
            for tap_col in range(3)
        ]
    )


def everywhere(*parts):
    devices = lax.axis_size("row") * lax.axis_size("col")
    flat = jnp.concatenate([part.reshape(-1) for part in parts])
    lanes = -(-flat.size // 128)
    flat = jnp.pad(flat, (0, lanes * 128 - flat.size)).reshape(1, lanes, 128)
    spread = jnp.broadcast_to(flat, (devices, lanes, 128))
    gathered = lax.all_to_all(spread, ("row", "col"), 0, 0).reshape(devices, lanes * 128)
    found = []
    start = 0
    for part in parts:
        found.append(gathered[:, start : start + part.size].reshape((devices,) + part.shape))
        start += part.size
    return found


def total(*parts):
    return [jnp.sum(found, axis=0) for found in everywhere(*parts)]


def norm_stats(tensor, pixel_count):
    local_count = float(tensor.size // tensor.shape[-1])
    local_mean = jnp.sum(tensor, axis=(0, 1, 2)) / local_count
    centred = tensor - local_mean
    means, squares = everywhere(local_mean, jnp.sum(centred * centred, axis=(0, 1, 2)))
    average = jnp.sum(means, axis=0) * (local_count / pixel_count)
    between = jnp.sum(jnp.square(means - average), axis=0) * local_count
    spread = (jnp.sum(squares, axis=0) + between) / pixel_count
    inverse = lax.rsqrt(spread + norm_eps)
    return ((tensor - average) * inverse, inverse)


def norm_back(grad_norm, normal_form, inverse, scaling, pixel_count):
    shift_grad, scale_grad = total(
        jnp.sum(grad_norm, axis=(0, 1, 2)), jnp.sum(grad_norm * normal_form, axis=(0, 1, 2))
    )
    grad_input = (
        scaling * inverse * (grad_norm - (shift_grad + normal_form * scale_grad) / pixel_count)
    )
    return (grad_input, scale_grad, shift_grad)


def swish_derivative(tensor):
    logistic = jax.nn.sigmoid(tensor)
    return logistic * (1.0 + tensor * (1.0 - logistic))


def smooth_pool(tensor):
    images, row_count, col_count, chan_count = tensor.shape
    blocks = tensor.reshape(images, row_count // 2, 2, col_count // 2, 2, chan_count)
    block_top = jnp.max(blocks, axis=(2, 4), keepdims=True)
    expo_vals = jnp.exp(blocks - block_top)
    block_total = jnp.sum(expo_vals, axis=(2, 4), keepdims=True)
    pooled = (block_top + jnp.log(block_total))[:, :, 0, :, 0, :]
    shares = (expo_vals / block_total).reshape(tensor.shape)
    return (pooled, shares)


def expand(tensor):
    return jnp.repeat(jnp.repeat(tensor, 2, axis=1), 2, axis=2)


def block_sum(tensor):
    images, row_count, col_count, chan_count = tensor.shape
    return jnp.sum(
        tensor.reshape(images, row_count // 2, 2, col_count // 2, 2, chan_count), axis=(2, 4)
    )


def adamw(master, moment, square, grad, rate):
    new_moment = beta_one * moment + (1.0 - beta_one) * grad
    new_square = beta_two * square + (1.0 - beta_two) * grad * grad
    moment_hat = new_moment / (1.0 - beta_one**STEP)
    square_hat = new_square / (1.0 - beta_two**STEP)
    new_master = master - rate * (
        moment_hat / (jnp.sqrt(square_hat) + adam_eps) + weight_decay * master
    )
    return (new_master, new_moment, new_square)


def local(
    image_batch,
    valid_mask,
    flow_target,
    cell_labels,
    w_first,
    w_convs,
    w_style,
    w_head,
    batch_norm_table,
    mom_first,
    mom_convs,
    mom_style,
    mom_head,
    mom_norms,
    sqr_first,
    sqr_convs,
    sqr_style,
    sqr_head,
    sqr_norms,
):
    images, row_count, col_count, chan_in = image_batch.shape
    grid_total = lax.axis_size("row") * lax.axis_size("col")
    pixel_count = float(images * row_count * col_count * grid_total)
    pool_cells = float(row_count * col_count * grid_total // 4)
    first_low = w_first.astype(jnp.bfloat16)
    convs_low = w_convs.astype(jnp.bfloat16)
    head_low = w_head.astype(jnp.bfloat16)
    scale_factors = batch_norm_table[0]
    shift_values = batch_norm_table[1]
    padded_image = widen(image_batch)
    pre_first = conv_valid(padded_image, first_low[:9])
    skip_proj = jnp.einsum(
        "bhwc,cd->bhwd", image_batch, first_low[9], preferred_element_type=jnp.float32
    )
    first_preactivation, first_inverse_spread = norm_stats(pre_first, pixel_count)
    first_normalized = first_preactivation * scale_factors[0] + shift_values[0]
    hidden_one = jax.nn.silu(first_normalized).astype(jnp.bfloat16)
    padded_one = widen(hidden_one)
    summed_two = conv_valid(padded_one, convs_low[0]) + skip_proj
    second_preactivation, second_inverse_spread = norm_stats(summed_two, pixel_count)
    second_normalized = second_preactivation * scale_factors[1] + shift_values[1]
    encoded = jax.nn.silu(second_normalized)
    pooled, shares = smooth_pool(encoded)
    style = total(jnp.sum(pooled, axis=(1, 2)))[0] / pool_cells
    merged = (expand(pooled) + encoded).astype(jnp.bfloat16)
    padded_merged = widen(merged)
    style_one = jnp.dot(style, w_style[0], precision=highest)[:, None, None, :]
    decode_one = conv_valid(padded_merged, convs_low[1]) + style_one
    third_preactivation, inverse_three = norm_stats(decode_one, pixel_count)
    third_normalized = third_preactivation * scale_factors[2] + shift_values[2]
    hidden_three = jax.nn.silu(third_normalized).astype(jnp.bfloat16)
    padded_three = widen(hidden_three)
    style_two = jnp.dot(style, w_style[1], precision=highest)[:, None, None, :]
    residual = conv_valid(padded_three, convs_low[2]) + style_two + merged.astype(jnp.float32)
    fourth_preactivation, fourth_inverse_spread = norm_stats(residual, pixel_count)
    fourth_normalized = fourth_preactivation * scale_factors[3] + shift_values[3]
    decoded = jax.nn.silu(fourth_normalized).astype(jnp.bfloat16)
    head_out = jnp.einsum(
        "bhwc,ck->bhwk", decoded, head_low[:-1], preferred_element_type=jnp.float32
    ) + head_low[-1].astype(jnp.float32)
    flows = head_out[..., :2]
    logits = head_out[..., 2]
    weights = valid_mask.astype(jnp.float32)
    targets = flow_target.astype(jnp.float32) / flow_scale
    labels = cell_labels.astype(jnp.float32)
    per_pixel = (
        jnp.sum(jnp.square(flows - targets), axis=-1) + jax.nn.softplus(logits) - labels * logits
    )
    loss_total, valid_count = total(jnp.sum(weights * per_pixel), jnp.sum(weights))
    flow_grad = 2.0 * weights[..., None] * (flows - targets) / valid_count
    logit_grad = weights * (jax.nn.sigmoid(logits) - labels) / valid_count
    grad_out = jnp.concatenate([flow_grad, logit_grad[..., None]], axis=-1).astype(jnp.bfloat16)
    head_grad = jnp.concatenate(
        [
            jnp.einsum("bhwc,bhwk->ck", decoded, grad_out, preferred_element_type=jnp.float32),
            jnp.sum(grad_out.astype(jnp.float32), axis=(0, 1, 2))[None],
        ],
        axis=0,
    )
    decoded_gradient = jnp.einsum(
        "bhwk,ck->bhwc", grad_out, head_low[:-1], preferred_element_type=jnp.float32
    )
    grad_resid, scale_four, shift_four = norm_back(
        decoded_gradient * swish_derivative(fourth_normalized),
        fourth_preactivation,
        fourth_inverse_spread,
        scale_factors[3],
        pixel_count,
    )
    grad_two_low = grad_resid.astype(jnp.bfloat16)
    conv_three = tap_grads(padded_three, grad_two_low)
    grad_hidden_three = conv_input_grad(grad_two_low, convs_low[2])
    grad_one_full, scale_three, shift_three = norm_back(
        grad_hidden_three * swish_derivative(third_normalized),
        third_preactivation,
        inverse_three,
        scale_factors[2],
        pixel_count,
    )
    grad_one_low = grad_one_full.astype(jnp.bfloat16)
    conv_two = tap_grads(padded_merged, grad_one_low)
    grad_merged = grad_resid + conv_input_grad(grad_one_low, convs_low[1])
    style_one_sum, style_two_sum = total(
        jnp.sum(grad_one_low.astype(jnp.float32), axis=(1, 2)),
        jnp.sum(grad_two_low.astype(jnp.float32), axis=(1, 2)),
    )
    style_grad = jnp.stack(
        [
            jnp.dot(style.T, style_one_sum, precision=highest),
            jnp.dot(style.T, style_two_sum, precision=highest),
        ]
    )
    grad_style = jnp.dot(style_one_sum, w_style[0].T, precision=highest) + jnp.dot(
        style_two_sum, w_style[1].T, precision=highest
    )
    grad_pooled = block_sum(grad_merged) + grad_style[:, None, None, :] / pool_cells
    encoded_gradient = grad_merged + expand(grad_pooled) * shares
    grad_sum_full, scale_two, shift_two = norm_back(
        encoded_gradient * swish_derivative(second_normalized),
        second_preactivation,
        second_inverse_spread,
        scale_factors[1],
        pixel_count,
    )
    grad_sum_low = grad_sum_full.astype(jnp.bfloat16)
    conv_one = tap_grads(padded_one, grad_sum_low)
    proj_grad = jnp.einsum(
        "bhwc,bhwd->cd", image_batch, grad_sum_low, preferred_element_type=jnp.float32
    )
    first_hidden_gradient = conv_input_grad(grad_sum_low, convs_low[0])
    grad_first_full, scale_one, shift_one = norm_back(
        first_hidden_gradient * swish_derivative(first_normalized),
        first_preactivation,
        first_inverse_spread,
        scale_factors[0],
        pixel_count,
    )
    first_taps = tap_grads(padded_image, grad_first_full.astype(jnp.bfloat16))
    first_grad = jnp.concatenate([first_taps, proj_grad[None]], axis=0)
    first_sum, convs_sum, head_sum = lax.psum(
        (first_grad, jnp.stack([conv_one, conv_two, conv_three]), head_grad), ("row", "col")
    )
    norms_grad = jnp.stack(
        [
            jnp.stack([scale_one, scale_two, scale_three, scale_four]),
            jnp.stack([shift_one, shift_two, shift_three, shift_four]),
        ]
    )
    masters = (w_first, w_convs, w_style, w_head, batch_norm_table)
    moments = (mom_first, mom_convs, mom_style, mom_head, mom_norms)
    squares = (sqr_first, sqr_convs, sqr_style, sqr_head, sqr_norms)
    grads = (first_sum, convs_sum, style_grad, head_sum, norms_grad)
    updated = [
        adamw(masters[index], moments[index], squares[index], grads[index], rate_table[index])
        for index in range(5)
    ]
    return (
        loss_total,
        valid_count,
        updated[0][0],
        updated[0][1],
        updated[0][2],
        updated[0][0].astype(jnp.bfloat16),
        updated[1][0],
        updated[1][1],
        updated[1][2],
        updated[1][0].astype(jnp.bfloat16),
        updated[2][0],
        updated[2][1],
        updated[2][2],
        updated[3][0],
        updated[3][1],
        updated[3][2],
        updated[3][0].astype(jnp.bfloat16),
        updated[4][0],
        updated[4][1],
        updated[4][2],
    )


def solution(mesh):
    return jax.shard_map(
        local,
        mesh=mesh,
        in_specs=(
            P(None, "row", "col", None),
            P(None, "row", "col"),
            P(None, "row", "col", None),
            P(None, "row", "col"),
            P(),
            P(),
            P(),
            P(),
            P(),
            P(),
            P(),
            P(),
            P(),
            P(),
            P(),
            P(),
            P(),
            P(),
            P(),
        ),
        out_specs=(
            P(),
            P(),
            P(),
            P(),
            P(),
            P(),
            P(),
            P(),
            P(),
            P(),
            P(),
            P(),
            P(),
            P(),
            P(),
            P(),
            P(),
            P(),
            P(),
            P(),
        ),
        check_vma=False,
    )
```

```python
import functools

import jax
import jax.numpy as jnp
from jax import lax
from jax.experimental import pallas as pl
from jax.experimental.pallas import tpu as pltpu
from jax.sharding import PartitionSpec as P

STEP = 5

highest = lax.Precision.HIGHEST
norm_eps = 1e-05
flow_scale = 32.0
adam_eps = 1e-08
weight_decay = 0.01
beta_one = 0.5
beta_two = 0.5
rate_table = (0.2, 0.05, 0.15, 0.15, 0.2)

CH = 32
GRP = 4
LANES = 128
RIM = 8
PITCH = 64
F32 = jnp.float32
BF16 = jnp.bfloat16
VMEM_LIMIT = 40 * 1024 * 1024


def lane_of(shape):
    return lax.broadcasted_iota(jnp.int32, shape, len(shape) - 1)


def row_of(shape):
    return lax.broadcasted_iota(jnp.int32, shape, 0)


def group_of(shape):
    return lane_of(shape) >> 5


def fold(v):
    v = v + pltpu.roll(v, 64, axis=1)
    return v + pltpu.roll(v, 32, axis=1)


def spread(v, k):
    return fold(jnp.where(group_of(v.shape) == k, v, 0.0))


def partner(v):
    odd = (group_of(v.shape) & 1) == 1
    return jnp.where(odd, pltpu.roll(v, 32, axis=1), pltpu.roll(v, 96, axis=1))


def tile4(v):
    return jnp.concatenate([v, v, v, v], axis=1)


def col_sum(v):
    return jnp.sum(v, axis=0, keepdims=True)


def pack_images(v):
    group = group_of((4, LANES))
    out = jnp.zeros((4, LANES), F32)
    for b in range(4):
        out = jnp.where(group == b, v[4 * b : 4 * b + 4], out)
    return out


def unpack_images(u):
    return jnp.concatenate([spread(u, b) for b in range(4)], axis=0)


def low(v):
    return v.astype(BF16).astype(F32)


def sig_of(v):
    return 1.0 / (1.0 + jnp.exp(-v))


def slope(n, sig):
    return sig * (1.0 + n * (1.0 - sig))


def flat(v):
    return v.reshape(-1, LANES)


def conv(src, taps, row, rows, col, blocks, back=False):
    pieces = []
    for r in range(3):
        for c in range(3):
            dr, dc = (2 - r, 2 - c) if back else (r, c)
            pieces.append(flat(src[pl.ds(row + dr, rows), col + dc : col + dc + blocks]))
    wide = jnp.concatenate(pieces, axis=1)
    y = jnp.dot(wide, taps[...], preferred_element_type=F32)
    return y.reshape(rows, blocks, -1, LANES)


def loop(count, body):
    def step(i, carry):
        body(i)
        return carry

    lax.fori_loop(0, count, step, 0)


def blank_outside(ref, flags, rows, cols):
    height, width = ref.shape[0], ref.shape[1]

    @pl.when(flags[0] == 1)
    def _():
        ref[0:rows] = jnp.zeros((rows,) + ref.shape[1:], ref.dtype)

    @pl.when(flags[1] == 1)
    def _():
        ref[height - rows : height] = jnp.zeros((rows,) + ref.shape[1:], ref.dtype)

    @pl.when(flags[2] == 1)
    def _():
        ref[:, 0:cols] = jnp.zeros((height, cols) + ref.shape[2:], ref.dtype)

    @pl.when(flags[3] == 1)
    def _():
        ref[:, width - cols : width] = jnp.zeros((height, cols) + ref.shape[2:], ref.dtype)


def blank_ends(ref):
    height, width = ref.shape[0], ref.shape[1]
    ref[:, 0:1] = jnp.zeros((height, 1) + ref.shape[2:], ref.dtype)
    ref[:, width - 1 : width] = jnp.zeros((height, 1) + ref.shape[2:], ref.dtype)


def local_stats(v, count):
    mean = fold(col_sum(v)) / count
    centred = v - mean
    return mean, fold(col_sum(centred * centred))


def merge_stats(pay, local_count, pixel_count):
    devices = pay.shape[0]
    whole = col_sum(pay)
    mean = spread(whole, 0) / devices
    away = pay - mean
    between = spread(col_sum(away * away), 0)
    spread_sum = spread(whole, 1) + local_count * between
    return mean, lax.rsqrt(spread_sum / pixel_count + norm_eps)


def three(first, second, third):
    group = group_of(first.shape)
    return jnp.where(group == 0, first, jnp.where(group == 1, second, third))


def prepare(w_first, w_convs, w_style, w_head, table, banded, skip, taps, back, head_mat, head_bias, style_mat, tab):
    blocks = banded.shape[2] // LANES
    col = row_of((PITCH, LANES))
    out_col = group_of((PITCH, LANES))
    first = [[tile4(low(w_first[t][c : c + 1])) for c in range(2)] for t in range(10)]

    def one(j):
        at = pl.ds(pl.multiple_of(j * LANES, LANES), LANES)
        here = col - GRP * j - out_col
        for c in range(2):
            part = pl.ds(c * PITCH, PITCH)
            for r in range(3):
                val = jnp.zeros((PITCH, LANES), F32)
                for s in range(3):
                    val = jnp.where(here == s - 1, first[3 * r + s][c], val)
                banded[r, part, at] = val.astype(BF16)
            skip[part, at] = jnp.where(here == 0, first[9][c], 0.0).astype(BF16)

    loop(blocks, one)

    group = group_of((CH, LANES))

    def layer(i):
        for r in range(3):
            ks = [w_convs[i, 3 * r + s] for s in range(3)]
            wide = [tile4(k) for k in ks]
            tall = [jnp.concatenate([k, k, k, k], axis=0).T for k in ks]
            for d in range(3):
                for a in range(GRP):
                    at = (3 * r + d) * LANES + CH * a
                    val = jnp.zeros((CH, LANES), F32)
                    inv = jnp.zeros((CH, LANES), F32)
                    for s in range(3):
                        val = jnp.where(group == GRP * (d - 1) + a + 1 - s, wide[s], val)
                        inv = jnp.where(group == s - 1 + a - GRP * (d - 1), tall[s], inv)
                    taps[i, at : at + CH, :] = val.astype(BF16)
                    back[i, at : at + CH, :] = inv.astype(BF16)

    loop(3, layer)

    lane = lane_of((CH, 2 * LANES))
    head = jnp.zeros((CH, 2 * LANES), F32)
    bias = jnp.zeros((1, 2 * LANES), F32)
    for k in range(3):
        head = jnp.where((lane >> 6) == k, low(w_head[0:CH, k : k + 1]), head)
        bias = jnp.where((lane[0:1] >> 6) == k, low(w_head[CH : CH + 1, k : k + 1]), bias)
    head_bias[...] = bias
    for j in range(head_mat.shape[0] // LANES):
        for b in range(GRP):
            at = j * LANES + CH * b
            hit = (lane & 63) == GRP * (j + 1) + b
            head_mat[at : at + CH, :] = jnp.where(hit, head, 0.0).astype(BF16)
    for i in range(2):
        wide = tile4(w_style[i])
        for b in range(GRP):
            style_mat[i, CH * b : CH * b + CH, :] = jnp.where(group == b, wide, 0.0)
    for i in range(2):
        tab[4 * i : 4 * i + 4, :] = tile4(table[i])


def start_kernel(up, own, down, banded, valid, image, pay, *, local_count):
    rim, height, images = up.shape[0], own.shape[0], own.shape[1]
    image[0:rim] = up[:, :, 0:LANES]
    image[rim : rim + height] = own[:, :, 0:LANES]
    image[rim + height : rim + height + rim] = down[:, :, 0:LANES]
    blocks = banded.shape[2] // LANES - 4
    lo = 2 * LANES
    y = jnp.zeros((height * images, blocks * LANES), F32)
    for r in range(3):
        x = image[rim - 1 + r : rim - 1 + r + height].reshape(height * images, LANES)
        y = y + jnp.dot(x, banded[r, :, lo : lo + blocks * LANES], preferred_element_type=F32)
    total = jnp.zeros((1, LANES), F32)
    for j in range(blocks):
        total = total + col_sum(y[:, j * LANES : (j + 1) * LANES])
    mean = fold(total) / local_count
    square = jnp.zeros((1, LANES), F32)
    for j in range(blocks):
        centred = y[:, j * LANES : (j + 1) * LANES] - mean
        square = square + col_sum(centred * centred)
    count = jnp.sum(valid[...].astype(F32))
    row = three(mean, fold(square), jnp.full((1, LANES), count, F32))
    pay[...] = jnp.broadcast_to(row.reshape(1, 1, LANES), pay.shape)


def first_kernel(flags, got, image, banded, skip, taps, tab, hidden, xhat, summed, pay, vec, *, local_count, pixel_count):
    mean, inverse = merge_stats(got[:, 0, :], local_count, pixel_count)
    vec[...] = jnp.broadcast_to(inverse, vec.shape)
    gain, bias = tab[0:1], tab[4:5]
    rows, images = hidden.shape[0], hidden.shape[2]
    blocks = hidden.shape[1] - 2
    height = xhat.shape[0]
    rim = (rows - height) // 2

    def pair(jp):
        at = pl.ds(pl.multiple_of(jp * 2 * LANES, 2 * LANES), 2 * LANES)
        y = jnp.zeros((rows * images, 2 * LANES), F32)
        for r in range(3):
            x = image[r : r + rows].reshape(rows * images, LANES)
            y = y + jnp.dot(x, banded[r, :, at], preferred_element_type=F32)
        for half in range(2):
            norm = (y[:, half * LANES : (half + 1) * LANES] - mean) * inverse
            n = norm * gain + bias
            h = (n * sig_of(n)).astype(BF16)
            hidden[:, pl.ds(2 * jp + half + 1, 1)] = h.reshape(rows, 1, images, LANES)
            xhat[:, pl.ds(2 * jp + half, 1)] = norm[rim * images : (rim + height) * images].reshape(
                height, 1, images, LANES
            )

    loop(blocks // 2, pair)
    blank_ends(hidden)
    blank_outside(hidden, flags, rim, 3)
    out_rows = summed.shape[0]
    step = 4

    def chunk(i):
        row = i * step
        y = conv(hidden, taps, row, step, 0, blocks)
        x = image[pl.ds(row + 2, step)].reshape(step * images, LANES)
        side = jnp.dot(x, skip[...], preferred_element_type=F32).reshape(step, images, blocks * LANES)
        for j in range(blocks):
            summed[pl.ds(row, step), j] = y[:, j] + side[:, :, j * LANES : (j + 1) * LANES]

    loop(out_rows // step, chunk)
    low_row = (out_rows - height) // 2
    own = flat(summed[low_row : low_row + height, 2 : blocks - 2])
    m, s = local_stats(own, local_count)
    row = three(m, s, jnp.zeros((1, LANES), F32))
    pay[...] = jnp.broadcast_to(row.reshape(1, 1, LANES), pay.shape)


def pool_kernel(
    flags, got, summed, taps, tab, merged, xhat, slopes, shared, raw, pay, vec, *, local_count, pixel_count
):
    mean, inverse = merge_stats(got[:, 0, :], local_count, pixel_count)
    vec[...] = jnp.broadcast_to(inverse, vec.shape)
    gain, bias = tab[1:2], tab[5:6]
    rows, blocks, images = summed.shape[0], summed.shape[1], summed.shape[2]
    kept = xhat.shape[0]
    height = kept - 4
    skip_rows = (rows - kept) // 2

    def work(p, keep, own):
        xs, es, ns, ss = [], [], [], []
        for half in range(2):
            x = (flat(summed[2 * p + half]) - mean) * inverse
            n = x * gain + bias
            s = sig_of(n)
            xs.append(x)
            ns.append(n)
            ss.append(s)
            es.append(n * s)
        top = jnp.maximum(es[0], es[1])
        top = jnp.maximum(top, partner(top))
        exps = [jnp.exp(e - top) for e in es]
        whole = exps[0] + exps[1]
        whole = whole + partner(whole)
        pooled = top + jnp.log(whole)
        for half in range(2):
            m = (es[half] + pooled).astype(BF16)
            merged[pl.ds(2 * p + half, 1), 1 : blocks + 1] = m.reshape(1, blocks, images, LANES)
        if not keep:
            return None
        over = 1.0 / whole
        sums = []
        for half in range(2):
            ds = slope(ns[half], ss[half])
            sh = exps[half] * over * ds
            at = pl.ds(2 * p + half - skip_rows, 1)
            cut = lambda v: v.reshape(1, blocks, images, LANES)[:, 1 : blocks - 1]
            xhat[at] = cut(xs[half])
            slopes[at] = cut(ds)
            shared[at] = cut(sh)
            if own:
                sums.append((sh, sh * xs[half]))
        if not own:
            return None
        inner = lambda v: jnp.sum(v.reshape(blocks, images, LANES)[2 : blocks - 2], axis=0)
        return inner(pooled), inner(sums[0][0] + sums[1][0]), inner(sums[0][1] + sums[1][1])

    edge = skip_rows // 2
    own_lo = edge + 1
    own_pairs = height // 2

    def outer(i):
        work(i, False, False)
        work(rows // 2 - 1 - i, False, False)

    loop(edge, outer)
    work(edge, True, False)
    work(own_lo + own_pairs, True, False)

    def inner_step(i, carry):
        found = work(own_lo + i, True, True)
        return tuple(a + b for a, b in zip(carry, found))

    zero = jnp.zeros((images, LANES), F32)
    pool_sum, share_sum, share_x = lax.fori_loop(0, own_pairs, inner_step, (zero, zero, zero))
    blank_ends(merged)
    blank_outside(merged, flags, (rows - height) // 2, 3)
    out_rows = raw.shape[0]
    step = 3

    def chunk(i):
        raw[pl.ds(i * step, step)] = conv(merged, taps, i * step, step, 0, blocks)

    loop(out_rows // step, chunk)
    low_row = (out_rows - height) // 2
    own = raw[low_row : low_row + height, 2 : blocks - 2].reshape(-1, images, LANES)
    per_image = float(own.shape[0] * GRP)
    centre = fold(jnp.sum(own, axis=0)) / per_image
    away = own - centre[None]
    square = fold(col_sum(jnp.sum(away * away, axis=0)))
    devices = pay.shape[0]
    pay[:, 0] = jnp.broadcast_to(pack_images(centre)[None], (devices, 4, LANES))
    pay[:, 1] = jnp.broadcast_to(pack_images(0.5 * fold(pool_sum))[None], (devices, 4, LANES))
    pay[:, 2] = jnp.broadcast_to(square[None], (devices, 4, LANES))
    slots = jnp.concatenate([fold(share_sum), fold(share_x)], axis=0)
    pay[0 : 2 * images, 2, 1, :] = slots


def style_kernel(
    flags, got, raw, merged, taps, tab, style_mat, hidden, xhat, resid, pay, vec, style_out, *, local_count, pixel_count, pool_cells
):
    devices = got.shape[0]
    rows, blocks, images = raw.shape[0], raw.shape[1], raw.shape[2]
    centres = got[:, 0]
    packed = jnp.sum(centres, axis=0) / devices
    away = centres - packed[None]
    within = fold(col_sum(jnp.sum(away * away, axis=0)))
    style = unpack_images(jnp.sum(got[:, 1], axis=0)) / pool_cells
    style_out[...] = style
    one = jnp.dot(style, style_mat[0], precision=highest, preferred_element_type=F32)
    two = jnp.dot(style, style_mat[1], precision=highest, preferred_element_type=F32)
    centre = unpack_images(packed) + one
    mean = col_sum(centre) / images
    off = centre - mean
    between = col_sum(off * off)
    tail = jnp.sum(got[:, 2], axis=0)
    spread_sum = tail[0:1] + (local_count / images) * within + (pixel_count / images) * between
    inverse = lax.rsqrt(spread_sum / pixel_count + norm_eps)
    vec[...] = jnp.broadcast_to(inverse, vec.shape)
    gain, bias = tab[2:3], tab[6:7]
    shift = one - mean
    kept = xhat.shape[0]
    drop = (rows - kept) // 2

    def norm_row(i, keep):
        x = (raw[i] + shift[None]) * inverse[None]
        n = x * gain[None] + bias[None]
        h = (n * sig_of(n)).astype(BF16)
        hidden[i, 1 : blocks + 1] = h
        if keep:
            xhat[i - drop] = x[1 : blocks - 1]

    for i in range(drop):
        norm_row(i, False)
        norm_row(rows - 1 - i, False)
    loop(kept, lambda i: norm_row(i + drop, True))
    blank_ends(hidden)
    height = kept - 6
    blank_outside(hidden, flags, (rows - height) // 2, 3)
    out_rows = resid.shape[0]
    step = 4

    def chunk(i):
        row = i * step
        y = conv(hidden, taps, row, step, 1, blocks - 2)
        m = merged[pl.ds(row + 2, step), 2 : blocks].astype(F32)
        resid[pl.ds(row, step)] = y + two[None, None] + m

    loop(out_rows // step, chunk)
    low_row = (out_rows - height) // 2
    own = flat(resid[low_row : low_row + height, 1 : blocks - 3])
    m, s = local_stats(own, local_count)
    row = three(m, s, tail[1:2])
    pay[...] = jnp.broadcast_to(row.reshape(1, 1, LANES), pay.shape)


def head_kernel(
    got, got_count, resid, up, own, down, head_mat, head_bias, tab, grad, xhat, pay, vec, decoded, slopes, *, local_count, pixel_count
):
    mean, inverse = merge_stats(got[:, 0, :], local_count, pixel_count)
    vec[...] = jnp.broadcast_to(inverse, vec.shape)
    gain, bias = tab[3:4], tab[7:8]
    rows, blocks, images = resid.shape[0], resid.shape[1], resid.shape[2]
    height = own.shape[0]
    rim = (rows - height) // 2
    step = 2

    def norm_rows(i):
        at = pl.ds(i * step, step)
        x = (resid[at] - mean) * inverse
        n = x * gain + bias
        s = sig_of(n)
        xhat[at] = x
        slopes[at] = slope(n, s)
        decoded[at] = (n * s).astype(BF16)

    loop(rows // step, norm_rows)
    wide = jnp.concatenate([decoded[:, j].reshape(rows * images, LANES) for j in range(blocks)], axis=1)
    out = jnp.dot(wide, head_mat[...], preferred_element_type=F32) + head_bias[...]
    sides = jnp.concatenate([up[rim:], own[...], down[:rim]], axis=0)
    sides = sides.reshape(rows * images, 3 * LANES).astype(F32)
    target = sides[:, LANES : 2 * LANES] / flow_scale
    tail = sides[:, 2 * LANES :]
    swapped = pltpu.roll(tail, 64, axis=1)
    lane = lane_of(tail.shape)
    first_half = lane < 64
    mask = jnp.where(first_half, swapped, tail)
    column = lane & 63
    count = jnp.sum(got_count[:, 0, 64:65])
    diff = out[:, 0:LANES] - target
    logit = out[:, LANES:]
    label = tail
    hinge = jnp.maximum(logit, 0.0) + jnp.log1p(jnp.exp(-jnp.abs(logit)))
    loss = mask * diff * diff + jnp.where(first_half, mask * (hinge - label * logit), 0.0)
    grad_flow = (2.0 * mask * diff / count).astype(BF16)
    grad_logit = jnp.where(first_half, mask * (sig_of(logit) - label) / count, 0.0).astype(BF16)
    grad_out = jnp.concatenate([grad_flow, grad_logit], axis=1)
    mine = slice(rim * images, (rim + height) * images)
    inside = (column >= 8) & (column < 8 + GRP * (blocks - 2))
    loss_sum = jnp.sum(jnp.where(inside, loss, 0.0)[mine])
    mine_out = grad_out[mine]
    acc = jnp.zeros((2 * LANES, LANES), F32)
    at_col = (row_of((2 * LANES, LANES)) & 63) - group_of((2 * LANES, LANES))
    for j in range(1, blocks - 1):
        d = decoded[rim : rim + height, j].reshape(height * images, LANES)
        part = lax.dot_general(mine_out, d, (((0,), (0,)), ((), ())), preferred_element_type=F32)
        acc = jnp.where(at_col == GRP * (j + 1), part, acc)
    whole = [fold(col_sum(acc[PITCH * k : PITCH * k + PITCH])) for k in range(3)]
    outs = jnp.where(
        (lane_of((1, 2 * LANES)) & 63 >= 8) & (lane_of((1, 2 * LANES)) & 63 < 8 + GRP * (blocks - 2)),
        col_sum(mine_out.astype(F32)),
        0.0,
    )
    lane_one = lane_of((1, LANES))
    group = lane_one >> 5
    head_row = jnp.where(group == 0, whole[0], jnp.where(group == 1, whole[1], whole[2]))
    biases = [
        jnp.sum(jnp.where(lane_one < 64, outs[:, 0:LANES], 0.0)),
        jnp.sum(jnp.where(lane_one >= 64, outs[:, 0:LANES], 0.0)),
        jnp.sum(outs[:, LANES:]),
    ]
    for k in range(3):
        head_row = jnp.where(lane_one == 3 * CH + k, biases[k], head_row)
    shift_sum = jnp.zeros((1, LANES), F32)
    scale_sum = jnp.zeros((1, LANES), F32)
    for j in range(blocks):
        g = lax.dot_general(
            grad_out, head_mat[j * LANES : (j + 1) * LANES, :], (((1,), (1,)), ((), ())), preferred_element_type=F32
        )
        g = g * slopes[:, j].reshape(rows * images, LANES)
        grad[:, j] = g.reshape(rows, images, LANES)
        if 0 < j < blocks - 1:
            x = xhat[rim : rim + height, j].reshape(height * images, LANES)
            shift_sum = shift_sum + col_sum(g[mine])
            scale_sum = scale_sum + col_sum(g[mine] * x)
    row = three(fold(shift_sum), fold(scale_sum), jnp.full((1, LANES), loss_sum, F32))
    devices = pay.shape[0]
    pay[:, 0, :] = jnp.broadcast_to(row, (devices, LANES))
    pay[:, 1, :] = jnp.broadcast_to(head_row, (devices, LANES))


def back_sums(got):
    whole = col_sum(got)
    return spread(whole, 0), spread(whole, 1)


def residual_back_kernel(
    flags, got, grad, xhat, vec, xhat_below, back, tab, grad_low, below, kept_grad, pay, *, pixel_count
):
    shift, scale = back_sums(got[:, 0, :])
    rows, blocks, images = grad.shape[0], grad.shape[1], grad.shape[2]
    out_rows = below.shape[0]
    height = rows - 8
    factor = tab[3:4] * vec[0:1]
    shift, scale = shift / pixel_count, scale / pixel_count
    kept = kept_grad.shape[0]
    drop = (rows - kept) // 2

    def row_step(i, keep):
        g = factor[None] * (grad[i] - (shift[None] + xhat[i] * scale[None]))
        grad_low[i, 1 : blocks + 1] = g.astype(BF16)
        if keep:
            kept_grad[i - drop] = g

    for i in range(drop):
        row_step(i, False)
        row_step(rows - 1 - i, False)
    loop(kept, lambda i: row_step(i + drop, True))
    blank_ends(grad_low)
    blank_outside(grad_low, flags, (rows - height) // 2, 2)
    gain, bias = tab[2:3], tab[6:7]
    step = 2

    def chunk(i):
        row = i * step
        y = conv(grad_low, back, row, step, 0, blocks, True)
        n = xhat_below[pl.ds(row, step)] * gain + bias
        below[pl.ds(row, step)] = y * slope(n, sig_of(n))

    loop(out_rows // step, chunk)
    low_row = (out_rows - height) // 2
    g = flat(below[low_row : low_row + height, 1 : blocks - 1])
    x = flat(xhat_below[low_row : low_row + height, 1 : blocks - 1])
    mine = grad_low[(rows - height) // 2 : (rows + height) // 2, 2:blocks].astype(F32)
    image_sum = fold(jnp.sum(mine.reshape(-1, images, LANES), axis=0))
    row = three(fold(col_sum(g)), fold(col_sum(g * x)), jnp.zeros((1, LANES), F32))
    pay[...] = jnp.broadcast_to(row.reshape(1, 1, LANES), pay.shape)
    pay[0:images, 0, :] = jnp.where(group_of((images, LANES)) == 2, image_sum, row)


def merged_back_kernel(
    flags, got, grad, xhat, vec, kept_grad, slopes, shared, xhat_below, back, tab, scatter, grad_low, below, pay, *, pixel_count
):
    devices = got.shape[0]
    shift, scale = back_sums(got[:, 0, :])
    slot = spread(col_sum(got[:, 0, :]), 2)
    rows, blocks, images = grad.shape[0], grad.shape[1], grad.shape[2]
    out_rows = below.shape[0]
    height = rows - 6
    factor = tab[2:3] * vec[0:1]
    shift, scale = shift / pixel_count, scale / pixel_count

    def row_step(i):
        g = factor[None] * (grad[i] - (shift[None] + xhat[i] * scale[None]))
        grad_low[i, 1 : blocks + 1] = g.astype(BF16)

    loop(rows, row_step)
    blank_ends(grad_low)
    blank_outside(grad_low, flags, (rows - height) // 2, 2)

    def chunk(i):
        row = i * 2
        at = pl.ds(row, 2)
        g = conv(grad_low, back, row, 2, 0, blocks, True) + kept_grad[at]
        both = flat(g[0] + g[1])
        both = (both + partner(both)).reshape(1, blocks, images, LANES)
        below[at] = g * slopes[at] + both * shared[at]

    loop(out_rows // 2, chunk)
    low_row = (out_rows - height) // 2
    g = flat(below[low_row : low_row + height, 1 : blocks - 1])
    x = flat(xhat_below[low_row : low_row + height, 1 : blocks - 1])
    mine = grad_low[(rows - height) // 2 : (rows + height) // 2, 2:blocks].astype(F32)
    image_sum = fold(jnp.sum(mine.reshape(-1, images, LANES), axis=0))
    row = three(fold(col_sum(g)), fold(col_sum(g * x)), slot)
    pay[:, 0] = jnp.broadcast_to(row[None], (devices, 4, LANES))
    pay[:, 1] = jnp.broadcast_to(pack_images(image_sum)[None], (devices, 4, LANES))
    pay[0:CH, 0, 1:4, :] = scatter[:, 0:3, :]


def tap_sums(field, grad, out):
    rows, blocks = grad.shape[0], grad.shape[1]
    g = flat(grad)
    pieces = [flat(field[r : r + rows, c : c + blocks]) for r in range(3) for c in range(3)]
    found = lax.dot_general(g, jnp.concatenate(pieces, axis=1), (((0,), (0,)), ((), ())), preferred_element_type=F32)
    group = group_of((CH, LANES))
    taps = []
    for r in range(3):
        for s in range(3):
            val = jnp.zeros((CH, LANES), F32)
            for b in range(GRP):
                d, a = divmod(b + s - 1 + GRP, GRP)
                at = (3 * r + d) * LANES
                val = jnp.where(group == a, found[CH * b : CH * b + CH, at : at + LANES], val)
            taps.append(fold(val))
    for q in range(3):
        val = taps[4 * q]
        for b in range(1, min(4, 9 - 4 * q)):
            val = jnp.where(group == b, taps[4 * q + b], val)
        out[:, q, :] = val


def taps_kernel(field, grad, out, *, rows, cols, grad_rows, grad_cols):
    height, width = grad_rows[1] - grad_rows[0], grad_cols[1] - grad_cols[0]
    tap_sums(
        field[rows : rows + height + 2, cols : cols + width + 2],
        grad[grad_rows[0] : grad_rows[1], grad_cols[0] : grad_cols[1]],
        out,
    )


def summed_back_kernel(
    flags, got, got_slots, grad, shared, xhat, vec, style_mat, back, tab, xhat_below, field, scatter, grad_low, below, pay, sums, image_sums, *, pixel_count, pool_cells
):
    devices = got.shape[0]
    rows, blocks, images = grad.shape[0], grad.shape[1], grad.shape[2]
    height = xhat_below.shape[0]
    one = unpack_images(jnp.sum(got[:, 1], axis=0))
    two = spread(got[0:images, 0, 0, :], 2)
    image_sums[0] = one
    image_sums[1] = two
    dims = (((1,), (1,)), ((), ()))
    grad_style = lax.dot_general(one, style_mat[0], dims, precision=highest, preferred_element_type=F32)
    grad_style = grad_style + lax.dot_general(two, style_mat[1], dims, precision=highest, preferred_element_type=F32)
    grad_style = grad_style / pool_cells
    first = jnp.sum(got[:, 0], axis=0)[0:1]
    shift = spread(first, 0) + col_sum(grad_style * spread(got_slots[0:images, 0, :], 2))
    scale = spread(first, 1) + col_sum(grad_style * spread(got_slots[images : 2 * images, 0, :], 2))
    sums[...] = jnp.where(row_of((8, LANES)) == 0, scale, shift)
    factor = tab[1:2] * vec[0:1]
    shift, scale = shift / pixel_count, scale / pixel_count
    out_rows = grad_low.shape[0]

    def row_step(i):
        g = grad[i + 1] + shared[i + 1] * grad_style[None]
        g = factor[None] * (g - (shift[None] + xhat[i + 1] * scale[None]))
        grad_low[i, 1 : blocks + 1] = g.astype(BF16)

    loop(out_rows, row_step)
    blank_ends(grad_low)
    blank_outside(grad_low, flags, 1, 2)
    gain, bias = tab[0:1], tab[4:5]
    step = 4

    def chunk(i):
        row = i * step
        y = conv(grad_low, back, row, step, 1, blocks - 2, True)
        n = xhat_below[pl.ds(row, step), 2:blocks] * gain + bias
        below[pl.ds(row, step)] = y * slope(n, sig_of(n))

    loop(height // step, chunk)
    g = flat(below[...])
    x = flat(xhat_below[:, 2:blocks])
    row = fold(col_sum(g))
    row = three(row, fold(col_sum(g * x)), jnp.zeros((1, LANES), F32))
    gathered = jnp.sum(got[:, 0], axis=0)
    pay[:, 0] = jnp.broadcast_to(jnp.where(row_of((4, LANES)) == 0, row, gathered)[None], (devices, 4, LANES))
    pay[0:CH, 1] = scatter[...]
    if devices > CH:
        pay[CH:, 1] = jnp.zeros((devices - CH, 4, LANES), F32)
        pay[CH:, 2] = jnp.zeros((devices - CH, 4, LANES), F32)
    tap_sums(field[6 : 8 + height, 2 : blocks + 2], grad_low[1 : 1 + height, 2:blocks], pay.at[0:CH, 2])
    pay[0:CH, 2, 3, :] = jnp.zeros((CH, LANES), F32)


def pixel_taps(image, grad, row, shift):
    height, blocks, images = grad.shape[0], grad.shape[1], grad.shape[2]
    x = image[row : row + height].reshape(height * images, LANES)
    found = [jnp.zeros((LANES, LANES), F32) for _ in shift]
    here = (row_of((LANES, LANES)) & 63) - group_of((LANES, LANES))
    for j in range(blocks):
        g = grad[:, j].reshape(height * images, LANES)
        part = lax.dot_general(x, g, (((0,), (0,)), ((), ())), preferred_element_type=F32)
        for k, s in enumerate(shift):
            found[k] = jnp.where(here == GRP * (j + 2) + s, part, found[k])
    return [[fold(col_sum(f[PITCH * c : PITCH * c + PITCH])) for c in range(2)] for f in found]


def first_back_kernel(got, grad, xhat, vec, tab, image, summed_low, pay, *, pixel_count):
    devices = got.shape[0]
    height, blocks = grad.shape[0], grad.shape[1]
    whole = jnp.sum(got[:, 0], axis=0)[0:1]
    shift, scale = spread(whole, 0), spread(whole, 1)
    factor = tab[0:1] * vec[0:1]
    x = xhat[:, 2 : blocks + 2]
    low_grad = (factor * (grad[...] - (shift + x * scale) / pixel_count)).astype(BF16)
    entries = []
    for r in range(3):
        for tap in pixel_taps(image, low_grad, RIM - 1 + r, (-1, 0, 1)):
            entries.extend(tap)
    entries.extend(pixel_taps(image, summed_low[1 : 1 + height, 2 : blocks + 2], RIM, (0,))[0])
    group = group_of((1, LANES))
    rows = []
    for q in range(5):
        val = entries[4 * q]
        for b in range(1, 4):
            val = jnp.where(group == b, entries[4 * q + b], val)
        rows.append(val)
    conv_one = jnp.sum(got[:, 1], axis=0)
    conv_zero = jnp.sum(got[:, 2], axis=0)
    chunk = [
        jnp.concatenate(rows[0:4], axis=0),
        jnp.concatenate([rows[4], conv_one[0:3]], axis=0),
        conv_zero,
    ]
    for k in range(3):
        pay[:, k] = jnp.broadcast_to(chunk[k][None], (devices, 4, LANES))


def adamw(master, moment, square, grad, rate):
    new_moment = beta_one * moment + (1.0 - beta_one) * grad
    new_square = beta_two * square + (1.0 - beta_two) * grad * grad
    moment_hat = new_moment / (1.0 - beta_one**STEP)
    square_hat = new_square / (1.0 - beta_two**STEP)
    new_master = master - rate * (moment_hat / (jnp.sqrt(square_hat) + adam_eps) + weight_decay * master)
    return new_master, new_moment, new_square


def update_kernel(
    got, got_first, got_head, got_two, got_count, sums, style, image_sums,
    w_first, w_convs, w_style, w_head, table,
    m_first, m_convs, m_style, m_head, m_norms,
    s_first, s_convs, s_style, s_head, s_norms,
    loss_out, count_out,
    first_master, first_moment, first_square, first_copy,
    convs_master, convs_moment, convs_square, convs_copy,
    style_master, style_moment, style_square,
    head_master, head_moment, head_square, head_copy,
    norms_master, norms_moment, norms_square,
):
    count_out[0, 0] = jnp.sum(got_count[:, 0, 64:65])
    loss_out[0, 0] = jnp.sum(got_head[:, 0, 64:65])

    def put(at, master, moment, square, grad, rate, outs, copy):
        found = adamw(master[at], moment[at], square[at], grad, rate)
        for out, value in zip(outs, found):
            out[at] = value
        if copy is not None:
            copy[at] = found[0].astype(BF16)

    sources = [got[0:CH, 2, 0:3, :], got[0:CH, 1, 1:4, :], got_first[0:CH, 0, 1:4, :]]
    refs = (w_convs, m_convs, s_convs)
    outs = (convs_master, convs_moment, convs_square)
    for i in range(3):
        for q in range(3):
            taps = min(4, 9 - 4 * q)
            grad = sources[i][:, q, :].T
            for b in range(taps):
                put((i, 4 * q + b), *refs, grad[CH * b : CH * b + CH], rate_table[1], outs, convs_copy)

    first = jnp.concatenate([jnp.sum(got[:, 0], axis=0), jnp.sum(got[:, 1], axis=0)[0:1]], axis=0)
    for t in range(10):
        pair = [spread(first[e // 4 : e // 4 + 1], e % 4)[:, 0:CH] for e in (2 * t, 2 * t + 1)]
        grad = jnp.concatenate(pair, axis=0)
        put((t,), w_first, m_first, s_first, grad, rate_table[0], (first_master, first_moment, first_square), first_copy)

    dims = (((0,), (0,)), ((), ()))
    for i in range(2):
        grad = lax.dot_general(style[...], image_sums[i], dims, precision=highest, preferred_element_type=F32)
        put((i,), w_style, m_style, s_style, grad[0:CH, 0:CH], rate_table[2], (style_master, style_moment, style_square), None)

    head = col_sum(got_head[:, 1, :])
    shape = (40, LANES)
    entry = row_of(shape)
    lane = lane_of(shape)
    grad = jnp.zeros(shape, F32)
    for k in range(3):
        hit = lane == jnp.where(entry < CH, CH * k + entry, 3 * CH + k)
        value = jnp.sum(jnp.where(hit, head, 0.0), axis=1, keepdims=True)
        grad = jnp.where(lane == k, value, grad)
    put((slice(None),), w_head, m_head, s_head, grad[0 : CH + 1, 0:3], rate_table[3], (head_master, head_moment, head_square), head_copy)

    three_sums = col_sum(got_head[:, 0, :])
    two_sums = col_sum(got_two[:, 0, :])
    zero_sums = jnp.sum(got_first[:, 0], axis=0)[0:1]
    scales = [spread(zero_sums, 1), sums[0:1], spread(two_sums, 1), spread(three_sums, 1)]
    shifts = [spread(zero_sums, 0), sums[1:2], spread(two_sums, 0), spread(three_sums, 0)]
    for i, rows in enumerate((scales, shifts)):
        grad = jnp.concatenate(rows, axis=0)[:, 0:CH]
        put((i,), table, m_norms, s_norms, grad, rate_table[4], (norms_master, norms_moment, norms_square), None)


def call(kernel, outs, *operands, scalars=0, scratch=(), scalar_outs=(), name):
    smem = pl.BlockSpec(memory_space=pltpu.SMEM)
    vmem = pl.BlockSpec(memory_space=pltpu.VMEM)
    return pl.pallas_call(
        kernel,
        out_shape=[jax.ShapeDtypeStruct(shape, dtype) for shape, dtype in outs],
        in_specs=[smem] * scalars + [vmem] * (len(operands) - scalars),
        out_specs=[smem if i in scalar_outs else vmem for i in range(len(outs))],
        scratch_shapes=[pltpu.VMEM(shape, dtype) for shape, dtype in scratch],
        compiler_params=pltpu.CompilerParams(vmem_limit_bytes=VMEM_LIMIT),
        name=name,
    )(*operands)


def exchange(pay):
    return lax.all_to_all(pay, ("row", "col"), 0, 0)


def shifted(block, axis):
    count = lax.axis_size(axis)
    forward = [(i, i + 1) for i in range(count - 1)]
    backward = [(target, source) for source, target in forward]
    return forward, backward


def local(
    image_batch, valid_mask, flow_target, cell_labels,
    w_first, w_convs, w_style, w_head, batch_norm_table,
    mom_first, mom_convs, mom_style, mom_head, mom_norms,
    sqr_first, sqr_convs, sqr_style, sqr_head, sqr_norms,
):
    images, height, width, _ = image_batch.shape
    devices = lax.axis_size("row") * lax.axis_size("col")
    local_count = float(images * height * width)
    pixel_count = local_count * devices
    pool_cells = float(height * width * devices // 4)
    blocks = width // GRP
    wide = blocks + 4
    part = functools.partial
    counts = dict(local_count=local_count, pixel_count=pixel_count)

    row, col = lax.axis_index("row"), lax.axis_index("col")
    flags = jnp.stack(
        [row == 0, row == lax.axis_size("row") - 1, col == 0, col == lax.axis_size("col") - 1]
    ).astype(jnp.int32)

    sides = jnp.concatenate(
        [
            jnp.transpose(image_batch, (1, 0, 3, 2)),
            jnp.transpose(flow_target.astype(BF16), (1, 0, 3, 2)),
            jnp.transpose(cell_labels.astype(BF16), (1, 0, 2))[:, :, None],
            jnp.transpose(valid_mask.astype(BF16), (1, 0, 2))[:, :, None],
        ],
        axis=2,
    )
    forward, backward = shifted(sides, "col")
    left = lax.ppermute(sides[..., width - RIM :], "col", forward)
    right = lax.ppermute(sides[..., :RIM], "col", backward)
    gap = jnp.zeros(sides.shape[:3] + (PITCH - width - 2 * RIM,), BF16)
    own = jnp.concatenate([left, sides, right, gap], axis=3).reshape(height, images, 6 * PITCH)
    forward, backward = shifted(own, "row")
    up = lax.ppermute(own[height - RIM :], "row", forward)
    down = lax.ppermute(own[:RIM], "row", backward)

    banded, skip, taps, back, head_mat, head_bias, style_mat, tab = call(
        prepare,
        [
            ((3, LANES, wide * LANES), BF16),
            ((LANES, wide * LANES), BF16),
            ((3, 9 * LANES, LANES), BF16),
            ((3, 9 * LANES, LANES), BF16),
            (((blocks + 2) * LANES, 2 * LANES), BF16),
            ((1, 2 * LANES), F32),
            ((2, LANES, LANES), F32),
            ((8, LANES), F32),
        ],
        w_first, w_convs, w_style, w_head, batch_norm_table,
        name="prepare",
    )

    tail = (images, LANES)
    vec = ((8, LANES), F32)
    one_row = ((devices, 1, LANES), F32)
    image, pay = call(
        part(start_kernel, local_count=local_count),
        [((height + 2 * RIM, images, LANES), BF16), one_row],
        up, own, down, banded, valid_mask,
        name="image_stats",
    )
    got_zero = exchange(pay)

    hidden_one, xhat_zero, summed, pay, inv_zero = call(
        part(first_kernel, **counts),
        [
            ((height + 14, wide + 2) + tail, BF16),
            ((height, wide) + tail, F32),
            ((height + 12, wide) + tail, F32),
            one_row,
            vec,
        ],
        flags, got_zero, image, banded, skip, taps[0], tab,
        scalars=1, name="first_block",
    )
    got_one = exchange(pay)

    near = ((height + 4, blocks + 2) + tail, F32)
    merged, xhat_one, slope_one, shared, raw, pay, inv_one = call(
        part(pool_kernel, **counts),
        [
            ((height + 12, wide + 2) + tail, BF16),
            near,
            near,
            near,
            ((height + 10, wide) + tail, F32),
            ((devices, 3, 4, LANES), F32),
            vec,
        ],
        flags, got_one, summed, taps[1], tab,
        scalars=1, name="pool_and_merge",
    )
    got_style = exchange(pay)

    hidden_three, xhat_two, resid, pay, inv_two, style = call(
        part(style_kernel, pool_cells=pool_cells, **counts),
        [
            ((height + 10, wide + 2) + tail, BF16),
            ((height + 6, blocks + 2) + tail, F32),
            ((height + 8, blocks + 2) + tail, F32),
            one_row,
            vec,
            (tail, F32),
        ],
        flags, got_style, raw, merged, taps[2], tab, style_mat,
        scalars=1, name="decoder",
    )
    got_three = exchange(pay)

    at_head = ((height + 8, blocks + 2) + tail, F32)
    grad_three, xhat_three, pay, inv_three = call(
        part(head_kernel, **counts),
        [at_head, at_head, ((devices, 2, LANES), F32), vec],
        got_three, got_zero, resid, up, own, down, head_mat, head_bias, tab,
        scratch=[((height + 8, blocks + 2) + tail, BF16), at_head],
        name="head",
    )
    got_head = exchange(pay)

    low_two, grad_two, grad_resid, pay = call(
        part(residual_back_kernel, pixel_count=pixel_count),
        [
            ((height + 8, wide) + tail, BF16),
            ((height + 6, blocks + 2) + tail, F32),
            near,
            one_row,
        ],
        flags, got_head, grad_three, xhat_three, inv_three, xhat_two, back[2], tab,
        scalars=1, name="residual_back",
    )
    got_two = exchange(pay)
    (taps_two,) = call(
        part(taps_kernel, rows=4, cols=2, grad_rows=(4, 4 + height), grad_cols=(2, 2 + blocks)),
        [((CH, 4, LANES), F32)],
        hidden_three, low_two,
        name="taps_two",
    )

    low_one, grad_one, pay = call(
        part(merged_back_kernel, pixel_count=pixel_count),
        [((height + 6, wide) + tail, BF16), near, ((devices, 2, 4, LANES), F32)],
        flags, got_two, grad_two, xhat_two, inv_two, grad_resid, slope_one, shared, xhat_one, back[1], tab, taps_two,
        scalars=1, name="merged_back",
    )
    got_one_back = exchange(pay)
    (taps_one,) = call(
        part(taps_kernel, rows=5, cols=2, grad_rows=(3, 3 + height), grad_cols=(2, 2 + blocks)),
        [((CH, 4, LANES), F32)],
        merged, low_one,
        name="taps_one",
    )

    low_zero, grad_zero, pay, sums_one, image_sums = call(
        part(summed_back_kernel, pixel_count=pixel_count, pool_cells=pool_cells),
        [
            ((height + 2, wide) + tail, BF16),
            ((height, blocks) + tail, F32),
            ((devices, 3, 4, LANES), F32),
            vec,
            ((2,) + tail, F32),
        ],
        flags, got_one_back, got_three, grad_one, shared, xhat_one, inv_one, style_mat, back[0], tab, xhat_zero,
        hidden_one, taps_one,
        scalars=1, name="summed_back",
    )
    got_first = exchange(pay)

    (pay,) = call(
        part(first_back_kernel, pixel_count=pixel_count),
        [((devices, 3, 4, LANES), F32)],
        got_first, grad_zero, xhat_zero, inv_zero, tab, image, low_zero,
        name="first_back",
    )
    got_last = exchange(pay)

    params = (w_first, w_convs, w_style, w_head, batch_norm_table)
    moments = (mom_first, mom_convs, mom_style, mom_head, mom_norms)
    squares = (sqr_first, sqr_convs, sqr_style, sqr_head, sqr_norms)
    outs = [((1, 1), F32), ((1, 1), F32)]
    for index, param in enumerate(params):
        outs += [(param.shape, F32)] * 3
        if index in (0, 1, 3):
            outs.append((param.shape, BF16))
    found = call(
        update_kernel,
        outs,
        got_last, got_first, got_head, got_two, got_zero, sums_one, style, image_sums,
        *params, *moments, *squares,
        scalar_outs=(0, 1), name="update",
    )
    return (found[0].reshape(()), found[1].reshape(())) + tuple(found[2:])


def solution(mesh):
    field = P(None, "row", "col", None)
    plane = P(None, "row", "col")
    return jax.shard_map(
        local,
        mesh=mesh,
        in_specs=(field, plane, field, plane) + (P(),) * 15,
        out_specs=(P(),) * 20,
        check_vma=False,
    )
```

```python
import functools

import jax
import jax.numpy as jnp
from jax import lax
from jax.experimental import pallas as pl
from jax.experimental.pallas import tpu as pltpu
from jax.sharding import PartitionSpec as P

STEP = 5

highest = lax.Precision.HIGHEST
norm_eps = 1e-05
flow_scale = 32.0
adam_eps = 1e-08
weight_decay = 0.01
beta_one = 0.5
beta_two = 0.5
rate_table = (0.2, 0.05, 0.15, 0.15, 0.2)

CH = 32
GRP = 4
SEG = 8
LANES = 128
RIM = 8
FLOW, LABEL, MASK = 16, 32, 40
LEFT, RIGHT = 64, 96
F32 = jnp.float32
BF16 = jnp.bfloat16
VMEM_LIMIT = 36 * 1024 * 1024
STORE_BYTES = 32 * 1024 * 1024
FORWARD = 10 * LANES
BACK = 9 * LANES
HEAD_AT = 3 * FORWARD + 3 * BACK


def lane_of(shape):
    return lax.broadcasted_iota(jnp.int32, shape, len(shape) - 1)


def row_of(shape):
    return lax.broadcasted_iota(jnp.int32, shape, 0)


def group_of(shape):
    return lane_of(shape) >> 5


def fold(v):
    v = v + pltpu.roll(v, 64, axis=1)
    return v + pltpu.roll(v, 32, axis=1)


def spread(v, k):
    return fold(jnp.where(group_of(v.shape) == k, v, 0.0))


def partner(v):
    odd = (group_of(v.shape) & 1) == 1
    return jnp.where(odd, pltpu.roll(v, 32, axis=1), pltpu.roll(v, 96, axis=1))


def tile4(v):
    return jnp.concatenate([v, v, v, v], axis=1)


def col_sum(v):
    return jnp.sum(v, axis=0, keepdims=True)


def zero_row():
    return jnp.zeros((1, LANES), F32)


def groups(*values):
    group = group_of(values[0].shape)
    out = values[-1]
    for k in range(len(values) - 2, -1, -1):
        out = jnp.where(group == k, values[k], out)
    return out


def low(v):
    return v.astype(BF16).astype(F32)


def sig_of(v):
    return 0.5 + 0.5 * jnp.tanh(0.5 * v)


def slope(n, sig):
    return sig * (1.0 + n * (1.0 - sig))


def slope_at(x, gain, bias):
    n = x * gain + bias
    return slope(n, sig_of(n))


def flat(v):
    return v.reshape(-1, LANES)


def loop(count, body):
    def step(i, carry):
        body(i)
        return carry

    lax.fori_loop(0, count, step, 0)


def copies(sems, *pairs):
    found = []
    for i, (source, target) in enumerate(pairs):
        found.append(pltpu.make_async_copy(source, target, sems.at[i]))
        found[-1].start()
    return found


def wait(started):
    for copy in started:
        copy.wait()


def shift_segments(v, way):
    half = v.shape[1]
    at = lax.broadcasted_iota(jnp.int32, v.shape, 1)
    if way == 1:
        return jnp.where(at == 0, 0.0, pltpu.roll(v, 1, axis=1))
    return jnp.where(at == half - 1, 0.0, pltpu.roll(v, half - 1, axis=1))


def beside(first, second):
    half = first.shape[1] // 2
    left = jnp.concatenate([shift_segments(second[:, half:], 1), second[:, :half]], axis=1)
    right = jnp.concatenate([first[:, half:], shift_segments(first[:, :half], -1)], axis=1)
    return left, right


def put_low(ref, row, first, second):
    left, right = beside(first, second)
    edge = jnp.where(lane_of(left.shape) < 64, right, left)
    at = pl.ds(row + 1, first.shape[0])
    for k, v in enumerate((first, second, edge)):
        ref[at, k] = v.astype(BF16)


def blank(ref):
    zero = jnp.zeros((1,) + ref.shape[1:], ref.dtype)
    ref[0:1] = zero
    ref[ref.shape[0] - 1 : ref.shape[0]] = zero


def views(src, row, rows):
    return [flat(src[pl.ds(row + r, rows), k]) for r in range(3) for k in (2, 0, 1)]


def conv(src, mat, row, rows, *more):
    wide = jnp.concatenate(views(src, row, rows) + list(more), axis=1)
    return jnp.dot(wide, mat[...], preferred_element_type=F32)


def blocks_of(y, rows):
    return [y[:, k * LANES : (k + 1) * LANES].reshape(rows, -1, LANES) for k in range(2)]


def local_stats(v, first, rows, count):
    def add(i, total):
        return total + v[first + i, 0] + v[first + i, 1]

    zero = jnp.zeros(v.shape[2:], F32)
    mean = fold(col_sum(lax.fori_loop(0, rows, add, zero, unroll=8))) / count

    def add_square(i, total):
        a, b = v[first + i, 0] - mean, v[first + i, 1] - mean
        return total + a * a + b * b

    return mean, fold(col_sum(lax.fori_loop(0, rows, add_square, zero, unroll=8)))


def merge_stats(pay, local_count, pixel_count):
    devices = pay.shape[0]
    whole = col_sum(pay)
    mean = spread(whole, 0) / devices
    away = pay - mean
    between = spread(col_sum(away * away), 0)
    spread_sum = spread(whole, 1) + local_count * between
    return mean, lax.rsqrt(spread_sum / pixel_count + norm_eps)


def send(pay, row):
    pay[...] = jnp.broadcast_to(row.reshape(1, 1, LANES), pay.shape)


def notes(ref, *rows):
    for i, row in enumerate(rows):
        ref[i : i + 1, :] = row


def taps_at(store, i):
    return store.at[FORWARD * i : FORWARD * i + (BACK if i else FORWARD)]


def back_at(store, i):
    return store.at[3 * FORWARD + BACK * i : 3 * FORWARD + BACK * (i + 1)]


def pack_kernel(image, flow, labels, valid, out):
    images, height, _, width = image.shape
    parts = out.shape[0] // images
    fields = [image[:, :, c, :].astype(F32) for c in range(2)]
    fields += [flow[:, :, c, :].astype(F32) for c in range(2)]
    fields += [labels[...].astype(F32), valid[...].astype(F32)]
    halves = width // 16
    shape = (width, halves * LANES)
    lane = lane_of(shape)
    column = (lane >> 7) * 16 + ((lane >> 6) & 1) * 8 + (lane & 7)
    hit = row_of(shape) == column
    which = (lane >> 3) & 7
    total = jnp.zeros((images * height, halves * LANES), F32)
    for k, v in enumerate(fields):
        x = v.reshape(images * height, width).astype(BF16)
        mat = jnp.where(hit & (which == k), 1.0, 0.0).astype(BF16)
        total = total + jnp.dot(x, mat, preferred_element_type=F32)
    for b in range(images):
        rows = total[b * height : (b + 1) * height]
        slot = jnp.concatenate([rows[:, h * LANES : (h + 1) * LANES] for h in range(halves)], axis=0).astype(BF16)
        for p in range(parts):
            out[b * parts + p] = slot


def prepare(w_first, w_convs, w_style, w_head, table, store, first_mat, head_bias, style_mat, tab, mats, sems):
    lane = lane_of((LANES, 2 * LANES))
    at = row_of((LANES, 2 * LANES))
    column = lane >> 5
    kind = at >> 5
    here = (at & 7) + jnp.where(kind == LEFT // 32, -SEG, jnp.where(kind == RIGHT // 32, SEG, 0))
    image_lane = (kind != 1) & ((at & 31) < 16)
    channel = (at >> 3) & 1
    rows = [[None] * 2 for _ in range(10)]
    for t in range(10):
        for c in range(2):
            v = tile4(low(w_first[t][c : c + 1]))
            rows[t][c] = jnp.concatenate([v, v], axis=1)
    for r in range(3):
        val = jnp.zeros((LANES, 2 * LANES), F32)
        for s in range(3):
            for c in range(2):
                hit = image_lane & (channel == c) & (here == column + s - 1)
                val = jnp.where(hit, rows[3 * r + s][c], val)
        first_mat[r] = val.astype(BF16)
    val = jnp.zeros((LANES, 2 * LANES), F32)
    for c in range(2):
        val = jnp.where((at < 16) & (channel == c) & (here == column), rows[9][c], val)
    mats[BACK:FORWARD, :] = val.astype(BF16)

    out_at = group_of((CH, 2 * LANES))
    columns = ((8, None, None, -1), (0, 1, 2, 3), (4, 5, 6, 7))

    def layer(i):
        for r in range(3):
            wide, tall = [], []
            for s in range(3):
                k = tile4(w_convs[i, 3 * r + s])
                wide.append(jnp.concatenate([k, k], axis=1))
                k = w_convs[i, 3 * (2 - r) + s]
                k = jnp.concatenate([k, k, k, k], axis=0).T
                tall.append(jnp.concatenate([k, k], axis=1))
            for d in range(3):
                for a in range(GRP):
                    spot = (3 * r + d) * LANES + CH * a
                    val = jnp.zeros((CH, 2 * LANES), F32)
                    inv = jnp.zeros((CH, 2 * LANES), F32)
                    at_column = columns[d][a]
                    if at_column is not None:
                        for s in range(3):
                            val = jnp.where(out_at == at_column + 1 - s, wide[s], val)
                            inv = jnp.where(out_at == at_column + s - 1, tall[s], inv)
                    mats[pl.ds(i * FORWARD + spot, CH), :] = val.astype(BF16)
                    mats[pl.ds(3 * FORWARD + i * BACK + spot, CH), :] = inv.astype(BF16)

    loop(3, layer)

    lane = lane_of((CH, LANES))
    head = jnp.zeros((CH, LANES), F32)
    bias = zero_row()
    diagonal = row_of((CH, CH)) == lane_of((CH, CH))
    for k in range(3):
        column = jnp.sum(jnp.where(diagonal, low(w_head[k : k + 1, 0:CH]), 0.0), axis=1, keepdims=True)
        mine = (lane >> 3) == FLOW // 8 + k
        head = jnp.where(mine, column, head)
        bias = jnp.where(mine[0:1], low(w_head[k : k + 1, CH : CH + 1]), bias)
    head_bias[...] = bias
    empty = jnp.zeros((CH, LANES), F32)
    for y in range(SEG):
        val = jnp.where((lane & 7) == y, head, 0.0)
        mats[HEAD_AT + CH * y : HEAD_AT + CH * (y + 1), :] = jnp.concatenate([val, empty], axis=1).astype(BF16)
    group = group_of((CH, LANES))
    for i in range(2):
        wide = tile4(w_style[i])
        for b in range(GRP):
            style_mat[i, CH * b : CH * b + CH, :] = jnp.where(group == b, wide, 0.0)
    for i in range(2):
        tab[4 * i : 4 * i + 4, :] = tile4(table[i])
    wait(copies(sems, (mats, store.at[0 : mats.shape[0]])))


def start_kernel(place, got, first_mat, sides, raw, pay, *, local_count, height, sources):
    rows, segments = raw.shape[0], raw.shape[2]
    off, block = place[0], place[1]
    blank(sides)

    def eight(t):
        v = got[pl.ds((block + t) * sources, sources)].astype(F32)
        v = jnp.swapaxes(v.reshape(segments // 2, 8, LANES), 0, 1)
        near = lane_of(v.shape) < 64
        v = jnp.concatenate([jnp.where(near, v, 0.0), jnp.where(near, pltpu.roll(v, 64, axis=2), 0.0)], axis=1)
        pixels = jnp.where(lane_of(v.shape) < 16, v, 0.0)
        left, right = beside(pixels, pixels)
        v = v + pltpu.roll(left, LEFT, axis=2) + pltpu.roll(right, RIGHT, axis=2)
        sides[pl.ds(8 * t + 1, 8)] = v.astype(BF16)

    loop(rows // 8, eight)
    y = None
    for r in range(3):
        part = jnp.dot(flat(sides[r : r + rows]), first_mat[r], preferred_element_type=F32)
        y = part if y is None else y + part
    raw[:, 0], raw[:, 1] = blocks_of(y, rows)
    mean, square = local_stats(raw, off, height, local_count)
    mask = jnp.zeros(sides.shape[1:], F32)
    for i in range(height):
        mask = mask + sides[off + 1 + i].astype(F32)
    lane = lane_of(mask.shape)
    count = jnp.sum(jnp.where((lane >= MASK) & (lane < MASK + 8), mask, 0.0))
    send(pay, groups(mean, square, jnp.full((1, LANES), count, F32)))


def first_kernel(place, got, raw, sides, tab, weights, summed, pay, vec, fields, lows, hidden, xhat, taps, sems, *, spots, local_count, pixel_count, height):
    fetched = copies(sems, (taps_at(weights, 0), taps))
    mean, inverse = merge_stats(got[:, 0, :], local_count, pixel_count)
    notes(vec, inverse)
    gain, bias = tab[0:1], tab[4:5]
    rows = raw.shape[0]

    def norm_rows(i):
        at = pl.ds(4 * i, 4)
        out = []
        for k in range(2):
            x = (raw[at, k] - mean) * inverse
            xhat[at, k] = x
            n = x * gain + bias
            out.append(n * sig_of(n))
        put_low(hidden, 4 * i, *out)

    blank(hidden)
    loop(rows // 4, norm_rows)
    stored = copies(sems.at[1:], (xhat, spots(fields, "xhat_zero")), (hidden, spots(lows, "hidden_one")))
    wait(fetched)
    y = conv(hidden, taps, 0, rows, flat(sides[1 : rows + 1]))
    summed[:, 0], summed[:, 1] = blocks_of(y, rows)
    send(pay, groups(*local_stats(summed, place[0], height, local_count), zero_row()))
    wait(stored)


def pool_kernel(place, got, summed, tab, weights, fields_in, lows_in, raw, pay, vec, fields, lows, merged, xhat, shared, taps, sems, *, spots, local_count, pixel_count, height):
    fetched = copies(sems, (taps_at(weights, 1), taps))
    mean, inverse = merge_stats(got[:, 0, :], local_count, pixel_count)
    gain, bias = tab[1:2], tab[5:6]
    rows, segments = summed.shape[0], summed.shape[2]
    own = place[0] // 2

    def pair(p, carry):
        out = [[None, None], [None, None]]
        sums = [jnp.zeros((segments, LANES), F32) for _ in range(3)]
        for k in range(2):
            xs, es, ns, ss = [], [], [], []
            for h in range(2):
                x = (summed[2 * p + h, k] - mean) * inverse
                n = x * gain + bias
                s = sig_of(n)
                xs.append(x)
                ns.append(n)
                ss.append(s)
                es.append(n * s)
            top = jnp.maximum(es[0], es[1])
            top = jnp.maximum(top, partner(top))
            exps = [jnp.exp(e - top) for e in es]
            whole = exps[0] + exps[1]
            whole = whole + partner(whole)
            pooled = top + jnp.log(whole)
            over = 1.0 / whole
            sums[0] = sums[0] + pooled
            for h in range(2):
                share = exps[h] * over * slope(ns[h], ss[h])
                xhat[2 * p + h, k] = xs[h]
                shared[2 * p + h, k] = share
                sums[1] = sums[1] + share
                sums[2] = sums[2] + share * xs[h]
                out[h][k] = (es[h] + pooled)[None]
        for h in range(2):
            put_low(merged, 2 * p + h, *out[h])
        mine = (p >= own) & (p < own + height // 2)
        keep = jnp.where(mine, 1.0, 0.0)
        return tuple(a + keep * b for a, b in zip(carry, sums))

    blank(merged)
    zero = jnp.zeros((segments, LANES), F32)
    sums = lax.fori_loop(0, rows // 2, pair, (zero, zero, zero))
    pool_sum, share_sum, share_x = [fold(col_sum(v)) for v in sums]
    stored = copies(
        sems.at[1:],
        (xhat, spots(fields, "xhat_one")),
        (shared, spots(fields, "shared")),
        (merged, spots(lows, "merged")),
    )
    wait(fetched)
    raw[:, 0], raw[:, 1] = blocks_of(conv(merged, taps, 0, rows), rows)
    mean, square = local_stats(raw, place[0], height, local_count)
    send(pay, groups(mean, square, 0.5 * pool_sum, share_sum))
    notes(vec, inverse, share_x)
    wait(stored)


def by_image(v, parts):
    devices = v.shape[0]
    shape = (devices, devices)
    same = row_of(shape) // parts == lane_of(shape) // parts
    return jnp.dot(jnp.where(same, 1.0, 0.0), v, precision=highest, preferred_element_type=F32)


def mine_of(v, me):
    return col_sum(jnp.where(row_of(v.shape) == me, v, 0.0))


def style_kernel(place, got, raw, vec_one, tab, style_mat, weights, fields_in, lows_in, resid, pay, vec, style_out, fields, lows, hidden, xhat, merged, taps, sems, *, spots, local_count, pixel_count, pool_cells, height, parts):
    fetched = copies(sems, (taps_at(weights, 2), taps), (spots(lows_in, "merged"), merged))
    got = got[:, 0, :]
    devices = got.shape[0]
    style = by_image(spread(got, 2), parts) / pool_cells
    style_out[...] = style
    one = jnp.dot(style, style_mat[0], precision=highest, preferred_element_type=F32)
    two = jnp.dot(style, style_mat[1], precision=highest, preferred_element_type=F32)
    centre = spread(got, 0) + one
    mean = col_sum(centre) / devices
    off = centre - mean
    spread_sum = spread(col_sum(got), 1) + local_count * col_sum(off * off)
    inverse = lax.rsqrt(spread_sum / pixel_count + norm_eps)
    notes(vec, inverse)
    gain, bias = tab[2:3], tab[6:7]
    rows = raw.shape[0]
    me = place[2]
    shift = mine_of(one, me) - mean
    two = mine_of(two, me)

    def norm_rows(i):
        at = pl.ds(4 * i, 4)
        out = []
        for k in range(2):
            x = (raw[at, k] + shift) * inverse
            xhat[at, k] = x
            n = x * gain + bias
            out.append(n * sig_of(n))
        put_low(hidden, 4 * i, *out)

    blank(hidden)
    loop(rows // 4, norm_rows)
    stored = copies(sems.at[2:], (xhat, spots(fields, "xhat_two")), (hidden, spots(lows, "hidden_three")))
    wait(fetched)
    for k, y in enumerate(blocks_of(conv(hidden, taps, 0, rows), rows)):
        resid[:, k] = y + two + merged[1 : rows + 1, k].astype(F32)
    send(pay, groups(*local_stats(resid, place[0], height, local_count), vec_one[1:2]))
    wait(stored)


def head_kernel(place, got, got_count, resid, sides, head_bias, tab, weights, grad, xhat, pay, vec, decoded, slopes, mat, sems, *, local_count, pixel_count, height):
    fetched = copies(sems, (weights.at[HEAD_AT : HEAD_AT + 2 * LANES], mat))
    mean, inverse = merge_stats(got[:, 0, :], local_count, pixel_count)
    notes(vec, inverse)
    gain, bias = tab[3:4], tab[7:8]
    rows, segments = resid.shape[0], resid.shape[2]
    off = place[0]

    def norm_rows(i):
        at = pl.ds(4 * i, 4)
        for k in range(2):
            x = (resid[at, k] - mean) * inverse
            n = x * gain + bias
            s = sig_of(n)
            xhat[at, k] = x
            slopes[at, k] = slope(n, s)
            decoded[at, k] = (n * s).astype(BF16)

    loop(rows // 4, norm_rows)
    wait(fetched)
    head = mat[:, 0:LANES]
    wide = jnp.concatenate([flat(decoded[:, 0]), flat(decoded[:, 1])], axis=1)
    out = jnp.dot(wide, head, preferred_element_type=F32) + head_bias[...]
    given = flat(sides[1 : rows + 1]).astype(F32)
    lane = lane_of(given.shape)
    is_flow = lane < LABEL
    near = [pltpu.roll(given, LANES - MASK + first, axis=1) for first in (FLOW, FLOW + 8, LABEL)]
    mask = jnp.where(lane < FLOW + 8, near[0], jnp.where(is_flow, near[1], near[2]))
    mask = jnp.where((lane >= FLOW) & (lane < LABEL + 8), mask, 0.0)
    count = jnp.sum(got_count[:, 0, 64:65])
    diff = out - given / flow_scale
    hinge = jnp.maximum(out, 0.0) + jnp.log1p(jnp.exp(-jnp.abs(out)))
    loss = mask * jnp.where(is_flow, diff * diff, hinge - given * out)
    grad_out = (mask * jnp.where(is_flow, 2.0 * diff, sig_of(out) - given) / count).astype(BF16)
    at_row = lax.broadcasted_iota(jnp.int32, loss.shape, 0)
    inside = (at_row >= off * segments) & (at_row < (off + height) * segments)
    loss_sum = jnp.sum(jnp.where(inside, loss, 0.0))
    mine_out = jnp.where(inside, grad_out.astype(F32), 0.0).astype(BF16)
    outs = col_sum(mine_out.astype(F32))
    found = lax.dot_general(mine_out, wide, (((0,), (0,)), ((), ())), preferred_element_type=F32)
    shape = found.shape
    found = jnp.where((row_of(shape) & 7) == group_of(shape), found, 0.0)
    whole = [col_sum(found[FLOW + 8 * k : FLOW + 8 * k + 8]) for k in range(3)]
    whole = [fold(v[:, 0:LANES] + v[:, LANES:]) for v in whole]
    row = groups(*whole, zero_row())
    lane = lane_of((1, LANES))
    for k in range(3):
        row = jnp.where(lane == 3 * CH + k, jnp.sum(jnp.where((lane >> 3) == FLOW // 8 + k, outs, 0.0)), row)
    row = jnp.where(lane == 3 * CH + 3, loss_sum, row)
    y = lax.dot_general(grad_out, head, (((1,), (1,)), ((), ())), preferred_element_type=F32)
    for k, g in enumerate(blocks_of(y, rows)):
        grad[:, k] = g * slopes[:, k]
    shift_sum, scale_sum = own_sums(grad, xhat, off, height)
    devices = pay.shape[0]
    pay[:, 0, :] = jnp.broadcast_to(groups(shift_sum, scale_sum, zero_row()), (devices, LANES))
    pay[:, 1, :] = jnp.broadcast_to(row, (devices, LANES))


def own_sums(grad, xhat, first, rows):
    def add(i, carry):
        shift, scale = carry
        for k in range(2):
            g = grad[first + i, k]
            shift = shift + g
            scale = scale + g * xhat[first + i, k]
        return shift, scale

    zero = jnp.zeros(grad.shape[2:], F32)
    shift, scale = lax.fori_loop(0, rows, add, (zero, zero), unroll=8)
    return fold(col_sum(shift)), fold(col_sum(scale))


def back_sums(got, pixel_count):
    whole = col_sum(got)
    return spread(whole, 0) / pixel_count, spread(whole, 1) / pixel_count


def low_sum(grad_low, first, rows):
    def add(i, total):
        return total + grad_low[first + 1 + i, 0].astype(F32) + grad_low[first + 1 + i, 1].astype(F32)

    return fold(col_sum(lax.fori_loop(0, rows, add, jnp.zeros(grad_low.shape[2:], F32), unroll=8)))


def norm_back(grad, xhat, factor, shift, scale):
    return factor * (grad - (shift + xhat * scale))


def back_rows(grad_low, rows, value):
    def some(i):
        put_low(grad_low, 4 * i, *[value(pl.ds(4 * i, 4), k) for k in range(2)])

    blank(grad_low)
    loop(rows // 4, some)


def tap_sums(field, grad, first, rows, out):
    at = pl.ds(first + 1, rows)
    g = jnp.concatenate([flat(grad[at, 0]), flat(grad[at, 1])], axis=1)
    wide = jnp.concatenate(views(field, first, rows), axis=1)
    found = lax.dot_general(g, wide, (((0,), (0,)), ((), ())), preferred_element_type=F32)
    group = group_of((CH, LANES))
    taps = []
    for r in range(3):
        for s in range(3):
            val = jnp.zeros((CH, LANES), F32)
            for y in range(SEG):
                x = y + s - 1
                d, a = (0, 3) if x < 0 else (0, 0) if x == SEG else (1 + x // GRP, x % GRP)
                spot = (3 * r + d) * LANES
                val = val + jnp.where(group == a, found[CH * y : CH * y + CH, spot : spot + LANES], 0.0)
            taps.append(fold(val))
    for q in range(3):
        val = taps[4 * q]
        for b in range(1, min(4, 9 - 4 * q)):
            val = jnp.where(group == b, taps[4 * q + b], val)
        out[:, q, :] = val


def residual_kernel(place, got, grad, xhat, vec, tab, weights, fields_in, lows, below, below_x, pay, fields, grad_low, kept_grad, back, field, sems, *, spots, pixel_count, height):
    fetched = copies(sems, (back_at(weights, 2), back), (spots(fields_in, "xhat_two"), below_x), (spots(lows, "hidden_three"), field))
    devices = got.shape[0]
    shift, scale = back_sums(got[:, 0, :], pixel_count)
    factor = tab[3:4] * vec[0:1]
    rows = grad.shape[0]
    off = place[0]

    def value(at, k):
        g = norm_back(grad[at, k], xhat[at, k], factor, shift, scale)
        kept_grad[at, k] = g
        return g

    back_rows(grad_low, rows, value)
    stored = copies(sems.at[3:], (kept_grad, spots(fields, "grad_resid")))
    image_sum = low_sum(grad_low, off, height)
    gain, bias = tab[2:3], tab[6:7]
    wait(fetched)
    for k, y in enumerate(blocks_of(conv(grad_low, back, 0, rows), rows)):
        below[:, k] = y * slope_at(below_x[:, k], gain, bias)
    row = groups(*own_sums(below, below_x, off, height), image_sum, zero_row())
    pay[...] = jnp.broadcast_to(row[None], pay.shape)
    tap_sums(field, grad_low, off, height, pay.at[0:CH, 1:4])
    wait(stored)


def merged_kernel(place, got, grad, xhat, vec, tab, weights, fields, lows, below, pay, kept_grad, below_x, shared, grad_low, back, field, sems, *, spots, pixel_count, height):
    fetched = copies(
        sems,
        (back_at(weights, 1), back),
        (spots(fields, "grad_resid"), kept_grad),
        (spots(fields, "xhat_one"), below_x),
        (spots(fields, "shared"), shared),
        (spots(lows, "merged"), field),
    )
    devices = got.shape[0]
    gathered = jnp.sum(got[...], axis=0)
    shift, scale = spread(gathered[0:1], 0) / pixel_count, spread(gathered[0:1], 1) / pixel_count
    factor = tab[2:3] * vec[0:1]
    rows = grad.shape[0]
    off = place[0]
    back_rows(grad_low, rows, lambda at, k: norm_back(grad[at, k], xhat[at, k], factor, shift, scale))
    image_sum = low_sum(grad_low, off, height)
    gain, bias = tab[1:2], tab[5:6]
    wait(fetched)
    for k, y in enumerate(blocks_of(conv(grad_low, back, 0, rows), rows)):
        g = (y + kept_grad[:, k]).reshape(rows // 2, 2, -1, LANES)
        both = flat(g[:, 0] + g[:, 1])
        both = (both + partner(both)).reshape(rows // 2, 1, -1, LANES)
        g = g * slope_at(below_x[:, k], gain, bias).reshape(g.shape) + both * shared[:, k].reshape(g.shape)
        below[:, k] = g.reshape(rows, -1, LANES)
    row = groups(*own_sums(below, below_x, off, height), image_sum, zero_row())
    first = jnp.where(row_of((4, LANES)) == 0, row, gathered)
    pay[:, 0] = jnp.broadcast_to(first[None], (devices, 4, LANES))
    if devices > CH:
        pay[CH:, 1] = jnp.zeros((devices - CH, 4, LANES), F32)
    tap_sums(field, grad_low, off, height, pay.at[0:CH, 1])
    pay[0:CH, 1, 3, :] = jnp.zeros((CH, LANES), F32)


def summed_kernel(place, got, got_two, got_style, got_three, grad, vec, tab, style_mat, sides, weights, fields, lows, below, below_x, pay, more, shared, xhat, back, field, grad_low, sems, *, spots, pixel_count, pool_cells, height, parts):
    fetched = copies(
        sems,
        (spots(fields, "shared"), shared),
        (spots(fields, "xhat_one"), xhat),
        (back_at(weights, 0), back),
        (spots(fields, "xhat_zero"), below_x),
        (spots(lows, "hidden_one"), field),
    )
    devices = got.shape[0]
    off = place[0]
    rows = grad.shape[0]
    dims = (((1,), (1,)), ((), ()))
    first = got[:, 0, 0, :]
    grad_style = lax.dot_general(spread(first, 2), style_mat[0], dims, precision=highest, preferred_element_type=F32)
    grad_style = grad_style + lax.dot_general(
        spread(got_two[:, 0, :], 2), style_mat[1], dims, precision=highest, preferred_element_type=F32
    )
    grad_style = by_image(grad_style, parts) / pool_cells
    total = col_sum(first)
    shift = spread(total, 0) + col_sum(grad_style * spread(got_style[:, 0, :], 3))
    scale = spread(total, 1) + col_sum(grad_style * spread(got_three[:, 0, :], 2))
    mine = mine_of(grad_style, place[2])
    factor = tab[1:2] * vec[0:1]
    shift_mean, scale_mean = shift / pixel_count, scale / pixel_count
    wait(fetched[:2])

    def value(at, k):
        return norm_back(grad[at, k] + shared[at, k] * mine, xhat[at, k], factor, shift_mean, scale_mean)

    back_rows(grad_low, rows, value)
    gain, bias = tab[0:1], tab[4:5]
    wait(fetched[2:])
    for k, y in enumerate(blocks_of(conv(grad_low, back, 0, rows), rows)):
        below[:, k] = y * slope_at(below_x[:, k], gain, bias)
    row = groups(*own_sums(below, below_x, off, height), zero_row())
    gathered = jnp.sum(got[:, 1], axis=0)
    chunk = jnp.concatenate([row, gathered[0:3]], axis=0)
    pay[:, 0] = jnp.broadcast_to(chunk[None], (devices, 4, LANES))
    if devices > CH:
        pay[CH:, 1] = jnp.zeros((devices - CH, 4, LANES), F32)
    tap_sums(field, grad_low, off, height, pay.at[0:CH, 1])
    pay[0:CH, 1, 3, :] = jnp.zeros((CH, LANES), F32)
    at = pl.ds(off + 1, height)
    low_own = jnp.concatenate([flat(grad_low[at, 0]), flat(grad_low[at, 1])], axis=1)
    side = pixel_taps(sides, off + 1, height, low_own, (0,))[0]
    notes(more, scale, shift, *side)


def pixel_taps(sides, row, rows, grad, shift):
    x = flat(sides[pl.ds(row, rows)])
    found = lax.dot_general(x, grad, (((0,), (0,)), ((), ())), preferred_element_type=F32)
    at = row_of(found.shape)
    kind = at >> 5
    here = (at & 7) + jnp.where(kind == LEFT // 32, -SEG, jnp.where(kind == RIGHT // 32, SEG, 0)) - group_of(found.shape)
    image_lane = (kind != 1) & ((at & 31) < 16)
    out = []
    for s in shift:
        both = []
        for c in range(2):
            hit = image_lane & (((at >> 3) & 1) == c) & (here == s)
            v = col_sum(jnp.where(hit, found, 0.0))
            both.append(fold(v[:, 0:LANES] + v[:, LANES:]))
        out.append(both)
    return out


def first_back_kernel(place, got, grad, xhat, vec, more, tab, sides, pay, *, pixel_count, height):
    devices = got.shape[0]
    off = place[0]
    whole = col_sum(got[:, 0, 0, :])
    shift, scale = spread(whole, 0) / pixel_count, spread(whole, 1) / pixel_count
    factor = tab[0:1] * vec[0:1]
    at = pl.ds(off, height)
    low_grad = jnp.concatenate(
        [flat(norm_back(grad[at, k], xhat[at, k], factor, shift, scale).astype(BF16)) for k in range(2)], axis=1
    )
    entries = []
    for r in range(3):
        for tap in pixel_taps(sides, off + r, height, low_grad, (-1, 0, 1)):
            entries.extend(tap)
    entries.extend([more[2:3], more[3:4]])
    rows = [groups(*entries[4 * q : 4 * q + 4]) for q in range(5)]
    conv_zero = jnp.sum(got[:, 1], axis=0)
    chunk = [jnp.concatenate(rows[0:4], axis=0), jnp.concatenate([rows[4], conv_zero[0:3]], axis=0)]
    for k in range(2):
        pay[:, k] = jnp.broadcast_to(chunk[k][None], (devices, 4, LANES))


def adamw(master, moment, square, grad, rate):
    new_moment = beta_one * moment + (1.0 - beta_one) * grad
    new_square = beta_two * square + (1.0 - beta_two) * grad * grad
    moment_hat = new_moment / (1.0 - beta_one**STEP)
    square_hat = new_square / (1.0 - beta_two**STEP)
    new_master = master - rate * (moment_hat / (jnp.sqrt(square_hat) + adam_eps) + weight_decay * master)
    return new_master, new_moment, new_square


def put(at, refs, grad, rate, outs):
    found = adamw(*[ref[at] for ref in refs], grad, rate)
    for out, value in zip(outs, found + (found[0].astype(BF16),)):
        out[at] = value


def update_early(
    got_first, got_one_back, got_two, got_head, got_count, pay, more, style,
    w_style, w_head, table, m_style, m_head, m_norms, s_style, s_head, s_norms,
    loss_out, count_out,
    style_master, style_moment, style_square,
    head_master, head_moment, head_square, head_copy,
    norms_master, norms_moment, norms_square,
):
    count_out[0, 0] = jnp.sum(got_count[:, 0, 64:65])
    loss_out[0, 0] = jnp.sum(got_head[:, 1, 99:100])
    dims = (((0,), (0,)), ((), ()))
    for i, sums in enumerate((got_one_back[:, 0, 0, :], got_two[:, 0, :])):
        grad = lax.dot_general(style[...], spread(sums, 2), dims, precision=highest, preferred_element_type=F32)
        put(i, (w_style, m_style, s_style), grad[0:CH, 0:CH], rate_table[2], (style_master, style_moment, style_square))

    head = col_sum(got_head[:, 1, :])
    lane = lane_of((1, LANES))
    rows = []
    for k in range(3):
        last = jnp.sum(jnp.where(lane == 3 * CH + k, head, 0.0), axis=1, keepdims=True)
        rows.append(jnp.where(lane < CH, spread(head, k), last))
    grad = jnp.concatenate(rows, axis=0)[:, 0 : CH + 1]
    put(slice(None), (w_head, m_head, s_head), grad, rate_table[3], (head_master, head_moment, head_square, head_copy))

    three_sums = col_sum(got_head[:, 0, :])
    two_sums = col_sum(got_two[:, 0, :])
    zero_sums = col_sum(got_first[:, 0, 0, :])
    scales = [spread(zero_sums, 1), more[0:1], spread(two_sums, 1), spread(three_sums, 1)]
    shifts = [spread(zero_sums, 0), more[1:2], spread(two_sums, 0), spread(three_sums, 0)]
    for i, rows in enumerate((scales, shifts)):
        grad = jnp.concatenate(rows, axis=0)[:, 0:CH]
        put(i, (table, m_norms, s_norms), grad, rate_table[4], (norms_master, norms_moment, norms_square))


def update_late(
    got, got_first, got_one_back, w_first, w_convs, m_first, m_convs, s_first, s_convs,
    first_master, first_moment, first_square, first_copy,
    convs_master, convs_moment, convs_square, convs_copy,
):
    sources = [got[0:CH, 1, 1:4, :], got_first[0:CH, 0, 1:4, :], got_one_back[0:CH, 0, 1:4, :]]
    refs = (w_convs, m_convs, s_convs)
    outs = (convs_master, convs_moment, convs_square, convs_copy)
    for i in range(3):
        for q in range(3):
            grad = sources[i][:, q, :].T
            for b in range(min(4, 9 - 4 * q)):
                put((i, 4 * q + b), refs, grad[CH * b : CH * b + CH], rate_table[1], outs)

    first = jnp.concatenate([jnp.sum(got[:, 0], axis=0), jnp.sum(got[:, 1], axis=0)[0:1]], axis=0)
    refs = (w_first, m_first, s_first)
    outs = (first_master, first_moment, first_square, first_copy)
    for t in range(10):
        pair = [spread(first[e // 4 : e // 4 + 1], e % 4)[:, 0:CH] for e in (2 * t, 2 * t + 1)]
        put(t, refs, jnp.concatenate(pair, axis=0), rate_table[0], outs)


def far(x):
    return ("far", x)


def call(kernel, outs, *operands, scalars=0, scratch=(), sems=0, scalar_outs=(), aliases=None, name):
    smem = pl.BlockSpec(memory_space=pltpu.SMEM)
    vmem = pl.BlockSpec(memory_space=pltpu.VMEM)
    hbm = pl.BlockSpec(memory_space=pltpu.HBM)
    is_far = lambda x: isinstance(x, tuple) and x[0] == "far"
    in_specs = [smem if i < scalars else hbm if is_far(x) else vmem for i, x in enumerate(operands)]
    out_specs = [smem if i in scalar_outs else hbm if is_far(x) else vmem for i, x in enumerate(outs)]
    plain = lambda x: x[1] if is_far(x) else x
    shapes = [pltpu.VMEM(shape, dtype) for shape, dtype in scratch]
    if sems:
        shapes.append(pltpu.SemaphoreType.DMA((sems,)))
    return pl.pallas_call(
        kernel,
        out_shape=[jax.ShapeDtypeStruct(*plain(x)) for x in outs],
        in_specs=in_specs,
        out_specs=out_specs,
        scratch_shapes=shapes,
        input_output_aliases=aliases or {},
        compiler_params=pltpu.CompilerParams(vmem_limit_bytes=VMEM_LIMIT),
        name=name,
    )(*[plain(x) for x in operands])


def exchange(pay):
    return lax.all_to_all(pay, ("row", "col"), 0, 0)


def local(
    image_batch, valid_mask, flow_target, cell_labels,
    w_first, w_convs, w_style, w_head, batch_norm_table,
    mom_first, mom_convs, mom_style, mom_head, mom_norms,
    sqr_first, sqr_convs, sqr_style, sqr_head, sqr_norms,
):
    images, block_rows, block_cols, _ = image_batch.shape
    row_count, col_count = lax.axis_size("row"), lax.axis_size("col")
    devices = row_count * col_count
    parts = devices // images
    image_rows, image_cols = row_count * block_rows, col_count * block_cols
    assert devices == parts * images and block_rows == RIM and block_cols == 2 * block_rows * 2
    assert image_rows % (parts * RIM) == 0 and devices >= CH
    height = image_rows // parts
    rows = min(image_rows, height + RIM * min(2, parts - 1))
    segments = image_cols // SEG
    local_count = float(height * image_cols)
    pixel_count = local_count * devices
    pool_cells = float(image_rows * image_cols // 4)
    part = functools.partial
    counts = dict(local_count=local_count, pixel_count=pixel_count, height=height)
    backs = dict(pixel_count=pixel_count, height=height)
    styled = dict(pool_cells=pool_cells, parts=parts)

    me = lax.axis_index("row") * col_count + lax.axis_index("col")
    first_row = (me % parts) * height
    start = jnp.clip(first_row - RIM, 0, image_rows - rows)
    place = jnp.stack([first_row - start, start // block_rows, me]).astype(jnp.int32)

    field = ((rows, 2, segments, LANES), F32)
    low_field = ((rows + 2, 3, segments, LANES), BF16)
    vec = ((8, LANES), F32)
    one_row = ((devices, 1, LANES), F32)
    two_chunks = ((devices, 2, 4, LANES), F32)
    taps_scratch = ((FORWARD, 2 * LANES), BF16)
    nine_scratch = ((BACK, 2 * LANES), BF16)

    places = {
        name: i * count
        for count, names in (
            (rows, ("xhat_zero", "xhat_one", "shared", "xhat_two", "grad_resid")),
            (rows + 2, ("hidden_one", "hidden_three", "merged")),
        )
        for i, name in enumerate(names)
    }

    def spots(store, name):
        count = rows if name[0] in "xsg" else rows + 2
        return store.at[places[name] : places[name] + count]

    def store_of(like):
        shape, dtype = like
        row_bytes = shape[1] * segments * LANES * jnp.dtype(dtype).itemsize
        return far(((-(-STORE_BYTES // row_bytes),) + shape[1:], dtype))

    (pay,) = call(
        pack_kernel,
        [((devices, 16, LANES), BF16)],
        jnp.transpose(image_batch, (0, 1, 3, 2)), jnp.transpose(flow_target, (0, 1, 3, 2)), cell_labels, valid_mask,
        name="pack",
    )
    got_inputs = exchange(pay)
    weights, first_mat, head_bias, style_mat, tab = call(
        prepare,
        [
            far(((STORE_BYTES // (4 * LANES), 2 * LANES), BF16)),
            ((3, LANES, 2 * LANES), BF16),
            ((1, LANES), F32),
            ((2, LANES, LANES), F32),
            vec,
        ],
        w_first, w_convs, w_style, w_head.T, batch_norm_table,
        scratch=[((HEAD_AT + 2 * LANES, 2 * LANES), BF16)], sems=1, name="prepare",
    )

    sides, raw, pay = call(
        part(start_kernel, local_count=local_count, height=height, sources=col_count),
        [((rows + 2, segments, LANES), BF16), field, one_row],
        place, got_inputs, first_mat,
        scalars=1, name="image_conv",
    )
    got_zero = exchange(pay)

    summed, pay, inv_zero, fields, lows = call(
        part(first_kernel, spots=spots, **counts),
        [field, one_row, vec, store_of(field), store_of(low_field)],
        place, got_zero, raw, sides, tab, far(weights),
        scalars=1, scratch=[low_field, field, taps_scratch], sems=3, name="first_block",
    )
    got_one = exchange(pay)

    raw, pay, inv_one, fields, lows = call(
        part(pool_kernel, spots=spots, **counts),
        [field, one_row, vec, store_of(field), store_of(low_field)],
        place, got_one, summed, tab, far(weights), far(fields), far(lows),
        scalars=1, scratch=[low_field, field, field, nine_scratch], sems=4,
        aliases={5: 3, 6: 4}, name="pool_and_merge",
    )
    got_style = exchange(pay)

    resid, pay, inv_two, style, fields, lows = call(
        part(style_kernel, spots=spots, **styled, **counts),
        [field, one_row, vec, ((devices, LANES), F32), store_of(field), store_of(low_field)],
        place, got_style, raw, inv_one, tab, style_mat, far(weights), far(fields), far(lows),
        scalars=1, scratch=[low_field, field, low_field, nine_scratch], sems=4,
        aliases={7: 4, 8: 5}, name="decoder",
    )
    got_three = exchange(pay)

    grad_three, xhat_three, pay, inv_three = call(
        part(head_kernel, **counts),
        [field, field, ((devices, 2, LANES), F32), vec],
        place, got_three, got_zero, resid, sides, head_bias, tab, far(weights),
        scalars=1, scratch=[((rows, 2, segments, LANES), BF16), field, ((2 * LANES, 2 * LANES), BF16)], sems=1,
        name="head",
    )
    got_head = exchange(pay)

    grad_two, xhat_two, pay, fields = call(
        part(residual_kernel, spots=spots, **backs),
        [field, field, ((devices, 4, LANES), F32), store_of(field)],
        place, got_head, grad_three, xhat_three, inv_three, tab, far(weights), far(fields), far(lows),
        scalars=1, scratch=[low_field, field, nine_scratch, low_field], sems=4,
        aliases={7: 3}, name="residual_back",
    )
    got_two = exchange(pay)

    grad_one, pay = call(
        part(merged_kernel, spots=spots, **backs),
        [field, two_chunks],
        place, got_two, grad_two, xhat_two, inv_two, tab, far(weights), far(fields), far(lows),
        scalars=1, scratch=[field, field, field, low_field, nine_scratch, low_field], sems=5, name="merged_back",
    )
    got_one_back = exchange(pay)

    grad_zero, xhat_zero, pay, more = call(
        part(summed_kernel, spots=spots, **styled, **backs),
        [field, field, two_chunks, vec],
        place, got_one_back, got_two, got_style, got_three, grad_one, inv_one, tab, style_mat, sides,
        far(weights), far(fields), far(lows),
        scalars=1, scratch=[field, field, nine_scratch, low_field, low_field], sems=5, name="summed_back",
    )
    got_first = exchange(pay)

    (pay,) = call(
        part(first_back_kernel, **backs),
        [two_chunks],
        place, got_first, grad_zero, xhat_zero, inv_zero, more, tab, sides,
        scalars=1, name="first_back",
    )
    got_last = exchange(pay)

    def results(param, copy):
        return [(param.shape, F32)] * 3 + [(param.shape, BF16)] * copy

    head_rows = w_head.T
    early = call(
        update_early,
        [((1, 1), F32), ((1, 1), F32)] + results(w_style, 0) + results(head_rows, 1) + results(batch_norm_table, 0),
        got_first, got_one_back, got_two, got_head, got_zero, far(pay), more, style,
        w_style, head_rows, batch_norm_table, mom_style, mom_head.T, mom_norms, sqr_style, sqr_head.T, sqr_norms,
        scalar_outs=(0, 1), name="update_early",
    )
    late = call(
        update_late,
        results(w_first, 1) + results(w_convs, 1),
        got_last, got_first, got_one_back, w_first, w_convs, mom_first, mom_convs, sqr_first, sqr_convs,
        name="update_late",
    )
    loss, count = early[0].reshape(()), early[1].reshape(())
    head = tuple(value.T for value in early[5:9])
    return (loss, count, *late, *early[2:5], *head, *early[9:12])


def solution(mesh):
    field = P(None, "row", "col", None)
    plane = P(None, "row", "col")
    return jax.shard_map(
        local,
        mesh=mesh,
        in_specs=(field, plane, field, plane) + (P(),) * 15,
        out_specs=(P(),) * 20,
        check_vma=False,
    )
```

```python
import functools

import jax
import jax.numpy as jnp
from jax import lax
from jax.experimental import pallas as pl
from jax.experimental.pallas import tpu as pltpu
from jax.sharding import PartitionSpec as P

STEP = 5

highest = lax.Precision.HIGHEST
norm_eps = 1e-05
flow_scale = 32.0
adam_eps = 1e-08
weight_decay = 0.01
beta_one = 0.5
beta_two = 0.5
rate_table = (0.2, 0.05, 0.15, 0.15, 0.2)

CH = 32
GRP = 4
SEG = 8
LANES = 128
RIM = 8
FLOW, LABEL, MASK = 16, 32, 40
LEFT, RIGHT = 64, 96
F32 = jnp.float32
BF16 = jnp.bfloat16
VMEM_LIMIT = 36 * 1024 * 1024
WHOLE_VMEM = 56 * 1024 * 1024
STORE_BYTES = 32 * 1024 * 1024
FORWARD = 10 * LANES
BACK = 9 * LANES


def lane_of(shape):
    return lax.broadcasted_iota(jnp.int32, shape, len(shape) - 1)


def row_of(shape):
    return lax.broadcasted_iota(jnp.int32, shape, 0)


def group_of(shape):
    return lane_of(shape) >> 5


def fold(v):
    return v + pltpu.roll(v, 32, axis=1) + (pltpu.roll(v, 64, axis=1) + pltpu.roll(v, 96, axis=1))


def spread(v, k):
    return fold(jnp.where(group_of(v.shape) == k, v, 0.0))


def partner(v):
    odd = (group_of(v.shape) & 1) == 1
    return jnp.where(odd, pltpu.roll(v, 32, axis=1), pltpu.roll(v, 96, axis=1))


def tile4(v):
    return jnp.concatenate([v, v, v, v], axis=1)


def col_sum(v):
    return jnp.sum(v, axis=0, keepdims=True)


def zero_row():
    return jnp.zeros((1, LANES), F32)


def groups(*values):
    group = group_of(values[0].shape)
    out = values[-1]
    for k in range(len(values) - 2, -1, -1):
        out = jnp.where(group == k, values[k], out)
    return out


def low(v):
    return v.astype(BF16).astype(F32)


def sig_of(v):
    return 0.5 + 0.5 * jnp.tanh(0.5 * v)


def slope(n, sig):
    return sig * (1.0 + n * (1.0 - sig))


def slope_at(x, gain, bias):
    n = x * gain + bias
    return slope(n, sig_of(n))


def flat(v):
    return v.reshape(-1, LANES)


def loop(count, body):
    def step(i, carry):
        body(i)
        return carry

    lax.fori_loop(0, count, step, 0, unroll=min(count, 5))


def copies(sems, *pairs):
    found = []
    for i, (source, target) in enumerate(pairs):
        found.append(pltpu.make_async_copy(source, target, sems.at[i]))
        found[-1].start()
    return found


def wait(started):
    for copy in started:
        copy.wait()


def shift_segments(v, way):
    half = v.shape[1]
    at = lax.broadcasted_iota(jnp.int32, v.shape, 1)
    if way == 1:
        return jnp.where(at == 0, 0.0, pltpu.roll(v, 1, axis=1))
    return jnp.where(at == half - 1, 0.0, pltpu.roll(v, half - 1, axis=1))


def beside(first, second):
    half = first.shape[1] // 2
    left = jnp.concatenate([shift_segments(second[:, half:], 1), second[:, :half]], axis=1)
    right = jnp.concatenate([first[:, half:], shift_segments(first[:, :half], -1)], axis=1)
    return left, right


def put_low(ref, row, first, second):
    left, right = beside(first, second)
    edge = jnp.where(lane_of(left.shape) < 64, right, left)
    at = pl.ds(row + 1, first.shape[0])
    for k, v in enumerate((first, second, edge)):
        ref[at, k] = v.astype(BF16)


def blank(ref):
    zero = jnp.zeros((1,) + ref.shape[1:], ref.dtype)
    ref[0:1] = zero
    ref[ref.shape[0] - 1 : ref.shape[0]] = zero


def views(src, row, rows):
    return [flat(src[pl.ds(row + r, rows), k]) for r in range(3) for k in (2, 0, 1)]


def conv(src, mat, row, rows, *more):
    wide = jnp.concatenate(views(src, row, rows) + list(more), axis=1)
    return jnp.dot(wide, mat[...], preferred_element_type=F32)


def blocks_of(y, rows):
    return [y[:, k * LANES : (k + 1) * LANES].reshape(rows, -1, LANES) for k in range(2)]


def narrow(v):
    while v.shape[0] > 1:
        half = v.shape[0] // 2
        v = v[:half] + v[half:]
    return v[0]


def row_sums(first, rows, values):
    step = 4

    def add(i, carry):
        found = [values(pl.ds(first + step * i, step), k) for k in range(2)]
        return tuple(c + a + b for c, a, b in zip(carry, *found))

    shapes = jax.eval_shape(lambda: values(pl.ds(0, step), 0))
    zeros = tuple(jnp.zeros(v.shape, F32) for v in shapes)
    found = lax.fori_loop(0, rows // step, add, zeros, unroll=min(rows // step, 8))
    return [col_sum(narrow(v)) for v in found]


def local_stats(v, first, rows, count):
    mean = row_sums(first, rows, lambda at, k: (v[at, k],))[0] * (GRP / count)

    def square(at, k):
        away = v[at, k] - mean
        return (away * away,)

    return mean, row_sums(first, rows, square)[0]


def merge_stats(means, squares, local_count, pixel_count):
    mean = fold(col_sum(means)) / (GRP * means.shape[0])
    away = means - mean
    total = fold(col_sum(squares + (local_count / GRP) * (away * away)))
    return mean, lax.rsqrt(total / pixel_count + norm_eps)


def send(pay, *rows):
    value = rows[-1]
    if len(rows) > 1:
        at = row_of(pay.shape[1:])
        value = jnp.broadcast_to(value, pay.shape[1:])
        for k in range(len(rows) - 2, -1, -1):
            value = jnp.where(at == k, rows[k], value)
    pay[...] = jnp.broadcast_to(value[None], pay.shape)


def affine(table, q):
    return tile4(table[0, q : q + 1, :]), tile4(table[1, q : q + 1, :])


def diagonal_blocks(mat):
    wide = tile4(mat)
    group = group_of(wide.shape)
    return jnp.concatenate([jnp.where(group == b, wide, 0.0) for b in range(GRP)], axis=0)


def notes(ref, *rows):
    for i, row in enumerate(rows):
        ref[i : i + 1, :] = row


def taps_at(store, i):
    return store.at[FORWARD * i : FORWARD * i + (BACK if i else FORWARD)]


def pack_kernel(image_in, flow_in, labels_in, valid_in, out, image, flow, labels, valid, sems):
    fetched = copies(sems, (image_in, image), (flow_in, flow), (labels_in, labels), (valid_in, valid))
    images, height, _, width = image.shape
    parts = out.shape[0] // images
    wait(fetched)
    fields = [image[:, :, c, :].astype(F32) for c in range(2)]
    fields += [flow[:, :, c, :].astype(F32) for c in range(2)]
    fields += [labels[...].astype(F32), valid[...].astype(F32)]
    halves = width // 16
    shape = (width, halves * LANES)
    lane = lane_of(shape)
    column = (lane >> 7) * 16 + ((lane >> 6) & 1) * 8 + (lane & 7)
    hit = row_of(shape) == column
    which = (lane >> 3) & 7
    total = jnp.zeros((images * height, halves * LANES), F32)
    for k, v in enumerate(fields):
        x = v.reshape(images * height, width).astype(BF16)
        mat = jnp.where(hit & (which == k), 1.0, 0.0).astype(BF16)
        total = total + jnp.dot(x, mat, preferred_element_type=F32)
    for b in range(images):
        rows = total[b * height : (b + 1) * height]
        slot = jnp.concatenate([rows[:, h * LANES : (h + 1) * LANES] for h in range(halves)], axis=0).astype(BF16)
        for p in range(parts):
            out[b * parts + p] = slot


COLUMNS = ((8, None, None, -1), (0, 1, 2, 3), (4, 5, 6, 7))


def conv_matrix(taps, mats, base, back):
    out_at = group_of((CH, 2 * LANES))
    for r in range(3):
        wide = []
        for s in range(3):
            if back:
                k = taps[3 * (2 - r) + s]
                k = jnp.concatenate([k, k, k, k], axis=0).T
            else:
                k = tile4(taps[3 * r + s])
            wide.append(jnp.concatenate([k, k], axis=1))
        for d in range(3):
            for a in range(GRP):
                val = jnp.zeros((CH, 2 * LANES), F32)
                column = COLUMNS[d][a]
                if column is not None:
                    for s in range(3):
                        val = jnp.where(out_at == (column + s - 1 if back else column + 1 - s), wide[s], val)
                mats[pl.ds(base + (3 * r + d) * LANES + CH * a, CH), :] = val.astype(BF16)


def image_lanes(shape):
    at = row_of(shape)
    kind = at >> 5
    column = (at & 7) + jnp.where(kind == LEFT // 32, -SEG, jnp.where(kind == RIGHT // 32, SEG, 0))
    return (kind != 1) & ((at & 31) < 16), (at >> 3) & 1, column


def first_taps(w_first, t):
    found = [tile4(low(w_first[t][c : c + 1])) for c in range(2)]
    return [jnp.concatenate([v, v], axis=1) for v in found]


def image_matrix(w_first, r):
    shape = (LANES, 2 * LANES)
    inside, channel, here = image_lanes(shape)
    val = jnp.zeros(shape, F32)
    for s in range(3):
        for c, tap in enumerate(first_taps(w_first, 3 * r + s)):
            val = jnp.where(inside & (channel == c) & (here == group_of(shape) + s - 1), tap, val)
    return val.astype(BF16)


def prepare(w_first_in, w_convs_in, w_head_in, store, back_zero, back_one, back_two, head_mat, w_first, w_convs, w_head, mats, sems):
    wait(copies(sems, (w_first_in, w_first), (w_convs_in, w_convs), (w_head_in, w_head)))
    shape = (LANES, 2 * LANES)
    inside, channel, here = image_lanes(shape)
    val = jnp.zeros(shape, F32)
    for c, tap in enumerate(first_taps(w_first, 9)):
        val = jnp.where((row_of(shape) < 16) & (channel == c) & (here == group_of(shape)), tap, val)
    mats[BACK:FORWARD, :] = val.astype(BF16)
    stored = []
    for i in range(3):
        conv_matrix(w_convs.at[i], mats, FORWARD * i, False)
        stored += copies(sems.at[i:], (taps_at(mats, i), taps_at(store, i)))
    for i, back in enumerate((back_zero, back_one, back_two)):
        conv_matrix(w_convs.at[i], back, 0, True)
    lane = lane_of((CH, LANES))
    head = jnp.zeros((CH, LANES), F32)
    diagonal = row_of((CH, CH)) == lane_of((CH, CH))
    for k in range(3):
        column = jnp.sum(jnp.where(diagonal, low(w_head[k : k + 1, 0:CH]), 0.0), axis=1, keepdims=True)
        head = jnp.where((lane >> 3) == FLOW // 8 + k, column, head)
    for y in range(SEG):
        head_mat[CH * y : CH * (y + 1), :] = jnp.where((lane & 7) == y, head, 0.0).astype(BF16)
    wait(stored)


def start_kernel(place, got, w_first, prepared, sides, raw, pay, vec, *, local_count, height, sources):
    rows, segments = raw.shape[0], raw.shape[2]
    off, block = place[0], place[1]
    blank(sides)

    def eight(t):
        v = got[pl.ds((block + t) * sources, sources)].astype(F32)
        v = jnp.swapaxes(v.reshape(segments // 2, 8, LANES), 0, 1)
        near = lane_of(v.shape) < 64
        v = jnp.concatenate([jnp.where(near, v, 0.0), jnp.where(near, pltpu.roll(v, 64, axis=2), 0.0)], axis=1)
        pixels = jnp.where(lane_of(v.shape) < 16, v, 0.0)
        left, right = beside(pixels, pixels)
        v = v + pltpu.roll(left, LEFT, axis=2) + pltpu.roll(right, RIGHT, axis=2)
        sides[pl.ds(8 * t + 1, 8)] = v.astype(BF16)

    loop(rows // 8, eight)
    y = None
    for r in range(3):
        part = jnp.dot(flat(sides[r : r + rows]), image_matrix(w_first, r), preferred_element_type=F32)
        y = part if y is None else y + part
    raw[:, 0], raw[:, 1] = blocks_of(y, rows)
    mean, square = local_stats(raw, off, height, local_count)
    mask = jnp.zeros(sides.shape[1:], F32)
    for i in range(height):
        mask = mask + sides[off + 1 + i].astype(F32)
    lane = lane_of(mask.shape)
    count = jnp.sum(jnp.where((lane >= MASK) & (lane < MASK + 8), mask, 0.0))
    send(pay, mean, square)
    notes(vec, jnp.full((1, LANES), count, F32))


def first_kernel(place, got, raw, sides, table, weights, summed, pay, vec, fields, lows, hidden, xhat, taps, sems, *, spots, local_count, pixel_count, height):
    fetched = copies(sems, (taps_at(weights, 0), taps))
    mean, inverse = merge_stats(got[:, 0, :], got[:, 1, :], local_count, pixel_count)
    notes(vec, inverse)
    gain, bias = affine(table, 0)
    rows = raw.shape[0]

    def norm_rows(i):
        at = pl.ds(4 * i, 4)
        out = []
        for k in range(2):
            x = (raw[at, k] - mean) * inverse
            xhat[at, k] = x
            n = x * gain + bias
            out.append(n * sig_of(n))
        put_low(hidden, 4 * i, *out)

    blank(hidden)
    loop(rows // 4, norm_rows)
    stored = copies(sems.at[1:], (xhat, spots(fields, "xhat_zero")), (hidden, spots(lows, "hidden_one")))
    wait(fetched)
    y = conv(hidden, taps, 0, rows, flat(sides[1 : rows + 1]))
    summed[:, 0], summed[:, 1] = blocks_of(y, rows)
    send(pay, *local_stats(summed, place[0], height, local_count))
    wait(stored)


def pool_kernel(place, got, summed, count_in, table, weights, fields_in, lows_in, raw, pay, vec, fields, lows, merged, xhat, shared, taps, sems, *, spots, local_count, pixel_count, height):
    fetched = copies(sems, (taps_at(weights, 1), taps))
    mean, inverse = merge_stats(got[:, 0, :], got[:, 1, :], local_count, pixel_count)
    gain, bias = affine(table, 1)
    rows, segments = summed.shape[0], summed.shape[2]
    off = place[0]

    step = 4

    def some(i, carry):
        at = pl.ds(step * i, step)
        pairs = (step // 2, 2, segments, LANES)
        outs, sums = [], [jnp.zeros((step // 2 * segments, LANES), F32) for _ in range(3)]
        for k in range(2):
            x = (summed[at, k] - mean) * inverse
            n = x * gain + bias
            sig = sig_of(n)
            e = (n * sig).reshape(pairs)
            top = flat(jnp.maximum(e[:, 0], e[:, 1]))
            top = jnp.maximum(top, partner(top))
            wide_top = top.reshape(step // 2, 1, segments, LANES)
            exps = jnp.exp(e - wide_top)
            whole = flat(exps[:, 0] + exps[:, 1])
            whole = whole + partner(whole)
            pooled = top + jnp.log(whole)
            outs.append((e + pooled.reshape(wide_top.shape)).reshape(step, segments, LANES))
            share = exps * (1.0 / whole).reshape(wide_top.shape) * slope(n, sig).reshape(pairs)
            share_x = share * x.reshape(pairs)
            xhat[at, k] = x
            shared[at, k] = share.reshape(step, segments, LANES)
            sums[0] = sums[0] + pooled
            sums[1] = sums[1] + flat(share[:, 0] + share[:, 1])
            sums[2] = sums[2] + flat(share_x[:, 0] + share_x[:, 1])
        put_low(merged, step * i, *outs)
        mine = (step * i >= off) & (step * i < off + height)
        keep = jnp.where(mine, 1.0, 0.0)
        return tuple(a + keep * b for a, b in zip(carry, sums))

    blank(merged)
    zero = jnp.zeros((step // 2 * segments, LANES), F32)
    sums = lax.fori_loop(0, rows // step, some, (zero, zero, zero), unroll=min(rows // step, 5))
    pool_sum, share_sum, share_x = [fold(col_sum(v)) for v in sums]
    stored = copies(
        sems.at[1:],
        (xhat, spots(fields, "xhat_one")),
        (shared, spots(fields, "shared")),
        (merged, spots(lows, "merged")),
    )
    wait(fetched)
    raw[:, 0], raw[:, 1] = blocks_of(conv(merged, taps, 0, rows), rows)
    mean, square = local_stats(raw, place[0], height, local_count)
    send(pay, mean, square, groups(0.5 * pool_sum, share_sum, share_x, count_in[0:1]))
    notes(vec, inverse)
    wait(stored)


def by_image(v, parts):
    devices = v.shape[0]
    step = 1
    while step < parts:
        upper = (row_of(v.shape) // step) % 2 == 1
        v = v + jnp.where(upper, pltpu.roll(v, step, axis=0), pltpu.roll(v, devices - step, axis=0))
        step *= 2
    return v


def mine_of(v, me):
    return col_sum(jnp.where(row_of(v.shape) == me, v, 0.0))


def style_kernel(place, got, raw, table, w_style, weights, fields_in, lows_in, resid, pay, vec, style_out, fields, lows, hidden, xhat, merged, taps, sems, *, spots, local_count, pixel_count, pool_cells, height, parts):
    fetched = copies(sems, (taps_at(weights, 2), taps), (spots(lows_in, "merged"), merged))
    style = by_image(spread(got[:, 2, :], 0), parts) / pool_cells
    style_out[...] = style
    one, two = [
        jnp.dot(style, diagonal_blocks(w_style[i]), precision=highest, preferred_element_type=F32) for i in range(2)
    ]
    mean, inverse = merge_stats(got[:, 0, :] + one, got[:, 1, :], local_count, pixel_count)
    notes(vec, inverse)
    gain, bias = affine(table, 2)
    rows = raw.shape[0]
    me = place[2]
    shift = mine_of(one, me) - mean
    two = mine_of(two, me)

    def norm_rows(i):
        at = pl.ds(4 * i, 4)
        out = []
        for k in range(2):
            x = (raw[at, k] + shift) * inverse
            xhat[at, k] = x
            n = x * gain + bias
            out.append(n * sig_of(n))
        put_low(hidden, 4 * i, *out)

    blank(hidden)
    loop(rows // 4, norm_rows)
    stored = copies(sems.at[2:], (xhat, spots(fields, "xhat_two")), (hidden, spots(lows, "hidden_three")))
    wait(fetched)
    for k, y in enumerate(blocks_of(conv(hidden, taps, 0, rows), rows)):
        resid[:, k] = y + two + merged[1 : rows + 1, k].astype(F32)
    send(pay, *local_stats(resid, place[0], height, local_count))
    wait(stored)


def head_kernel(place, got, got_style, resid, sides, head_mat, w_head, table, grad, xhat, pay, vec, decoded, slopes, *, local_count, pixel_count, height):
    mean, inverse = merge_stats(got[:, 0, :], got[:, 1, :], local_count, pixel_count)
    notes(vec, inverse)
    gain, bias = affine(table, 3)
    rows, segments = resid.shape[0], resid.shape[2]
    off = place[0]

    def norm_rows(i):
        at = pl.ds(4 * i, 4)
        for k in range(2):
            x = (resid[at, k] - mean) * inverse
            n = x * gain + bias
            s = sig_of(n)
            xhat[at, k] = x
            slopes[at, k] = slope(n, s)
            decoded[at, k] = (n * s).astype(BF16)

    loop(rows // 4, norm_rows)
    head = head_mat[...]
    wide = jnp.concatenate([flat(decoded[:, 0]), flat(decoded[:, 1])], axis=1)
    bias_row = zero_row()
    for k in range(3):
        mine = (lane_of((1, LANES)) >> 3) == FLOW // 8 + k
        bias_row = jnp.where(mine, low(w_head[k : k + 1, CH : CH + 1]), bias_row)
    out = jnp.dot(wide, head, preferred_element_type=F32) + bias_row
    given = flat(sides[1 : rows + 1]).astype(F32)
    lane = lane_of(given.shape)
    is_flow = lane < LABEL
    near = [pltpu.roll(given, LANES - MASK + first, axis=1) for first in (FLOW, FLOW + 8, LABEL)]
    mask = jnp.where(lane < FLOW + 8, near[0], jnp.where(is_flow, near[1], near[2]))
    mask = jnp.where((lane >= FLOW) & (lane < LABEL + 8), mask, 0.0)
    count = jnp.sum(got_style[:, 2, 3 * CH : 3 * CH + 1])
    diff = out - given / flow_scale
    hinge = jnp.maximum(out, 0.0) + jnp.log1p(jnp.exp(-jnp.abs(out)))
    loss = mask * jnp.where(is_flow, diff * diff, hinge - given * out)
    grad_out = (mask * jnp.where(is_flow, 2.0 * diff, sig_of(out) - given) / count).astype(BF16)
    at_row = lax.broadcasted_iota(jnp.int32, loss.shape, 0)
    inside = (at_row >= off * segments) & (at_row < (off + height) * segments)
    loss_sum = jnp.sum(jnp.where(inside, loss, 0.0))
    mine_out = jnp.where(inside, grad_out.astype(F32), 0.0).astype(BF16)
    outs = col_sum(mine_out.astype(F32))
    found = lax.dot_general(mine_out, wide, (((0,), (0,)), ((), ())), preferred_element_type=F32)
    shape = found.shape
    found = jnp.where((row_of(shape) & 7) == group_of(shape), found, 0.0)
    whole = [col_sum(found[FLOW + 8 * k : FLOW + 8 * k + 8]) for k in range(3)]
    whole = [fold(v[:, 0:LANES] + v[:, LANES:]) for v in whole]
    row = groups(*whole, zero_row())
    lane = lane_of((1, LANES))
    for k in range(3):
        row = jnp.where(lane == 3 * CH + k, jnp.sum(jnp.where((lane >> 3) == FLOW // 8 + k, outs, 0.0)), row)
    row = jnp.where(lane == 3 * CH + 3, loss_sum, row)
    y = lax.dot_general(grad_out, head, (((1,), (1,)), ((), ())), preferred_element_type=F32)
    for k, g in enumerate(blocks_of(y, rows)):
        grad[:, k] = g * slopes[:, k]
    shift_sum, scale_sum = own_sums(grad, xhat, off, height)
    devices = pay.shape[0]
    pay[:, 0, :] = jnp.broadcast_to(groups(shift_sum, scale_sum, zero_row()), (devices, LANES))
    pay[:, 1, :] = jnp.broadcast_to(row, (devices, LANES))


def own_sums(grad, xhat, first, rows):
    def both(at, k):
        g = grad[at, k]
        return g, g * xhat[at, k]

    return [fold(v) for v in row_sums(first, rows, both)]


def back_sums(got, pixel_count):
    whole = col_sum(got)
    return spread(whole, 0) / pixel_count, spread(whole, 1) / pixel_count


def low_sum(grad_low, first, rows):
    return fold(row_sums(first + 1, rows, lambda at, k: (grad_low[at, k].astype(F32),))[0])


def norm_back(grad, xhat, factor, shift, scale):
    return factor * (grad - (shift + xhat * scale))


def back_rows(grad_low, rows, value):
    def some(i):
        put_low(grad_low, 4 * i, *[value(pl.ds(4 * i, 4), k) for k in range(2)])

    blank(grad_low)
    loop(rows // 4, some)


def tap_sums(field, grad, first, rows, out):
    at = pl.ds(first + 1, rows)
    g = jnp.concatenate([flat(grad[at, 0]), flat(grad[at, 1])], axis=1)
    wide = jnp.concatenate(views(field, first, rows), axis=1)
    found = lax.dot_general(g, wide, (((0,), (0,)), ((), ())), preferred_element_type=F32)
    group = group_of((CH, LANES))
    taps = []
    for r in range(3):
        for s in range(3):
            val = jnp.zeros((CH, LANES), F32)
            for y in range(SEG):
                x = y + s - 1
                d, a = (0, 3) if x < 0 else (0, 0) if x == SEG else (1 + x // GRP, x % GRP)
                spot = (3 * r + d) * LANES
                val = val + jnp.where(group == a, found[CH * y : CH * y + CH, spot : spot + LANES], 0.0)
            taps.append(fold(val))
    for q in range(3):
        val = taps[4 * q]
        for b in range(1, min(4, 9 - 4 * q)):
            val = jnp.where(group == b, taps[4 * q + b], val)
        out[:, q, :] = val


def residual_kernel(place, got, grad, xhat, vec, table, back, fields_in, lows, below, below_x, pay, fields, grad_low, kept_grad, field, sems, *, spots, pixel_count, height):
    fetched = copies(sems, (spots(fields_in, "xhat_two"), below_x), (spots(lows, "hidden_three"), field))
    devices = got.shape[0]
    shift, scale = back_sums(got[:, 0, :], pixel_count)
    factor = affine(table, 3)[0] * vec[0:1]
    rows = grad.shape[0]
    off = place[0]

    def value(at, k):
        g = norm_back(grad[at, k], xhat[at, k], factor, shift, scale)
        kept_grad[at, k] = g
        return g

    back_rows(grad_low, rows, value)
    stored = copies(sems.at[2:], (kept_grad, spots(fields, "grad_resid")))
    image_sum = low_sum(grad_low, off, height)
    gain, bias = affine(table, 2)
    wait(fetched)
    for k, y in enumerate(blocks_of(conv(grad_low, back, 0, rows), rows)):
        below[:, k] = y * slope_at(below_x[:, k], gain, bias)
    row = groups(*own_sums(below, below_x, off, height), image_sum, zero_row())
    send(pay, row)
    tap_sums(field, grad_low, off, height, pay.at[0:CH, 1:4])
    wait(stored)


def merged_kernel(place, got, grad, xhat, vec, table, back, fields, lows, below, below_x, shared, pay, kept_grad, grad_low, field, sems, *, spots, pixel_count, height):
    fetched = copies(
        sems,
        (spots(fields, "grad_resid"), kept_grad),
        (spots(fields, "xhat_one"), below_x),
        (spots(fields, "shared"), shared),
        (spots(lows, "merged"), field),
    )
    devices = got.shape[0]
    gathered = jnp.sum(got[...], axis=0)
    shift, scale = spread(gathered[0:1], 0) / pixel_count, spread(gathered[0:1], 1) / pixel_count
    factor = affine(table, 2)[0] * vec[0:1]
    rows = grad.shape[0]
    off = place[0]
    back_rows(grad_low, rows, lambda at, k: norm_back(grad[at, k], xhat[at, k], factor, shift, scale))
    image_sum = low_sum(grad_low, off, height)
    gain, bias = affine(table, 1)
    wait(fetched)
    for k, y in enumerate(blocks_of(conv(grad_low, back, 0, rows), rows)):
        g = (y + kept_grad[:, k]).reshape(rows // 2, 2, -1, LANES)
        both = flat(g[:, 0] + g[:, 1])
        both = (both + partner(both)).reshape(rows // 2, 1, -1, LANES)
        g = g * slope_at(below_x[:, k], gain, bias).reshape(g.shape) + both * shared[:, k].reshape(g.shape)
        below[:, k] = g.reshape(rows, -1, LANES)
    row = groups(*own_sums(below, below_x, off, height), image_sum, zero_row())
    first = jnp.where(row_of((4, LANES)) == 0, row, gathered)
    pay[:, 0] = jnp.broadcast_to(first[None], (devices, 4, LANES))
    if devices > CH:
        pay[CH:, 1] = jnp.zeros((devices - CH, 4, LANES), F32)
    tap_sums(field, grad_low, off, height, pay.at[0:CH, 1])
    pay[0:CH, 1, 3, :] = jnp.zeros((CH, LANES), F32)


def summed_kernel(place, got, got_two, got_style, grad, xhat, shared, vec, table, w_style, sides, back, fields, lows, below, below_x, pay, more, field, grad_low, sems, *, spots, pixel_count, pool_cells, height, parts):
    fetched = copies(
        sems,
        (spots(fields, "xhat_zero"), below_x),
        (spots(lows, "hidden_one"), field),
    )
    devices = got.shape[0]
    off = place[0]
    rows = grad.shape[0]
    dims = (((1,), (1,)), ((), ()))
    first = got[:, 0, 0, :]
    each = lax.dot_general(
        spread(first, 2), diagonal_blocks(w_style[0]), dims, precision=highest, preferred_element_type=F32
    ) + lax.dot_general(
        spread(got_two[:, 0, :], 2), diagonal_blocks(w_style[1]), dims, precision=highest, preferred_element_type=F32
    )
    each = each / pool_cells
    total = col_sum(first)
    shift = spread(total, 0) + col_sum(each * by_image(spread(got_style[:, 2, :], 1), parts))
    scale = spread(total, 1) + col_sum(each * by_image(spread(got_style[:, 2, :], 2), parts))
    mine = col_sum(jnp.where(row_of(each.shape) // parts == place[2] // parts, each, 0.0))
    factor = affine(table, 1)[0] * vec[0:1]
    shift_mean, scale_mean = shift / pixel_count, scale / pixel_count
    def value(at, k):
        return norm_back(grad[at, k] + shared[at, k] * mine, xhat[at, k], factor, shift_mean, scale_mean)

    back_rows(grad_low, rows, value)
    gain, bias = affine(table, 0)
    wait(fetched)
    for k, y in enumerate(blocks_of(conv(grad_low, back, 0, rows), rows)):
        below[:, k] = y * slope_at(below_x[:, k], gain, bias)
    row = groups(*own_sums(below, below_x, off, height), zero_row())
    gathered = jnp.sum(got[:, 1], axis=0)
    chunk = jnp.concatenate([row, gathered[0:3]], axis=0)
    pay[:, 0] = jnp.broadcast_to(chunk[None], (devices, 4, LANES))
    if devices > CH:
        pay[CH:, 1] = jnp.zeros((devices - CH, 4, LANES), F32)
    tap_sums(field, grad_low, off, height, pay.at[0:CH, 1])
    pay[0:CH, 1, 3, :] = jnp.zeros((CH, LANES), F32)
    at = pl.ds(off + 1, height)
    low_own = jnp.concatenate([flat(grad_low[at, 0]), flat(grad_low[at, 1])], axis=1)
    side = pixel_taps(sides, off + 1, height, low_own, (0,))[0]
    notes(more, scale, shift, *side)


def pixel_taps(sides, row, rows, grad, shift):
    x = flat(sides[pl.ds(row, rows)])
    found = lax.dot_general(x, grad, (((0,), (0,)), ((), ())), preferred_element_type=F32)
    inside, channel, here = image_lanes(found.shape)
    here = here - group_of(found.shape)
    out = []
    for s in shift:
        both = []
        for c in range(2):
            hit = inside & (channel == c) & (here == s)
            v = col_sum(jnp.where(hit, found, 0.0))
            both.append(fold(v[:, 0:LANES] + v[:, LANES:]))
        out.append(both)
    return out


def first_back_kernel(place, got, grad, xhat, vec, more, table, sides, pay, *, pixel_count, height):
    devices = got.shape[0]
    off = place[0]
    whole = col_sum(got[:, 0, 0, :])
    shift, scale = spread(whole, 0) / pixel_count, spread(whole, 1) / pixel_count
    factor = affine(table, 0)[0] * vec[0:1]
    at = pl.ds(off, height)
    low_grad = jnp.concatenate(
        [flat(norm_back(grad[at, k], xhat[at, k], factor, shift, scale).astype(BF16)) for k in range(2)], axis=1
    )
    entries = []
    for r in range(3):
        for tap in pixel_taps(sides, off + r, height, low_grad, (-1, 0, 1)):
            entries.extend(tap)
    entries.extend([more[2:3], more[3:4]])
    rows = [groups(*entries[4 * q : 4 * q + 4]) for q in range(5)]
    conv_zero = jnp.sum(got[:, 1], axis=0)
    chunk = [jnp.concatenate(rows[0:4], axis=0), jnp.concatenate([rows[4], conv_zero[0:3]], axis=0)]
    for k in range(2):
        pay[:, k] = jnp.broadcast_to(chunk[k][None], (devices, 4, LANES))


def adamw(master, moment, square, grad, rate):
    new_moment = beta_one * moment + (1.0 - beta_one) * grad
    new_square = beta_two * square + (1.0 - beta_two) * grad * grad
    moment_hat = new_moment / (1.0 - beta_one**STEP)
    square_hat = new_square / (1.0 - beta_two**STEP)
    new_master = master - rate * (moment_hat / (jnp.sqrt(square_hat) + adam_eps) + weight_decay * master)
    return new_master, new_moment, new_square


def put(at, refs, grad, rate, outs):
    found = adamw(*[ref[at] for ref in refs], grad, rate)
    for out, value in zip(outs, found + (found[0].astype(BF16),)):
        out[at] = value


def update_early(
    got_first, got_one_back, got_two, got_head, got_style, pay, more, style,
    w_style, w_head, table, m_style, m_head, m_norms, s_style, s_head, s_norms,
    loss_out, count_out,
    style_master, style_moment, style_square,
    head_master, head_moment, head_square, head_copy,
    norms_master, norms_moment, norms_square,
):
    count_out[0, 0] = jnp.sum(got_style[:, 2, 3 * CH : 3 * CH + 1])
    loss_out[0, 0] = jnp.sum(got_head[:, 1, 99:100])
    dims = (((0,), (0,)), ((), ()))
    for i, sums in enumerate((got_one_back[:, 0, 0, :], got_two[:, 0, :])):
        grad = lax.dot_general(style[...], spread(sums, 2), dims, precision=highest, preferred_element_type=F32)
        put(i, (w_style, m_style, s_style), grad[0:CH, 0:CH], rate_table[2], (style_master, style_moment, style_square))

    head = col_sum(got_head[:, 1, :])
    lane = lane_of((1, LANES))
    rows = []
    for k in range(3):
        last = jnp.sum(jnp.where(lane == 3 * CH + k, head, 0.0), axis=1, keepdims=True)
        rows.append(jnp.where(lane < CH, spread(head, k), last))
    grad = jnp.concatenate(rows, axis=0)[:, 0 : CH + 1]
    put(slice(None), (w_head, m_head, s_head), grad, rate_table[3], (head_master, head_moment, head_square, head_copy))

    three_sums = col_sum(got_head[:, 0, :])
    two_sums = col_sum(got_two[:, 0, :])
    zero_sums = col_sum(got_first[:, 0, 0, :])
    scales = [spread(zero_sums, 1), more[0:1], spread(two_sums, 1), spread(three_sums, 1)]
    shifts = [spread(zero_sums, 0), more[1:2], spread(two_sums, 0), spread(three_sums, 0)]
    for i, rows in enumerate((scales, shifts)):
        grad = jnp.concatenate(rows, axis=0)[:, 0:CH]
        put(i, (table, m_norms, s_norms), grad, rate_table[4], (norms_master, norms_moment, norms_square))


def update_late(
    got, got_first, got_one_back, w_first, w_convs, m_first, m_convs, s_first, s_convs,
    first_master, first_moment, first_square, first_copy,
    convs_master, convs_moment, convs_square, convs_copy,
):
    sources = [got[0:CH, 1, 1:4, :], got_first[0:CH, 0, 1:4, :], got_one_back[0:CH, 0, 1:4, :]]
    refs = (w_convs, m_convs, s_convs)
    outs = (convs_master, convs_moment, convs_square, convs_copy)
    for i in range(3):
        for q in range(3):
            grad = sources[i][:, q, :].T
            for b in range(min(4, 9 - 4 * q)):
                put((i, 4 * q + b), refs, grad[CH * b : CH * b + CH], rate_table[1], outs)

    first = jnp.concatenate([jnp.sum(got[:, 0], axis=0), jnp.sum(got[:, 1], axis=0)[0:1]], axis=0)
    refs = (w_first, m_first, s_first)
    outs = (first_master, first_moment, first_square, first_copy)
    for t in range(10):
        pair = [spread(first[e // 4 : e // 4 + 1], e % 4)[:, 0:CH] for e in (2 * t, 2 * t + 1)]
        put(t, refs, jnp.concatenate(pair, axis=0), rate_table[0], outs)


def far(x):
    return ("far", x)


def call(kernel, outs, *operands, scalars=0, scratch=(), sems=0, scalar_outs=(), aliases=None, limit=VMEM_LIMIT, name):
    smem = pl.BlockSpec(memory_space=pltpu.SMEM)
    vmem = pl.BlockSpec(memory_space=pltpu.VMEM)
    hbm = pl.BlockSpec(memory_space=pltpu.HBM)
    is_far = lambda x: isinstance(x, tuple) and x[0] == "far"
    in_specs = [smem if i < scalars else hbm if is_far(x) else vmem for i, x in enumerate(operands)]
    out_specs = [smem if i in scalar_outs else hbm if is_far(x) else vmem for i, x in enumerate(outs)]
    plain = lambda x: x[1] if is_far(x) else x
    shapes = [pltpu.VMEM(shape, dtype) for shape, dtype in scratch]
    if sems:
        shapes.append(pltpu.SemaphoreType.DMA((sems,)))
    return pl.pallas_call(
        kernel,
        out_shape=[jax.ShapeDtypeStruct(*plain(x)) for x in outs],
        in_specs=in_specs,
        out_specs=out_specs,
        scratch_shapes=shapes,
        input_output_aliases=aliases or {},
        compiler_params=pltpu.CompilerParams(vmem_limit_bytes=limit),
        name=name,
    )(*[plain(x) for x in operands])


def exchange(pay):
    return lax.all_to_all(pay, ("row", "col"), 0, 0)


def local(
    image_batch, valid_mask, flow_target, cell_labels,
    w_first, w_convs, w_style, w_head, batch_norm_table,
    mom_first, mom_convs, mom_style, mom_head, mom_norms,
    sqr_first, sqr_convs, sqr_style, sqr_head, sqr_norms,
):
    images, block_rows, block_cols, _ = image_batch.shape
    row_count, col_count = lax.axis_size("row"), lax.axis_size("col")
    devices = row_count * col_count
    parts = devices // images
    image_rows, image_cols = row_count * block_rows, col_count * block_cols
    assert devices == parts * images and block_rows == RIM and block_cols == 2 * block_rows * 2
    assert image_rows % (parts * RIM) == 0 and devices >= CH
    height = image_rows // parts
    rows = min(image_rows, height + RIM * min(2, parts - 1))
    segments = image_cols // SEG
    local_count = float(height * image_cols)
    pixel_count = local_count * devices
    pool_cells = float(image_rows * image_cols // 4)
    part = functools.partial
    counts = dict(local_count=local_count, pixel_count=pixel_count, height=height)
    backs = dict(pixel_count=pixel_count, height=height)
    styled = dict(pool_cells=pool_cells, parts=parts)

    me = lax.axis_index("row") * col_count + lax.axis_index("col")
    first_row = (me % parts) * height
    start = jnp.clip(first_row - RIM, 0, image_rows - rows)
    place = jnp.stack([first_row - start, start // block_rows, me]).astype(jnp.int32)

    field = ((rows, 2, segments, LANES), F32)
    low_field = ((rows + 2, 3, segments, LANES), BF16)
    vec = ((8, LANES), F32)
    two_rows = ((devices, 2, LANES), F32)
    four_rows = ((devices, 4, LANES), F32)
    two_chunks = ((devices, 2, 4, LANES), F32)
    nine = ((BACK, 2 * LANES), BF16)
    taps_scratch = ((FORWARD, 2 * LANES), BF16)

    places = {
        name: i * count
        for count, names in (
            (rows, ("xhat_zero", "xhat_one", "shared", "xhat_two", "grad_resid")),
            (rows + 2, ("hidden_one", "hidden_three", "merged")),
        )
        for i, name in enumerate(names)
    }

    def spots(store, name):
        count = rows if name[0] in "xsg" else rows + 2
        return store.at[places[name] : places[name] + count]

    def store_of(like):
        shape, dtype = like
        row_bytes = shape[1] * segments * LANES * jnp.dtype(dtype).itemsize
        return far(((-(-STORE_BYTES // row_bytes),) + shape[1:], dtype))

    inputs = (
        jnp.transpose(image_batch, (0, 1, 3, 2)), jnp.transpose(flow_target, (0, 1, 3, 2)), cell_labels, valid_mask
    )
    (pay,) = call(
        pack_kernel,
        [((devices, 16, LANES), BF16)],
        *[far(v) for v in inputs],
        scratch=[(v.shape, v.dtype) for v in inputs], sems=4, limit=WHOLE_VMEM, name="pack",
    )
    got_inputs = exchange(pay)
    head_rows = w_head.T
    weights, *back, head_mat = call(
        prepare,
        [far(((STORE_BYTES // (4 * LANES), 2 * LANES), BF16)), nine, nine, nine, ((2 * LANES, LANES), BF16)],
        far(w_first), far(w_convs), far(head_rows),
        scratch=[(w_first.shape, F32), (w_convs.shape, F32), (head_rows.shape, F32), ((3 * FORWARD, 2 * LANES), BF16)],
        sems=3, limit=WHOLE_VMEM, name="prepare",
    )

    sides, raw, pay, count = call(
        part(start_kernel, local_count=local_count, height=height, sources=col_count),
        [((rows + 2, segments, LANES), BF16), field, two_rows, vec],
        place, got_inputs, w_first, far(weights),
        scalars=1, name="image_conv",
    )
    got_zero = exchange(pay)
    summed, pay, inv_zero, fields, lows = call(
        part(first_kernel, spots=spots, **counts),
        [field, two_rows, vec, store_of(field), store_of(low_field)],
        place, got_zero, raw, sides, batch_norm_table, far(weights),
        scalars=1, scratch=[low_field, field, taps_scratch], sems=3, name="first_block",
    )
    got_one = exchange(pay)

    raw, pay, inv_one, fields, lows = call(
        part(pool_kernel, spots=spots, **counts),
        [field, four_rows, vec, store_of(field), store_of(low_field)],
        place, got_one, summed, count, batch_norm_table, far(weights), far(fields), far(lows),
        scalars=1, scratch=[low_field, field, field, nine], sems=4,
        aliases={6: 3, 7: 4}, name="pool_and_merge",
    )
    got_style = exchange(pay)

    resid, pay, inv_two, style, fields, lows = call(
        part(style_kernel, spots=spots, **styled, **counts),
        [field, two_rows, vec, ((devices, LANES), F32), store_of(field), store_of(low_field)],
        place, got_style, raw, batch_norm_table, w_style, far(weights), far(fields), far(lows),
        scalars=1, scratch=[low_field, field, low_field, nine], sems=4,
        aliases={6: 4, 7: 5}, name="decoder",
    )
    got_three = exchange(pay)

    grad_three, xhat_three, pay, inv_three = call(
        part(head_kernel, **counts),
        [field, field, two_rows, vec],
        place, got_three, got_style, resid, sides, head_mat, head_rows, batch_norm_table,
        scalars=1, scratch=[((rows, 2, segments, LANES), BF16), field],
        name="head",
    )
    got_head = exchange(pay)

    grad_two, xhat_two, pay, fields = call(
        part(residual_kernel, spots=spots, **backs),
        [field, field, four_rows, store_of(field)],
        place, got_head, grad_three, xhat_three, inv_three, batch_norm_table, back[2], far(fields), far(lows),
        scalars=1, scratch=[low_field, field, low_field], sems=3,
        aliases={7: 3}, name="residual_back",
    )
    got_two = exchange(pay)

    grad_one, xhat_one, shared, pay = call(
        part(merged_kernel, spots=spots, **backs),
        [field, field, field, two_chunks],
        place, got_two, grad_two, xhat_two, inv_two, batch_norm_table, back[1], far(fields), far(lows),
        scalars=1, scratch=[field, low_field, low_field], sems=4, name="merged_back",
    )
    got_one_back = exchange(pay)

    grad_zero, xhat_zero, pay, more = call(
        part(summed_kernel, spots=spots, **styled, **backs),
        [field, field, two_chunks, vec],
        place, got_one_back, got_two, got_style, grad_one, xhat_one, shared, inv_one, batch_norm_table, w_style, sides,
        back[0], far(fields), far(lows),
        scalars=1, scratch=[low_field, low_field], sems=2, name="summed_back",
    )
    got_first = exchange(pay)

    (pay,) = call(
        part(first_back_kernel, **backs),
        [two_chunks],
        place, got_first, grad_zero, xhat_zero, inv_zero, more, batch_norm_table, sides,
        scalars=1, name="first_back",
    )
    got_last = exchange(pay)

    def results(param, copy):
        return [(param.shape, F32)] * 3 + [(param.shape, BF16)] * copy

    early = call(
        update_early,
        [((1, 1), F32), ((1, 1), F32)] + results(w_style, 0) + results(head_rows, 1) + results(batch_norm_table, 0),
        got_first, got_one_back, got_two, got_head, got_style, far(pay), more, style,
        w_style, head_rows, batch_norm_table, mom_style, mom_head.T, mom_norms, sqr_style, sqr_head.T, sqr_norms,
        scalar_outs=(0, 1), name="update_early",
    )
    late = call(
        update_late,
        results(w_first, 1) + results(w_convs, 1),
        got_last, got_first, got_one_back, w_first, w_convs, mom_first, mom_convs, sqr_first, sqr_convs,
        name="update_late",
    )
    loss, count = early[0].reshape(()), early[1].reshape(())
    head = tuple(value.T for value in early[5:9])
    return (loss, count, *late, *early[2:5], *head, *early[9:12])


def solution(mesh):
    field = P(None, "row", "col", None)
    plane = P(None, "row", "col")
    return jax.shard_map(
        local,
        mesh=mesh,
        in_specs=(field, plane, field, plane) + (P(),) * 15,
        out_specs=(P(),) * 20,
        check_vma=False,
    )
```

```python
import functools

import jax
import jax.numpy as jnp
from jax import lax
from jax.experimental import pallas as pl
from jax.experimental.pallas import tpu as pltpu
from jax.sharding import PartitionSpec as P

STEP = 5

highest = lax.Precision.HIGHEST
norm_eps = 1e-05
flow_scale = 32.0
adam_eps = 1e-08
weight_decay = 0.01
beta_one = 0.5
beta_two = 0.5
rate_table = (0.2, 0.05, 0.15, 0.15, 0.2)

CH = 32
GRP = 4
SEG = 8
LANES = 128
RIM = 8
FLOW, LABEL, MASK = 16, 32, 40
LEFT, RIGHT = 64, 96
AFTER, ROW, BEFORE = 32, 33, 64
F32 = jnp.float32
BF16 = jnp.bfloat16
VMEM_LIMIT = 36 * 1024 * 1024
WHOLE_VMEM = 56 * 1024 * 1024
STORE_BYTES = 32 * 1024 * 1024
FORWARD = 10 * LANES
BACK = 9 * LANES


def lane_of(shape):
    return lax.broadcasted_iota(jnp.int32, shape, len(shape) - 1)


def row_of(shape):
    return lax.broadcasted_iota(jnp.int32, shape, 0)


def group_of(shape):
    return lane_of(shape) >> 5


def fold(v):
    return v + pltpu.roll(v, 32, axis=1) + (pltpu.roll(v, 64, axis=1) + pltpu.roll(v, 96, axis=1))


def spread(v, k):
    return fold(jnp.where(group_of(v.shape) == k, v, 0.0))


def partner(v):
    odd = (group_of(v.shape) & 1) == 1
    return jnp.where(odd, pltpu.roll(v, 32, axis=1), pltpu.roll(v, 96, axis=1))


def tile4(v):
    return jnp.concatenate([v, v, v, v], axis=1)


def col_sum(v):
    return jnp.sum(v, axis=0, keepdims=True)


def zero_row():
    return jnp.zeros((1, LANES), F32)


def groups(*values):
    group = group_of(values[0].shape)
    out = values[-1]
    for k in range(len(values) - 2, -1, -1):
        out = jnp.where(group == k, values[k], out)
    return out


def low(v):
    return v.astype(BF16).astype(F32)


def sig_of(v):
    return 0.5 + 0.5 * jnp.tanh(0.5 * v)


def slope(n, sig):
    return sig * (1.0 + n * (1.0 - sig))


def slope_at(x, gain, bias):
    n = x * gain + bias
    return slope(n, sig_of(n))


def flat(v):
    return v.reshape(-1, LANES)


def loop(count, body):
    def step(i, carry):
        body(i)
        return carry

    lax.fori_loop(0, count, step, 0, unroll=min(count, 5))


def copies(sems, *pairs):
    found = []
    for i, (source, target) in enumerate(pairs):
        found.append(pltpu.make_async_copy(source, target, sems.at[i]))
        found[-1].start()
    return found


def wait(started):
    for copy in started:
        copy.wait()


def shift_segments(v, way):
    half = v.shape[1]
    at = lax.broadcasted_iota(jnp.int32, v.shape, 1)
    if way == 1:
        return jnp.where(at == 0, 0.0, pltpu.roll(v, 1, axis=1))
    return jnp.where(at == half - 1, 0.0, pltpu.roll(v, half - 1, axis=1))


def beside(first, second):
    half = first.shape[1] // 2
    left = jnp.concatenate([shift_segments(second[:, half:], 1), second[:, :half]], axis=1)
    right = jnp.concatenate([first[:, half:], shift_segments(first[:, :half], -1)], axis=1)
    return left, right


def put_low(ref, row, first, second, marked=False):
    left, right = beside(first, second)
    lane = lane_of(left.shape)
    edge = jnp.where(lane < 64, right, left)
    if marked:
        at = lax.broadcasted_iota(jnp.int32, left.shape, 1)
        edge = jnp.where(lane == ROW, 1.0, edge)
        edge = jnp.where(lane == AFTER, jnp.where(at == left.shape[1] - 1, 0.0, 1.0), edge)
        edge = jnp.where(lane == BEFORE, jnp.where(at == 0, 0.0, 1.0), edge)
    at = pl.ds(row + 1, first.shape[0])
    for k, v in enumerate((first, second, edge)):
        ref[at, k] = v.astype(BF16)


def blank(ref):
    zero = jnp.zeros((1,) + ref.shape[1:], ref.dtype)
    ref[0:1] = zero
    ref[ref.shape[0] - 1 : ref.shape[0]] = zero


def views(src, row, rows):
    return [flat(src[pl.ds(row + r, rows), k]) for r in range(3) for k in (2, 0, 1)]


def conv(src, mat, row, rows, *more):
    wide = jnp.concatenate(views(src, row, rows) + list(more), axis=1)
    return jnp.dot(wide, mat[...], preferred_element_type=F32)


def blocks_of(y, rows):
    return [y[:, k * LANES : (k + 1) * LANES].reshape(rows, -1, LANES) for k in range(2)]


def narrow(v):
    while v.shape[0] > 1:
        half = v.shape[0] // 2
        v = v[:half] + v[half:]
    return v[0]


def row_sums(first, rows, values):
    step = 4

    def add(i, carry):
        found = [values(pl.ds(first + step * i, step), k) for k in range(2)]
        return tuple(c + a + b for c, a, b in zip(carry, *found))

    shapes = jax.eval_shape(lambda: values(pl.ds(0, step), 0))
    zeros = tuple(jnp.zeros(v.shape, F32) for v in shapes)
    found = lax.fori_loop(0, rows // step, add, zeros, unroll=min(rows // step, 8))
    return [col_sum(narrow(v)) for v in found]


def local_stats(v, first, rows, count):
    mean = row_sums(first, rows, lambda at, k: (v[at, k],))[0] * (GRP / count)

    def square(at, k):
        away = v[at, k] - mean
        return (away * away,)

    return mean, row_sums(first, rows, square)[0]


def merge_stats(means, squares, local_count, pixel_count):
    mean = fold(col_sum(means)) / (GRP * means.shape[0])
    away = means - mean
    total = fold(col_sum(squares + (local_count / GRP) * (away * away)))
    return mean, lax.rsqrt(total / pixel_count + norm_eps)


def send(pay, *rows):
    value = rows[-1]
    if len(rows) > 1:
        at = row_of(pay.shape[1:])
        value = jnp.broadcast_to(value, pay.shape[1:])
        for k in range(len(rows) - 2, -1, -1):
            value = jnp.where(at == k, rows[k], value)
    pay[...] = jnp.broadcast_to(value[None], pay.shape)


def affine(table, q):
    return tile4(table[0, q : q + 1, :]), tile4(table[1, q : q + 1, :])


def diagonal_blocks(mat):
    wide = tile4(mat)
    group = group_of(wide.shape)
    return jnp.concatenate([jnp.where(group == b, wide, 0.0) for b in range(GRP)], axis=0)


def notes(ref, *rows):
    for i, row in enumerate(rows):
        ref[i : i + 1, :] = row


def taps_at(store, i):
    return store.at[FORWARD * i : FORWARD * i + (BACK if i else FORWARD)]


def pack_kernel(image_in, flow_in, labels_in, valid_in, out, image, flow, labels, valid, sems):
    fetched = copies(sems, (image_in, image), (flow_in, flow), (labels_in, labels), (valid_in, valid))
    images, height, _, width = image.shape
    parts = out.shape[0] // images
    wait(fetched)
    fields = [image[:, :, c, :].astype(F32) for c in range(2)]
    fields += [flow[:, :, c, :].astype(F32) for c in range(2)]
    fields += [labels[...].astype(F32), valid[...].astype(F32)]
    halves = width // 16
    shape = (width, halves * LANES)
    lane = lane_of(shape)
    column = (lane >> 7) * 16 + ((lane >> 6) & 1) * 8 + (lane & 7)
    hit = row_of(shape) == column
    which = (lane >> 3) & 7
    total = jnp.zeros((images * height, halves * LANES), F32)
    for k, v in enumerate(fields):
        x = v.reshape(images * height, width).astype(BF16)
        mat = jnp.where(hit & (which == k), 1.0, 0.0).astype(BF16)
        total = total + jnp.dot(x, mat, preferred_element_type=F32)
    for b in range(images):
        rows = total[b * height : (b + 1) * height]
        slot = jnp.concatenate([rows[:, h * LANES : (h + 1) * LANES] for h in range(halves)], axis=0).astype(BF16)
        for p in range(parts):
            out[b * parts + p] = slot


COLUMNS = ((8, None, None, -1), (0, 1, 2, 3), (4, 5, 6, 7))


def conv_matrix(taps, mats, base, back):
    out_at = group_of((CH, 2 * LANES))
    for r in range(3):
        wide = []
        for s in range(3):
            if back:
                k = taps[3 * (2 - r) + s]
                k = jnp.concatenate([k, k, k, k], axis=0).T
            else:
                k = tile4(taps[3 * r + s])
            wide.append(jnp.concatenate([k, k], axis=1))
        for d in range(3):
            for a in range(GRP):
                val = jnp.zeros((CH, 2 * LANES), F32)
                column = COLUMNS[d][a]
                if column is not None:
                    for s in range(3):
                        val = jnp.where(out_at == (column + s - 1 if back else column + 1 - s), wide[s], val)
                mats[pl.ds(base + (3 * r + d) * LANES + CH * a, CH), :] = val.astype(BF16)


def image_lanes(shape):
    at = row_of(shape)
    kind = at >> 5
    column = (at & 7) + jnp.where(kind == LEFT // 32, -SEG, jnp.where(kind == RIGHT // 32, SEG, 0))
    return (kind != 1) & ((at & 31) < 16), (at >> 3) & 1, column


def first_taps(w_first, t):
    found = [tile4(low(w_first[t][c : c + 1])) for c in range(2)]
    return [jnp.concatenate([v, v], axis=1) for v in found]


def image_matrix(w_first, r):
    shape = (LANES, 2 * LANES)
    inside, channel, here = image_lanes(shape)
    val = jnp.zeros(shape, F32)
    for s in range(3):
        for c, tap in enumerate(first_taps(w_first, 3 * r + s)):
            val = jnp.where(inside & (channel == c) & (here == group_of(shape) + s - 1), tap, val)
    return val.astype(BF16)


def prepare(w_first_in, w_convs_in, w_head_in, store, back_zero, back_one, back_two, head_mat, w_first, w_convs, w_head, mats, sems):
    wait(copies(sems, (w_first_in, w_first), (w_convs_in, w_convs), (w_head_in, w_head)))
    shape = (LANES, 2 * LANES)
    inside, channel, here = image_lanes(shape)
    val = jnp.zeros(shape, F32)
    for c, tap in enumerate(first_taps(w_first, 9)):
        val = jnp.where((row_of(shape) < 16) & (channel == c) & (here == group_of(shape)), tap, val)
    mats[BACK:FORWARD, :] = val.astype(BF16)
    stored = []
    for i in range(3):
        conv_matrix(w_convs.at[i], mats, FORWARD * i, False)
        stored += copies(sems.at[i:], (taps_at(mats, i), taps_at(store, i)))
    for i, back in enumerate((back_zero, back_one, back_two)):
        conv_matrix(w_convs.at[i], back, 0, True)
    lane = lane_of((CH, LANES))
    head = jnp.zeros((CH, LANES), F32)
    diagonal = row_of((CH, CH)) == lane_of((CH, CH))
    for k in range(3):
        column = jnp.sum(jnp.where(diagonal, low(w_head[k : k + 1, 0:CH]), 0.0), axis=1, keepdims=True)
        head = jnp.where((lane >> 3) == FLOW // 8 + k, column, head)
    for y in range(SEG):
        head_mat[CH * y : CH * (y + 1), :] = jnp.where((lane & 7) == y, head, 0.0).astype(BF16)
    wait(stored)


def start_kernel(place, got, w_first, prepared, sides, raw, pay, vec, *, local_count, height, sources):
    rows, segments = raw.shape[0], raw.shape[2]
    off, block = place[0], place[1]
    blank(sides)

    def eight(t):
        v = got[pl.ds((block + t) * sources, sources)].astype(F32)
        v = jnp.swapaxes(v.reshape(segments // 2, 8, LANES), 0, 1)
        near = lane_of(v.shape) < 64
        v = jnp.concatenate([jnp.where(near, v, 0.0), jnp.where(near, pltpu.roll(v, 64, axis=2), 0.0)], axis=1)
        pixels = jnp.where(lane_of(v.shape) < 16, v, 0.0)
        left, right = beside(pixels, pixels)
        v = v + pltpu.roll(left, LEFT, axis=2) + pltpu.roll(right, RIGHT, axis=2)
        sides[pl.ds(8 * t + 1, 8)] = v.astype(BF16)

    loop(rows // 8, eight)
    y = None
    for r in range(3):
        part = jnp.dot(flat(sides[r : r + rows]), image_matrix(w_first, r), preferred_element_type=F32)
        y = part if y is None else y + part
    raw[:, 0], raw[:, 1] = blocks_of(y, rows)
    mean, square = local_stats(raw, off, height, local_count)
    mask = jnp.zeros(sides.shape[1:], F32)
    for i in range(height):
        mask = mask + sides[off + 1 + i].astype(F32)
    lane = lane_of(mask.shape)
    count = jnp.sum(jnp.where((lane >= MASK) & (lane < MASK + 8), mask, 0.0))
    send(pay, mean, square)
    notes(vec, jnp.full((1, LANES), count, F32))


def first_kernel(place, got, raw, sides, table, weights, summed, pay, vec, fields, lows, hidden, xhat, taps, sems, *, spots, local_count, pixel_count, height):
    fetched = copies(sems, (taps_at(weights, 0), taps))
    mean, inverse = merge_stats(got[:, 0, :], got[:, 1, :], local_count, pixel_count)
    notes(vec, inverse)
    gain, bias = affine(table, 0)
    rows = raw.shape[0]

    def norm_rows(i):
        at = pl.ds(4 * i, 4)
        out = []
        for k in range(2):
            x = (raw[at, k] - mean) * inverse
            xhat[at, k] = x
            n = x * gain + bias
            out.append(n * sig_of(n))
        put_low(hidden, 4 * i, *out)

    blank(hidden)
    loop(rows // 4, norm_rows)
    stored = copies(sems.at[1:], (xhat, spots(fields, "xhat_zero")), (hidden, spots(lows, "hidden_one")))
    wait(fetched)
    y = conv(hidden, taps, 0, rows, flat(sides[1 : rows + 1]))
    summed[:, 0], summed[:, 1] = blocks_of(y, rows)
    send(pay, *local_stats(summed, place[0], height, local_count))
    wait(stored)


def pool_kernel(place, got, summed, count_in, table, weights, fields_in, lows_in, raw, pay, vec, fields, lows, merged, xhat, shared, taps, sems, *, spots, local_count, pixel_count, height):
    fetched = copies(sems, (taps_at(weights, 1), taps))
    mean, inverse = merge_stats(got[:, 0, :], got[:, 1, :], local_count, pixel_count)
    gain, bias = affine(table, 1)
    rows, segments = summed.shape[0], summed.shape[2]
    off = place[0]

    step = 4

    def some(i, carry):
        at = pl.ds(step * i, step)
        pairs = (step // 2, 2, segments, LANES)
        outs, sums = [], [jnp.zeros((step // 2 * segments, LANES), F32) for _ in range(3)]
        for k in range(2):
            x = (summed[at, k] - mean) * inverse
            n = x * gain + bias
            sig = sig_of(n)
            e = (n * sig).reshape(pairs)
            top = flat(jnp.maximum(e[:, 0], e[:, 1]))
            top = jnp.maximum(top, partner(top))
            wide_top = top.reshape(step // 2, 1, segments, LANES)
            exps = jnp.exp(e - wide_top)
            whole = flat(exps[:, 0] + exps[:, 1])
            whole = whole + partner(whole)
            pooled = top + jnp.log(whole)
            outs.append((e + pooled.reshape(wide_top.shape)).reshape(step, segments, LANES))
            share = exps * (1.0 / whole).reshape(wide_top.shape) * slope(n, sig).reshape(pairs)
            share_x = share * x.reshape(pairs)
            xhat[at, k] = x
            shared[at, k] = share.reshape(step, segments, LANES)
            sums[0] = sums[0] + pooled
            sums[1] = sums[1] + flat(share[:, 0] + share[:, 1])
            sums[2] = sums[2] + flat(share_x[:, 0] + share_x[:, 1])
        put_low(merged, step * i, *outs)
        mine = (step * i >= off) & (step * i < off + height)
        keep = jnp.where(mine, 1.0, 0.0)
        return tuple(a + keep * b for a, b in zip(carry, sums))

    blank(merged)
    zero = jnp.zeros((step // 2 * segments, LANES), F32)
    sums = lax.fori_loop(0, rows // step, some, (zero, zero, zero), unroll=min(rows // step, 5))
    pool_sum, share_sum, share_x = [fold(col_sum(v)) for v in sums]
    stored = copies(
        sems.at[1:],
        (xhat, spots(fields, "xhat_one")),
        (shared, spots(fields, "shared")),
        (merged, spots(lows, "merged")),
    )
    wait(fetched)
    raw[:, 0], raw[:, 1] = blocks_of(conv(merged, taps, 0, rows), rows)
    mean, square = local_stats(raw, place[0], height, local_count)
    send(pay, mean, square, groups(0.5 * pool_sum, share_sum, share_x, count_in[0:1]))
    notes(vec, inverse)
    wait(stored)


def by_image(v, parts):
    devices = v.shape[0]
    step = 1
    while step < parts:
        upper = (row_of(v.shape) // step) % 2 == 1
        v = v + jnp.where(upper, pltpu.roll(v, step, axis=0), pltpu.roll(v, devices - step, axis=0))
        step *= 2
    return v


def mine_of(v, me):
    return col_sum(jnp.where(row_of(v.shape) == me, v, 0.0))


def style_kernel(place, got, raw, table, w_style, w_convs_in, weights, fields_in, lows_in, resid, pay, vec, style_out, fields, lows, hidden, xhat, merged, slopes, w_conv, taps, sems, *, spots, local_count, pixel_count, pool_cells, height, parts):
    fetched = copies(sems, (taps_at(weights, 2), taps), (spots(lows_in, "merged"), merged), (w_convs_in.at[2], w_conv))
    style = by_image(spread(got[:, 2, :], 0), parts) / pool_cells
    style_out[...] = style
    one, two = [
        jnp.dot(style, diagonal_blocks(w_style[i]), precision=highest, preferred_element_type=F32) for i in range(2)
    ]
    mean, inverse = merge_stats(got[:, 0, :] + one, got[:, 1, :], local_count, pixel_count)
    notes(vec, inverse)
    gain, bias = affine(table, 2)
    rows = raw.shape[0]
    me = place[2]
    shift = mine_of(one, me) - mean
    two = mine_of(two, me)

    def norm_rows(i):
        at = pl.ds(4 * i, 4)
        out = []
        for k in range(2):
            x = (raw[at, k] + shift) * inverse
            xhat[at, k] = x
            n = x * gain + bias
            sig = sig_of(n)
            slopes[at, k] = slope(n, sig)
            out.append(n * sig)
        put_low(hidden, 4 * i, *out)

    blank(hidden)
    loop(rows // 4, norm_rows)
    stored = copies(sems.at[3:], (xhat, spots(fields, "xhat_two")), (hidden, spots(lows, "hidden_three")))
    wait(fetched)
    for k, y in enumerate(blocks_of(conv(hidden, taps, 0, rows), rows)):
        resid[:, k] = y + two + merged[1 : rows + 1, k].astype(F32)
    wait(stored)
    off = place[0]
    means, squares = local_stats(resid, off, height, local_count)
    centre = fold(means) / GRP
    at = pl.ds(off, height)
    probe = [slopes[at, k] for k in range(2)]
    probe += [slopes[at, k] * xhat[at, k] for k in range(2)]
    probe = jnp.concatenate([flat(v).astype(BF16) for v in probe], axis=1)

    def centred(i):
        at = pl.ds(4 * i, 4)
        put_low(hidden, 4 * i, resid[at, 0] - centre, resid[at, 1] - centre, True)

    loop(rows // 4, centred)
    send(pay, means, squares)
    pay[0:CH, 2, :] = norm_links(hidden, probe, off, height, w_conv, centre)


def norm_links(field, probe, first, rows, taps, centre):
    wide = jnp.concatenate(views(field, first, rows), axis=1)
    found = lax.dot_general(probe, wide, (((0,), (0,)), ((), ())), preferred_element_type=F32)
    group = group_of((CH, LANES))
    out = []
    for half in range(2):

        def piece(y, chunk):
            at = 2 * LANES * half + CH * y
            return found[at : at + CH, chunk * LANES : (chunk + 1) * LANES]

        plain = jnp.zeros((CH, LANES), F32)
        moved = jnp.zeros((CH, LANES), F32)
        for r in range(3):
            first_edge, last_edge = piece(0, 3 * r), piece(SEG - 1, 3 * r)
            edge = first_edge + last_edge
            for y in range(1, SEG - 1):
                edge = edge + piece(y, 3 * r)
            inside = edge[:, ROW : ROW + 1]
            counts = (
                inside + (first_edge[:, BEFORE : BEFORE + 1] - first_edge[:, ROW : ROW + 1]),
                inside,
                inside + (last_edge[:, AFTER : AFTER + 1] - last_edge[:, ROW : ROW + 1]),
            )
            for c in range(3):
                tap = tile4(low(taps[3 * (2 - r) + 2 - c]))
                val = jnp.zeros((CH, LANES), F32)
                for y in range(SEG):
                    d, a = spot_of(y + c - 1)
                    val = val + jnp.where(group == a, piece(y, 3 * r + d), 0.0)
                plain = plain + tap * counts[c]
                moved = moved + tap * val
        out += [plain, fold(moved) + centre * plain]
    return groups(*out)


def spot_of(x):
    if x < 0:
        return 0, 3
    if x == SEG:
        return 0, 0
    return 1 + x // GRP, x % GRP


def head_kernel(place, got, got_style, resid, sides, head_mat, w_head, table, back, fields, grad, xhat, pay, vec, decoded, slopes, grad_low, below_x, sems, *, spots, local_count, pixel_count, height):
    fetched = copies(sems, (spots(fields, "xhat_two"), below_x))
    mean, inverse = merge_stats(got[:, 0, :], got[:, 1, :], local_count, pixel_count)
    notes(vec, inverse, mean)
    gain, bias = affine(table, 3)
    rows, segments = resid.shape[0], resid.shape[2]
    off = place[0]

    def norm_rows(i):
        at = pl.ds(4 * i, 4)
        for k in range(2):
            x = (resid[at, k] - mean) * inverse
            n = x * gain + bias
            s = sig_of(n)
            xhat[at, k] = x
            slopes[at, k] = slope(n, s)
            decoded[at, k] = (n * s).astype(BF16)

    loop(rows // 4, norm_rows)
    head = head_mat[...]
    wide = jnp.concatenate([flat(decoded[:, 0]), flat(decoded[:, 1])], axis=1)
    bias_row = zero_row()
    for k in range(3):
        mine = (lane_of((1, LANES)) >> 3) == FLOW // 8 + k
        bias_row = jnp.where(mine, low(w_head[k : k + 1, CH : CH + 1]), bias_row)
    out = jnp.dot(wide, head, preferred_element_type=F32) + bias_row
    given = flat(sides[1 : rows + 1]).astype(F32)
    lane = lane_of(given.shape)
    is_flow = lane < LABEL
    near = [pltpu.roll(given, LANES - MASK + first, axis=1) for first in (FLOW, FLOW + 8, LABEL)]
    mask = jnp.where(lane < FLOW + 8, near[0], jnp.where(is_flow, near[1], near[2]))
    mask = jnp.where((lane >= FLOW) & (lane < LABEL + 8), mask, 0.0)
    count = jnp.sum(got_style[:, 2, 3 * CH : 3 * CH + 1])
    diff = out - given / flow_scale
    hinge = jnp.maximum(out, 0.0) + jnp.log1p(jnp.exp(-jnp.abs(out)))
    loss = mask * jnp.where(is_flow, diff * diff, hinge - given * out)
    grad_out = (mask * jnp.where(is_flow, 2.0 * diff, sig_of(out) - given) / count).astype(BF16)
    at_row = lax.broadcasted_iota(jnp.int32, loss.shape, 0)
    inside = (at_row >= off * segments) & (at_row < (off + height) * segments)
    loss_sum = jnp.sum(jnp.where(inside, loss, 0.0))
    mine_out = jnp.where(inside, grad_out.astype(F32), 0.0).astype(BF16)
    outs = col_sum(mine_out.astype(F32))
    found = lax.dot_general(mine_out, wide, (((0,), (0,)), ((), ())), preferred_element_type=F32)
    shape = found.shape
    found = jnp.where((row_of(shape) & 7) == group_of(shape), found, 0.0)
    whole = [col_sum(found[FLOW + 8 * k : FLOW + 8 * k + 8]) for k in range(3)]
    whole = [fold(v[:, 0:LANES] + v[:, LANES:]) for v in whole]
    row = groups(*whole, zero_row())
    lane = lane_of((1, LANES))
    for k in range(3):
        row = jnp.where(lane == 3 * CH + k, jnp.sum(jnp.where((lane >> 3) == FLOW // 8 + k, outs, 0.0)), row)
    row = jnp.where(lane == 3 * CH + 3, loss_sum, row)
    y = lax.dot_general(grad_out, head, (((1,), (1,)), ((), ())), preferred_element_type=F32)
    for k, g in enumerate(blocks_of(y, rows)):
        grad[:, k] = g * slopes[:, k]
    factor = gain * inverse
    back_rows(grad_low, rows, lambda at, k: factor * grad[at, k])
    shift_sum, scale_sum = own_sums(grad, xhat, off, height)
    wait(fetched)
    y = conv(grad_low, back, 0, rows)
    slopes[:, 0], slopes[:, 1] = blocks_of(y, rows)
    gain, bias = affine(table, 2)

    def links(at, k):
        x = below_x[at, k]
        g = slopes[at, k] * slope_at(x, gain, bias)
        return g, g * x

    below = [fold(v) for v in row_sums(off, height, links)]
    send(pay, groups(shift_sum, scale_sum, *below), row, col_sum(got[:, 2, :]))


def own_sums(grad, xhat, first, rows):
    def both(at, k):
        g = grad[at, k]
        return g, g * xhat[at, k]

    return [fold(v) for v in row_sums(first, rows, both)]


def back_sums(got, pixel_count):
    whole = col_sum(got)
    return spread(whole, 0) / pixel_count, spread(whole, 1) / pixel_count


def low_sum(grad_low, first, rows):
    return fold(row_sums(first + 1, rows, lambda at, k: (grad_low[at, k].astype(F32),))[0])


def norm_back(grad, xhat, factor, shift, scale):
    return factor * (grad - (shift + xhat * scale))


def back_rows(grad_low, rows, value):
    def some(i):
        put_low(grad_low, 4 * i, *[value(pl.ds(4 * i, 4), k) for k in range(2)])

    blank(grad_low)
    loop(rows // 4, some)


def tap_sums(field, grad, first, rows, out):
    at = pl.ds(first + 1, rows)
    g = jnp.concatenate([flat(grad[at, 0]), flat(grad[at, 1])], axis=1)
    wide = jnp.concatenate(views(field, first, rows), axis=1)
    found = lax.dot_general(g, wide, (((0,), (0,)), ((), ())), preferred_element_type=F32)
    group = group_of((CH, LANES))
    taps = []
    for r in range(3):
        for s in range(3):
            val = jnp.zeros((CH, LANES), F32)
            for y in range(SEG):
                x = y + s - 1
                d, a = spot_of(x)
                spot = (3 * r + d) * LANES
                val = val + jnp.where(group == a, found[CH * y : CH * y + CH, spot : spot + LANES], 0.0)
            taps.append(fold(val))
    for q in range(3):
        val = taps[4 * q]
        for b in range(1, min(4, 9 - 4 * q)):
            val = jnp.where(group == b, taps[4 * q + b], val)
        out[:, q, :] = val


def decoder_back_kernel(place, got, grad, xhat, vec, vec_two, table, back_two, back_one, fields, lows, below, below_x, shared, pay, more, kept_grad, mid_x, mid, low_two, low_one, field_two, field_one, sems, *, spots, pixel_count, height):
    fetched = copies(
        sems,
        (spots(fields, "xhat_two"), mid_x),
        (spots(fields, "xhat_one"), below_x),
        (spots(fields, "shared"), shared),
        (spots(lows, "hidden_three"), field_two),
        (spots(lows, "merged"), field_one),
    )
    devices = got.shape[0]
    rows = grad.shape[0]
    off = place[0]
    total = col_sum(got[:, 0, :])
    shift, scale = spread(total, 0) / pixel_count, spread(total, 1) / pixel_count
    inverse, mean = vec[0:1], vec[1:2]
    factor = affine(table, 3)[0] * inverse
    slant = scale * inverse
    held, carried = factor * (shift - slant * mean), factor * slant
    links = got[0:CH, 2, :] * groups(held, carried, held, carried)
    group = group_of(links.shape)
    mine = (lane_of(links.shape) & 31) == row_of(links.shape)

    def across(pick):
        column = jnp.sum(jnp.where(pick, links, 0.0), axis=1, keepdims=True)
        return col_sum(jnp.where(mine, column, 0.0))

    shift_two = spread(total, 2) - across(group < 2)
    scale_two = spread(total, 3) - across(group >= 2)
    notes(more, scale_two, shift_two)

    def value(at, k):
        g = norm_back(grad[at, k], xhat[at, k], factor, shift, scale)
        kept_grad[at, k] = g
        return g

    back_rows(low_two, rows, value)
    wait(fetched)
    mid[:, 0], mid[:, 1] = blocks_of(conv(low_two, back_two, 0, rows), rows)
    gain, bias = affine(table, 2)
    factor = gain * vec_two[0:1]
    shift, scale = shift_two / pixel_count, scale_two / pixel_count

    def value_two(at, k):
        x = mid_x[at, k]
        return norm_back(mid[at, k] * slope_at(x, gain, bias), x, factor, shift, scale)

    back_rows(low_one, rows, value_two)
    sum_two = low_sum(low_two, off, height)
    sum_one = low_sum(low_one, off, height)
    y = conv(low_one, back_one, 0, rows)
    gain, bias = affine(table, 1)
    for k, y in enumerate(blocks_of(y, rows)):
        g = (y + kept_grad[:, k]).reshape(rows // 2, 2, -1, LANES)
        both = flat(g[:, 0] + g[:, 1])
        both = (both + partner(both)).reshape(rows // 2, 1, -1, LANES)
        g = g * slope_at(below_x[:, k], gain, bias).reshape(g.shape) + both * shared[:, k].reshape(g.shape)
        below[:, k] = g.reshape(rows, -1, LANES)
    row = groups(*own_sums(below, below_x, off, height), sum_one, sum_two)
    pay[:, 0] = jnp.broadcast_to(row[None], (devices, 4, LANES))
    if devices > CH:
        pay[CH:, 1] = jnp.zeros((devices - CH, 4, LANES), F32)
    tap_sums(field_two, low_two, off, height, pay.at[0:CH, 0, 1:4])
    tap_sums(field_one, low_one, off, height, pay.at[0:CH, 1])
    pay[0:CH, 1, 3, :] = jnp.zeros((CH, LANES), F32)


def summed_kernel(place, got, got_style, grad, xhat, shared, vec, table, w_style, sides, back, fields, lows, below, below_x, pay, more, field, grad_low, sems, *, spots, pixel_count, pool_cells, height, parts):
    fetched = copies(
        sems,
        (spots(fields, "xhat_zero"), below_x),
        (spots(lows, "hidden_one"), field),
    )
    devices = got.shape[0]
    off = place[0]
    rows = grad.shape[0]
    dims = (((1,), (1,)), ((), ()))
    first = got[:, 0, 0, :]
    each = lax.dot_general(
        spread(first, 2), diagonal_blocks(w_style[0]), dims, precision=highest, preferred_element_type=F32
    ) + lax.dot_general(
        spread(first, 3), diagonal_blocks(w_style[1]), dims, precision=highest, preferred_element_type=F32
    )
    each = each / pool_cells
    total = col_sum(first)
    shift = spread(total, 0) + col_sum(each * by_image(spread(got_style[:, 2, :], 1), parts))
    scale = spread(total, 1) + col_sum(each * by_image(spread(got_style[:, 2, :], 2), parts))
    mine = col_sum(jnp.where(row_of(each.shape) // parts == place[2] // parts, each, 0.0))
    factor = affine(table, 1)[0] * vec[0:1]
    shift_mean, scale_mean = shift / pixel_count, scale / pixel_count
    def value(at, k):
        return norm_back(grad[at, k] + shared[at, k] * mine, xhat[at, k], factor, shift_mean, scale_mean)

    back_rows(grad_low, rows, value)
    gain, bias = affine(table, 0)
    wait(fetched)
    for k, y in enumerate(blocks_of(conv(grad_low, back, 0, rows), rows)):
        below[:, k] = y * slope_at(below_x[:, k], gain, bias)
    two, one = jnp.sum(got[:, 0], axis=0), jnp.sum(got[:, 1], axis=0)
    row = groups(*own_sums(below, below_x, off, height), two[3:4], one[2:3])
    chunk = jnp.concatenate([row, two[1:3], one[0:1]], axis=0)
    pay[:, 0] = jnp.broadcast_to(chunk[None], (devices, 4, LANES))
    pay[:, 1] = jnp.broadcast_to(one[1:2][None], (devices, 4, LANES))
    tap_sums(field, grad_low, off, height, pay.at[0:CH, 1, 1:4])
    at = pl.ds(off + 1, height)
    low_own = jnp.concatenate([flat(grad_low[at, 0]), flat(grad_low[at, 1])], axis=1)
    side = pixel_taps(sides, off + 1, height, low_own, (0,))[0]
    notes(more, scale, shift, *side)


def pixel_taps(sides, row, rows, grad, shift):
    x = flat(sides[pl.ds(row, rows)])
    found = lax.dot_general(x, grad, (((0,), (0,)), ((), ())), preferred_element_type=F32)
    inside, channel, here = image_lanes(found.shape)
    here = here - group_of(found.shape)
    out = []
    for s in shift:
        both = []
        for c in range(2):
            hit = inside & (channel == c) & (here == s)
            v = col_sum(jnp.where(hit, found, 0.0))
            both.append(fold(v[:, 0:LANES] + v[:, LANES:]))
        out.append(both)
    return out


def first_back_kernel(place, got, grad, xhat, vec, more, table, sides, pay, *, pixel_count, height):
    devices = got.shape[0]
    off = place[0]
    whole = col_sum(got[:, 0, 0, :])
    shift, scale = spread(whole, 0) / pixel_count, spread(whole, 1) / pixel_count
    factor = affine(table, 0)[0] * vec[0:1]
    at = pl.ds(off, height)
    low_grad = jnp.concatenate(
        [flat(norm_back(grad[at, k], xhat[at, k], factor, shift, scale).astype(BF16)) for k in range(2)], axis=1
    )
    entries = []
    for r in range(3):
        for tap in pixel_taps(sides, off + r, height, low_grad, (-1, 0, 1)):
            entries.extend(tap)
    entries.extend([more[2:3], more[3:4]])
    rows = [groups(*entries[4 * q : 4 * q + 4]) for q in range(5)]
    conv_zero = jnp.sum(got[:, 1], axis=0)
    chunk = [jnp.concatenate(rows[0:4], axis=0), jnp.concatenate([rows[4], conv_zero[1:4]], axis=0)]
    for k in range(2):
        pay[:, k] = jnp.broadcast_to(chunk[k][None], (devices, 4, LANES))


def adamw(master, moment, square, grad, rate):
    new_moment = beta_one * moment + (1.0 - beta_one) * grad
    new_square = beta_two * square + (1.0 - beta_two) * grad * grad
    moment_hat = new_moment / (1.0 - beta_one**STEP)
    square_hat = new_square / (1.0 - beta_two**STEP)
    new_master = master - rate * (moment_hat / (jnp.sqrt(square_hat) + adam_eps) + weight_decay * master)
    return new_master, new_moment, new_square


def put(at, refs, grad, rate, outs):
    found = adamw(*[ref[at] for ref in refs], grad, rate)
    for out, value in zip(outs, found + (found[0].astype(BF16),)):
        out[at] = value


def update_early(
    got_first, got_one_back, got_head, got_style, pay, more, more_two, style,
    w_style, w_head, table, m_style, m_head, m_norms, s_style, s_head, s_norms,
    loss_out, count_out,
    style_master, style_moment, style_square,
    head_master, head_moment, head_square, head_copy,
    norms_master, norms_moment, norms_square,
):
    count_out[0, 0] = jnp.sum(got_style[:, 2, 3 * CH : 3 * CH + 1])
    loss_out[0, 0] = jnp.sum(got_head[:, 1, 99:100])
    dims = (((0,), (0,)), ((), ()))
    for i in range(2):
        sums = spread(got_one_back[:, 0, 0, :], 2 + i)
        grad = lax.dot_general(style[...], sums, dims, precision=highest, preferred_element_type=F32)
        put(i, (w_style, m_style, s_style), grad[0:CH, 0:CH], rate_table[2], (style_master, style_moment, style_square))

    head = col_sum(got_head[:, 1, :])
    lane = lane_of((1, LANES))
    rows = []
    for k in range(3):
        last = jnp.sum(jnp.where(lane == 3 * CH + k, head, 0.0), axis=1, keepdims=True)
        rows.append(jnp.where(lane < CH, spread(head, k), last))
    grad = jnp.concatenate(rows, axis=0)[:, 0 : CH + 1]
    put(slice(None), (w_head, m_head, s_head), grad, rate_table[3], (head_master, head_moment, head_square, head_copy))

    three_sums = col_sum(got_head[:, 0, :])
    zero_sums = col_sum(got_first[:, 0, 0, :])
    scales = [spread(zero_sums, 1), more[0:1], more_two[0:1], spread(three_sums, 1)]
    shifts = [spread(zero_sums, 0), more[1:2], more_two[1:2], spread(three_sums, 0)]
    for i, rows in enumerate((scales, shifts)):
        grad = jnp.concatenate(rows, axis=0)[:, 0:CH]
        put(i, (table, m_norms, s_norms), grad, rate_table[4], (norms_master, norms_moment, norms_square))


def update_late(
    got, got_first, w_first, w_convs, m_first, m_convs, s_first, s_convs,
    first_master, first_moment, first_square, first_copy,
    convs_master, convs_moment, convs_square, convs_copy,
):
    refs = (w_convs, m_convs, s_convs)
    outs = (convs_master, convs_moment, convs_square, convs_copy)
    last = got_first[0:CH, 0, 0, :].T
    packs = (
        [got[0:CH, 1, q, :].T for q in (1, 2, 3)],
        [got_first[0:CH, 0, 3, :].T, got_first[0:CH, 1, 0, :].T, last[3 * CH :]],
        [got_first[0:CH, 0, 1, :].T, got_first[0:CH, 0, 2, :].T, last[2 * CH : 3 * CH]],
    )
    for i, pack in enumerate(packs):
        for t in range(9):
            b = t % 4
            put((i, t), refs, pack[t // 4][CH * b : CH * b + CH], rate_table[1], outs)

    first = jnp.concatenate([jnp.sum(got[:, 0], axis=0), jnp.sum(got[:, 1], axis=0)[0:1]], axis=0)
    refs = (w_first, m_first, s_first)
    outs = (first_master, first_moment, first_square, first_copy)
    for t in range(10):
        pair = [spread(first[e // 4 : e // 4 + 1], e % 4)[:, 0:CH] for e in (2 * t, 2 * t + 1)]
        put(t, refs, jnp.concatenate(pair, axis=0), rate_table[0], outs)


def far(x):
    return ("far", x)


def call(kernel, outs, *operands, scalars=0, scratch=(), sems=0, scalar_outs=(), aliases=None, limit=VMEM_LIMIT, name):
    smem = pl.BlockSpec(memory_space=pltpu.SMEM)
    vmem = pl.BlockSpec(memory_space=pltpu.VMEM)
    hbm = pl.BlockSpec(memory_space=pltpu.HBM)
    is_far = lambda x: isinstance(x, tuple) and x[0] == "far"
    in_specs = [smem if i < scalars else hbm if is_far(x) else vmem for i, x in enumerate(operands)]
    out_specs = [smem if i in scalar_outs else hbm if is_far(x) else vmem for i, x in enumerate(outs)]
    plain = lambda x: x[1] if is_far(x) else x
    shapes = [pltpu.VMEM(shape, dtype) for shape, dtype in scratch]
    if sems:
        shapes.append(pltpu.SemaphoreType.DMA((sems,)))
    return pl.pallas_call(
        kernel,
        out_shape=[jax.ShapeDtypeStruct(*plain(x)) for x in outs],
        in_specs=in_specs,
        out_specs=out_specs,
        scratch_shapes=shapes,
        input_output_aliases=aliases or {},
        compiler_params=pltpu.CompilerParams(vmem_limit_bytes=limit),
        name=name,
    )(*[plain(x) for x in operands])


def exchange(pay):
    return lax.all_to_all(pay, ("row", "col"), 0, 0)


def local(
    image_batch, valid_mask, flow_target, cell_labels,
    w_first, w_convs, w_style, w_head, batch_norm_table,
    mom_first, mom_convs, mom_style, mom_head, mom_norms,
    sqr_first, sqr_convs, sqr_style, sqr_head, sqr_norms,
):
    images, block_rows, block_cols, _ = image_batch.shape
    row_count, col_count = lax.axis_size("row"), lax.axis_size("col")
    devices = row_count * col_count
    parts = devices // images
    image_rows, image_cols = row_count * block_rows, col_count * block_cols
    assert devices == parts * images and block_rows == RIM and block_cols == 2 * block_rows * 2
    assert image_rows % (parts * RIM) == 0 and devices >= CH
    height = image_rows // parts
    rows = min(image_rows, height + RIM * min(2, parts - 1))
    segments = image_cols // SEG
    local_count = float(height * image_cols)
    pixel_count = local_count * devices
    pool_cells = float(image_rows * image_cols // 4)
    part = functools.partial
    counts = dict(local_count=local_count, pixel_count=pixel_count, height=height)
    backs = dict(pixel_count=pixel_count, height=height)
    styled = dict(pool_cells=pool_cells, parts=parts)

    me = lax.axis_index("row") * col_count + lax.axis_index("col")
    first_row = (me % parts) * height
    start = jnp.clip(first_row - RIM, 0, image_rows - rows)
    place = jnp.stack([first_row - start, start // block_rows, me]).astype(jnp.int32)

    field = ((rows, 2, segments, LANES), F32)
    low_field = ((rows + 2, 3, segments, LANES), BF16)
    vec = ((8, LANES), F32)
    two_rows = ((devices, 2, LANES), F32)
    four_rows = ((devices, 4, LANES), F32)
    two_chunks = ((devices, 2, 4, LANES), F32)
    nine = ((BACK, 2 * LANES), BF16)
    taps_scratch = ((FORWARD, 2 * LANES), BF16)

    places = {
        name: i * count
        for count, names in (
            (rows, ("xhat_zero", "xhat_one", "shared", "xhat_two")),
            (rows + 2, ("hidden_one", "hidden_three", "merged")),
        )
        for i, name in enumerate(names)
    }

    def spots(store, name):
        count = rows if name[0] in "xs" else rows + 2
        return store.at[places[name] : places[name] + count]

    def store_of(like):
        shape, dtype = like
        row_bytes = shape[1] * segments * LANES * jnp.dtype(dtype).itemsize
        return far(((-(-STORE_BYTES // row_bytes),) + shape[1:], dtype))

    inputs = (
        jnp.transpose(image_batch, (0, 1, 3, 2)), jnp.transpose(flow_target, (0, 1, 3, 2)), cell_labels, valid_mask
    )
    (pay,) = call(
        pack_kernel,
        [((devices, 16, LANES), BF16)],
        *[far(v) for v in inputs],
        scratch=[(v.shape, v.dtype) for v in inputs], sems=4, limit=WHOLE_VMEM, name="pack",
    )
    got_inputs = exchange(pay)
    head_rows = w_head.T
    weights, *back, head_mat = call(
        prepare,
        [far(((STORE_BYTES // (4 * LANES), 2 * LANES), BF16)), nine, nine, nine, ((2 * LANES, LANES), BF16)],
        far(w_first), far(w_convs), far(head_rows),
        scratch=[(w_first.shape, F32), (w_convs.shape, F32), (head_rows.shape, F32), ((3 * FORWARD, 2 * LANES), BF16)],
        sems=3, limit=WHOLE_VMEM, name="prepare",
    )

    sides, raw, pay, count = call(
        part(start_kernel, local_count=local_count, height=height, sources=col_count),
        [((rows + 2, segments, LANES), BF16), field, two_rows, vec],
        place, got_inputs, w_first, far(weights),
        scalars=1, name="image_conv",
    )
    got_zero = exchange(pay)
    summed, pay, inv_zero, fields, lows = call(
        part(first_kernel, spots=spots, **counts),
        [field, two_rows, vec, store_of(field), store_of(low_field)],
        place, got_zero, raw, sides, batch_norm_table, far(weights),
        scalars=1, scratch=[low_field, field, taps_scratch], sems=3, name="first_block",
    )
    got_one = exchange(pay)

    raw, pay, inv_one, fields, lows = call(
        part(pool_kernel, spots=spots, **counts),
        [field, four_rows, vec, store_of(field), store_of(low_field)],
        place, got_one, summed, count, batch_norm_table, far(weights), far(fields), far(lows),
        scalars=1, scratch=[low_field, field, field, nine], sems=4,
        aliases={6: 3, 7: 4}, name="pool_and_merge",
    )
    got_style = exchange(pay)

    resid, pay, inv_two, style, fields, lows = call(
        part(style_kernel, spots=spots, **styled, **counts),
        [field, four_rows, vec, ((devices, LANES), F32), store_of(field), store_of(low_field)],
        place, got_style, raw, batch_norm_table, w_style, far(w_convs), far(weights), far(fields), far(lows),
        scalars=1, scratch=[low_field, field, low_field, field, (w_convs.shape[1:], F32), nine], sems=5,
        aliases={7: 4, 8: 5}, name="decoder",
    )
    got_three = exchange(pay)

    grad_three, xhat_three, pay, inv_three = call(
        part(head_kernel, spots=spots, **counts),
        [field, field, four_rows, vec],
        place, got_three, got_style, resid, sides, head_mat, head_rows, batch_norm_table, back[2], far(fields),
        scalars=1, scratch=[((rows, 2, segments, LANES), BF16), field, low_field, field], sems=1, name="head",
    )
    got_head = exchange(pay)

    grad_one, xhat_one, shared, pay, more_two = call(
        part(decoder_back_kernel, spots=spots, **backs),
        [field, field, field, two_chunks, vec],
        place, got_head, grad_three, xhat_three, inv_three, inv_two, batch_norm_table, back[2], back[1],
        far(fields), far(lows),
        scalars=1, scratch=[field, field, field, low_field, low_field, low_field, low_field], sems=5,
        name="decoder_back",
    )
    got_one_back = exchange(pay)

    grad_zero, xhat_zero, pay, more = call(
        part(summed_kernel, spots=spots, **styled, **backs),
        [field, field, two_chunks, vec],
        place, got_one_back, got_style, grad_one, xhat_one, shared, inv_one, batch_norm_table, w_style, sides,
        back[0], far(fields), far(lows),
        scalars=1, scratch=[low_field, low_field], sems=2, name="summed_back",
    )
    got_first = exchange(pay)

    (pay,) = call(
        part(first_back_kernel, **backs),
        [two_chunks],
        place, got_first, grad_zero, xhat_zero, inv_zero, more, batch_norm_table, sides,
        scalars=1, name="first_back",
    )
    got_last = exchange(pay)

    def results(param, copy):
        return [(param.shape, F32)] * 3 + [(param.shape, BF16)] * copy

    early = call(
        update_early,
        [((1, 1), F32), ((1, 1), F32)] + results(w_style, 0) + results(head_rows, 1) + results(batch_norm_table, 0),
        got_first, got_one_back, got_head, got_style, far(pay), more, more_two, style,
        w_style, head_rows, batch_norm_table, mom_style, mom_head.T, mom_norms, sqr_style, sqr_head.T, sqr_norms,
        scalar_outs=(0, 1), name="update_early",
    )
    late = call(
        update_late,
        results(w_first, 1) + results(w_convs, 1),
        got_last, got_first, w_first, w_convs, mom_first, mom_convs, sqr_first, sqr_convs,
        name="update_late",
    )
    loss, count = early[0].reshape(()), early[1].reshape(())
    head = tuple(value.T for value in early[5:9])
    return (loss, count, *late, *early[2:5], *head, *early[9:12])


def solution(mesh):
    field = P(None, "row", "col", None)
    plane = P(None, "row", "col")
    return jax.shard_map(
        local,
        mesh=mesh,
        in_specs=(field, plane, field, plane) + (P(),) * 15,
        out_specs=(P(),) * 20,
        check_vma=False,
    )
```

```python
import functools

import jax
import jax.numpy as jnp
from jax import lax
from jax.experimental import pallas as pl
from jax.experimental.pallas import tpu as pltpu
from jax.sharding import PartitionSpec as P

STEP = 5

highest = lax.Precision.HIGHEST
norm_eps = 1e-05
flow_scale = 32.0
adam_eps = 1e-08
weight_decay = 0.01
beta_one = 0.5
beta_two = 0.5
rate_table = (0.2, 0.05, 0.15, 0.15, 0.2)

CH = 32
GRP = 4
SEG = 8
LANES = 128
RIM = 8
FLOW, LABEL, MASK = 16, 32, 40
LEFT, RIGHT = 64, 96
AFTER, ROW, BEFORE = 32, 33, 64
F32 = jnp.float32
BF16 = jnp.bfloat16
VMEM_LIMIT = 36 * 1024 * 1024
WHOLE_VMEM = 56 * 1024 * 1024
STORE_BYTES = 32 * 1024 * 1024
FORWARD = 10 * LANES
BACK = 9 * LANES
IMAGE_AT = 3 * FORWARD


def lane_of(shape):
    return lax.broadcasted_iota(jnp.int32, shape, len(shape) - 1)


def row_of(shape):
    return lax.broadcasted_iota(jnp.int32, shape, 0)


def group_of(shape):
    return lane_of(shape) >> 5


def fold(v):
    return v + pltpu.roll(v, 32, axis=1) + (pltpu.roll(v, 64, axis=1) + pltpu.roll(v, 96, axis=1))


def spread(v, k):
    return fold(jnp.where(group_of(v.shape) == k, v, 0.0))


def partner(v):
    odd = (group_of(v.shape) & 1) == 1
    return jnp.where(odd, pltpu.roll(v, 32, axis=1), pltpu.roll(v, 96, axis=1))


def tile4(v):
    return jnp.concatenate([v, v, v, v], axis=1)


def col_sum(v):
    return jnp.sum(v, axis=0, keepdims=True)


def zero_row():
    return jnp.zeros((1, LANES), F32)


def groups(*values):
    group = group_of(values[0].shape)
    out = values[-1]
    for k in range(len(values) - 2, -1, -1):
        out = jnp.where(group == k, values[k], out)
    return out


def low(v):
    return v.astype(BF16).astype(F32)


def sig_of(v):
    return 0.5 + 0.5 * jnp.tanh(0.5 * v)


def slope(n, sig):
    return sig * (1.0 + n * (1.0 - sig))


def slope_at(x, gain, bias):
    n = x * gain + bias
    return slope(n, sig_of(n))


def flat(v):
    return v.reshape(-1, LANES)


def loop(count, body):
    def step(i, carry):
        body(i)
        return carry

    lax.fori_loop(0, count, step, 0, unroll=min(count, 5))


def copies(sems, *pairs):
    found = []
    for i, (source, target) in enumerate(pairs):
        found.append(pltpu.make_async_copy(source, target, sems.at[i]))
        found[-1].start()
    return found


def wait(started):
    for copy in started:
        copy.wait()


def shift_segments(v, way):
    half = v.shape[1]
    at = lax.broadcasted_iota(jnp.int32, v.shape, 1)
    if way == 1:
        return jnp.where(at == 0, 0.0, pltpu.roll(v, 1, axis=1))
    return jnp.where(at == half - 1, 0.0, pltpu.roll(v, half - 1, axis=1))


def beside(first, second):
    half = first.shape[1] // 2
    left = jnp.concatenate([shift_segments(second[:, half:], 1), second[:, :half]], axis=1)
    right = jnp.concatenate([first[:, half:], shift_segments(first[:, :half], -1)], axis=1)
    return left, right


def put_low(ref, row, first, second, marked=False):
    left, right = beside(first, second)
    lane = lane_of(left.shape)
    edge = jnp.where(lane < 64, right, left)
    if marked:
        at = lax.broadcasted_iota(jnp.int32, left.shape, 1)
        edge = jnp.where(lane == ROW, 1.0, edge)
        edge = jnp.where(lane == AFTER, jnp.where(at == left.shape[1] - 1, 0.0, 1.0), edge)
        edge = jnp.where(lane == BEFORE, jnp.where(at == 0, 0.0, 1.0), edge)
    at = pl.ds(row + 1, first.shape[0])
    for k, v in enumerate((first, second, edge)):
        ref[at, k] = v.astype(BF16)


def blank(ref):
    zero = jnp.zeros((1,) + ref.shape[1:], ref.dtype)
    ref[0:1] = zero
    ref[ref.shape[0] - 1 : ref.shape[0]] = zero


def views(src, row, rows):
    return [flat(src[pl.ds(row + r, rows), k]) for r in range(3) for k in (2, 0, 1)]


def conv(src, mat, row, rows, *more):
    wide = jnp.concatenate(views(src, row, rows) + list(more), axis=1)
    return jnp.dot(wide, mat[...], preferred_element_type=F32)


def blocks_of(y, rows):
    return [y[:, k * LANES : (k + 1) * LANES].reshape(rows, -1, LANES) for k in range(2)]


def narrow(v):
    while v.shape[0] > 1:
        half = v.shape[0] // 2
        v = v[:half] + v[half:]
    return v[0]


def row_sums(first, rows, values):
    step = 4

    def add(i, carry):
        found = [values(pl.ds(first + step * i, step), k) for k in range(2)]
        return tuple(c + a + b for c, a, b in zip(carry, *found))

    shapes = jax.eval_shape(lambda: values(pl.ds(0, step), 0))
    zeros = tuple(jnp.zeros(v.shape, F32) for v in shapes)
    found = lax.fori_loop(0, rows // step, add, zeros, unroll=min(rows // step, 8))
    return [col_sum(narrow(v)) for v in found]


def local_stats(v, first, rows, count):
    mean = row_sums(first, rows, lambda at, k: (v[at, k],))[0] * (GRP / count)

    def square(at, k):
        away = v[at, k] - mean
        return (away * away,)

    return mean, row_sums(first, rows, square)[0]


def merge_stats(means, squares, local_count, pixel_count):
    mean = fold(col_sum(means)) / (GRP * means.shape[0])
    away = means - mean
    total = fold(col_sum(squares + (local_count / GRP) * (away * away)))
    return mean, lax.rsqrt(total / pixel_count + norm_eps)


def send(pay, *rows):
    value = rows[-1]
    if len(rows) > 1:
        at = row_of(pay.shape[1:])
        value = jnp.broadcast_to(value, pay.shape[1:])
        for k in range(len(rows) - 2, -1, -1):
            value = jnp.where(at == k, rows[k], value)
    pay[...] = jnp.broadcast_to(value[None], pay.shape)


def affine(table, q):
    return tile4(table[0, q : q + 1, :]), tile4(table[1, q : q + 1, :])


def diagonal_blocks(mat):
    wide = tile4(mat)
    group = group_of(wide.shape)
    return jnp.concatenate([jnp.where(group == b, wide, 0.0) for b in range(GRP)], axis=0)


def notes(ref, *rows):
    for i, row in enumerate(rows):
        ref[i : i + 1, :] = row


def taps_at(store, i):
    return store.at[FORWARD * i : FORWARD * i + (BACK if i else FORWARD)]


def image_at(store):
    return store.at[IMAGE_AT : IMAGE_AT + 3 * LANES]


def pack_kernel(image_in, flow_in, labels_in, valid_in, out, image, flow, labels, valid, sems):
    fetched = copies(sems, (image_in, image), (flow_in, flow), (labels_in, labels), (valid_in, valid))
    images, height, _, width = image.shape
    parts = out.shape[0] // images
    wait(fetched)
    fields = [image[:, :, c, :].astype(F32) for c in range(2)]
    fields += [flow[:, :, c, :].astype(F32) for c in range(2)]
    fields += [labels[...].astype(F32), valid[...].astype(F32)]
    halves = width // 16
    shape = (width, halves * LANES)
    lane = lane_of(shape)
    column = (lane >> 7) * 16 + ((lane >> 6) & 1) * 8 + (lane & 7)
    hit = row_of(shape) == column
    which = (lane >> 3) & 7
    total = jnp.zeros((images * height, halves * LANES), F32)
    for k, v in enumerate(fields):
        x = v.reshape(images * height, width).astype(BF16)
        mat = jnp.where(hit & (which == k), 1.0, 0.0).astype(BF16)
        total = total + jnp.dot(x, mat, preferred_element_type=F32)
    for b in range(images):
        rows = total[b * height : (b + 1) * height]
        slot = jnp.concatenate([rows[:, h * LANES : (h + 1) * LANES] for h in range(halves)], axis=0).astype(BF16)
        for p in range(parts):
            out[b * parts + p] = slot


COLUMNS = ((8, None, None, -1), (0, 1, 2, 3), (4, 5, 6, 7))


def conv_matrix(taps, mats, base, back):
    out_at = group_of((CH, 2 * LANES))
    for r in range(3):
        wide = []
        for s in range(3):
            if back:
                k = taps[3 * (2 - r) + s]
                k = jnp.concatenate([k, k, k, k], axis=0).T
            else:
                k = tile4(taps[3 * r + s])
            wide.append(jnp.concatenate([k, k], axis=1))
        for d in range(3):
            for a in range(GRP):
                val = jnp.zeros((CH, 2 * LANES), F32)
                column = COLUMNS[d][a]
                if column is not None:
                    for s in range(3):
                        val = jnp.where(out_at == (column + s - 1 if back else column + 1 - s), wide[s], val)
                mats[pl.ds(base + (3 * r + d) * LANES + CH * a, CH), :] = val.astype(BF16)


def image_lanes(shape):
    at = row_of(shape)
    kind = at >> 5
    column = (at & 7) + jnp.where(kind == LEFT // 32, -SEG, jnp.where(kind == RIGHT // 32, SEG, 0))
    return (kind != 1) & ((at & 31) < 16), (at >> 3) & 1, column


def first_taps(w_first, t):
    found = [tile4(low(w_first[t][c : c + 1])) for c in range(2)]
    return [jnp.concatenate([v, v], axis=1) for v in found]


def image_matrix(w_first, r):
    shape = (LANES, 2 * LANES)
    inside, channel, here = image_lanes(shape)
    val = jnp.zeros(shape, F32)
    for s in range(3):
        for c, tap in enumerate(first_taps(w_first, 3 * r + s)):
            val = jnp.where(inside & (channel == c) & (here == group_of(shape) + s - 1), tap, val)
    return val.astype(BF16)


def prepare(w_first_in, w_convs_in, w_head_in, store, back_zero, back_one, back_two, head_mat, w_first, w_convs, w_head, mats, sems):
    wait(copies(sems, (w_first_in, w_first), (w_convs_in, w_convs), (w_head_in, w_head)))
    shape = (LANES, 2 * LANES)
    inside, channel, here = image_lanes(shape)
    val = jnp.zeros(shape, F32)
    for c, tap in enumerate(first_taps(w_first, 9)):
        val = jnp.where((row_of(shape) < 16) & (channel == c) & (here == group_of(shape)), tap, val)
    mats[BACK:FORWARD, :] = val.astype(BF16)
    for r in range(3):
        mats[IMAGE_AT + LANES * r : IMAGE_AT + LANES * (r + 1), :] = image_matrix(w_first, r)
    stored = copies(sems, (image_at(mats), image_at(store)))
    for i in range(3):
        conv_matrix(w_convs.at[i], mats, FORWARD * i, False)
        stored += copies(sems.at[1 + i :], (taps_at(mats, i), taps_at(store, i)))
    for i, back in enumerate((back_zero, back_one, back_two)):
        conv_matrix(w_convs.at[i], back, 0, True)
    lane = lane_of((CH, LANES))
    head = jnp.zeros((CH, LANES), F32)
    diagonal = row_of((CH, CH)) == lane_of((CH, CH))
    for k in range(3):
        column = jnp.sum(jnp.where(diagonal, low(w_head[k : k + 1, 0:CH]), 0.0), axis=1, keepdims=True)
        head = jnp.where((lane >> 3) == FLOW // 8 + k, column, head)
    for y in range(SEG):
        head_mat[CH * y : CH * (y + 1), :] = jnp.where((lane & 7) == y, head, 0.0).astype(BF16)
    wait(stored)


def start_kernel(place, got, weights, sides, raw, pay, vec, taps, first_mat, sems, *, local_count, height, sources):
    fetched = copies(sems, (image_at(weights), first_mat), (taps_at(weights, 0), taps))
    rows, segments = raw.shape[0], raw.shape[2]
    off, block = place[0], place[1]
    blank(sides)

    def eight(t):
        v = got[pl.ds((block + t) * sources, sources)].astype(F32)
        v = jnp.swapaxes(v.reshape(segments // 2, 8, LANES), 0, 1)
        near = lane_of(v.shape) < 64
        v = jnp.concatenate([jnp.where(near, v, 0.0), jnp.where(near, pltpu.roll(v, 64, axis=2), 0.0)], axis=1)
        pixels = jnp.where(lane_of(v.shape) < 16, v, 0.0)
        left, right = beside(pixels, pixels)
        v = v + pltpu.roll(left, LEFT, axis=2) + pltpu.roll(right, RIGHT, axis=2)
        sides[pl.ds(8 * t + 1, 8)] = v.astype(BF16)

    loop(rows // 8, eight)
    wait(fetched[:1])
    y = None
    for r in range(3):
        part = jnp.dot(flat(sides[r : r + rows]), first_mat[LANES * r : LANES * (r + 1)], preferred_element_type=F32)
        y = part if y is None else y + part
    raw[:, 0], raw[:, 1] = blocks_of(y, rows)
    mean, square = local_stats(raw, off, height, local_count)
    mask = jnp.zeros(sides.shape[1:], F32)
    for i in range(height):
        mask = mask + sides[off + 1 + i].astype(F32)
    lane = lane_of(mask.shape)
    count = jnp.sum(jnp.where((lane >= MASK) & (lane < MASK + 8), mask, 0.0))
    send(pay, mean, square)
    notes(vec, jnp.full((1, LANES), count, F32))
    wait(fetched[1:])


def first_kernel(place, got, raw, sides, table, taps, summed, pay, vec, fields, lows, hidden, xhat, sems, *, spots, local_count, pixel_count, height):
    mean, inverse = merge_stats(got[:, 0, :], got[:, 1, :], local_count, pixel_count)
    notes(vec, inverse)
    gain, bias = affine(table, 0)
    rows = raw.shape[0]

    def norm_rows(i):
        at = pl.ds(4 * i, 4)
        out = []
        for k in range(2):
            x = (raw[at, k] - mean) * inverse
            xhat[at, k] = x
            n = x * gain + bias
            out.append(n * sig_of(n))
        put_low(hidden, 4 * i, *out)

    blank(hidden)
    loop(rows // 4, norm_rows)
    stored = copies(sems, (xhat, spots(fields, "xhat_zero")), (hidden, spots(lows, "hidden_one")))

    @pl.when(place[0] >= 0)
    def _():
        y = conv(hidden, taps, 0, rows, flat(sides[1 : rows + 1]))
        summed[:, 0], summed[:, 1] = blocks_of(y, rows)

    send(pay, *local_stats(summed, place[0], height, local_count))
    wait(stored)


def pool_kernel(place, got, summed, count_in, table, weights, fields_in, lows_in, raw, pay, vec, merged, taps_next, fields, lows, xhat, shared, taps, sems, *, spots, local_count, pixel_count, height):
    fetched = copies(sems, (taps_at(weights, 1), taps), (taps_at(weights, 2), taps_next))
    mean, inverse = merge_stats(got[:, 0, :], got[:, 1, :], local_count, pixel_count)
    gain, bias = affine(table, 1)
    rows, segments = summed.shape[0], summed.shape[2]
    off = place[0]

    step = 4

    def some(i, carry):
        at = pl.ds(step * i, step)
        pairs = (step // 2, 2, segments, LANES)
        outs, sums = [], [jnp.zeros((step // 2 * segments, LANES), F32) for _ in range(3)]
        for k in range(2):
            x = (summed[at, k] - mean) * inverse
            n = x * gain + bias
            sig = sig_of(n)
            e = (n * sig).reshape(pairs)
            top = flat(jnp.maximum(e[:, 0], e[:, 1]))
            top = jnp.maximum(top, partner(top))
            wide_top = top.reshape(step // 2, 1, segments, LANES)
            exps = jnp.exp(e - wide_top)
            whole = flat(exps[:, 0] + exps[:, 1])
            whole = whole + partner(whole)
            pooled = top + jnp.log(whole)
            outs.append((e + pooled.reshape(wide_top.shape)).reshape(step, segments, LANES))
            share = exps * (1.0 / whole).reshape(wide_top.shape) * slope(n, sig).reshape(pairs)
            share_x = share * x.reshape(pairs)
            xhat[at, k] = x
            shared[at, k] = share.reshape(step, segments, LANES)
            sums[0] = sums[0] + pooled
            sums[1] = sums[1] + flat(share[:, 0] + share[:, 1])
            sums[2] = sums[2] + flat(share_x[:, 0] + share_x[:, 1])
        put_low(merged, step * i, *outs)
        mine = (step * i >= off) & (step * i < off + height)
        keep = jnp.where(mine, 1.0, 0.0)
        return tuple(a + keep * b for a, b in zip(carry, sums))

    blank(merged)
    zero = jnp.zeros((step // 2 * segments, LANES), F32)
    sums = lax.fori_loop(0, rows // step, some, (zero, zero, zero), unroll=min(rows // step, 5))
    pool_sum, share_sum, share_x = [fold(col_sum(v)) for v in sums]
    stored = copies(
        sems.at[2:],
        (xhat, spots(fields, "xhat_one")),
        (shared, spots(fields, "shared")),
        (merged, spots(lows, "merged")),
    )
    wait(fetched)
    raw[:, 0], raw[:, 1] = blocks_of(conv(merged, taps, 0, rows), rows)
    mean, square = local_stats(raw, place[0], height, local_count)
    send(pay, mean, square, groups(0.5 * pool_sum, share_sum, share_x, count_in[0:1]))
    notes(vec, inverse)
    wait(stored)


def by_image(v, parts):
    devices = v.shape[0]
    step = 1
    while step < parts:
        upper = (row_of(v.shape) // step) % 2 == 1
        v = v + jnp.where(upper, pltpu.roll(v, step, axis=0), pltpu.roll(v, devices - step, axis=0))
        step *= 2
    return v


def mine_of(v, me):
    return col_sum(jnp.where(row_of(v.shape) == me, v, 0.0))


def style_kernel(place, got, raw, merged, table, w_style, w_convs_in, taps, lows_in, resid, pay, vec, style_out, xhat, lows, hidden, slopes, w_conv, sems, *, spots, local_count, pixel_count, pool_cells, height, parts):
    fetched = copies(sems, (w_convs_in.at[2], w_conv))
    style = by_image(spread(got[:, 2, :], 0), parts) / pool_cells
    style_out[...] = style
    one, two = [
        jnp.dot(style, diagonal_blocks(w_style[i]), precision=highest, preferred_element_type=F32) for i in range(2)
    ]
    mean, inverse = merge_stats(got[:, 0, :] + one, got[:, 1, :], local_count, pixel_count)
    notes(vec, inverse)
    gain, bias = affine(table, 2)
    rows = raw.shape[0]
    me = place[2]
    shift = mine_of(one, me) - mean
    two = mine_of(two, me)

    def norm_rows(i):
        at = pl.ds(4 * i, 4)
        out = []
        for k in range(2):
            x = (raw[at, k] + shift) * inverse
            xhat[at, k] = x
            n = x * gain + bias
            sig = sig_of(n)
            slopes[at, k] = slope(n, sig)
            out.append(n * sig)
        put_low(hidden, 4 * i, *out)

    blank(hidden)
    loop(rows // 4, norm_rows)
    stored = copies(sems.at[1:], (hidden, spots(lows, "hidden_three")))

    @pl.when(place[0] >= 0)
    def _():
        for k, y in enumerate(blocks_of(conv(hidden, taps, 0, rows), rows)):
            resid[:, k] = y + two + merged[1 : rows + 1, k].astype(F32)

    wait(fetched + stored)
    off = place[0]
    means, squares = local_stats(resid, off, height, local_count)
    centre = fold(means) / GRP
    at = pl.ds(off, height)
    probe = [slopes[at, k] for k in range(2)]
    probe += [slopes[at, k] * xhat[at, k] for k in range(2)]
    probe = jnp.concatenate([flat(v).astype(BF16) for v in probe], axis=1)

    def centred(i):
        at = pl.ds(4 * i, 4)
        put_low(hidden, 4 * i, resid[at, 0] - centre, resid[at, 1] - centre, True)

    loop(rows // 4, centred)
    send(pay, means, squares)
    pay[0:CH, 2, :] = norm_links(hidden, probe, off, height, w_conv, centre)


def norm_links(field, probe, first, rows, taps, centre):
    wide = jnp.concatenate(views(field, first, rows), axis=1)
    found = lax.dot_general(probe, wide, (((0,), (0,)), ((), ())), preferred_element_type=F32)
    group = group_of((CH, LANES))
    out = []
    for half in range(2):

        def piece(y, chunk):
            at = 2 * LANES * half + CH * y
            return found[at : at + CH, chunk * LANES : (chunk + 1) * LANES]

        plain = jnp.zeros((CH, LANES), F32)
        moved = jnp.zeros((CH, LANES), F32)
        for r in range(3):
            first_edge, last_edge = piece(0, 3 * r), piece(SEG - 1, 3 * r)
            edge = first_edge + last_edge
            for y in range(1, SEG - 1):
                edge = edge + piece(y, 3 * r)
            inside = edge[:, ROW : ROW + 1]
            counts = (
                inside + (first_edge[:, BEFORE : BEFORE + 1] - first_edge[:, ROW : ROW + 1]),
                inside,
                inside + (last_edge[:, AFTER : AFTER + 1] - last_edge[:, ROW : ROW + 1]),
            )
            for c in range(3):
                tap = tile4(low(taps[3 * (2 - r) + 2 - c]))
                val = jnp.zeros((CH, LANES), F32)
                for y in range(SEG):
                    d, a = spot_of(y + c - 1)
                    val = val + jnp.where(group == a, piece(y, 3 * r + d), 0.0)
                plain = plain + tap * counts[c]
                moved = moved + tap * val
        out += [plain, fold(moved) + centre * plain]
    return groups(*out)


def spot_of(x):
    if x < 0:
        return 0, 3
    if x == SEG:
        return 0, 0
    return 1 + x // GRP, x % GRP


def head_kernel(place, got, got_style, resid, sides, head_mat, w_head, below_x, table, back, grad, xhat, pay, vec, decoded, slopes, grad_low, *, local_count, pixel_count, height):
    mean, inverse = merge_stats(got[:, 0, :], got[:, 1, :], local_count, pixel_count)
    notes(vec, inverse, mean)
    gain, bias = affine(table, 3)
    rows, segments = resid.shape[0], resid.shape[2]
    off = place[0]

    def norm_rows(i):
        at = pl.ds(4 * i, 4)
        for k in range(2):
            x = (resid[at, k] - mean) * inverse
            n = x * gain + bias
            s = sig_of(n)
            xhat[at, k] = x
            slopes[at, k] = slope(n, s)
            decoded[at, k] = (n * s).astype(BF16)

    loop(rows // 4, norm_rows)
    head = head_mat[...]
    wide = jnp.concatenate([flat(decoded[:, 0]), flat(decoded[:, 1])], axis=1)
    bias_row = zero_row()
    for k in range(3):
        mine = (lane_of((1, LANES)) >> 3) == FLOW // 8 + k
        bias_row = jnp.where(mine, low(w_head[k : k + 1, CH : CH + 1]), bias_row)
    out = jnp.dot(wide, head, preferred_element_type=F32) + bias_row
    given = flat(sides[1 : rows + 1]).astype(F32)
    lane = lane_of(given.shape)
    is_flow = lane < LABEL
    near = [pltpu.roll(given, LANES - MASK + first, axis=1) for first in (FLOW, FLOW + 8, LABEL)]
    mask = jnp.where(lane < FLOW + 8, near[0], jnp.where(is_flow, near[1], near[2]))
    mask = jnp.where((lane >= FLOW) & (lane < LABEL + 8), mask, 0.0)
    count = jnp.sum(got_style[:, 2, 3 * CH : 3 * CH + 1])
    diff = out - given / flow_scale
    hinge = jnp.maximum(out, 0.0) + jnp.log1p(jnp.exp(-jnp.abs(out)))
    loss = mask * jnp.where(is_flow, diff * diff, hinge - given * out)
    grad_out = (mask * jnp.where(is_flow, 2.0 * diff, sig_of(out) - given) / count).astype(BF16)
    at_row = lax.broadcasted_iota(jnp.int32, loss.shape, 0)
    inside = (at_row >= off * segments) & (at_row < (off + height) * segments)
    loss_sum = jnp.sum(jnp.where(inside, loss, 0.0))
    mine_out = jnp.where(inside, grad_out.astype(F32), 0.0).astype(BF16)
    outs = col_sum(mine_out.astype(F32))
    found = lax.dot_general(mine_out, wide, (((0,), (0,)), ((), ())), preferred_element_type=F32)
    shape = found.shape
    found = jnp.where((row_of(shape) & 7) == group_of(shape), found, 0.0)
    whole = [col_sum(found[FLOW + 8 * k : FLOW + 8 * k + 8]) for k in range(3)]
    whole = [fold(v[:, 0:LANES] + v[:, LANES:]) for v in whole]
    row = groups(*whole, zero_row())
    lane = lane_of((1, LANES))
    for k in range(3):
        row = jnp.where(lane == 3 * CH + k, jnp.sum(jnp.where((lane >> 3) == FLOW // 8 + k, outs, 0.0)), row)
    row = jnp.where(lane == 3 * CH + 3, loss_sum, row)
    y = lax.dot_general(grad_out, head, (((1,), (1,)), ((), ())), preferred_element_type=F32)
    for k, g in enumerate(blocks_of(y, rows)):
        grad[:, k] = g * slopes[:, k]
    factor = gain * inverse
    back_rows(grad_low, rows, lambda at, k: factor * grad[at, k])
    shift_sum, scale_sum = own_sums(grad, xhat, off, height)

    @pl.when(place[0] >= 0)
    def _():
        y = conv(grad_low, back, off, height)
        slopes[0:height, 0], slopes[0:height, 1] = blocks_of(y, height)

    gain, bias = affine(table, 2)

    def links(at, k):
        x = below_x[pl.ds(off + at.start, at.size), k]
        g = slopes[at, k] * slope_at(x, gain, bias)
        return g, g * x

    below = [fold(v) for v in row_sums(0, height, links)]
    send(pay, groups(shift_sum, scale_sum, *below), row, col_sum(got[:, 2, :]))


def own_sums(grad, xhat, first, rows):
    def both(at, k):
        g = grad[at, k]
        return g, g * xhat[at, k]

    return [fold(v) for v in row_sums(first, rows, both)]


def back_sums(got, pixel_count):
    whole = col_sum(got)
    return spread(whole, 0) / pixel_count, spread(whole, 1) / pixel_count


def low_sum(grad_low, first, rows):
    return fold(row_sums(first + 1, rows, lambda at, k: (grad_low[at, k].astype(F32),))[0])


def norm_back(grad, xhat, factor, shift, scale):
    return factor * (grad - (shift + xhat * scale))


def back_rows(grad_low, rows, value):
    def some(i):
        put_low(grad_low, 4 * i, *[value(pl.ds(4 * i, 4), k) for k in range(2)])

    blank(grad_low)
    loop(rows // 4, some)


def tap_sums(field, grad, first, rows, out):
    at = pl.ds(first + 1, rows)
    g = jnp.concatenate([flat(grad[at, 0]), flat(grad[at, 1])], axis=1)
    wide = jnp.concatenate(views(field, first, rows), axis=1)
    found = lax.dot_general(g, wide, (((0,), (0,)), ((), ())), preferred_element_type=F32)
    group = group_of((CH, LANES))
    taps = []
    for r in range(3):
        for s in range(3):
            val = jnp.zeros((CH, LANES), F32)
            for y in range(SEG):
                x = y + s - 1
                d, a = spot_of(x)
                spot = (3 * r + d) * LANES
                val = val + jnp.where(group == a, found[CH * y : CH * y + CH, spot : spot + LANES], 0.0)
            taps.append(fold(val))
    for q in range(3):
        val = taps[4 * q]
        for b in range(1, min(4, 9 - 4 * q)):
            val = jnp.where(group == b, taps[4 * q + b], val)
        out[:, q, :] = val


def decoder_back_kernel(place, got, grad, xhat, mid_x, vec, vec_two, table, back_two, back_one, fields, lows, below, below_x, shared, pay, more, kept_grad, mid, low_two, low_one, field_two, field_one, sems, *, spots, pixel_count, height):
    fetched = copies(
        sems,
        (spots(fields, "xhat_one"), below_x),
        (spots(fields, "shared"), shared),
        (spots(lows, "hidden_three"), field_two),
        (spots(lows, "merged"), field_one),
    )
    devices = got.shape[0]
    rows = grad.shape[0]
    off = place[0]
    total = col_sum(got[:, 0, :])
    shift, scale = spread(total, 0) / pixel_count, spread(total, 1) / pixel_count
    inverse, mean = vec[0:1], vec[1:2]
    factor = affine(table, 3)[0] * inverse
    slant = scale * inverse
    held, carried = factor * (shift - slant * mean), factor * slant
    links = got[0:CH, 2, :] * groups(held, carried, held, carried)
    group = group_of(links.shape)
    mine = (lane_of(links.shape) & 31) == row_of(links.shape)

    def across(pick):
        column = jnp.sum(jnp.where(pick, links, 0.0), axis=1, keepdims=True)
        return col_sum(jnp.where(mine, column, 0.0))

    shift_two = spread(total, 2) - across(group < 2)
    scale_two = spread(total, 3) - across(group >= 2)
    notes(more, scale_two, shift_two)

    def value(at, k):
        g = norm_back(grad[at, k], xhat[at, k], factor, shift, scale)
        kept_grad[at, k] = g
        return g

    back_rows(low_two, rows, value)

    @pl.when(place[0] >= 0)
    def _():
        mid[:, 0], mid[:, 1] = blocks_of(conv(low_two, back_two, 0, rows), rows)

    gain, bias = affine(table, 2)
    factor = gain * vec_two[0:1]
    shift, scale = shift_two / pixel_count, scale_two / pixel_count

    def value_two(at, k):
        x = mid_x[at, k]
        return norm_back(mid[at, k] * slope_at(x, gain, bias), x, factor, shift, scale)

    back_rows(low_one, rows, value_two)
    wait(fetched)
    sum_two = low_sum(low_two, off, height)
    sum_one = low_sum(low_one, off, height)
    y = conv(low_one, back_one, 0, rows)
    gain, bias = affine(table, 1)
    for k, y in enumerate(blocks_of(y, rows)):
        g = (y + kept_grad[:, k]).reshape(rows // 2, 2, -1, LANES)
        both = flat(g[:, 0] + g[:, 1])
        both = (both + partner(both)).reshape(rows // 2, 1, -1, LANES)
        g = g * slope_at(below_x[:, k], gain, bias).reshape(g.shape) + both * shared[:, k].reshape(g.shape)
        below[:, k] = g.reshape(rows, -1, LANES)
    row = groups(*own_sums(below, below_x, off, height), sum_one, sum_two)
    pay[:, 0] = jnp.broadcast_to(row[None], (devices, 4, LANES))
    if devices > CH:
        pay[CH:, 1] = jnp.zeros((devices - CH, 4, LANES), F32)
    tap_sums(field_two, low_two, off, height, pay.at[0:CH, 0, 1:4])
    tap_sums(field_one, low_one, off, height, pay.at[0:CH, 1])
    pay[0:CH, 1, 3, :] = jnp.zeros((CH, LANES), F32)


def summed_kernel(place, got, got_style, grad, xhat, shared, vec, table, w_style, sides, back, fields, lows, below, below_x, pay, more, field, grad_low, sems, *, spots, pixel_count, pool_cells, parts):
    off = place[0]
    height = below.shape[0]
    fetched = copies(
        sems,
        (spots(fields, "xhat_zero").at[pl.ds(off, height)], below_x),
        (spots(lows, "hidden_one"), field),
    )
    devices = got.shape[0]
    rows = grad.shape[0]
    dims = (((1,), (1,)), ((), ()))
    first = got[:, 0, 0, :]
    each = lax.dot_general(
        spread(first, 2), diagonal_blocks(w_style[0]), dims, precision=highest, preferred_element_type=F32
    ) + lax.dot_general(
        spread(first, 3), diagonal_blocks(w_style[1]), dims, precision=highest, preferred_element_type=F32
    )
    each = each / pool_cells
    total = col_sum(first)
    shift = spread(total, 0) + col_sum(each * by_image(spread(got_style[:, 2, :], 1), parts))
    scale = spread(total, 1) + col_sum(each * by_image(spread(got_style[:, 2, :], 2), parts))
    mine = col_sum(jnp.where(row_of(each.shape) // parts == place[2] // parts, each, 0.0))
    factor = affine(table, 1)[0] * vec[0:1]
    shift_mean, scale_mean = shift / pixel_count, scale / pixel_count
    def value(at, k):
        return norm_back(grad[at, k] + shared[at, k] * mine, xhat[at, k], factor, shift_mean, scale_mean)

    back_rows(grad_low, rows, value)
    gain, bias = affine(table, 0)
    wait(fetched)
    for k, y in enumerate(blocks_of(conv(grad_low, back, off, height), height)):
        below[:, k] = y * slope_at(below_x[:, k], gain, bias)
    two, one = jnp.sum(got[:, 0], axis=0), jnp.sum(got[:, 1], axis=0)
    row = groups(*own_sums(below, below_x, 0, height), two[3:4], one[2:3])
    chunk = jnp.concatenate([row, two[1:3], one[0:1]], axis=0)
    pay[:, 0] = jnp.broadcast_to(chunk[None], (devices, 4, LANES))
    pay[:, 1] = jnp.broadcast_to(one[1:2][None], (devices, 4, LANES))
    tap_sums(field, grad_low, off, height, pay.at[0:CH, 1, 1:4])
    at = pl.ds(off + 1, height)
    low_own = jnp.concatenate([flat(grad_low[at, 0]), flat(grad_low[at, 1])], axis=1)
    side = pixel_taps(sides, off + 1, height, low_own, (0,))[0]
    notes(more, scale, shift, *side)


def pixel_taps(sides, row, rows, grad, shift):
    x = flat(sides[pl.ds(row, rows)])
    found = lax.dot_general(x, grad, (((0,), (0,)), ((), ())), preferred_element_type=F32)
    inside, channel, here = image_lanes(found.shape)
    here = here - group_of(found.shape)
    out = []
    for s in shift:
        both = []
        for c in range(2):
            hit = inside & (channel == c) & (here == s)
            v = col_sum(jnp.where(hit, found, 0.0))
            both.append(fold(v[:, 0:LANES] + v[:, LANES:]))
        out.append(both)
    return out


def first_back_kernel(place, got, grad, xhat, vec, more, table, sides, pay, *, pixel_count, height):
    devices = got.shape[0]
    off = place[0]
    whole = col_sum(got[:, 0, 0, :])
    shift, scale = spread(whole, 0) / pixel_count, spread(whole, 1) / pixel_count
    factor = affine(table, 0)[0] * vec[0:1]
    low_grad = jnp.concatenate(
        [flat(norm_back(grad[:, k], xhat[:, k], factor, shift, scale).astype(BF16)) for k in range(2)], axis=1
    )
    entries = []
    for r in range(3):
        for tap in pixel_taps(sides, off + r, height, low_grad, (-1, 0, 1)):
            entries.extend(tap)
    entries.extend([more[2:3], more[3:4]])
    rows = [groups(*entries[4 * q : 4 * q + 4]) for q in range(5)]
    conv_zero = jnp.sum(got[:, 1], axis=0)
    chunk = [jnp.concatenate(rows[0:4], axis=0), jnp.concatenate([rows[4], conv_zero[1:4]], axis=0)]
    for k in range(2):
        pay[:, k] = jnp.broadcast_to(chunk[k][None], (devices, 4, LANES))


def adamw(master, moment, square, grad, rate):
    new_moment = beta_one * moment + (1.0 - beta_one) * grad
    new_square = beta_two * square + (1.0 - beta_two) * grad * grad
    moment_hat = new_moment / (1.0 - beta_one**STEP)
    square_hat = new_square / (1.0 - beta_two**STEP)
    new_master = master - rate * (moment_hat / (jnp.sqrt(square_hat) + adam_eps) + weight_decay * master)
    return new_master, new_moment, new_square


def put(at, refs, grad, rate, outs):
    found = adamw(*[ref[at] for ref in refs], grad, rate)
    for out, value in zip(outs, found + (found[0].astype(BF16),)):
        out[at] = value


def update_early(
    got_first, got_one_back, got_head, got_style, pay, more, more_two, style,
    w_style, w_head, table, m_style, m_head, m_norms, s_style, s_head, s_norms,
    loss_out, count_out,
    style_master, style_moment, style_square,
    head_master, head_moment, head_square, head_copy,
    norms_master, norms_moment, norms_square,
):
    count_out[0, 0] = jnp.sum(got_style[:, 2, 3 * CH : 3 * CH + 1])
    loss_out[0, 0] = jnp.sum(got_head[:, 1, 99:100])
    dims = (((0,), (0,)), ((), ()))
    for i in range(2):
        sums = spread(got_one_back[:, 0, 0, :], 2 + i)
        grad = lax.dot_general(style[...], sums, dims, precision=highest, preferred_element_type=F32)
        put(i, (w_style, m_style, s_style), grad[0:CH, 0:CH], rate_table[2], (style_master, style_moment, style_square))

    head = col_sum(got_head[:, 1, :])
    lane = lane_of((1, LANES))
    rows = []
    for k in range(3):
        last = jnp.sum(jnp.where(lane == 3 * CH + k, head, 0.0), axis=1, keepdims=True)
        rows.append(jnp.where(lane < CH, spread(head, k), last))
    grad = jnp.concatenate(rows, axis=0)[:, 0 : CH + 1]
    put(slice(None), (w_head, m_head, s_head), grad, rate_table[3], (head_master, head_moment, head_square, head_copy))

    three_sums = col_sum(got_head[:, 0, :])
    zero_sums = col_sum(got_first[:, 0, 0, :])
    scales = [spread(zero_sums, 1), more[0:1], more_two[0:1], spread(three_sums, 1)]
    shifts = [spread(zero_sums, 0), more[1:2], more_two[1:2], spread(three_sums, 0)]
    for i, rows in enumerate((scales, shifts)):
        grad = jnp.concatenate(rows, axis=0)[:, 0:CH]
        put(i, (table, m_norms, s_norms), grad, rate_table[4], (norms_master, norms_moment, norms_square))


def update_late(
    got, got_first, w_first, w_convs, m_first, m_convs, s_first, s_convs,
    first_master, first_moment, first_square, first_copy,
    convs_master, convs_moment, convs_square, convs_copy,
):
    refs = (w_convs, m_convs, s_convs)
    outs = (convs_master, convs_moment, convs_square, convs_copy)
    last = got_first[0:CH, 0, 0, :].T
    packs = (
        [got[0:CH, 1, q, :].T for q in (1, 2, 3)],
        [got_first[0:CH, 0, 3, :].T, got_first[0:CH, 1, 0, :].T, last[3 * CH :]],
        [got_first[0:CH, 0, 1, :].T, got_first[0:CH, 0, 2, :].T, last[2 * CH : 3 * CH]],
    )
    for i, pack in enumerate(packs):
        for t in range(9):
            b = t % 4
            put((i, t), refs, pack[t // 4][CH * b : CH * b + CH], rate_table[1], outs)

    first = jnp.concatenate([jnp.sum(got[:, 0], axis=0), jnp.sum(got[:, 1], axis=0)[0:1]], axis=0)
    refs = (w_first, m_first, s_first)
    outs = (first_master, first_moment, first_square, first_copy)
    for t in range(10):
        pair = [spread(first[e // 4 : e // 4 + 1], e % 4)[:, 0:CH] for e in (2 * t, 2 * t + 1)]
        put(t, refs, jnp.concatenate(pair, axis=0), rate_table[0], outs)


def far(x):
    return ("far", x)


def call(kernel, outs, *operands, scalars=0, scratch=(), sems=0, scalar_outs=(), aliases=None, limit=VMEM_LIMIT, name):
    smem = pl.BlockSpec(memory_space=pltpu.SMEM)
    vmem = pl.BlockSpec(memory_space=pltpu.VMEM)
    hbm = pl.BlockSpec(memory_space=pltpu.HBM)
    is_far = lambda x: isinstance(x, tuple) and x[0] == "far"
    in_specs = [smem if i < scalars else hbm if is_far(x) else vmem for i, x in enumerate(operands)]
    out_specs = [smem if i in scalar_outs else hbm if is_far(x) else vmem for i, x in enumerate(outs)]
    plain = lambda x: x[1] if is_far(x) else x
    shapes = [pltpu.VMEM(shape, dtype) for shape, dtype in scratch]
    if sems:
        shapes.append(pltpu.SemaphoreType.DMA((sems,)))
    return pl.pallas_call(
        kernel,
        out_shape=[jax.ShapeDtypeStruct(*plain(x)) for x in outs],
        in_specs=in_specs,
        out_specs=out_specs,
        scratch_shapes=shapes,
        input_output_aliases=aliases or {},
        compiler_params=pltpu.CompilerParams(vmem_limit_bytes=limit),
        name=name,
    )(*[plain(x) for x in operands])


def exchange(pay):
    return lax.all_to_all(pay, ("row", "col"), 0, 0)


def local(
    image_batch, valid_mask, flow_target, cell_labels,
    w_first, w_convs, w_style, w_head, batch_norm_table,
    mom_first, mom_convs, mom_style, mom_head, mom_norms,
    sqr_first, sqr_convs, sqr_style, sqr_head, sqr_norms,
):
    images, block_rows, block_cols, _ = image_batch.shape
    row_count, col_count = lax.axis_size("row"), lax.axis_size("col")
    devices = row_count * col_count
    parts = devices // images
    image_rows, image_cols = row_count * block_rows, col_count * block_cols
    assert devices == parts * images and block_rows == RIM and block_cols == 2 * block_rows * 2
    assert image_rows % (parts * RIM) == 0 and devices >= CH
    height = image_rows // parts
    rows = min(image_rows, height + RIM * min(2, parts - 1))
    segments = image_cols // SEG
    local_count = float(height * image_cols)
    pixel_count = local_count * devices
    pool_cells = float(image_rows * image_cols // 4)
    part = functools.partial
    counts = dict(local_count=local_count, pixel_count=pixel_count, height=height)
    backs = dict(pixel_count=pixel_count, height=height)
    styled = dict(pool_cells=pool_cells, parts=parts)

    me = lax.axis_index("row") * col_count + lax.axis_index("col")
    first_row = (me % parts) * height
    start = jnp.clip(first_row - RIM, 0, image_rows - rows)
    place = jnp.stack([first_row - start, start // block_rows, me]).astype(jnp.int32)

    field = ((rows, 2, segments, LANES), F32)
    own_field = ((height,) + field[0][1:], F32)
    low_field = ((rows + 2, 3, segments, LANES), BF16)
    vec = ((8, LANES), F32)
    two_rows = ((devices, 2, LANES), F32)
    four_rows = ((devices, 4, LANES), F32)
    two_chunks = ((devices, 2, 4, LANES), F32)
    nine = ((BACK, 2 * LANES), BF16)
    ten = ((FORWARD, 2 * LANES), BF16)

    places = {
        name: i * count
        for count, names in (
            (rows, ("xhat_zero", "xhat_one", "shared")),
            (rows + 2, ("hidden_one", "hidden_three", "merged")),
        )
        for i, name in enumerate(names)
    }

    def spots(store, name):
        count = rows if name[0] in "xs" else rows + 2
        return store.at[places[name] : places[name] + count]

    def store_of(like):
        shape, dtype = like
        row_bytes = shape[1] * segments * LANES * jnp.dtype(dtype).itemsize
        return far(((-(-STORE_BYTES // row_bytes),) + shape[1:], dtype))

    inputs = (
        jnp.transpose(image_batch, (0, 1, 3, 2)), jnp.transpose(flow_target, (0, 1, 3, 2)), cell_labels, valid_mask
    )
    (pay,) = call(
        pack_kernel,
        [((devices, 16, LANES), BF16)],
        *[far(v) for v in inputs],
        scratch=[(v.shape, v.dtype) for v in inputs], sems=4, limit=WHOLE_VMEM, name="pack",
    )
    got_inputs = exchange(pay)
    head_rows = w_head.T
    weights, *back, head_mat = call(
        prepare,
        [far(((STORE_BYTES // (4 * LANES), 2 * LANES), BF16)), nine, nine, nine, ((2 * LANES, LANES), BF16)],
        far(w_first), far(w_convs), far(head_rows),
        scratch=[(w_first.shape, F32), (w_convs.shape, F32), (head_rows.shape, F32), ((IMAGE_AT + 3 * LANES, 2 * LANES), BF16)],
        sems=4, limit=WHOLE_VMEM, name="prepare",
    )

    sides, raw, pay, count, taps = call(
        part(start_kernel, local_count=local_count, height=height, sources=col_count),
        [((rows + 2, segments, LANES), BF16), field, two_rows, vec, ten],
        place, got_inputs, far(weights),
        scalars=1, scratch=[((3 * LANES, 2 * LANES), BF16)], sems=2, name="image_conv",
    )
    got_zero = exchange(pay)
    summed, pay, inv_zero, fields, lows = call(
        part(first_kernel, spots=spots, **counts),
        [field, two_rows, vec, store_of(field), store_of(low_field)],
        place, got_zero, raw, sides, batch_norm_table, taps,
        scalars=1, scratch=[low_field, field], sems=2, name="first_block",
    )
    got_one = exchange(pay)

    raw, pay, inv_one, merged, taps, fields, lows = call(
        part(pool_kernel, spots=spots, **counts),
        [field, four_rows, vec, low_field, nine, store_of(field), store_of(low_field)],
        place, got_one, summed, count, batch_norm_table, far(weights), far(fields), far(lows),
        scalars=1, scratch=[field, field, nine], sems=5,
        aliases={6: 5, 7: 6}, name="pool_and_merge",
    )
    got_style = exchange(pay)

    resid, pay, inv_two, style, xhat_two, lows = call(
        part(style_kernel, spots=spots, **styled, **counts),
        [field, four_rows, vec, ((devices, LANES), F32), field, store_of(low_field)],
        place, got_style, raw, merged, batch_norm_table, w_style, far(w_convs), taps, far(lows),
        scalars=1, scratch=[low_field, field, (w_convs.shape[1:], F32)], sems=2,
        aliases={8: 5}, name="decoder",
    )
    got_three = exchange(pay)

    grad_three, xhat_three, pay, inv_three = call(
        part(head_kernel, **counts),
        [field, field, four_rows, vec],
        place, got_three, got_style, resid, sides, head_mat, head_rows, xhat_two, batch_norm_table, back[2],
        scalars=1, scratch=[((rows, 2, segments, LANES), BF16), field, low_field], name="head",
    )
    got_head = exchange(pay)

    grad_one, xhat_one, shared, pay, more_two = call(
        part(decoder_back_kernel, spots=spots, **backs),
        [field, field, field, two_chunks, vec],
        place, got_head, grad_three, xhat_three, xhat_two, inv_three, inv_two, batch_norm_table, back[2], back[1],
        far(fields), far(lows),
        scalars=1, scratch=[field, field, low_field, low_field, low_field, low_field], sems=4, name="decoder_back",
    )
    got_one_back = exchange(pay)

    grad_zero, xhat_zero, pay, more = call(
        part(summed_kernel, spots=spots, pixel_count=pixel_count, **styled),
        [own_field, own_field, two_chunks, vec],
        place, got_one_back, got_style, grad_one, xhat_one, shared, inv_one, batch_norm_table, w_style, sides,
        back[0], far(fields), far(lows),
        scalars=1, scratch=[low_field, low_field], sems=2, name="summed_back",
    )
    got_first = exchange(pay)

    (pay,) = call(
        part(first_back_kernel, **backs),
        [two_chunks],
        place, got_first, grad_zero, xhat_zero, inv_zero, more, batch_norm_table, sides,
        scalars=1, name="first_back",
    )
    got_last = exchange(pay)

    def results(param, copy):
        return [(param.shape, F32)] * 3 + [(param.shape, BF16)] * copy

    early = call(
        update_early,
        [((1, 1), F32), ((1, 1), F32)] + results(w_style, 0) + results(head_rows, 1) + results(batch_norm_table, 0),
        got_first, got_one_back, got_head, got_style, far(pay), more, more_two, style,
        w_style, head_rows, batch_norm_table, mom_style, mom_head.T, mom_norms, sqr_style, sqr_head.T, sqr_norms,
        scalar_outs=(0, 1), name="update_early",
    )
    late = call(
        update_late,
        results(w_first, 1) + results(w_convs, 1),
        got_last, got_first, w_first, w_convs, mom_first, mom_convs, sqr_first, sqr_convs,
        name="update_late",
    )
    loss, count = early[0].reshape(()), early[1].reshape(())
    head = tuple(value.T for value in early[5:9])
    return (loss, count, *late, *early[2:5], *head, *early[9:12])


def solution(mesh):
    field = P(None, "row", "col", None)
    plane = P(None, "row", "col")
    return jax.shard_map(
        local,
        mesh=mesh,
        in_specs=(field, plane, field, plane) + (P(),) * 15,
        out_specs=(P(),) * 20,
        check_vma=False,
    )
```

```python
import functools

import jax
import jax.numpy as jnp
from jax import lax
from jax.experimental import pallas as pl
from jax.experimental.pallas import tpu as pltpu
from jax.sharding import PartitionSpec as P

STEP = 5

highest = lax.Precision.HIGHEST
norm_eps = 1e-05
flow_scale = 32.0
adam_eps = 1e-08
weight_decay = 0.01
beta_one = 0.5
beta_two = 0.5
rate_table = (0.2, 0.05, 0.15, 0.15, 0.2)

CH = 32
GRP = 4
SEG = 8
LANES = 128
RIM = 8
FLOW, LABEL, MASK = 16, 32, 40
LEFT, RIGHT = 64, 96
AFTER, ROW, BEFORE = 32, 33, 64
F32 = jnp.float32
BF16 = jnp.bfloat16
VMEM_LIMIT = 36 * 1024 * 1024
WHOLE_VMEM = 56 * 1024 * 1024
STORE_BYTES = 32 * 1024 * 1024
FORWARD = 10 * LANES
BACK = 9 * LANES
IMAGE_AT = 3 * FORWARD
BACK_AT = IMAGE_AT + 3 * LANES


def lane_of(shape):
    return lax.broadcasted_iota(jnp.int32, shape, len(shape) - 1)


def row_of(shape):
    return lax.broadcasted_iota(jnp.int32, shape, 0)


def group_of(shape):
    return lane_of(shape) >> 5


def fold(v):
    return v + pltpu.roll(v, 32, axis=1) + (pltpu.roll(v, 64, axis=1) + pltpu.roll(v, 96, axis=1))


def spread(v, k):
    return fold(jnp.where(group_of(v.shape) == k, v, 0.0))


def partner(v):
    odd = (group_of(v.shape) & 1) == 1
    return jnp.where(odd, pltpu.roll(v, 32, axis=1), pltpu.roll(v, 96, axis=1))


def tile4(v):
    return jnp.concatenate([v, v, v, v], axis=1)


def col_sum(v):
    return jnp.sum(v, axis=0, keepdims=True)


def zero_row():
    return jnp.zeros((1, LANES), F32)


def groups(*values):
    group = group_of(values[0].shape)
    out = values[-1]
    for k in range(len(values) - 2, -1, -1):
        out = jnp.where(group == k, values[k], out)
    return out


def low(v):
    return v.astype(BF16).astype(F32)


def sig_of(v):
    return 0.5 + 0.5 * jnp.tanh(0.5 * v)


def slope(n, sig):
    return sig * (1.0 + n * (1.0 - sig))


def slope_at(x, gain, bias):
    n = x * gain + bias
    return slope(n, sig_of(n))


def flat(v):
    return v.reshape(-1, LANES)


def loop(count, body):
    def step(i, carry):
        body(i)
        return carry

    lax.fori_loop(0, count, step, 0, unroll=min(count, 5))


def copies(sems, *pairs):
    found = []
    for i, (source, target) in enumerate(pairs):
        found.append(pltpu.make_async_copy(source, target, sems.at[i]))
        found[-1].start()
    return found


def wait(started):
    for copy in started:
        copy.wait()


def shift_segments(v, way):
    half = v.shape[1]
    at = lax.broadcasted_iota(jnp.int32, v.shape, 1)
    if way == 1:
        return jnp.where(at == 0, 0.0, pltpu.roll(v, 1, axis=1))
    return jnp.where(at == half - 1, 0.0, pltpu.roll(v, half - 1, axis=1))


def beside(first, second):
    half = first.shape[1] // 2
    left = jnp.concatenate([shift_segments(second[:, half:], 1), second[:, :half]], axis=1)
    right = jnp.concatenate([first[:, half:], shift_segments(first[:, :half], -1)], axis=1)
    return left, right


def put_low(ref, row, first, second, marked=False):
    left, right = beside(first, second)
    lane = lane_of(left.shape)
    edge = jnp.where(lane < 64, right, left)
    if marked:
        at = lax.broadcasted_iota(jnp.int32, left.shape, 1)
        edge = jnp.where(lane == ROW, 1.0, edge)
        edge = jnp.where(lane == AFTER, jnp.where(at == left.shape[1] - 1, 0.0, 1.0), edge)
        edge = jnp.where(lane == BEFORE, jnp.where(at == 0, 0.0, 1.0), edge)
    at = pl.ds(row + 1, first.shape[0])
    for k, v in enumerate((first, second, edge)):
        ref[at, k] = v.astype(BF16)


def blank(ref):
    zero = jnp.zeros((1,) + ref.shape[1:], ref.dtype)
    ref[0:1] = zero
    ref[ref.shape[0] - 1 : ref.shape[0]] = zero


def views(src, row, rows):
    return [flat(src[pl.ds(row + r, rows), k]) for r in range(3) for k in (2, 0, 1)]


def conv(src, mat, row, rows, *more):
    wide = jnp.concatenate(views(src, row, rows) + list(more), axis=1)
    return jnp.dot(wide, mat[...], preferred_element_type=F32)


def blocks_of(y, rows):
    return [y[:, k * LANES : (k + 1) * LANES].reshape(rows, -1, LANES) for k in range(2)]


def narrow(v):
    while v.shape[0] > 1:
        half = v.shape[0] // 2
        v = v[:half] + v[half:]
    return v[0]


def row_sums(first, rows, values):
    step = 4

    def add(i, carry):
        found = [values(pl.ds(first + step * i, step), k) for k in range(2)]
        return tuple(c + a + b for c, a, b in zip(carry, *found))

    shapes = jax.eval_shape(lambda: values(pl.ds(0, step), 0))
    zeros = tuple(jnp.zeros(v.shape, F32) for v in shapes)
    found = lax.fori_loop(0, rows // step, add, zeros, unroll=min(rows // step, 8))
    return [col_sum(narrow(v)) for v in found]


def local_stats(v, first, rows, count):
    mean = row_sums(first, rows, lambda at, k: (v[at, k],))[0] * (GRP / count)

    def square(at, k):
        away = v[at, k] - mean
        return (away * away,)

    return mean, row_sums(first, rows, square)[0]


def merge_stats(means, squares, local_count, pixel_count):
    mean = fold(col_sum(means)) / (GRP * means.shape[0])
    away = means - mean
    total = fold(col_sum(squares + (local_count / GRP) * (away * away)))
    return mean, lax.rsqrt(total / pixel_count + norm_eps)


def row_of_each(got, r):
    return got[:, r, 0, :]


def total_of(got, r):
    return col_sum(row_of_each(got, r))


def send(pay, *rows):
    for r, row in enumerate(rows):
        pay[:, r, 0, :] = jnp.broadcast_to(row, (pay.shape[0], LANES))


def send_parts(pay, first, count):
    devices = pay.shape[0]
    if devices > CH:
        for r in range(first, first + count):
            pay[CH:, r, 0, :] = jnp.zeros((devices - CH, LANES), F32)
    return pay.at[0:CH, first : first + count, 0]


def affine(table, q):
    return tile4(table[0, q : q + 1, :]), tile4(table[1, q : q + 1, :])


def diagonal_blocks(mat):
    wide = tile4(mat)
    group = group_of(wide.shape)
    return jnp.concatenate([jnp.where(group == b, wide, 0.0) for b in range(GRP)], axis=0)


def notes(ref, *rows):
    for i, row in enumerate(rows):
        ref[i : i + 1, :] = row


def taps_at(store, i):
    return store.at[FORWARD * i : FORWARD * i + (BACK if i else FORWARD)]


def image_at(store):
    return store.at[IMAGE_AT : IMAGE_AT + 3 * LANES]


def back_at(store):
    return store.at[BACK_AT : BACK_AT + BACK]


def pack_kernel(image_in, flow_in, labels_in, valid_in, out, image, flow, labels, valid, sems):
    fetched = copies(sems, (image_in, image), (flow_in, flow), (labels_in, labels), (valid_in, valid))
    images, height, _, width = image.shape
    parts = out.shape[0] // images
    wait(fetched)
    fields = [image[:, :, c, :].astype(F32) for c in range(2)]
    fields += [flow[:, :, c, :].astype(F32) for c in range(2)]
    fields += [labels[...].astype(F32), valid[...].astype(F32)]
    halves = width // 16
    shape = (width, halves * LANES)
    lane = lane_of(shape)
    column = (lane >> 7) * 16 + ((lane >> 6) & 1) * 8 + (lane & 7)
    hit = row_of(shape) == column
    which = (lane >> 3) & 7
    total = jnp.zeros((images * height, halves * LANES), F32)
    for k, v in enumerate(fields):
        x = v.reshape(images * height, width).astype(BF16)
        mat = jnp.where(hit & (which == k), 1.0, 0.0).astype(BF16)
        total = total + jnp.dot(x, mat, preferred_element_type=F32)
    for b in range(images):
        rows = total[b * height : (b + 1) * height]
        slot = jnp.concatenate([rows[:, h * LANES : (h + 1) * LANES] for h in range(halves)], axis=0).astype(BF16)
        for p in range(parts):
            out[b * parts + p] = slot


COLUMNS = ((8, None, None, -1), (0, 1, 2, 3), (4, 5, 6, 7))


def conv_matrix(taps, mats, base, back):
    out_at = group_of((CH, 2 * LANES))
    for r in range(3):
        wide = []
        for s in range(3):
            if back:
                k = taps[3 * (2 - r) + s]
                k = jnp.concatenate([k, k, k, k], axis=0).T
            else:
                k = tile4(taps[3 * r + s])
            wide.append(jnp.concatenate([k, k], axis=1))
        for d in range(3):
            for a in range(GRP):
                val = jnp.zeros((CH, 2 * LANES), F32)
                column = COLUMNS[d][a]
                if column is not None:
                    for s in range(3):
                        val = jnp.where(out_at == (column + s - 1 if back else column + 1 - s), wide[s], val)
                mats[pl.ds(base + (3 * r + d) * LANES + CH * a, CH), :] = val.astype(BF16)


def image_lanes(shape):
    at = row_of(shape)
    kind = at >> 5
    column = (at & 7) + jnp.where(kind == LEFT // 32, -SEG, jnp.where(kind == RIGHT // 32, SEG, 0))
    return (kind != 1) & ((at & 31) < 16), (at >> 3) & 1, column


def first_taps(w_first, t):
    found = [tile4(low(w_first[t][c : c + 1])) for c in range(2)]
    return [jnp.concatenate([v, v], axis=1) for v in found]


def image_matrix(w_first, r):
    shape = (LANES, 2 * LANES)
    inside, channel, here = image_lanes(shape)
    val = jnp.zeros(shape, F32)
    for s in range(3):
        for c, tap in enumerate(first_taps(w_first, 3 * r + s)):
            val = jnp.where(inside & (channel == c) & (here == group_of(shape) + s - 1), tap, val)
    return val.astype(BF16)


def prepare(w_first_in, w_convs_in, w_head_in, store, back_zero, back_two, head_mat, w_first, w_convs, w_head, mats, sems):
    wait(copies(sems, (w_first_in, w_first), (w_convs_in, w_convs), (w_head_in, w_head)))
    shape = (LANES, 2 * LANES)
    inside, channel, here = image_lanes(shape)
    val = jnp.zeros(shape, F32)
    for c, tap in enumerate(first_taps(w_first, 9)):
        val = jnp.where((row_of(shape) < 16) & (channel == c) & (here == group_of(shape)), tap, val)
    mats[BACK:FORWARD, :] = val.astype(BF16)
    for r in range(3):
        mats[IMAGE_AT + LANES * r : IMAGE_AT + LANES * (r + 1), :] = image_matrix(w_first, r)
    stored = copies(sems, (image_at(mats), image_at(store)))
    for i in range(3):
        conv_matrix(w_convs.at[i], mats, FORWARD * i, False)
        stored += copies(sems.at[1 + i :], (taps_at(mats, i), taps_at(store, i)))
    conv_matrix(w_convs.at[1], mats, BACK_AT, True)
    stored += copies(sems.at[4:], (back_at(mats), back_at(store)))
    conv_matrix(w_convs.at[2], back_two, 0, True)
    conv_matrix(w_convs.at[0], back_zero, 0, True)
    lane = lane_of((CH, LANES))
    head = jnp.zeros((CH, LANES), F32)
    diagonal = row_of((CH, CH)) == lane_of((CH, CH))
    for k in range(3):
        column = jnp.sum(jnp.where(diagonal, low(w_head[k : k + 1, 0:CH]), 0.0), axis=1, keepdims=True)
        head = jnp.where((lane >> 3) == FLOW // 8 + k, column, head)
    for y in range(SEG):
        head_mat[CH * y : CH * (y + 1), :] = jnp.where((lane & 7) == y, head, 0.0).astype(BF16)
    wait(stored)


def start_kernel(place, got, weights, sides, raw, pay, vec, taps, first_mat, sems, *, local_count, height, sources):
    fetched = copies(sems, (image_at(weights), first_mat), (taps_at(weights, 0), taps))
    rows, segments = raw.shape[0], raw.shape[2]
    off, block = place[0], place[1]
    blank(sides)

    def eight(t):
        v = got[pl.ds((block + t) * sources, sources)].astype(F32)
        v = jnp.swapaxes(v.reshape(segments // 2, 8, LANES), 0, 1)
        near = lane_of(v.shape) < 64
        v = jnp.concatenate([jnp.where(near, v, 0.0), jnp.where(near, pltpu.roll(v, 64, axis=2), 0.0)], axis=1)
        pixels = jnp.where(lane_of(v.shape) < 16, v, 0.0)
        left, right = beside(pixels, pixels)
        v = v + pltpu.roll(left, LEFT, axis=2) + pltpu.roll(right, RIGHT, axis=2)
        sides[pl.ds(8 * t + 1, 8)] = v.astype(BF16)

    loop(rows // 8, eight)
    wait(fetched[:1])
    y = None
    for r in range(3):
        part = jnp.dot(flat(sides[r : r + rows]), first_mat[LANES * r : LANES * (r + 1)], preferred_element_type=F32)
        y = part if y is None else y + part
    raw[:, 0], raw[:, 1] = blocks_of(y, rows)
    mean, square = local_stats(raw, off, height, local_count)
    mask = jnp.zeros(sides.shape[1:], F32)
    for i in range(height):
        mask = mask + sides[off + 1 + i].astype(F32)
    lane = lane_of(mask.shape)
    count = jnp.sum(jnp.where((lane >= MASK) & (lane < MASK + 8), mask, 0.0))
    send(pay, mean, square)
    notes(vec, jnp.full((1, LANES), count, F32))
    wait(fetched[1:])


def first_kernel(place, got, raw, sides, table, taps, summed, pay, vec, fields, lows, hidden, xhat, sems, *, spots, local_count, pixel_count, height):
    mean, inverse = merge_stats(row_of_each(got, 0), row_of_each(got, 1), local_count, pixel_count)
    notes(vec, inverse)
    gain, bias = affine(table, 0)
    rows = raw.shape[0]

    def norm_rows(i):
        at = pl.ds(4 * i, 4)
        out = []
        for k in range(2):
            x = (raw[at, k] - mean) * inverse
            xhat[at, k] = x
            n = x * gain + bias
            out.append(n * sig_of(n))
        put_low(hidden, 4 * i, *out)

    blank(hidden)
    loop(rows // 4, norm_rows)
    stored = copies(sems, (xhat, spots(fields, "xhat_zero")), (hidden, spots(lows, "hidden_one")))

    @pl.when(place[0] >= 0)
    def _():
        y = conv(hidden, taps, 0, rows, flat(sides[1 : rows + 1]))
        summed[:, 0], summed[:, 1] = blocks_of(y, rows)

    send(pay, *local_stats(summed, place[0], height, local_count))
    wait(stored)


def pool_kernel(place, got, summed, count_in, table, weights, fields_in, lows_in, raw, pay, vec, merged, taps_next, fields, lows, xhat, shared, taps, sems, *, spots, local_count, pixel_count, height):
    fetched = copies(sems, (taps_at(weights, 1), taps), (taps_at(weights, 2), taps_next))
    mean, inverse = merge_stats(row_of_each(got, 0), row_of_each(got, 1), local_count, pixel_count)
    gain, bias = affine(table, 1)
    rows, segments = summed.shape[0], summed.shape[2]
    off = place[0]

    step = 4

    def some(i, carry):
        at = pl.ds(step * i, step)
        pairs = (step // 2, 2, segments, LANES)
        outs, sums = [], [jnp.zeros((step // 2 * segments, LANES), F32) for _ in range(3)]
        for k in range(2):
            x = (summed[at, k] - mean) * inverse
            n = x * gain + bias
            sig = sig_of(n)
            e = (n * sig).reshape(pairs)
            top = flat(jnp.maximum(e[:, 0], e[:, 1]))
            top = jnp.maximum(top, partner(top))
            wide_top = top.reshape(step // 2, 1, segments, LANES)
            exps = jnp.exp(e - wide_top)
            whole = flat(exps[:, 0] + exps[:, 1])
            whole = whole + partner(whole)
            pooled = top + jnp.log(whole)
            outs.append((e + pooled.reshape(wide_top.shape)).reshape(step, segments, LANES))
            share = exps * (1.0 / whole).reshape(wide_top.shape) * slope(n, sig).reshape(pairs)
            share_x = share * x.reshape(pairs)
            xhat[at, k] = x
            shared[at, k] = share.reshape(step, segments, LANES)
            sums[0] = sums[0] + pooled
            sums[1] = sums[1] + flat(share[:, 0] + share[:, 1])
            sums[2] = sums[2] + flat(share_x[:, 0] + share_x[:, 1])
        put_low(merged, step * i, *outs)
        mine = (step * i >= off) & (step * i < off + height)
        keep = jnp.where(mine, 1.0, 0.0)
        return tuple(a + keep * b for a, b in zip(carry, sums))

    blank(merged)
    zero = jnp.zeros((step // 2 * segments, LANES), F32)
    sums = lax.fori_loop(0, rows // step, some, (zero, zero, zero), unroll=min(rows // step, 5))
    pool_sum, share_sum, share_x = [fold(col_sum(v)) for v in sums]
    stored = copies(
        sems.at[2:],
        (xhat, spots(fields, "xhat_one")),
        (shared, spots(fields, "shared")),
        (merged, spots(lows, "merged")),
    )
    wait(fetched)
    raw[:, 0], raw[:, 1] = blocks_of(conv(merged, taps, 0, rows), rows)
    mean, square = local_stats(raw, place[0], height, local_count)
    send(pay, mean, square, groups(0.5 * pool_sum, share_sum, share_x, count_in[0:1]))
    notes(vec, inverse)
    wait(stored)


def by_image(v, parts):
    devices = v.shape[0]
    step = 1
    while step < parts:
        upper = (row_of(v.shape) // step) % 2 == 1
        v = v + jnp.where(upper, pltpu.roll(v, step, axis=0), pltpu.roll(v, devices - step, axis=0))
        step *= 2
    return v


def mine_of(v, me):
    return col_sum(jnp.where(row_of(v.shape) == me, v, 0.0))


def style_kernel(place, got, raw, merged, table, w_style, w_convs_in, taps, lows_in, resid, pay, vec, style_out, xhat, lows, hidden, slopes, w_conv, sems, *, spots, local_count, pixel_count, pool_cells, height, parts):
    fetched = copies(sems, (w_convs_in.at[2], w_conv))
    style = by_image(spread(row_of_each(got, 2), 0), parts) / pool_cells
    style_out[...] = style
    one, two = [
        jnp.dot(style, diagonal_blocks(w_style[i]), precision=highest, preferred_element_type=F32) for i in range(2)
    ]
    mean, inverse = merge_stats(row_of_each(got, 0) + one, row_of_each(got, 1), local_count, pixel_count)
    notes(vec, inverse)
    gain, bias = affine(table, 2)
    rows = raw.shape[0]
    me = place[2]
    shift = mine_of(one, me) - mean
    two = mine_of(two, me)

    def norm_rows(i):
        at = pl.ds(4 * i, 4)
        out = []
        for k in range(2):
            x = (raw[at, k] + shift) * inverse
            xhat[at, k] = x
            n = x * gain + bias
            sig = sig_of(n)
            slopes[at, k] = slope(n, sig)
            out.append(n * sig)
        put_low(hidden, 4 * i, *out)

    blank(hidden)
    loop(rows // 4, norm_rows)
    stored = copies(sems.at[1:], (hidden, spots(lows, "hidden_three")))

    @pl.when(place[0] >= 0)
    def _():
        for k, y in enumerate(blocks_of(conv(hidden, taps, 0, rows), rows)):
            resid[:, k] = y + two + merged[1 : rows + 1, k].astype(F32)

    wait(fetched + stored)
    off = place[0]
    means, squares = local_stats(resid, off, height, local_count)
    centre = fold(means) / GRP
    at = pl.ds(off, height)
    probe = [slopes[at, k] for k in range(2)]
    probe += [slopes[at, k] * xhat[at, k] for k in range(2)]
    probe = jnp.concatenate([flat(v).astype(BF16) for v in probe], axis=1)

    def centred(i):
        at = pl.ds(4 * i, 4)
        put_low(hidden, 4 * i, resid[at, 0] - centre, resid[at, 1] - centre, True)

    loop(rows // 4, centred)
    send(pay, means, squares)
    links = norm_links(hidden, probe, off, height, w_conv, centre)
    send_parts(pay, 2, 1)[:, 0, :] = links


def norm_links(field, probe, first, rows, taps, centre):
    wide = jnp.concatenate(views(field, first, rows), axis=1)
    found = lax.dot_general(probe, wide, (((0,), (0,)), ((), ())), preferred_element_type=F32)
    group = group_of((CH, LANES))
    out = []
    for half in range(2):

        def piece(y, chunk):
            at = 2 * LANES * half + CH * y
            return found[at : at + CH, chunk * LANES : (chunk + 1) * LANES]

        plain = jnp.zeros((CH, LANES), F32)
        moved = jnp.zeros((CH, LANES), F32)
        for r in range(3):
            first_edge, last_edge = piece(0, 3 * r), piece(SEG - 1, 3 * r)
            edge = first_edge + last_edge
            for y in range(1, SEG - 1):
                edge = edge + piece(y, 3 * r)
            inside = edge[:, ROW : ROW + 1]
            counts = (
                inside + (first_edge[:, BEFORE : BEFORE + 1] - first_edge[:, ROW : ROW + 1]),
                inside,
                inside + (last_edge[:, AFTER : AFTER + 1] - last_edge[:, ROW : ROW + 1]),
            )
            for c in range(3):
                tap = tile4(low(taps[3 * (2 - r) + 2 - c]))
                val = jnp.zeros((CH, LANES), F32)
                for y in range(SEG):
                    d, a = spot_of(y + c - 1)
                    val = val + jnp.where(group == a, piece(y, 3 * r + d), 0.0)
                plain = plain + tap * counts[c]
                moved = moved + tap * val
        out += [plain, fold(moved) + centre * plain]
    return groups(*out)


def spot_of(x):
    if x < 0:
        return 0, 3
    if x == SEG:
        return 0, 0
    return 1 + x // GRP, x % GRP


def ahead_kernel(place, pay, sides, fields, lows, out, sums, below_x, xhat, shared, field, sems, *, spots, local_count):
    off = place[0]
    height = xhat.shape[0]
    own = pl.ds(off, height)
    fetched = copies(
        sems,
        (spots(fields, "xhat_one").at[own], xhat),
        (spots(fields, "shared").at[own], shared),
        (spots(fields, "xhat_zero").at[own], below_x),
        (spots(lows, "hidden_one"), field),
    )
    wait(fetched)
    at = pl.ds(0, height)
    centres = [fold(v) / local_count for v in row_sums(0, height, lambda at, k: (xhat[at, k], shared[at, k]))]
    probe = [flat(v[at, k] - c).astype(BF16) for v, c in zip((xhat, shared), centres) for k in range(2)]
    wide = jnp.concatenate(views(field, off, height), axis=1)
    found = lax.dot_general(
        jnp.concatenate(probe, axis=1), wide, (((0,), (0,)), ((), ())), preferred_element_type=F32
    )
    ones = jnp.ones((8, wide.shape[0]), BF16)
    plain = jnp.dot(ones, wide, preferred_element_type=F32)[0:1]
    group = group_of((1, LANES))
    hidden = []
    for r in range(3):
        for s in range(3):
            val = zero_row()
            for y in range(SEG):
                d, a = spot_of(y + s - 1)
                spot = (3 * r + d) * LANES
                val = val + jnp.where(group == a, plain[:, spot : spot + LANES], 0.0)
            hidden.append(fold(val))
    packed = [groups(*hidden[0:4]), groups(*hidden[4:8]), hidden[8]]
    notes(sums, *packed)
    packed = jnp.concatenate(packed, axis=0)
    for k in range(2):
        put_taps(found[2 * LANES * k : 2 * LANES * (k + 1)], out.at[:, 3 * k + 1 : 3 * k + 4, 0], (centres[k], packed))
    low_x = jnp.concatenate([own_lanes(below_x, at), jnp.ones((wide.shape[0], LANES), BF16)], axis=1)
    entries = []
    for r in range(3):
        for tap, alone in pixel_taps(sides, off + r, height, low_x, (-1, 0, 1), True):
            entries.extend(zip(tap, alone))
    rows = [groups(*entry, hidden[e] if e < 9 else zero_row(), zero_row()) for e, entry in enumerate(entries)]
    out[:, 0, 0, :] = jnp.concatenate(rows + [jnp.zeros((CH - len(rows), LANES), F32)], axis=0)


def head_kernel(place, got, got_style, resid, sides, head_mat, w_head, below_x, ahead, table, back, grad, xhat, pay, vec, decoded, slopes, grad_low, *, local_count, pixel_count, height):
    mean, inverse = merge_stats(row_of_each(got, 0), row_of_each(got, 1), local_count, pixel_count)
    notes(vec, inverse, mean)
    gain, bias = affine(table, 3)
    rows, segments = resid.shape[0], resid.shape[2]
    off = place[0]

    def norm_rows(i):
        at = pl.ds(4 * i, 4)
        for k in range(2):
            x = (resid[at, k] - mean) * inverse
            n = x * gain + bias
            s = sig_of(n)
            xhat[at, k] = x
            slopes[at, k] = slope(n, s)
            decoded[at, k] = (n * s).astype(BF16)

    loop(rows // 4, norm_rows)
    head = head_mat[...]
    wide = jnp.concatenate([flat(decoded[:, 0]), flat(decoded[:, 1])], axis=1)
    bias_row = zero_row()
    for k in range(3):
        mine = (lane_of((1, LANES)) >> 3) == FLOW // 8 + k
        bias_row = jnp.where(mine, low(w_head[k : k + 1, CH : CH + 1]), bias_row)
    out = jnp.dot(wide, head, preferred_element_type=F32) + bias_row
    given = flat(sides[1 : rows + 1]).astype(F32)
    lane = lane_of(given.shape)
    is_flow = lane < LABEL
    near = [pltpu.roll(given, LANES - MASK + first, axis=1) for first in (FLOW, FLOW + 8, LABEL)]
    mask = jnp.where(lane < FLOW + 8, near[0], jnp.where(is_flow, near[1], near[2]))
    mask = jnp.where((lane >= FLOW) & (lane < LABEL + 8), mask, 0.0)
    count = jnp.sum(got_style[:, 2, 0, 3 * CH : 3 * CH + 1])
    diff = out - given / flow_scale
    hinge = jnp.maximum(out, 0.0) + jnp.log1p(jnp.exp(-jnp.abs(out)))
    loss = mask * jnp.where(is_flow, diff * diff, hinge - given * out)
    grad_out = (mask * jnp.where(is_flow, 2.0 * diff, sig_of(out) - given) / count).astype(BF16)
    at_row = lax.broadcasted_iota(jnp.int32, loss.shape, 0)
    inside = (at_row >= off * segments) & (at_row < (off + height) * segments)
    loss_sum = jnp.sum(jnp.where(inside, loss, 0.0))
    mine_out = jnp.where(inside, grad_out.astype(F32), 0.0).astype(BF16)
    outs = col_sum(mine_out.astype(F32))
    found = lax.dot_general(mine_out, wide, (((0,), (0,)), ((), ())), preferred_element_type=F32)
    shape = found.shape
    found = jnp.where((row_of(shape) & 7) == group_of(shape), found, 0.0)
    whole = [col_sum(found[FLOW + 8 * k : FLOW + 8 * k + 8]) for k in range(3)]
    whole = [fold(v[:, 0:LANES] + v[:, LANES:]) for v in whole]
    row = groups(*whole, zero_row())
    lane = lane_of((1, LANES))
    for k in range(3):
        row = jnp.where(lane == 3 * CH + k, jnp.sum(jnp.where((lane >> 3) == FLOW // 8 + k, outs, 0.0)), row)
    row = jnp.where(lane == 3 * CH + 3, loss_sum, row)
    y = lax.dot_general(grad_out, head, (((1,), (1,)), ((), ())), preferred_element_type=F32)
    for k, g in enumerate(blocks_of(y, rows)):
        grad[:, k] = g * slopes[:, k]
    factor = gain * inverse
    back_rows(grad_low, rows, lambda at, k: factor * grad[at, k])
    shift_sum, scale_sum = own_sums(grad, xhat, off, height)

    @pl.when(place[0] >= 0)
    def _():
        y = conv(grad_low, back, off, height)
        slopes[0:height, 0], slopes[0:height, 1] = blocks_of(y, height)

    gain, bias = affine(table, 2)

    def links(at, k):
        x = below_x[pl.ds(off + at.start, at.size), k]
        g = slopes[at, k] * slope_at(x, gain, bias)
        return g, g * x

    below = [fold(v) for v in row_sums(0, height, links)]
    send(pay, groups(shift_sum, scale_sum, *below), row, total_of(got, 2))
    send_parts(pay, 3, 7)
    pay[0:CH, 3:10] = ahead[...]


def own_sums(grad, xhat, first, rows):
    def both(at, k):
        g = grad[at, k]
        return g, g * xhat[at, k]

    return [fold(v) for v in row_sums(first, rows, both)]


def back_sums(got, pixel_count):
    whole = col_sum(got)
    return spread(whole, 0) / pixel_count, spread(whole, 1) / pixel_count


def low_sum(grad_low, first, rows):
    return fold(row_sums(first + 1, rows, lambda at, k: (grad_low[at, k].astype(F32),))[0])


def norm_back(grad, xhat, factor, shift, scale):
    return factor * (grad - (shift + xhat * scale))


def back_rows(grad_low, rows, value):
    def some(i):
        put_low(grad_low, 4 * i, *[value(pl.ds(4 * i, 4), k) for k in range(2)])

    blank(grad_low)
    loop(rows // 4, some)


def own_lanes(grad, at):
    return jnp.concatenate([flat(grad[at, k]).astype(BF16) for k in range(2)], axis=1)


def tap_sums(field, grad, first, rows, out, more=None):
    wide = jnp.concatenate(views(field, first, rows), axis=1)
    found = lax.dot_general(grad, wide, (((0,), (0,)), ((), ())), preferred_element_type=F32)
    put_taps(found, out, more)


def put_taps(found, out, more=None):
    group = group_of((CH, LANES))
    taps = []
    for r in range(3):
        for s in range(3):
            val = jnp.zeros((CH, LANES), F32)
            for y in range(SEG):
                d, a = spot_of(y + s - 1)
                spot = (3 * r + d) * LANES
                val = val + jnp.where(group == a, found[CH * y : CH * y + CH, spot : spot + LANES], 0.0)
            taps.append(fold(val))
    for q in range(3):
        val = taps[4 * q]
        for b in range(1, min(4, 9 - 4 * q)):
            val = jnp.where(group == b, taps[4 * q + b], val)
        if more is not None:
            centre, sums = more
            val = val + column_of(centre) * sums[q : q + 1]
        out[:, q, :] = val


def column_of(v):
    shape = (CH, LANES)
    return jnp.sum(jnp.where(row_of(shape) == lane_of(shape), v, 0.0), axis=1, keepdims=True)


def at_lane(v, k):
    return jnp.sum(jnp.where(lane_of(v.shape) == k, v, 0.0), axis=1, keepdims=True)


def decoder_back_kernel(place, got, grad, xhat, mid_x, vec, vec_two, sums, table, back_two, weights, fields, lows, below, below_x, shared, pay, more, kept_grad, mid, low_two, low_one, field_two, field_one, field_zero, back_one, sems, *, spots, local_count, pixel_count, height):
    fetched = copies(
        sems,
        (back_at(weights), back_one),
        (spots(fields, "xhat_one"), below_x),
        (spots(fields, "shared"), shared),
        (spots(lows, "hidden_three"), field_two),
        (spots(lows, "merged"), field_one),
        (spots(lows, "hidden_one"), field_zero),
    )
    devices = got.shape[0]
    rows = grad.shape[0]
    off = place[0]
    total = total_of(got, 0)
    shift, scale = spread(total, 0) / pixel_count, spread(total, 1) / pixel_count
    inverse, mean = vec[0:1], vec[1:2]
    factor = affine(table, 3)[0] * inverse
    slant = scale * inverse
    held, carried = factor * (shift - slant * mean), factor * slant
    links = got[0:CH, 2, 0, :] * groups(held, carried, held, carried)
    group = group_of(links.shape)
    mine = (lane_of(links.shape) & 31) == row_of(links.shape)

    def across(pick):
        column = jnp.sum(jnp.where(pick, links, 0.0), axis=1, keepdims=True)
        return col_sum(jnp.where(mine, column, 0.0))

    shift_two = spread(total, 2) - across(group < 2)
    scale_two = spread(total, 3) - across(group >= 2)
    notes(more, scale_two, shift_two, *[total_of(got, r) for r in (4, 5, 6)])

    def value(at, k):
        g = norm_back(grad[at, k], xhat[at, k], factor, shift, scale)
        kept_grad[at, k] = g
        return g

    back_rows(low_two, rows, value)

    @pl.when(place[0] >= 0)
    def _():
        mid[:, 0], mid[:, 1] = blocks_of(conv(low_two, back_two, 0, rows), rows)

    gain, bias = affine(table, 2)
    factor = gain * vec_two[0:1]
    shift, scale = shift_two / pixel_count, scale_two / pixel_count

    def value_two(at, k):
        x = mid_x[at, k]
        return norm_back(mid[at, k] * slope_at(x, gain, bias), x, factor, shift, scale)

    back_rows(low_one, rows, value_two)
    wait(fetched)
    sum_two = low_sum(low_two, off, height)
    sum_one = low_sum(low_one, off, height)
    y = conv(low_one, back_one, 0, rows)
    gain, bias = affine(table, 1)
    for k, y in enumerate(blocks_of(y, rows)):
        g = (y + kept_grad[:, k]).reshape(rows // 2, 2, -1, LANES)
        both = flat(g[:, 0] + g[:, 1])
        both = (both + partner(both)).reshape(rows // 2, 1, -1, LANES)
        g = g * slope_at(below_x[:, k], gain, bias).reshape(g.shape) + both * shared[:, k].reshape(g.shape)
        below[:, k] = g.reshape(rows, -1, LANES)
    shift_sum, scale_sum = own_sums(below, below_x, off, height)
    send(pay, groups(shift_sum, scale_sum, sum_one, sum_two))
    pay[:, 7, 0, :] = jnp.broadcast_to(total_of(got, 3), (devices, LANES))
    at = pl.ds(off + 1, height)
    tap_sums(field_two, own_lanes(low_two, at), off, height, send_parts(pay, 1, 3))
    tap_sums(field_one, own_lanes(low_one, at), off, height, send_parts(pay, 4, 3))
    centre = shift_sum / local_count
    at = pl.ds(off, height)
    grad = jnp.concatenate([flat(below[at, k] - centre).astype(BF16) for k in range(2)], axis=1)
    tap_sums(field_zero, grad, off, height, send_parts(pay, 8, 3), (centre, sums))


def summed_kernel(place, got, got_style, got_head, grad, xhat, shared, vec, more_two, table, w_style, sides, back, fields, pay, more, below, below_x, grad_low, sems, *, spots, pixel_count, pool_cells, parts):
    off = place[0]
    height = below.shape[0]
    fetched = copies(sems, (spots(fields, "xhat_zero").at[pl.ds(off, height)], below_x))
    devices = got.shape[0]
    rows = grad.shape[0]
    dims = (((1,), (1,)), ((), ()))
    first = row_of_each(got, 0)
    each = lax.dot_general(
        spread(first, 2), diagonal_blocks(w_style[0]), dims, precision=highest, preferred_element_type=F32
    ) + lax.dot_general(
        spread(first, 3), diagonal_blocks(w_style[1]), dims, precision=highest, preferred_element_type=F32
    )
    each = each / pool_cells
    total = col_sum(first)
    shift = spread(total, 0) + col_sum(each * by_image(spread(row_of_each(got_style, 2), 1), parts))
    scale = spread(total, 1) + col_sum(each * by_image(spread(row_of_each(got_style, 2), 2), parts))
    mine = col_sum(jnp.where(row_of(each.shape) // parts == place[2] // parts, each, 0.0))
    factor = affine(table, 1)[0] * vec[0:1]
    shift_mean, scale_mean = shift / pixel_count, scale / pixel_count
    def value(at, k):
        return norm_back(grad[at, k] + shared[at, k] * mine, xhat[at, k], factor, shift_mean, scale_mean)

    back_rows(grad_low, rows, value)
    gain, bias = affine(table, 0)
    wait(fetched)
    for k, y in enumerate(blocks_of(conv(grad_low, back, off, height), height)):
        below[:, k] = y * slope_at(below_x[:, k], gain, bias)
    me = place[2]
    weights = at_lane(by_image(each, parts), me)
    entries = got[0:CH, 7, 0, :]
    hidden = spread(entries, 2)
    hidden = [groups(*[hidden[t : t + 1] for t in range(4 * q, min(4 * q + 4, 9))]) for q in range(3)]
    shard = []
    for q in range(3):
        val = total_of(got, 8 + q) + col_sum(weights * row_of_each(got_head, 7 + q))
        val = val - at_lane(shift_mean, me) * hidden[q] - at_lane(scale_mean, me) * more_two[2 + q : 3 + q]
        shard.append(at_lane(factor, me) * val)
    at = pl.ds(off + 1, height)
    side = pixel_taps(sides, off + 1, height, own_lanes(grad_low, at), (0,))[0]
    low_below = own_lanes(below, pl.ds(0, height))
    taps = []
    for r in range(3):
        for tap in pixel_taps(sides, off + r, height, low_below, (-1, 0, 1)):
            taps.extend(tap)
    two, one = [total_of(got, r) for r in (1, 2, 3)], [total_of(got, r) for r in (4, 5, 6)]
    taps = [shard[2]] + taps + side
    send(
        pay,
        groups(*own_sums(below, below_x, 0, height), two[2], one[2]),
        *two[0:2],
        *one[0:2],
        *shard[0:2],
        *[groups(*(taps[4 * q : 4 * q + 4] + [zero_row()])[0:4]) for q in range(6)],
    )
    notes(more, scale, shift)


def pixel_taps(sides, row, rows, grad, shift, alone=False):
    x = flat(sides[pl.ds(row, rows)])
    found = lax.dot_general(x, grad, (((0,), (0,)), ((), ())), preferred_element_type=F32)
    inside, channel, column = image_lanes((LANES, 2 * LANES))
    here = column - group_of((LANES, 2 * LANES))
    out = []
    for s in shift:
        both, bare = [], []
        for c in range(2):
            v = col_sum(jnp.where(inside & (channel == c) & (here == s), found[:, 0 : 2 * LANES], 0.0))
            both.append(fold(v[:, 0:LANES] + v[:, LANES:]))
            if alone:
                cut = slice(0, LANES)
                hit = (inside & (channel == c) & (column >= s) & (column < s + SEG))[:, cut]
                bare.append(col_sum(jnp.where(hit, found[:, 2 * LANES :], 0.0)))
        out.append((both, bare) if alone else both)
    return out


def adamw(master, moment, square, grad, rate):
    new_moment = beta_one * moment + (1.0 - beta_one) * grad
    new_square = beta_two * square + (1.0 - beta_two) * grad * grad
    moment_hat = new_moment / (1.0 - beta_one**STEP)
    square_hat = new_square / (1.0 - beta_two**STEP)
    new_master = master - rate * (moment_hat / (jnp.sqrt(square_hat) + adam_eps) + weight_decay * master)
    return new_master, new_moment, new_square


def put(at, refs, grad, rate, outs):
    found = adamw(*[ref[at] for ref in refs], grad, rate)
    for out, value in zip(outs, found + (found[0].astype(BF16),)):
        out[at] = value


def update_early(
    got_one_back, got_head, got_style, pay, style, w_style, w_head, m_style, m_head, s_style, s_head,
    loss_out, count_out, style_master, style_moment, style_square, head_master, head_moment, head_square, head_copy,
):
    count_out[0, 0] = jnp.sum(got_style[:, 2, 0, 3 * CH : 3 * CH + 1])
    loss_out[0, 0] = jnp.sum(got_head[:, 1, 0, 99:100])
    dims = (((0,), (0,)), ((), ()))
    for i in range(2):
        sums = spread(row_of_each(got_one_back, 0), 2 + i)
        grad = lax.dot_general(style[...], sums, dims, precision=highest, preferred_element_type=F32)
        put(i, (w_style, m_style, s_style), grad[0:CH, 0:CH], rate_table[2], (style_master, style_moment, style_square))

    head = total_of(got_head, 1)
    lane = lane_of((1, LANES))
    rows = []
    for k in range(3):
        last = jnp.sum(jnp.where(lane == 3 * CH + k, head, 0.0), axis=1, keepdims=True)
        rows.append(jnp.where(lane < CH, spread(head, k), last))
    grad = jnp.concatenate(rows, axis=0)[:, 0 : CH + 1]
    put(slice(None), (w_head, m_head, s_head), grad, rate_table[3], (head_master, head_moment, head_square, head_copy))


def update_late(
    got, got_one_back, got_head, more, more_two, vec, w_first, w_convs, table, m_first, m_convs, m_norms, s_first, s_convs, s_norms,
    first_master, first_moment, first_square, first_copy,
    convs_master, convs_moment, convs_square, convs_copy,
    norms_master, norms_moment, norms_square, *, pixel_count
):
    refs = (w_convs, m_convs, s_convs)
    outs = (convs_master, convs_moment, convs_square, convs_copy)
    packs = [[got[0:CH, k, 0, :].T for k in ks] for ks in ((5, 6, 7), (3, 4, 0), (1, 2, 0))]
    for i, pack in enumerate(packs):
        for t in range(9):
            b = t % 4 if t < 8 else (0, 3, 2)[i]
            put((i, t), refs, pack[t // 4][CH * b : CH * b + CH], rate_table[1], outs)

    zero_sums = total_of(got, 0)
    totals = [total_of(got, r) for r in range(7, 13)]
    shift, scale = spread(zero_sums, 0), spread(zero_sums, 1)
    factor = affine(table, 0)[0] * vec[0:1]
    entries = got_one_back[0:CH, 7, 0, :]
    by_x, alone = spread(entries, 0), spread(entries, 1)
    refs = (w_first, m_first, s_first)
    outs = (first_master, first_moment, first_square, first_copy)
    for t in range(10):
        pair = []
        for e in (2 * t, 2 * t + 1):
            k, b = divmod(1 + e, 4)
            v = spread(totals[k], b)
            if t < 9:
                v = factor * (v - (alone[e : e + 1] * shift + by_x[e : e + 1] * scale) / pixel_count)
            pair.append(v[:, 0:CH])
        put(t, refs, jnp.concatenate(pair, axis=0), rate_table[0], outs)

    three_sums = total_of(got_head, 0)
    scales = [scale, more[0:1], more_two[0:1], spread(three_sums, 1)]
    shifts = [shift, more[1:2], more_two[1:2], spread(three_sums, 0)]
    for i, rows in enumerate((scales, shifts)):
        grad = jnp.concatenate(rows, axis=0)[:, 0:CH]
        put(i, (table, m_norms, s_norms), grad, rate_table[4], (norms_master, norms_moment, norms_square))


def far(x):
    return ("far", x)


def call(kernel, outs, *operands, scalars=0, scratch=(), sems=0, scalar_outs=(), aliases=None, limit=VMEM_LIMIT, name):
    smem = pl.BlockSpec(memory_space=pltpu.SMEM)
    vmem = pl.BlockSpec(memory_space=pltpu.VMEM)
    hbm = pl.BlockSpec(memory_space=pltpu.HBM)
    is_far = lambda x: isinstance(x, tuple) and x[0] == "far"
    in_specs = [smem if i < scalars else hbm if is_far(x) else vmem for i, x in enumerate(operands)]
    out_specs = [smem if i in scalar_outs else hbm if is_far(x) else vmem for i, x in enumerate(outs)]
    plain = lambda x: x[1] if is_far(x) else x
    shapes = [pltpu.VMEM(shape, dtype) for shape, dtype in scratch]
    if sems:
        shapes.append(pltpu.SemaphoreType.DMA((sems,)))
    return pl.pallas_call(
        kernel,
        out_shape=[jax.ShapeDtypeStruct(*plain(x)) for x in outs],
        in_specs=in_specs,
        out_specs=out_specs,
        scratch_shapes=shapes,
        input_output_aliases=aliases or {},
        compiler_params=pltpu.CompilerParams(vmem_limit_bytes=limit),
        name=name,
    )(*[plain(x) for x in operands])


def exchange(pay):
    return lax.all_to_all(pay, ("row", "col"), 0, 0)


def local(
    image_batch, valid_mask, flow_target, cell_labels,
    w_first, w_convs, w_style, w_head, batch_norm_table,
    mom_first, mom_convs, mom_style, mom_head, mom_norms,
    sqr_first, sqr_convs, sqr_style, sqr_head, sqr_norms,
):
    images, block_rows, block_cols, _ = image_batch.shape
    row_count, col_count = lax.axis_size("row"), lax.axis_size("col")
    devices = row_count * col_count
    parts = devices // images
    image_rows, image_cols = row_count * block_rows, col_count * block_cols
    assert devices == parts * images and block_rows == RIM and block_cols == 2 * block_rows * 2
    assert image_rows % (parts * RIM) == 0 and devices >= CH
    height = image_rows // parts
    rows = min(image_rows, height + RIM * min(2, parts - 1))
    segments = image_cols // SEG
    local_count = float(height * image_cols)
    pixel_count = local_count * devices
    pool_cells = float(image_rows * image_cols // 4)
    part = functools.partial
    counts = dict(local_count=local_count, pixel_count=pixel_count, height=height)
    styled = dict(pool_cells=pool_cells, parts=parts)

    me = lax.axis_index("row") * col_count + lax.axis_index("col")
    first_row = (me % parts) * height
    start = jnp.clip(first_row - RIM, 0, image_rows - rows)
    place = jnp.stack([first_row - start, start // block_rows, me]).astype(jnp.int32)

    field = ((rows, 2, segments, LANES), F32)
    own_field = ((height,) + field[0][1:], F32)
    low_field = ((rows + 2, 3, segments, LANES), BF16)
    vec = ((8, LANES), F32)

    def payload(count):
        return ((devices, count, 1, LANES), F32)

    nine = ((BACK, 2 * LANES), BF16)
    ten = ((FORWARD, 2 * LANES), BF16)

    places = {
        name: i * count
        for count, names in (
            (rows, ("xhat_zero", "xhat_one", "shared")),
            (rows + 2, ("hidden_one", "hidden_three", "merged")),
        )
        for i, name in enumerate(names)
    }

    def spots(store, name):
        count = rows if name[0] in "xs" else rows + 2
        return store.at[places[name] : places[name] + count]

    def store_of(like):
        shape, dtype = like
        row_bytes = shape[1] * segments * LANES * jnp.dtype(dtype).itemsize
        return far(((-(-STORE_BYTES // row_bytes),) + shape[1:], dtype))

    inputs = (
        jnp.transpose(image_batch, (0, 1, 3, 2)), jnp.transpose(flow_target, (0, 1, 3, 2)), cell_labels, valid_mask
    )
    (pay,) = call(
        pack_kernel,
        [((devices, 16, LANES), BF16)],
        *[far(v) for v in inputs],
        scratch=[(v.shape, v.dtype) for v in inputs], sems=4, limit=WHOLE_VMEM, name="pack",
    )
    got_inputs = exchange(pay)
    head_rows = w_head.T
    weights, back_zero, back_two, head_mat = call(
        prepare,
        [far(((STORE_BYTES // (4 * LANES), 2 * LANES), BF16)), nine, nine, ((2 * LANES, LANES), BF16)],
        far(w_first), far(w_convs), far(head_rows),
        scratch=[
            (w_first.shape, F32), (w_convs.shape, F32), (head_rows.shape, F32), ((BACK_AT + BACK, 2 * LANES), BF16)
        ],
        sems=5, limit=WHOLE_VMEM, name="prepare",
    )

    sides, raw, pay, count, taps = call(
        part(start_kernel, local_count=local_count, height=height, sources=col_count),
        [((rows + 2, segments, LANES), BF16), field, payload(2), vec, ten],
        place, got_inputs, far(weights),
        scalars=1, scratch=[((3 * LANES, 2 * LANES), BF16)], sems=2, name="image_conv",
    )
    got_zero = exchange(pay)
    summed, pay, inv_zero, fields, lows = call(
        part(first_kernel, spots=spots, **counts),
        [field, payload(2), vec, store_of(field), store_of(low_field)],
        place, got_zero, raw, sides, batch_norm_table, taps,
        scalars=1, scratch=[low_field, field], sems=2, name="first_block",
    )
    got_one = exchange(pay)

    raw, pay, inv_one, merged, taps, fields, lows = call(
        part(pool_kernel, spots=spots, **counts),
        [field, payload(3), vec, low_field, nine, store_of(field), store_of(low_field)],
        place, got_one, summed, count, batch_norm_table, far(weights), far(fields), far(lows),
        scalars=1, scratch=[field, field, nine], sems=5,
        aliases={6: 5, 7: 6}, name="pool_and_merge",
    )
    got_style = exchange(pay)

    resid, pay, inv_two, style, xhat_two, lows = call(
        part(style_kernel, spots=spots, **styled, **counts),
        [field, payload(3), vec, ((devices, LANES), F32), field, store_of(low_field)],
        place, got_style, raw, merged, batch_norm_table, w_style, far(w_convs), taps, far(lows),
        scalars=1, scratch=[low_field, field, (w_convs.shape[1:], F32)], sems=2,
        aliases={8: 5}, name="decoder",
    )
    got_three = exchange(pay)
    ahead, hidden_sums = call(
        part(ahead_kernel, spots=spots, local_count=local_count),
        [((CH, 7, 1, LANES), F32), vec],
        place, far(pay), sides, far(fields), far(lows),
        scalars=1, scratch=[own_field, own_field, own_field, low_field], sems=4, name="ahead",
    )

    grad_three, xhat_three, pay, inv_three = call(
        part(head_kernel, **counts),
        [field, field, payload(10), vec],
        place, got_three, got_style, resid, sides, head_mat, head_rows, xhat_two, ahead, batch_norm_table, back_two,
        scalars=1, scratch=[((rows, 2, segments, LANES), BF16), field, low_field], name="head",
    )
    got_head = exchange(pay)

    grad_one, xhat_one, shared, pay, more_two = call(
        part(decoder_back_kernel, spots=spots, **counts),
        [field, field, field, payload(11), vec],
        place, got_head, grad_three, xhat_three, xhat_two, inv_three, inv_two, hidden_sums, batch_norm_table, back_two, far(weights),
        far(fields), far(lows),
        scalars=1, scratch=[field, field, low_field, low_field, low_field, low_field, low_field, nine], sems=6,
        name="decoder_back",
    )
    got_one_back = exchange(pay)

    pay, more = call(
        part(summed_kernel, spots=spots, pixel_count=pixel_count, **styled),
        [payload(13), vec],
        place, got_one_back, got_style, got_head, grad_one, xhat_one, shared, inv_one, more_two, batch_norm_table, w_style,
        sides, back_zero, far(fields),
        scalars=1, scratch=[own_field, own_field, low_field], sems=1, name="summed_back",
    )
    got_last = exchange(pay)

    def results(param, copy):
        return [(param.shape, F32)] * 3 + [(param.shape, BF16)] * copy

    early = call(
        update_early,
        [((1, 1), F32), ((1, 1), F32)] + results(w_style, 0) + results(head_rows, 1),
        got_one_back, got_head, got_style, far(pay), style,
        w_style, head_rows, mom_style, mom_head.T, sqr_style, sqr_head.T,
        scalar_outs=(0, 1), name="update_early",
    )
    late = call(
        part(update_late, pixel_count=pixel_count),
        results(w_first, 1) + results(w_convs, 1) + results(batch_norm_table, 0),
        got_last, got_one_back, got_head, more, more_two, inv_zero,
        w_first, w_convs, batch_norm_table, mom_first, mom_convs, mom_norms, sqr_first, sqr_convs, sqr_norms,
        name="update_late",
    )
    loss, count = early[0].reshape(()), early[1].reshape(())
    head = tuple(value.T for value in early[5:9])
    return (loss, count, *late[0:8], *early[2:5], *head, *late[8:11])


def solution(mesh):
    field = P(None, "row", "col", None)
    plane = P(None, "row", "col")
    return jax.shard_map(
        local,
        mesh=mesh,
        in_specs=(field, plane, field, plane) + (P(),) * 15,
        out_specs=(P(),) * 20,
        check_vma=False,
    )
```

```python
import functools

import jax
import jax.numpy as jnp
from jax import lax
from jax.experimental import pallas as pl
from jax.experimental.pallas import tpu as pltpu
from jax.sharding import PartitionSpec as P

STEP = 5

highest = lax.Precision.HIGHEST
norm_eps = 1e-05
flow_scale = 32.0
adam_eps = 1e-08
weight_decay = 0.01
beta_one = 0.5
beta_two = 0.5
rate_table = (0.2, 0.05, 0.15, 0.15, 0.2)

CH = 32
GRP = 4
SEG = 8
LANES = 128
RIM = 8
FLOW, LABEL, MASK = 16, 32, 40
LEFT, RIGHT = 64, 96
ALONE = 100
AFTER, ROW, BEFORE = 32, 33, 64
F32 = jnp.float32
BF16 = jnp.bfloat16
VMEM_LIMIT = 36 * 1024 * 1024
WHOLE_VMEM = 56 * 1024 * 1024
STORE_BYTES = 32 * 1024 * 1024
FORWARD = 10 * LANES
BACK = 9 * LANES
IMAGE_AT = 3 * FORWARD
BACK_AT = IMAGE_AT + 3 * LANES


def lane_of(shape):
    return lax.broadcasted_iota(jnp.int32, shape, len(shape) - 1)


def row_of(shape):
    return lax.broadcasted_iota(jnp.int32, shape, 0)


def group_of(shape):
    return lane_of(shape) >> 5


def fold(v):
    return v + pltpu.roll(v, 32, axis=1) + (pltpu.roll(v, 64, axis=1) + pltpu.roll(v, 96, axis=1))


def spread(v, k):
    return fold(jnp.where(group_of(v.shape) == k, v, 0.0))


def partner(v):
    odd = (group_of(v.shape) & 1) == 1
    return jnp.where(odd, pltpu.roll(v, 32, axis=1), pltpu.roll(v, 96, axis=1))


def tile4(v):
    return jnp.concatenate([v, v, v, v], axis=1)


def col_sum(v):
    return jnp.sum(v, axis=0, keepdims=True)


def zero_row():
    return jnp.zeros((1, LANES), F32)


def groups(*values):
    group = group_of(values[0].shape)
    out = values[-1]
    for k in range(len(values) - 2, -1, -1):
        out = jnp.where(group == k, values[k], out)
    return out


def low(v):
    return v.astype(BF16).astype(F32)


def sig_of(v):
    return 0.5 + 0.5 * jnp.tanh(0.5 * v)


def slope(n, sig):
    return sig * (1.0 + n * (1.0 - sig))


def slope_at(x, gain, bias):
    n = x * gain + bias
    return slope(n, sig_of(n))


def flat(v):
    return v.reshape(-1, LANES)


def loop(count, body, unroll=5):
    def step(i, carry):
        body(i)
        return carry

    lax.fori_loop(0, count, step, 0, unroll=min(count, unroll))


def copies(sems, *pairs):
    found = []
    for i, (source, target) in enumerate(pairs):
        found.append(pltpu.make_async_copy(source, target, sems.at[i]))
        found[-1].start()
    return found


def wait(started):
    for copy in started:
        copy.wait()


def shift_segments(v, way):
    half = v.shape[1]
    at = lax.broadcasted_iota(jnp.int32, v.shape, 1)
    if way == 1:
        return jnp.where(at == 0, 0.0, pltpu.roll(v, 1, axis=1))
    return jnp.where(at == half - 1, 0.0, pltpu.roll(v, half - 1, axis=1))


def beside(first, second):
    half = first.shape[1] // 2
    left = jnp.concatenate([shift_segments(second[:, half:], 1), second[:, :half]], axis=1)
    right = jnp.concatenate([first[:, half:], shift_segments(first[:, :half], -1)], axis=1)
    return left, right


def put_low(ref, row, first, second, marked=False):
    left, right = beside(first, second)
    lane = lane_of(left.shape)
    edge = jnp.where(lane < 64, right, left)
    if marked:
        at = lax.broadcasted_iota(jnp.int32, left.shape, 1)
        edge = jnp.where(lane == ROW, 1.0, edge)
        edge = jnp.where(lane == AFTER, jnp.where(at == left.shape[1] - 1, 0.0, 1.0), edge)
        edge = jnp.where(lane == BEFORE, jnp.where(at == 0, 0.0, 1.0), edge)
    at = pl.ds(row + 1, first.shape[0])
    for k, v in enumerate((first, second, edge)):
        ref[at, k] = v.astype(BF16)


def blank(ref):
    zero = jnp.zeros((1,) + ref.shape[1:], ref.dtype)
    ref[0:1] = zero
    ref[ref.shape[0] - 1 : ref.shape[0]] = zero


def views(src, row, rows):
    return [flat(src[pl.ds(row + r, rows), k]) for r in range(3) for k in (2, 0, 1)]


def conv(src, mat, row, rows, *more):
    wide = jnp.concatenate(views(src, row, rows) + list(more), axis=1)
    return jnp.dot(wide, mat[...], preferred_element_type=F32)


def blocks_of(y, rows):
    return [y[:, k * LANES : (k + 1) * LANES].reshape(rows, -1, LANES) for k in range(2)]


def narrow(v):
    while v.shape[0] > 1:
        half = v.shape[0] // 2
        v = v[:half] + v[half:]
    return v[0]


def row_sums(first, rows, values):
    step = 4

    def add(i, carry):
        found = [values(pl.ds(first + step * i, step), k) for k in range(2)]
        return tuple(c + a + b for c, a, b in zip(carry, *found))

    shapes = jax.eval_shape(lambda: values(pl.ds(0, step), 0))
    zeros = tuple(jnp.zeros(v.shape, F32) for v in shapes)
    found = lax.fori_loop(0, rows // step, add, zeros, unroll=min(rows // step, 8))
    return [col_sum(narrow(v)) for v in found]


def local_stats(v, first, rows, count):
    count = count / GRP
    pivot = col_sum(v[first, 0] + v[first, 1]) / (2 * v.shape[2])

    def moments(at, k):
        away = v[at, k] - pivot
        return away, away * away

    total, square = row_sums(first, rows, moments)
    return pivot + total / count, square - total * (total / count)


def merge_stats(means, squares, local_count, pixel_count):
    mean = fold(col_sum(means)) / (GRP * means.shape[0])
    away = means - mean
    total = fold(col_sum(squares + (local_count / GRP) * (away * away)))
    return mean, lax.rsqrt(total / pixel_count + norm_eps)


def row_of_each(got, r):
    return got[:, r, 0, :]


def total_of(got, r):
    return col_sum(row_of_each(got, r))


def send(pay, *rows):
    for r, row in enumerate(rows):
        pay[:, r, 0, :] = jnp.broadcast_to(row, (pay.shape[0], LANES))


def send_parts(pay, first, count):
    devices = pay.shape[0]
    if devices > CH:
        for r in range(first, first + count):
            pay[CH:, r, 0, :] = jnp.zeros((devices - CH, LANES), F32)
    return pay.at[0:CH, first : first + count, 0]


def affine(table, q):
    return tile4(table[0, q : q + 1, :]), tile4(table[1, q : q + 1, :])


def diagonal_blocks(mat):
    wide = tile4(mat)
    group = group_of(wide.shape)
    return jnp.concatenate([jnp.where(group == b, wide, 0.0) for b in range(GRP)], axis=0)


def notes(ref, *rows):
    for i, row in enumerate(rows):
        ref[i : i + 1, :] = row


def taps_at(store, i):
    return store.at[FORWARD * i : FORWARD * i + (BACK if i else FORWARD)]


def image_at(store):
    return store.at[IMAGE_AT : IMAGE_AT + 3 * LANES]


def back_at(store):
    return store.at[BACK_AT : BACK_AT + BACK]


def pack_kernel(image_in, flow_in, labels_in, valid_in, out, image, flow, labels, valid, sems):
    fetched = copies(sems, (image_in, image), (flow_in, flow), (labels_in, labels), (valid_in, valid))
    images, height, _, width = image.shape
    parts = out.shape[0] // images
    wait(fetched)
    fields = [image[:, :, c, :].astype(F32) for c in range(2)]
    fields += [flow[:, :, c, :].astype(F32) for c in range(2)]
    fields += [labels[...].astype(F32), valid[...].astype(F32)]
    halves = width // 16
    shape = (width, halves * LANES)
    lane = lane_of(shape)
    column = (lane >> 7) * 16 + ((lane >> 6) & 1) * 8 + (lane & 7)
    hit = row_of(shape) == column
    which = (lane >> 3) & 7
    total = jnp.zeros((images * height, halves * LANES), F32)
    for k, v in enumerate(fields):
        x = v.reshape(images * height, width).astype(BF16)
        mat = jnp.where(hit & (which == k), 1.0, 0.0).astype(BF16)
        total = total + jnp.dot(x, mat, preferred_element_type=F32)
    for b in range(images):
        rows = total[b * height : (b + 1) * height]
        slot = jnp.concatenate([rows[:, h * LANES : (h + 1) * LANES] for h in range(halves)], axis=0).astype(BF16)
        for p in range(parts):
            out[b * parts + p] = slot


COLUMNS = ((8, None, None, -1), (0, 1, 2, 3), (4, 5, 6, 7))


def conv_matrix(taps, mats, base, back):
    out_at = group_of((CH, 2 * LANES))
    for r in range(3):
        wide = []
        for s in range(3):
            if back:
                k = taps[3 * (2 - r) + s]
                k = jnp.concatenate([k, k, k, k], axis=0).T
            else:
                k = tile4(taps[3 * r + s])
            wide.append(jnp.concatenate([k, k], axis=1))
        for d in range(3):
            for a in range(GRP):
                val = jnp.zeros((CH, 2 * LANES), F32)
                column = COLUMNS[d][a]
                if column is not None:
                    for s in range(3):
                        val = jnp.where(out_at == (column + s - 1 if back else column + 1 - s), wide[s], val)
                mats[pl.ds(base + (3 * r + d) * LANES + CH * a, CH), :] = val.astype(BF16)


def image_lanes(shape):
    at = row_of(shape)
    kind = at >> 5
    column = (at & 7) + jnp.where(kind == LEFT // 32, -SEG, jnp.where(kind == RIGHT // 32, SEG, 0))
    return (kind != 1) & ((at & 31) < 16), (at >> 3) & 1, column


def first_taps(w_first, t):
    found = [tile4(low(w_first[t][c : c + 1])) for c in range(2)]
    return [jnp.concatenate([v, v], axis=1) for v in found]


def image_matrix(w_first, r):
    shape = (LANES, 2 * LANES)
    inside, channel, here = image_lanes(shape)
    val = jnp.zeros(shape, F32)
    for s in range(3):
        for c, tap in enumerate(first_taps(w_first, 3 * r + s)):
            val = jnp.where(inside & (channel == c) & (here == group_of(shape) + s - 1), tap, val)
    return val.astype(BF16)


def prepare(w_first_in, w_convs_in, w_head_in, store, back_zero, back_two, head_mat, w_first, w_convs, w_head, mats, sems):
    wait(copies(sems, (w_first_in, w_first), (w_convs_in, w_convs), (w_head_in, w_head)))
    shape = (LANES, 2 * LANES)
    inside, channel, here = image_lanes(shape)
    val = jnp.zeros(shape, F32)
    for c, tap in enumerate(first_taps(w_first, 9)):
        val = jnp.where((row_of(shape) < 16) & (channel == c) & (here == group_of(shape)), tap, val)
    mats[BACK:FORWARD, :] = val.astype(BF16)
    for r in range(3):
        mats[IMAGE_AT + LANES * r : IMAGE_AT + LANES * (r + 1), :] = image_matrix(w_first, r)
    stored = copies(sems, (image_at(mats), image_at(store)))
    for i in range(3):
        conv_matrix(w_convs.at[i], mats, FORWARD * i, False)
        stored += copies(sems.at[1 + i :], (taps_at(mats, i), taps_at(store, i)))
    conv_matrix(w_convs.at[1], mats, BACK_AT, True)
    stored += copies(sems.at[4:], (back_at(mats), back_at(store)))
    conv_matrix(w_convs.at[2], back_two, 0, True)
    conv_matrix(w_convs.at[0], back_zero, 0, True)
    lane = lane_of((CH, LANES))
    head = jnp.zeros((CH, LANES), F32)
    diagonal = row_of((CH, CH)) == lane_of((CH, CH))
    for k in range(3):
        column = jnp.sum(jnp.where(diagonal, low(w_head[k : k + 1, 0:CH]), 0.0), axis=1, keepdims=True)
        head = jnp.where((lane >> 3) == FLOW // 8 + k, column, head)
    for y in range(SEG):
        head_mat[CH * y : CH * (y + 1), :] = jnp.where((lane & 7) == y, head, 0.0).astype(BF16)
    wait(stored)


def start_kernel(place, got, weights, sides, raw, pay, vec, taps, first_mat, sems, *, local_count, height, sources):
    fetched = copies(sems, (image_at(weights), first_mat), (taps_at(weights, 0), taps))
    rows, segments = raw.shape[0], raw.shape[2]
    off, block = place[0], place[1]
    blank(sides)

    def eight(t):
        v = got[pl.ds((block + t) * sources, sources)].astype(F32)
        v = jnp.swapaxes(v.reshape(segments // 2, 8, LANES), 0, 1)
        near = lane_of(v.shape) < 64
        v = jnp.concatenate([jnp.where(near, v, 0.0), jnp.where(near, pltpu.roll(v, 64, axis=2), 0.0)], axis=1)
        pixels = jnp.where(lane_of(v.shape) < 16, v, 0.0)
        left, right = beside(pixels, pixels)
        v = v + pltpu.roll(left, LEFT, axis=2) + pltpu.roll(right, RIGHT, axis=2)
        sides[pl.ds(8 * t + 1, 8)] = v.astype(BF16)

    loop(rows // 8, eight)
    wait(fetched[:1])
    y = None
    for r in range(3):
        part = jnp.dot(flat(sides[r : r + rows]), first_mat[LANES * r : LANES * (r + 1)], preferred_element_type=F32)
        y = part if y is None else y + part
    raw[:, 0], raw[:, 1] = blocks_of(y, rows)
    mean, square = local_stats(raw, off, height, local_count)
    mask = jnp.zeros(sides.shape[1:], F32)
    for i in range(height):
        mask = mask + sides[off + 1 + i].astype(F32)
    lane = lane_of(mask.shape)
    count = jnp.sum(jnp.where((lane >= MASK) & (lane < MASK + 8), mask, 0.0))
    send(pay, mean, square)
    notes(vec, jnp.full((1, LANES), count, F32))
    wait(fetched[1:])


def first_kernel(place, got, raw, sides, table, taps, summed, pay, vec, fields, lows, hidden, xhat, sems, *, spots, local_count, pixel_count, height):
    mean, inverse = merge_stats(row_of_each(got, 0), row_of_each(got, 1), local_count, pixel_count)
    notes(vec, inverse)
    gain, bias = affine(table, 0)
    rows = raw.shape[0]

    def norm_rows(i):
        at = pl.ds(4 * i, 4)
        out = []
        for k in range(2):
            x = (raw[at, k] - mean) * inverse
            xhat[at, k] = x
            n = x * gain + bias
            out.append(n * sig_of(n))
        put_low(hidden, 4 * i, *out)

    blank(hidden)
    loop(rows // 4, norm_rows)
    stored = copies(sems, (xhat, spots(fields, "xhat_zero")), (hidden, spots(lows, "hidden_one")))

    @pl.when(place[0] >= 0)
    def _():
        y = conv(hidden, taps, 0, rows, flat(sides[1 : rows + 1]))
        summed[:, 0], summed[:, 1] = blocks_of(y, rows)

    send(pay, *local_stats(summed, place[0], height, local_count))
    wait(stored)


def pool_kernel(place, got, summed, count_in, table, weights, fields_in, lows_in, raw, pay, vec, merged, taps_next, fields, lows, xhat, shared, taps, sems, *, spots, local_count, pixel_count, height):
    fetched = copies(sems, (taps_at(weights, 1), taps), (taps_at(weights, 2), taps_next))
    mean, inverse = merge_stats(row_of_each(got, 0), row_of_each(got, 1), local_count, pixel_count)
    gain, bias = affine(table, 1)
    rows, segments = summed.shape[0], summed.shape[2]
    off = place[0]

    step = 4

    def some(i, carry):
        at = pl.ds(step * i, step)
        pairs = (step // 2, 2, segments, LANES)
        outs, sums = [], [jnp.zeros((step // 2 * segments, LANES), F32) for _ in range(3)]
        for k in range(2):
            x = (summed[at, k] - mean) * inverse
            n = x * gain + bias
            sig = sig_of(n)
            e = (n * sig).reshape(pairs)
            top = flat(jnp.maximum(e[:, 0], e[:, 1]))
            top = jnp.maximum(top, partner(top))
            wide_top = top.reshape(step // 2, 1, segments, LANES)
            exps = jnp.exp(e - wide_top)
            whole = flat(exps[:, 0] + exps[:, 1])
            whole = whole + partner(whole)
            pooled = top + jnp.log(whole)
            outs.append((e + pooled.reshape(wide_top.shape)).reshape(step, segments, LANES))
            share = exps * (1.0 / whole).reshape(wide_top.shape) * slope(n, sig).reshape(pairs)
            share_x = share * x.reshape(pairs)
            xhat[at, k] = x
            shared[at, k] = share.reshape(step, segments, LANES)
            sums[0] = sums[0] + pooled
            sums[1] = sums[1] + flat(share[:, 0] + share[:, 1])
            sums[2] = sums[2] + flat(share_x[:, 0] + share_x[:, 1])
        put_low(merged, step * i, *outs)
        mine = (step * i >= off) & (step * i < off + height)
        keep = jnp.where(mine, 1.0, 0.0)
        return tuple(a + keep * b for a, b in zip(carry, sums))

    blank(merged)
    zero = jnp.zeros((step // 2 * segments, LANES), F32)
    sums = lax.fori_loop(0, rows // step, some, (zero, zero, zero), unroll=min(rows // step, 5))
    pool_sum, share_sum, share_x = [fold(col_sum(v)) for v in sums]
    stored = copies(
        sems.at[2:],
        (xhat, spots(fields, "xhat_one")),
        (shared, spots(fields, "shared")),
        (merged, spots(lows, "merged")),
    )
    wait(fetched)
    raw[:, 0], raw[:, 1] = blocks_of(conv(merged, taps, 0, rows), rows)
    mean, square = local_stats(raw, place[0], height, local_count)
    send(pay, mean, square, groups(0.5 * pool_sum, share_sum, share_x, count_in[0:1]))
    notes(vec, inverse)
    wait(stored)


def by_image(v, parts):
    devices = v.shape[0]
    step = 1
    while step < parts:
        upper = (row_of(v.shape) // step) % 2 == 1
        v = v + jnp.where(upper, pltpu.roll(v, step, axis=0), pltpu.roll(v, devices - step, axis=0))
        step *= 2
    return v


def wide_dot(a, b, dims=(((1,), (0,)), ((), ()))):
    (a_high, a_low), (b_high, b_low) = [[v.astype(BF16) for v in in_parts(x, 2)] for x in (a, b)]
    axis_a, axis_b = dims[0][0][0], dims[0][1][0]
    left = jnp.concatenate([a_high, a_high, a_low], axis=axis_a)
    right = jnp.concatenate([b_high, b_low, b_high], axis=axis_b)
    return lax.dot_general(left, right, dims, preferred_element_type=F32)


def in_parts(v, count):
    out = []
    for _ in range(count):
        out.append(low(v))
        v = v - out[-1]
    return out


def mine_of(v, me):
    return col_sum(jnp.where(row_of(v.shape) == me, v, 0.0))


def style_kernel(place, got, raw, merged, table, w_style, w_convs_in, taps, lows_in, resid, pay, vec, style_out, xhat, lows, hidden, slopes, w_conv, sems, *, spots, local_count, pixel_count, pool_cells, height, parts):
    fetched = copies(sems, (w_convs_in.at[2], w_conv))
    style = by_image(spread(row_of_each(got, 2), 0), parts) / pool_cells
    style_out[...] = style
    one, two = [
        wide_dot(style, diagonal_blocks(w_style[i])) for i in range(2)
    ]
    mean, inverse = merge_stats(row_of_each(got, 0) + one, row_of_each(got, 1), local_count, pixel_count)
    notes(vec, inverse)
    gain, bias = affine(table, 2)
    rows = raw.shape[0]
    me = place[2]
    shift = mine_of(one, me) - mean
    two = mine_of(two, me)

    def norm_rows(i):
        at = pl.ds(4 * i, 4)
        out = []
        for k in range(2):
            x = (raw[at, k] + shift) * inverse
            xhat[at, k] = x
            n = x * gain + bias
            sig = sig_of(n)
            slopes[at, k] = slope(n, sig)
            out.append(n * sig)
        put_low(hidden, 4 * i, *out)

    blank(hidden)
    loop(rows // 4, norm_rows)
    stored = copies(sems.at[1:], (hidden, spots(lows, "hidden_three")))

    @pl.when(place[0] >= 0)
    def _():
        for k, y in enumerate(blocks_of(conv(hidden, taps, 0, rows), rows)):
            resid[:, k] = y + two + merged[1 : rows + 1, k].astype(F32)

    wait(fetched + stored)
    off = place[0]
    means, squares = local_stats(resid, off, height, local_count)
    centre = fold(means) / GRP
    at = pl.ds(off, height)
    probe = [slopes[at, k] for k in range(2)]
    probe += [slopes[at, k] * xhat[at, k] for k in range(2)]
    probe = jnp.concatenate([flat(v).astype(BF16) for v in probe], axis=1)

    def centred(i):
        at = pl.ds(4 * i, 4)
        put_low(hidden, 4 * i, resid[at, 0] - centre, resid[at, 1] - centre, True)

    loop(rows // 4, centred)
    send(pay, means, squares)
    links = norm_links(hidden, probe, off, height, w_conv, centre)
    send_parts(pay, 2, 1)[:, 0, :] = links


def norm_links(field, probe, first, rows, taps, centre):
    wide = jnp.concatenate(views(field, first, rows), axis=1)
    found = lax.dot_general(probe, wide, (((0,), (0,)), ((), ())), preferred_element_type=F32)
    group = group_of((CH, LANES))
    out = []
    for half in range(2):

        def piece(y, chunk):
            at = 2 * LANES * half + CH * y
            return found[at : at + CH, chunk * LANES : (chunk + 1) * LANES]

        plain = jnp.zeros((CH, LANES), F32)
        moved = jnp.zeros((CH, LANES), F32)
        for r in range(3):
            first_edge, last_edge = piece(0, 3 * r), piece(SEG - 1, 3 * r)
            edge = first_edge + last_edge
            for y in range(1, SEG - 1):
                edge = edge + piece(y, 3 * r)
            inside = edge[:, ROW : ROW + 1]
            counts = (
                inside + (first_edge[:, BEFORE : BEFORE + 1] - first_edge[:, ROW : ROW + 1]),
                inside,
                inside + (last_edge[:, AFTER : AFTER + 1] - last_edge[:, ROW : ROW + 1]),
            )
            for c in range(3):
                tap = tile4(low(taps[3 * (2 - r) + 2 - c]))
                val = jnp.zeros((CH, LANES), F32)
                for y in range(SEG):
                    d, a = spot_of(y + c - 1)
                    val = val + jnp.where(group == a, piece(y, 3 * r + d), 0.0)
                plain = plain + tap * counts[c]
                moved = moved + tap * val
        out += [plain, fold(moved) + centre * plain]
    return groups(*out)


def spot_of(x):
    if x < 0:
        return 0, 3
    if x == SEG:
        return 0, 0
    return 1 + x // GRP, x % GRP


def ahead_kernel(place, pay, sides, fields, lows, out, sums, below_x, xhat, shared, field, sems, *, spots, local_count):
    off = place[0]
    height = xhat.shape[0]
    own = pl.ds(off, height)
    fetched = copies(
        sems,
        (spots(fields, "xhat_zero").at[own], below_x),
        (spots(fields, "xhat_one").at[own], xhat),
        (spots(fields, "shared").at[own], shared),
        (spots(lows, "hidden_one"), field),
    )
    wait(fetched[:1])
    at = pl.ds(0, height)
    low_x = jnp.concatenate([own_lanes(below_x, at), jnp.ones((height * field.shape[2], LANES), BF16)], axis=1)
    entries, alone = [], zero_row()
    lane = lane_of((1, LANES))
    for r in range(3):
        for tap, bare in pixel_taps(sides, off + r, height, low_x, (-1, 0, 1), True):
            for v, b in zip(tap, bare):
                alone = jnp.where(lane == ALONE + len(entries), b, alone)
                entries.append(v)
    wait(fetched[1:])
    centres = [fold(v) / local_count for v in row_sums(0, height, lambda at, k: (xhat[at, k], shared[at, k]))]
    probe = [flat(v[at, k] - c).astype(BF16) for v, c in zip((xhat, shared), centres) for k in range(2)]
    wide = jnp.concatenate(views(field, off, height), axis=1)
    found = lax.dot_general(
        jnp.concatenate(probe, axis=1), wide, (((0,), (0,)), ((), ())), preferred_element_type=F32
    )
    ones = jnp.ones((8, wide.shape[0]), BF16)
    plain = jnp.dot(ones, wide, preferred_element_type=F32)[0:1]
    group = group_of((1, LANES))
    hidden = []
    for r in range(3):
        for s in range(3):
            val = zero_row()
            for y in range(SEG):
                d, a = spot_of(y + s - 1)
                spot = (3 * r + d) * LANES
                val = val + jnp.where(group == a, plain[:, spot : spot + LANES], 0.0)
            hidden.append(fold(val))
    packed = [groups(*hidden[0:4]), groups(*hidden[4:8]), hidden[8]]
    all_hidden = jnp.concatenate(packed, axis=0)
    last = [
        put_taps(
            found[2 * LANES * k : 2 * LANES * (k + 1)], out.at[:, 2 * k + 1 : 2 * k + 3, 0], (centres[k], all_hidden)
        )
        for k in range(2)
    ]
    entries += hidden
    entries.append(jnp.zeros((CH - len(entries), LANES), F32))
    out[:, 0, 0, :] = groups(jnp.concatenate(entries, axis=0), *last, jnp.zeros((CH, LANES), F32))
    notes(sums, *packed, alone)


def head_kernel(place, got, got_style, resid, sides, head_mat, w_head, below_x, ahead, image_sums, table, back, grad, xhat, pay, vec, decoded, slopes, grad_low, *, local_count, pixel_count, height):
    mean, inverse = merge_stats(row_of_each(got, 0), row_of_each(got, 1), local_count, pixel_count)
    notes(vec, inverse, mean)
    gain, bias = affine(table, 3)
    rows, segments = resid.shape[0], resid.shape[2]
    off = place[0]

    def norm_rows(i):
        at = pl.ds(4 * i, 4)
        for k in range(2):
            x = (resid[at, k] - mean) * inverse
            n = x * gain + bias
            s = sig_of(n)
            xhat[at, k] = x
            slopes[at, k] = slope(n, s)
            decoded[at, k] = (n * s).astype(BF16)

    loop(rows // 4, norm_rows, 10)
    head = head_mat[...]
    wide = jnp.concatenate([flat(decoded[:, 0]), flat(decoded[:, 1])], axis=1)
    bias_row = zero_row()
    for k in range(3):
        mine = (lane_of((1, LANES)) >> 3) == FLOW // 8 + k
        bias_row = jnp.where(mine, low(w_head[k : k + 1, CH : CH + 1]), bias_row)
    out = jnp.dot(wide, head, preferred_element_type=F32) + bias_row
    given = flat(sides[1 : rows + 1]).astype(F32)
    lane = lane_of(given.shape)
    is_flow = lane < LABEL
    near = [pltpu.roll(given, LANES - MASK + first, axis=1) for first in (FLOW, FLOW + 8, LABEL)]
    mask = jnp.where(lane < FLOW + 8, near[0], jnp.where(is_flow, near[1], near[2]))
    mask = jnp.where((lane >= FLOW) & (lane < LABEL + 8), mask, 0.0)
    count = jnp.sum(got_style[:, 2, 0, 3 * CH : 3 * CH + 1])
    diff = out - given / flow_scale
    hinge = jnp.maximum(out, 0.0) + jnp.log1p(jnp.exp(-jnp.abs(out)))
    loss = mask * jnp.where(is_flow, diff * diff, hinge - given * out)
    grad_out = (mask * jnp.where(is_flow, 2.0 * diff, sig_of(out) - given) / count).astype(BF16)
    at_row = lax.broadcasted_iota(jnp.int32, loss.shape, 0)
    inside = (at_row >= off * segments) & (at_row < (off + height) * segments)
    loss_sum = jnp.sum(jnp.where(inside, loss, 0.0))
    mine_out = jnp.where(inside, grad_out.astype(F32), 0.0).astype(BF16)
    outs = col_sum(mine_out.astype(F32))
    found = lax.dot_general(mine_out, wide, (((0,), (0,)), ((), ())), preferred_element_type=F32)
    shape = found.shape
    found = jnp.where((row_of(shape) & 7) == group_of(shape), found, 0.0)
    whole = [col_sum(found[FLOW + 8 * k : FLOW + 8 * k + 8]) for k in range(3)]
    whole = [fold(v[:, 0:LANES] + v[:, LANES:]) for v in whole]
    row = groups(*whole, zero_row())
    lane = lane_of((1, LANES))
    for k in range(3):
        row = jnp.where(lane == 3 * CH + k, jnp.sum(jnp.where((lane >> 3) == FLOW // 8 + k, outs, 0.0)), row)
    row = jnp.where(lane == 3 * CH + 3, loss_sum, row)
    y = lax.dot_general(grad_out, head, (((1,), (1,)), ((), ())), preferred_element_type=F32)
    for k, g in enumerate(blocks_of(y, rows)):
        grad[:, k] = g * slopes[:, k]
    factor = gain * inverse
    back_rows(grad_low, rows, lambda at, k: factor * grad[at, k], 10)
    shift_sum, scale_sum = own_sums(grad, xhat, off, height)
    y = conv(grad_low, back, off, height)
    slopes[0:height, 0], slopes[0:height, 1] = blocks_of(y, height)
    gain, bias = affine(table, 2)

    def links(at, k):
        x = below_x[pl.ds(off + at.start, at.size), k]
        g = slopes[at, k] * slope_at(x, gain, bias)
        return g, g * x

    below = [fold(v) for v in row_sums(0, height, links)]
    send(pay, groups(shift_sum, scale_sum, *below), row + image_sums[3:4], total_of(got, 2))
    send_parts(pay, 3, 5)
    pay[0:CH, 3:8] = ahead[...]


def own_sums(grad, xhat, first, rows):
    def both(at, k):
        g = grad[at, k]
        return g, g * xhat[at, k]

    return [fold(v) for v in row_sums(first, rows, both)]


def back_sums(got, pixel_count):
    whole = col_sum(got)
    return spread(whole, 0) / pixel_count, spread(whole, 1) / pixel_count


def low_sum(grad_low, first, rows):
    return fold(row_sums(first + 1, rows, lambda at, k: (grad_low[at, k].astype(F32),))[0])


def norm_back(grad, xhat, factor, shift, scale):
    return factor * (grad - (shift + xhat * scale))


def back_rows(grad_low, rows, value, unroll=5):
    def some(i):
        put_low(grad_low, 4 * i, *[value(pl.ds(4 * i, 4), k) for k in range(2)])

    blank(grad_low)
    loop(rows // 4, some, unroll)


def own_lanes(grad, at):
    return jnp.concatenate([flat(grad[at, k]).astype(BF16) for k in range(2)], axis=1)


def tap_sums(field, grad, first, rows, out, more=None):
    wide = jnp.concatenate(views(field, first, rows), axis=1)
    found = lax.dot_general(grad, wide, (((0,), (0,)), ((), ())), preferred_element_type=F32)
    return put_taps(found, out, more)


def put_taps(found, out, more=None):
    group = group_of((CH, LANES))
    taps = []
    for r in range(3):
        for s in range(3):
            val = jnp.zeros((CH, LANES), F32)
            for y in range(SEG):
                d, a = spot_of(y + s - 1)
                spot = (3 * r + d) * LANES
                val = val + jnp.where(group == a, found[CH * y : CH * y + CH, spot : spot + LANES], 0.0)
            taps.append(fold(val))
    for q in range(3):
        val = taps[4 * q]
        for b in range(1, min(4, 9 - 4 * q)):
            val = jnp.where(group == b, taps[4 * q + b], val)
        if more is not None:
            centre, sums = more
            val = val + column_of(centre) * sums[q : q + 1]
        if q == 2:
            return val
        out[:, q, :] = val


def column_of(v):
    shape = (CH, LANES)
    return jnp.sum(jnp.where(row_of(shape) == lane_of(shape), v, 0.0), axis=1, keepdims=True)


def at_lane(v, k):
    return jnp.sum(jnp.where(lane_of(v.shape) == k, v, 0.0), axis=1, keepdims=True)


def decoder_back_kernel(place, got, grad, xhat, mid_x, vec, vec_two, sums, table, back_two, weights, fields, lows, below, below_x, shared, pay, more, kept_grad, mid, low_two, low_one, field_two, field_one, field_zero, back_one, sems, *, spots, local_count, pixel_count, height):
    fetched = copies(
        sems,
        (back_at(weights), back_one),
        (spots(fields, "xhat_one"), below_x),
        (spots(fields, "shared"), shared),
        (spots(lows, "hidden_three"), field_two),
        (spots(lows, "merged"), field_one),
        (spots(lows, "hidden_one"), field_zero),
    )
    devices = got.shape[0]
    rows = grad.shape[0]
    off = place[0]
    total = total_of(got, 0)
    shift, scale = spread(total, 0) / pixel_count, spread(total, 1) / pixel_count
    inverse, mean = vec[0:1], vec[1:2]
    factor = affine(table, 3)[0] * inverse
    slant = scale * inverse
    held, carried = factor * (shift - slant * mean), factor * slant
    links = got[0:CH, 2, 0, :] * groups(held, carried, held, carried)
    group = group_of(links.shape)
    mine = (lane_of(links.shape) & 31) == row_of(links.shape)

    def across(pick):
        column = jnp.sum(jnp.where(pick, links, 0.0), axis=1, keepdims=True)
        return col_sum(jnp.where(mine, column, 0.0))

    shift_two = spread(total, 2) - across(group < 2)
    scale_two = spread(total, 3) - across(group >= 2)
    entry = total_of(got, 3)
    notes(more, scale_two, shift_two, total_of(got, 4), total_of(got, 5), spread(entry, 1))

    def value(at, k):
        g = norm_back(grad[at, k], xhat[at, k], factor, shift, scale)
        kept_grad[at, k] = g
        return g

    back_rows(low_two, rows, value)

    @pl.when(place[0] >= 0)
    def _():
        mid[:, 0], mid[:, 1] = blocks_of(conv(low_two, back_two, 0, rows), rows)

    gain, bias = affine(table, 2)
    factor = gain * vec_two[0:1]
    shift, scale = shift_two / pixel_count, scale_two / pixel_count

    def value_two(at, k):
        x = mid_x[at, k]
        return norm_back(mid[at, k] * slope_at(x, gain, bias), x, factor, shift, scale)

    back_rows(low_one, rows, value_two)
    wait(fetched)
    sum_two = low_sum(low_two, off, height)
    sum_one = low_sum(low_one, off, height)
    y = conv(low_one, back_one, 0, rows)
    gain, bias = affine(table, 1)
    for k, y in enumerate(blocks_of(y, rows)):
        g = (y + kept_grad[:, k]).reshape(rows // 2, 2, -1, LANES)
        both = flat(g[:, 0] + g[:, 1])
        both = (both + partner(both)).reshape(rows // 2, 1, -1, LANES)
        g = g * slope_at(below_x[:, k], gain, bias).reshape(g.shape) + both * shared[:, k].reshape(g.shape)
        below[:, k] = g.reshape(rows, -1, LANES)
    shift_sum, scale_sum = own_sums(below, below_x, off, height)
    send(pay, groups(shift_sum, scale_sum, sum_one, sum_two))
    entry = spread(entry, 0)
    pay[:, 1, 0, :] = jnp.broadcast_to(entry, (devices, LANES))
    at = pl.ds(off + 1, height)
    last_two = tap_sums(field_two, own_lanes(low_two, at), off, height, send_parts(pay, 2, 2))
    last_one = tap_sums(field_one, own_lanes(low_one, at), off, height, send_parts(pay, 4, 2))
    centre = shift_sum / local_count
    at = pl.ds(off, height)
    grad = jnp.concatenate([flat(below[at, k] - centre).astype(BF16) for k in range(2)], axis=1)
    last_zero = tap_sums(field_zero, grad, off, height, send_parts(pay, 6, 2), (centre, sums))
    pay[0:CH, 1, 0, :] = groups(last_two, last_one, last_zero, jnp.broadcast_to(entry, (CH, LANES)))


def summed_kernel(place, got, got_style, got_head, grad, xhat, shared, vec, more_two, table, w_style, sides, back, fields, pay, more, below, below_x, grad_low, sems, *, spots, pixel_count, pool_cells, parts):
    off = place[0]
    height = below.shape[0]
    fetched = copies(sems, (spots(fields, "xhat_zero").at[pl.ds(off, height)], below_x))
    devices = got.shape[0]
    rows = grad.shape[0]
    dims = (((1,), (1,)), ((), ()))
    first = row_of_each(got, 0)
    each = wide_dot(spread(first, 2), diagonal_blocks(w_style[0]), dims) + wide_dot(
        spread(first, 3), diagonal_blocks(w_style[1]), dims
    )
    each = each / pool_cells
    total = col_sum(first)
    shift = spread(total, 0) + col_sum(each * by_image(spread(row_of_each(got_style, 2), 1), parts))
    scale = spread(total, 1) + col_sum(each * by_image(spread(row_of_each(got_style, 2), 2), parts))
    mine = col_sum(jnp.where(row_of(each.shape) // parts == place[2] // parts, each, 0.0))
    factor = affine(table, 1)[0] * vec[0:1]
    shift_mean, scale_mean = shift / pixel_count, scale / pixel_count
    def value(at, k):
        return norm_back(grad[at, k] + shared[at, k] * mine, xhat[at, k], factor, shift_mean, scale_mean)

    back_rows(grad_low, rows, value)
    gain, bias = affine(table, 0)
    wait(fetched)
    for k, y in enumerate(blocks_of(conv(grad_low, back, off, height), height)):
        below[:, k] = y * slope_at(below_x[:, k], gain, bias)
    me = place[2]
    weights = at_lane(by_image(each, parts), me)
    hidden = spread(got[0:CH, 1, 0, :], 3)
    hidden = [groups(*[hidden[18 + t : 19 + t] for t in range(4 * q, min(4 * q + 4, 9))]) for q in range(3)]
    last = total_of(got, 1)
    direct = [total_of(got, 6), total_of(got, 7), spread(last, 2)]
    shares = [row_of_each(got_head, 6), row_of_each(got_head, 7), spread(row_of_each(got_head, 3), 2)]
    shard = []
    for q in range(3):
        val = direct[q] + col_sum(weights * shares[q])
        val = val - at_lane(shift_mean, me) * hidden[q] - at_lane(scale_mean, me) * more_two[2 + q : 3 + q]
        shard.append(at_lane(factor, me) * val)
    at = pl.ds(off + 1, height)
    side = pixel_taps(sides, off + 1, height, own_lanes(grad_low, at), (0,))[0]
    low_below = own_lanes(below, pl.ds(0, height))
    taps = []
    for r in range(3):
        for tap in pixel_taps(sides, off + r, height, low_below, (-1, 0, 1)):
            taps.extend(tap)
    taps = [shard[2]] + taps + side
    send(
        pay,
        groups(*own_sums(below, below_x, 0, height), spread(last, 0), spread(last, 1)),
        *[total_of(got, r) for r in range(2, 6)],
        *shard[0:2],
        *[groups(*(taps[4 * q : 4 * q + 4] + [zero_row()])[0:4]) for q in range(6)],
    )
    notes(more, scale, shift)


def pixel_taps(sides, row, rows, grad, shift, alone=False):
    x = flat(sides[pl.ds(row, rows)])
    found = lax.dot_general(x, grad, (((0,), (0,)), ((), ())), preferred_element_type=F32)
    inside, channel, column = image_lanes((LANES, 2 * LANES))
    here = column - group_of((LANES, 2 * LANES))
    out = []
    for s in shift:
        both, bare = [], []
        for c in range(2):
            v = col_sum(jnp.where(inside & (channel == c) & (here == s), found[:, 0 : 2 * LANES], 0.0))
            both.append(fold(v[:, 0:LANES] + v[:, LANES:]))
            if alone:
                cut = slice(0, LANES)
                hit = (inside & (channel == c) & (column >= s) & (column < s + SEG))[:, cut]
                bare.append(col_sum(jnp.where(hit, found[:, 2 * LANES :], 0.0)))
        out.append((both, bare) if alone else both)
    return out


def adamw(master, moment, square, grad, rate):
    new_moment = beta_one * moment + (1.0 - beta_one) * grad
    new_square = beta_two * square + (1.0 - beta_two) * grad * grad
    moment_hat = new_moment / (1.0 - beta_one**STEP)
    square_hat = new_square / (1.0 - beta_two**STEP)
    new_master = master - rate * (moment_hat / (jnp.sqrt(square_hat) + adam_eps) + weight_decay * master)
    return new_master, new_moment, new_square


def put(at, refs, grad, rate, outs):
    found = adamw(*[ref[at] for ref in refs], grad, rate)
    for out, value in zip(outs, found + (found[0].astype(BF16),)):
        out[at] = value


def update_early(
    got_one_back, got_head, got_style, pay, style, w_style, w_head, m_style, m_head, s_style, s_head,
    loss_out, count_out, style_master, style_moment, style_square, head_master, head_moment, head_square, head_copy,
):
    count_out[0, 0] = jnp.sum(got_style[:, 2, 0, 3 * CH : 3 * CH + 1])
    loss_out[0, 0] = jnp.sum(got_head[:, 1, 0, 99:100])
    dims = (((0,), (0,)), ((), ()))
    for i in range(2):
        sums = spread(row_of_each(got_one_back, 0), 2 + i)
        grad = lax.dot_general(style[...], sums, dims, precision=highest, preferred_element_type=F32)
        put(i, (w_style, m_style, s_style), grad[0:CH, 0:CH], rate_table[2], (style_master, style_moment, style_square))

    head = total_of(got_head, 1)
    lane = lane_of((1, LANES))
    rows = []
    for k in range(3):
        last = jnp.sum(jnp.where(lane == 3 * CH + k, head, 0.0), axis=1, keepdims=True)
        rows.append(jnp.where(lane < CH, spread(head, k), last))
    grad = jnp.concatenate(rows, axis=0)[:, 0 : CH + 1]
    put(slice(None), (w_head, m_head, s_head), grad, rate_table[3], (head_master, head_moment, head_square, head_copy))


def update_late(
    got, got_one_back, got_head, more, more_two, vec, w_first, w_convs, table, m_first, m_convs, m_norms, s_first, s_convs, s_norms,
    first_master, first_moment, first_square, first_copy,
    convs_master, convs_moment, convs_square, convs_copy,
    norms_master, norms_moment, norms_square, *, pixel_count
):
    refs = (w_convs, m_convs, s_convs)
    outs = (convs_master, convs_moment, convs_square, convs_copy)
    packs = [[got[0:CH, k, 0, :].T for k in ks] for ks in ((5, 6, 7), (3, 4, 0), (1, 2, 0))]
    for i, pack in enumerate(packs):
        for t in range(9):
            b = t % 4 if t < 8 else (0, 3, 2)[i]
            put((i, t), refs, pack[t // 4][CH * b : CH * b + CH], rate_table[1], outs)

    zero_sums = total_of(got, 0)
    totals = [total_of(got, r) for r in range(7, 13)]
    shift, scale = spread(zero_sums, 0), spread(zero_sums, 1)
    factor = affine(table, 0)[0] * vec[0:1]
    by_x = spread(got_one_back[0:CH, 1, 0, :], 3)
    alone = total_of(got_head, 1)
    refs = (w_first, m_first, s_first)
    outs = (first_master, first_moment, first_square, first_copy)
    for t in range(10):
        pair = []
        for e in (2 * t, 2 * t + 1):
            k, b = divmod(1 + e, 4)
            v = spread(totals[k], b)
            if t < 9:
                v = factor * (v - (at_lane(alone, ALONE + e) * shift + by_x[e : e + 1] * scale) / pixel_count)
            pair.append(v[:, 0:CH])
        put(t, refs, jnp.concatenate(pair, axis=0), rate_table[0], outs)

    three_sums = total_of(got_head, 0)
    scales = [scale, more[0:1], more_two[0:1], spread(three_sums, 1)]
    shifts = [shift, more[1:2], more_two[1:2], spread(three_sums, 0)]
    for i, rows in enumerate((scales, shifts)):
        grad = jnp.concatenate(rows, axis=0)[:, 0:CH]
        put(i, (table, m_norms, s_norms), grad, rate_table[4], (norms_master, norms_moment, norms_square))


def far(x):
    return ("far", x)


def call(kernel, outs, *operands, scalars=0, scratch=(), sems=0, scalar_outs=(), aliases=None, limit=VMEM_LIMIT, name):
    smem = pl.BlockSpec(memory_space=pltpu.SMEM)
    vmem = pl.BlockSpec(memory_space=pltpu.VMEM)
    hbm = pl.BlockSpec(memory_space=pltpu.HBM)
    is_far = lambda x: isinstance(x, tuple) and x[0] == "far"
    in_specs = [smem if i < scalars else hbm if is_far(x) else vmem for i, x in enumerate(operands)]
    out_specs = [smem if i in scalar_outs else hbm if is_far(x) else vmem for i, x in enumerate(outs)]
    plain = lambda x: x[1] if is_far(x) else x
    shapes = [pltpu.VMEM(shape, dtype) for shape, dtype in scratch]
    if sems:
        shapes.append(pltpu.SemaphoreType.DMA((sems,)))
    return pl.pallas_call(
        kernel,
        out_shape=[jax.ShapeDtypeStruct(*plain(x)) for x in outs],
        in_specs=in_specs,
        out_specs=out_specs,
        scratch_shapes=shapes,
        input_output_aliases=aliases or {},
        compiler_params=pltpu.CompilerParams(vmem_limit_bytes=limit),
        name=name,
    )(*[plain(x) for x in operands])


def exchange(pay):
    return lax.all_to_all(pay, ("row", "col"), 0, 0)


def local(
    image_batch, valid_mask, flow_target, cell_labels,
    w_first, w_convs, w_style, w_head, batch_norm_table,
    mom_first, mom_convs, mom_style, mom_head, mom_norms,
    sqr_first, sqr_convs, sqr_style, sqr_head, sqr_norms,
):
    images, block_rows, block_cols, _ = image_batch.shape
    row_count, col_count = lax.axis_size("row"), lax.axis_size("col")
    devices = row_count * col_count
    parts = devices // images
    image_rows, image_cols = row_count * block_rows, col_count * block_cols
    assert devices == parts * images and block_rows == RIM and block_cols == 2 * block_rows * 2
    assert image_rows % (parts * RIM) == 0 and devices >= CH
    height = image_rows // parts
    rows = min(image_rows, height + RIM * min(2, parts - 1))
    segments = image_cols // SEG
    local_count = float(height * image_cols)
    pixel_count = local_count * devices
    pool_cells = float(image_rows * image_cols // 4)
    part = functools.partial
    counts = dict(local_count=local_count, pixel_count=pixel_count, height=height)
    styled = dict(pool_cells=pool_cells, parts=parts)

    me = lax.axis_index("row") * col_count + lax.axis_index("col")
    first_row = (me % parts) * height
    start = jnp.clip(first_row - RIM, 0, image_rows - rows)
    place = jnp.stack([first_row - start, start // block_rows, me]).astype(jnp.int32)

    field = ((rows, 2, segments, LANES), F32)
    own_field = ((height,) + field[0][1:], F32)
    low_field = ((rows + 2, 3, segments, LANES), BF16)
    vec = ((8, LANES), F32)

    def payload(count):
        return ((devices, count, 1, LANES), F32)

    nine = ((BACK, 2 * LANES), BF16)
    ten = ((FORWARD, 2 * LANES), BF16)

    places = {
        name: i * count
        for count, names in (
            (rows, ("xhat_zero", "xhat_one", "shared")),
            (rows + 2, ("hidden_one", "hidden_three", "merged")),
        )
        for i, name in enumerate(names)
    }

    def spots(store, name):
        count = rows if name[0] in "xs" else rows + 2
        return store.at[places[name] : places[name] + count]

    def store_of(like):
        shape, dtype = like
        row_bytes = shape[1] * segments * LANES * jnp.dtype(dtype).itemsize
        return far(((-(-STORE_BYTES // row_bytes),) + shape[1:], dtype))

    inputs = (
        jnp.transpose(image_batch, (0, 1, 3, 2)), jnp.transpose(flow_target, (0, 1, 3, 2)), cell_labels, valid_mask
    )
    (pay,) = call(
        pack_kernel,
        [((devices, 16, LANES), BF16)],
        *[far(v) for v in inputs],
        scratch=[(v.shape, v.dtype) for v in inputs], sems=4, limit=WHOLE_VMEM, name="pack",
    )
    got_inputs = exchange(pay)
    head_rows = w_head.T
    weights, back_zero, back_two, head_mat = call(
        prepare,
        [far(((STORE_BYTES // (4 * LANES), 2 * LANES), BF16)), nine, nine, ((2 * LANES, LANES), BF16)],
        far(w_first), far(w_convs), far(head_rows),
        scratch=[
            (w_first.shape, F32), (w_convs.shape, F32), (head_rows.shape, F32), ((BACK_AT + BACK, 2 * LANES), BF16)
        ],
        sems=5, limit=WHOLE_VMEM, name="prepare",
    )

    sides, raw, pay, count, taps = call(
        part(start_kernel, local_count=local_count, height=height, sources=col_count),
        [((rows + 2, segments, LANES), BF16), field, payload(2), vec, ten],
        place, got_inputs, far(weights),
        scalars=1, scratch=[((3 * LANES, 2 * LANES), BF16)], sems=2, name="image_conv",
    )
    got_zero = exchange(pay)
    summed, pay, inv_zero, fields, lows = call(
        part(first_kernel, spots=spots, **counts),
        [field, payload(2), vec, store_of(field), store_of(low_field)],
        place, got_zero, raw, sides, batch_norm_table, taps,
        scalars=1, scratch=[low_field, field], sems=2, name="first_block",
    )
    got_one = exchange(pay)

    raw, pay, inv_one, merged, taps, fields, lows = call(
        part(pool_kernel, spots=spots, **counts),
        [field, payload(3), vec, low_field, nine, store_of(field), store_of(low_field)],
        place, got_one, summed, count, batch_norm_table, far(weights), far(fields), far(lows),
        scalars=1, scratch=[field, field, nine], sems=5,
        aliases={6: 5, 7: 6}, name="pool_and_merge",
    )
    got_style = exchange(pay)

    resid, pay, inv_two, style, xhat_two, lows = call(
        part(style_kernel, spots=spots, **styled, **counts),
        [field, payload(3), vec, ((devices, LANES), F32), field, store_of(low_field)],
        place, got_style, raw, merged, batch_norm_table, w_style, far(w_convs), taps, far(lows),
        scalars=1, scratch=[low_field, field, (w_convs.shape[1:], F32)], sems=2,
        aliases={8: 5}, name="decoder",
    )
    got_three = exchange(pay)
    ahead, hidden_sums = call(
        part(ahead_kernel, spots=spots, local_count=local_count),
        [((CH, 5, 1, LANES), F32), vec],
        place, far(pay), sides, far(fields), far(lows),
        scalars=1, scratch=[own_field, own_field, own_field, low_field], sems=4, name="ahead",
    )

    grad_three, xhat_three, pay, inv_three = call(
        part(head_kernel, **counts),
        [field, field, payload(8), vec],
        place, got_three, got_style, resid, sides, head_mat, head_rows, xhat_two, ahead, hidden_sums, batch_norm_table, back_two,
        scalars=1, scratch=[((rows, 2, segments, LANES), BF16), field, low_field], name="head",
    )
    got_head = exchange(pay)

    grad_one, xhat_one, shared, pay, more_two = call(
        part(decoder_back_kernel, spots=spots, **counts),
        [field, field, field, payload(8), vec],
        place, got_head, grad_three, xhat_three, xhat_two, inv_three, inv_two, hidden_sums, batch_norm_table, back_two, far(weights),
        far(fields), far(lows),
        scalars=1, scratch=[field, field, low_field, low_field, low_field, low_field, low_field, nine], sems=6,
        name="decoder_back",
    )
    got_one_back = exchange(pay)

    pay, more = call(
        part(summed_kernel, spots=spots, pixel_count=pixel_count, **styled),
        [payload(13), vec],
        place, got_one_back, got_style, got_head, grad_one, xhat_one, shared, inv_one, more_two, batch_norm_table, w_style,
        sides, back_zero, far(fields),
        scalars=1, scratch=[own_field, own_field, low_field], sems=1, name="summed_back",
    )
    got_last = exchange(pay)

    def results(param, copy):
        return [(param.shape, F32)] * 3 + [(param.shape, BF16)] * copy

    early = call(
        update_early,
        [((1, 1), F32), ((1, 1), F32)] + results(w_style, 0) + results(head_rows, 1),
        got_one_back, got_head, got_style, far(pay), style,
        w_style, head_rows, mom_style, mom_head.T, sqr_style, sqr_head.T,
        scalar_outs=(0, 1), name="update_early",
    )
    late = call(
        part(update_late, pixel_count=pixel_count),
        results(w_first, 1) + results(w_convs, 1) + results(batch_norm_table, 0),
        got_last, got_one_back, got_head, more, more_two, inv_zero,
        w_first, w_convs, batch_norm_table, mom_first, mom_convs, mom_norms, sqr_first, sqr_convs, sqr_norms,
        name="update_late",
    )
    loss, count = early[0].reshape(()), early[1].reshape(())
    head = tuple(value.T for value in early[5:9])
    return (loss, count, *late[0:8], *early[2:5], *head, *late[8:11])


def solution(mesh):
    field = P(None, "row", "col", None)
    plane = P(None, "row", "col")
    return jax.shard_map(
        local,
        mesh=mesh,
        in_specs=(field, plane, field, plane) + (P(),) * 15,
        out_specs=(P(),) * 20,
        check_vma=False,
    )
```

```python
import functools

import jax
import jax.numpy as jnp
from jax import lax
from jax.experimental import pallas as pl
from jax.experimental.pallas import tpu as pltpu
from jax.sharding import PartitionSpec as P

STEP = 5

highest = lax.Precision.HIGHEST
norm_eps = 1e-05
flow_scale = 32.0
adam_eps = 1e-08
weight_decay = 0.01
beta_one = 0.5
beta_two = 0.5
rate_table = (0.2, 0.05, 0.15, 0.15, 0.2)

CH = 32
GRP = 4
SEG = 8
LANES = 128
RIM = 8
FLOW, LABEL, MASK = 16, 32, 40
LEFT, RIGHT = 64, 96
ALONE = 100
AFTER, ROW, BEFORE = 32, 33, 64
F32 = jnp.float32
BF16 = jnp.bfloat16
VMEM_LIMIT = 36 * 1024 * 1024
WHOLE_VMEM = 56 * 1024 * 1024
STORE_BYTES = 32 * 1024 * 1024
FORWARD = 10 * LANES
BACK = 9 * LANES
IMAGE_AT = 3 * FORWARD
BACK_AT = IMAGE_AT + 3 * LANES


def lane_of(shape):
    return lax.broadcasted_iota(jnp.int32, shape, len(shape) - 1)


def row_of(shape):
    return lax.broadcasted_iota(jnp.int32, shape, 0)


def group_of(shape):
    return lane_of(shape) >> 5


def fold(v):
    return v + pltpu.roll(v, 32, axis=1) + (pltpu.roll(v, 64, axis=1) + pltpu.roll(v, 96, axis=1))


def spread(v, k):
    return fold(jnp.where(group_of(v.shape) == k, v, 0.0))


def partner(v):
    odd = (group_of(v.shape) & 1) == 1
    return jnp.where(odd, pltpu.roll(v, 32, axis=1), pltpu.roll(v, 96, axis=1))


def tile4(v):
    return jnp.concatenate([v, v, v, v], axis=1)


def col_sum(v):
    return jnp.sum(v, axis=0, keepdims=True)


def zero_row():
    return jnp.zeros((1, LANES), F32)


def groups(*values):
    group = group_of(values[0].shape)
    out = values[-1]
    for k in range(len(values) - 2, -1, -1):
        out = jnp.where(group == k, values[k], out)
    return out


def low(v):
    return v.astype(BF16).astype(F32)


def sig_of(v):
    return 0.5 + 0.5 * jnp.tanh(0.5 * v)


def slope(n, sig):
    return sig * (1.0 + n * (1.0 - sig))


def slope_at(x, gain, bias):
    n = x * gain + bias
    return slope(n, sig_of(n))


def flat(v):
    return v.reshape(-1, LANES)


def loop(count, body, unroll=5):
    def step(i, carry):
        body(i)
        return carry

    lax.fori_loop(0, count, step, 0, unroll=min(count, unroll))


def copies(sems, *pairs):
    found = []
    for i, (source, target) in enumerate(pairs):
        found.append(pltpu.make_async_copy(source, target, sems.at[i]))
        found[-1].start()
    return found


def wait(started):
    for copy in started:
        copy.wait()


def shift_segments(v, way):
    half = v.shape[1]
    at = lax.broadcasted_iota(jnp.int32, v.shape, 1)
    if way == 1:
        return jnp.where(at == 0, 0.0, pltpu.roll(v, 1, axis=1))
    return jnp.where(at == half - 1, 0.0, pltpu.roll(v, half - 1, axis=1))


def beside(first, second):
    half = first.shape[1] // 2
    left = jnp.concatenate([shift_segments(second[:, half:], 1), second[:, :half]], axis=1)
    right = jnp.concatenate([first[:, half:], shift_segments(first[:, :half], -1)], axis=1)
    return left, right


def put_low(ref, row, first, second, marked=False):
    left, right = beside(first, second)
    lane = lane_of(left.shape)
    edge = jnp.where(lane < 64, right, left)
    if marked:
        at = lax.broadcasted_iota(jnp.int32, left.shape, 1)
        edge = jnp.where(lane == ROW, 1.0, edge)
        edge = jnp.where(lane == AFTER, jnp.where(at == left.shape[1] - 1, 0.0, 1.0), edge)
        edge = jnp.where(lane == BEFORE, jnp.where(at == 0, 0.0, 1.0), edge)
    at = pl.ds(row + 1, first.shape[0])
    for k, v in enumerate((first, second, edge)):
        ref[at, k] = v.astype(BF16)


def blank(ref):
    zero = jnp.zeros((1,) + ref.shape[1:], ref.dtype)
    ref[0:1] = zero
    ref[ref.shape[0] - 1 : ref.shape[0]] = zero


def views(src, row, rows):
    return [flat(src[pl.ds(row + r, rows), k]) for r in range(3) for k in (2, 0, 1)]


def conv(src, mat, row, rows, *more):
    wide = jnp.concatenate(views(src, row, rows) + list(more), axis=1)
    return jnp.dot(wide, mat[...], preferred_element_type=F32)


def blocks_of(y, rows):
    return [y[:, k * LANES : (k + 1) * LANES].reshape(rows, -1, LANES) for k in range(2)]


def narrow(v):
    while v.shape[0] > 1:
        half = v.shape[0] // 2
        v = v[:half] + v[half:]
    return v[0]


def row_sums(first, rows, values):
    step = 4

    def add(i, carry):
        found = [values(pl.ds(first + step * i, step), k) for k in range(2)]
        return tuple(c + a + b for c, a, b in zip(carry, *found))

    shapes = jax.eval_shape(lambda: values(pl.ds(0, step), 0))
    zeros = tuple(jnp.zeros(v.shape, F32) for v in shapes)
    found = lax.fori_loop(0, rows // step, add, zeros, unroll=min(rows // step, 8))
    return [col_sum(narrow(v)) for v in found]


def local_stats(v, first, rows, count):
    count = count / GRP
    pivot = col_sum(v[first, 0] + v[first, 1]) / (2 * v.shape[2])

    def moments(at, k):
        away = v[at, k] - pivot
        return away, away * away

    total, square = row_sums(first, rows, moments)
    return pivot + total / count, square - total * (total / count)


def merge_stats(means, squares, local_count, pixel_count):
    mean = fold(col_sum(means)) / (GRP * means.shape[0])
    away = means - mean
    total = fold(col_sum(squares + (local_count / GRP) * (away * away)))
    return mean, lax.rsqrt(total / pixel_count + norm_eps)


def row_of_each(got, r):
    return got[:, r, 0, :]


def total_of(got, r):
    return col_sum(row_of_each(got, r))


def send(pay, *rows):
    for r, row in enumerate(rows):
        pay[:, r, 0, :] = jnp.broadcast_to(row, (pay.shape[0], LANES))


def send_parts(pay, first, count):
    devices = pay.shape[0]
    if devices > CH:
        for r in range(first, first + count):
            pay[CH:, r, 0, :] = jnp.zeros((devices - CH, LANES), F32)
    return pay.at[0:CH, first : first + count, 0]


def affine(table, q):
    return tile4(table[0, q : q + 1, :]), tile4(table[1, q : q + 1, :])


def diagonal_blocks(mat):
    wide = tile4(mat)
    group = group_of(wide.shape)
    return jnp.concatenate([jnp.where(group == b, wide, 0.0) for b in range(GRP)], axis=0)


def notes(ref, *rows):
    for i, row in enumerate(rows):
        ref[i : i + 1, :] = row


def taps_at(store, i):
    return store.at[FORWARD * i : FORWARD * i + (BACK if i else FORWARD)]


def image_at(store):
    return store.at[IMAGE_AT : IMAGE_AT + 3 * LANES]


def back_at(store):
    return store.at[BACK_AT : BACK_AT + BACK]


def pack_kernel(image_in, flow_in, labels_in, valid_in, out, image, flow, labels, valid, sems):
    fetched = copies(sems, (image_in, image), (flow_in, flow), (labels_in, labels), (valid_in, valid))
    images, height, _, width = image.shape
    parts = out.shape[0] // images
    wait(fetched)
    fields = [image[:, :, c, :].astype(F32) for c in range(2)]
    fields += [flow[:, :, c, :].astype(F32) for c in range(2)]
    fields += [labels[...].astype(F32), valid[...].astype(F32)]
    halves = width // 16
    shape = (width, halves * LANES)
    lane = lane_of(shape)
    column = (lane >> 7) * 16 + ((lane >> 6) & 1) * 8 + (lane & 7)
    hit = row_of(shape) == column
    which = (lane >> 3) & 7
    total = jnp.zeros((images * height, halves * LANES), F32)
    for k, v in enumerate(fields):
        x = v.reshape(images * height, width).astype(BF16)
        mat = jnp.where(hit & (which == k), 1.0, 0.0).astype(BF16)
        total = total + jnp.dot(x, mat, preferred_element_type=F32)
    for b in range(images):
        rows = total[b * height : (b + 1) * height]
        slot = jnp.concatenate([rows[:, h * LANES : (h + 1) * LANES] for h in range(halves)], axis=0).astype(BF16)
        for p in range(parts):
            out[b * parts + p] = slot


COLUMNS = ((8, None, None, -1), (0, 1, 2, 3), (4, 5, 6, 7))


def conv_matrix(taps, mats, base, back):
    out_at = group_of((CH, 2 * LANES))
    for r in range(3):
        wide = []
        for s in range(3):
            if back:
                k = taps[3 * (2 - r) + s]
                k = jnp.concatenate([k, k, k, k], axis=0).T
            else:
                k = tile4(taps[3 * r + s])
            wide.append(jnp.concatenate([k, k], axis=1))
        for d in range(3):
            for a in range(GRP):
                val = jnp.zeros((CH, 2 * LANES), F32)
                column = COLUMNS[d][a]
                if column is not None:
                    for s in range(3):
                        val = jnp.where(out_at == (column + s - 1 if back else column + 1 - s), wide[s], val)
                mats[pl.ds(base + (3 * r + d) * LANES + CH * a, CH), :] = val.astype(BF16)


def image_lanes(shape):
    at = row_of(shape)
    kind = at >> 5
    column = (at & 7) + jnp.where(kind == LEFT // 32, -SEG, jnp.where(kind == RIGHT // 32, SEG, 0))
    return (kind != 1) & ((at & 31) < 16), (at >> 3) & 1, column


def first_taps(w_first, t):
    found = [tile4(low(w_first[t][c : c + 1])) for c in range(2)]
    return [jnp.concatenate([v, v], axis=1) for v in found]


def image_matrix(w_first, r):
    shape = (LANES, 2 * LANES)
    inside, channel, here = image_lanes(shape)
    val = jnp.zeros(shape, F32)
    for s in range(3):
        for c, tap in enumerate(first_taps(w_first, 3 * r + s)):
            val = jnp.where(inside & (channel == c) & (here == group_of(shape) + s - 1), tap, val)
    return val.astype(BF16)


def prepare(w_first_in, w_convs_in, w_head_in, store, back_zero, back_two, head_mat, w_first, w_convs, w_head, mats, sems):
    wait(copies(sems, (w_first_in, w_first), (w_convs_in, w_convs), (w_head_in, w_head)))
    shape = (LANES, 2 * LANES)
    inside, channel, here = image_lanes(shape)
    val = jnp.zeros(shape, F32)
    for c, tap in enumerate(first_taps(w_first, 9)):
        val = jnp.where((row_of(shape) < 16) & (channel == c) & (here == group_of(shape)), tap, val)
    mats[BACK:FORWARD, :] = val.astype(BF16)
    for r in range(3):
        mats[IMAGE_AT + LANES * r : IMAGE_AT + LANES * (r + 1), :] = image_matrix(w_first, r)
    stored = copies(sems, (image_at(mats), image_at(store)))
    for i in range(3):
        conv_matrix(w_convs.at[i], mats, FORWARD * i, False)
        stored += copies(sems.at[1 + i :], (taps_at(mats, i), taps_at(store, i)))
    conv_matrix(w_convs.at[1], mats, BACK_AT, True)
    stored += copies(sems.at[4:], (back_at(mats), back_at(store)))
    conv_matrix(w_convs.at[2], back_two, 0, True)
    conv_matrix(w_convs.at[0], back_zero, 0, True)
    lane = lane_of((CH, LANES))
    head = jnp.zeros((CH, LANES), F32)
    diagonal = row_of((CH, CH)) == lane_of((CH, CH))
    for k in range(3):
        column = jnp.sum(jnp.where(diagonal, low(w_head[k : k + 1, 0:CH]), 0.0), axis=1, keepdims=True)
        head = jnp.where((lane >> 3) == FLOW // 8 + k, column, head)
    for y in range(SEG):
        head_mat[CH * y : CH * (y + 1), :] = jnp.where((lane & 7) == y, head, 0.0).astype(BF16)
    wait(stored)


def start_kernel(place, got, weights, sides, raw, pay, vec, taps, first_mat, sems, *, local_count, height, sources):
    fetched = copies(sems, (image_at(weights), first_mat), (taps_at(weights, 0), taps))
    rows, segments = raw.shape[0], raw.shape[2]
    off, block = place[0], place[1]
    blank(sides)

    def eight(t):
        v = got[pl.ds((block + t) * sources, sources)].astype(F32)
        v = jnp.swapaxes(v.reshape(segments // 2, 8, LANES), 0, 1)
        near = lane_of(v.shape) < 64
        v = jnp.concatenate([jnp.where(near, v, 0.0), jnp.where(near, pltpu.roll(v, 64, axis=2), 0.0)], axis=1)
        pixels = jnp.where(lane_of(v.shape) < 16, v, 0.0)
        left, right = beside(pixels, pixels)
        v = v + pltpu.roll(left, LEFT, axis=2) + pltpu.roll(right, RIGHT, axis=2)
        sides[pl.ds(8 * t + 1, 8)] = v.astype(BF16)

    loop(rows // 8, eight)
    wait(fetched[:1])
    y = None
    for r in range(3):
        part = jnp.dot(flat(sides[r : r + rows]), first_mat[LANES * r : LANES * (r + 1)], preferred_element_type=F32)
        y = part if y is None else y + part
    raw[:, 0], raw[:, 1] = blocks_of(y, rows)
    mean, square = local_stats(raw, off, height, local_count)
    mask = jnp.zeros(sides.shape[1:], F32)
    for i in range(height):
        mask = mask + sides[off + 1 + i].astype(F32)
    lane = lane_of(mask.shape)
    count = jnp.sum(jnp.where((lane >= MASK) & (lane < MASK + 8), mask, 0.0))
    send(pay, mean, square)
    notes(vec, jnp.full((1, LANES), count, F32))
    wait(fetched[1:])


def first_kernel(place, got, raw, sides, table, taps, summed, pay, vec, fields, lows, hidden, xhat, sems, *, spots, local_count, pixel_count, height):
    mean, inverse = merge_stats(row_of_each(got, 0), row_of_each(got, 1), local_count, pixel_count)
    notes(vec, inverse)
    gain, bias = affine(table, 0)
    rows = raw.shape[0]

    def norm_rows(i):
        at = pl.ds(4 * i, 4)
        out = []
        for k in range(2):
            x = (raw[at, k] - mean) * inverse
            xhat[at, k] = x
            n = x * gain + bias
            out.append(n * sig_of(n))
        put_low(hidden, 4 * i, *out)

    blank(hidden)
    loop(rows // 4, norm_rows)
    stored = copies(sems, (xhat, spots(fields, "xhat_zero")), (hidden, spots(lows, "hidden_one")))

    @pl.when(place[0] >= 0)
    def _():
        y = conv(hidden, taps, 0, rows, flat(sides[1 : rows + 1]))
        summed[:, 0], summed[:, 1] = blocks_of(y, rows)

    send(pay, *local_stats(summed, place[0], height, local_count))
    wait(stored)


def pool_kernel(place, got, summed, count_in, table, weights, fields_in, lows_in, raw, pay, vec, merged, taps_next, fields, lows, xhat, shared, taps, sems, *, spots, local_count, pixel_count, height):
    fetched = copies(sems, (taps_at(weights, 1), taps), (taps_at(weights, 2), taps_next))
    mean, inverse = merge_stats(row_of_each(got, 0), row_of_each(got, 1), local_count, pixel_count)
    gain, bias = affine(table, 1)
    rows, segments = summed.shape[0], summed.shape[2]
    off = place[0]

    step = 4

    def some(i, carry):
        at = pl.ds(step * i, step)
        pairs = (step // 2, 2, segments, LANES)
        outs, sums = [], [jnp.zeros((step // 2 * segments, LANES), F32) for _ in range(3)]
        for k in range(2):
            x = (summed[at, k] - mean) * inverse
            n = x * gain + bias
            sig = sig_of(n)
            e = (n * sig).reshape(pairs)
            top = flat(jnp.maximum(e[:, 0], e[:, 1]))
            top = jnp.maximum(top, partner(top))
            wide_top = top.reshape(step // 2, 1, segments, LANES)
            exps = jnp.exp(e - wide_top)
            whole = flat(exps[:, 0] + exps[:, 1])
            whole = whole + partner(whole)
            pooled = top + jnp.log(whole)
            outs.append((e + pooled.reshape(wide_top.shape)).reshape(step, segments, LANES))
            share = exps * (1.0 / whole).reshape(wide_top.shape) * slope(n, sig).reshape(pairs)
            share_x = share * x.reshape(pairs)
            xhat[at, k] = x
            shared[at, k] = share.reshape(step, segments, LANES)
            sums[0] = sums[0] + pooled
            sums[1] = sums[1] + flat(share[:, 0] + share[:, 1])
            sums[2] = sums[2] + flat(share_x[:, 0] + share_x[:, 1])
        put_low(merged, step * i, *outs)
        mine = (step * i >= off) & (step * i < off + height)
        keep = jnp.where(mine, 1.0, 0.0)
        return tuple(a + keep * b for a, b in zip(carry, sums))

    blank(merged)
    zero = jnp.zeros((step // 2 * segments, LANES), F32)
    sums = lax.fori_loop(0, rows // step, some, (zero, zero, zero), unroll=min(rows // step, 5))
    pool_sum, share_sum, share_x = [fold(col_sum(v)) for v in sums]
    stored = copies(
        sems.at[2:],
        (xhat, spots(fields, "xhat_one")),
        (shared, spots(fields, "shared")),
        (merged, spots(lows, "merged")),
    )
    wait(fetched)
    raw[:, 0], raw[:, 1] = blocks_of(conv(merged, taps, 0, rows), rows)
    mean, square = local_stats(raw, place[0], height, local_count)
    send(pay, mean, square, groups(0.5 * pool_sum, share_sum, share_x, count_in[0:1]))
    notes(vec, inverse)
    wait(stored)


def by_image(v, parts):
    devices = v.shape[0]
    step = 1
    while step < parts:
        upper = (row_of(v.shape) // step) % 2 == 1
        v = v + jnp.where(upper, pltpu.roll(v, step, axis=0), pltpu.roll(v, devices - step, axis=0))
        step *= 2
    return v


def wide_dot(a, b, dims=(((1,), (0,)), ((), ()))):
    (a_high, a_low), (b_high, b_low) = [[v.astype(BF16) for v in in_parts(x, 2)] for x in (a, b)]
    axis_a, axis_b = dims[0][0][0], dims[0][1][0]
    left = jnp.concatenate([a_high, a_high, a_low], axis=axis_a)
    right = jnp.concatenate([b_high, b_low, b_high], axis=axis_b)
    return lax.dot_general(left, right, dims, preferred_element_type=F32)


def in_parts(v, count):
    out = []
    for _ in range(count):
        out.append(low(v))
        v = v - out[-1]
    return out


def mine_of(v, me):
    return col_sum(jnp.where(row_of(v.shape) == me, v, 0.0))


def style_kernel(place, got, raw, merged, table, w_style, w_convs_in, taps, lows_in, resid, pay, vec, style_out, xhat, lows, hidden, slopes, w_conv, sems, *, spots, local_count, pixel_count, pool_cells, height, parts):
    fetched = copies(sems, (w_convs_in.at[2], w_conv))
    style = by_image(spread(row_of_each(got, 2), 0), parts) / pool_cells
    style_out[...] = style
    one, two = [
        wide_dot(style, diagonal_blocks(w_style[i])) for i in range(2)
    ]
    mean, inverse = merge_stats(row_of_each(got, 0) + one, row_of_each(got, 1), local_count, pixel_count)
    notes(vec, inverse)
    gain, bias = affine(table, 2)
    rows, kept = raw.shape[0], resid.shape[0]
    off, skipped, mine = place[0], place[3], place[4]
    me = place[2]
    shift = mine_of(one, me) - mean
    two = mine_of(two, me)

    def norm_rows(i):
        at = pl.ds(4 * i, 4)
        out = []
        for k in range(2):
            x = (raw[at, k] + shift) * inverse
            xhat[at, k] = x
            n = x * gain + bias
            sig = sig_of(n)
            slopes[at, k] = slope(n, sig)
            out.append(n * sig)
        put_low(hidden, 4 * i, *out)

    blank(hidden)
    loop(rows // 4, norm_rows)
    stored = copies(sems.at[1:], (hidden, spots(lows, "hidden_three")))

    @pl.when(place[0] >= 0)
    def _():
        for k, y in enumerate(blocks_of(conv(hidden, taps, skipped, kept), kept)):
            resid[:, k] = y + two + merged[pl.ds(skipped + 1, kept), k].astype(F32)

    wait(fetched + stored)
    hidden[kept + 1 : kept + 2] = jnp.zeros((1,) + hidden.shape[1:], BF16)
    centre = fold(col_sum(resid[mine, 0] + resid[mine, 1])) / (SEG * raw.shape[2])
    at = pl.ds(off, height)
    probe = [slopes[at, k] for k in range(2)]
    probe += [slopes[at, k] * xhat[at, k] for k in range(2)]
    probe = jnp.concatenate([flat(v).astype(BF16) for v in probe], axis=1)

    def centred(i):
        at = pl.ds(4 * i, 4)
        put_low(hidden, 4 * i, resid[at, 0] - centre, resid[at, 1] - centre, True)

    loop(kept // 4, centred)
    links = norm_links(hidden, probe, mine, height, w_conv, centre)
    send(pay, *local_stats(resid, mine, height, local_count))
    send_parts(pay, 2, 1)[:, 0, :] = links


def norm_links(field, probe, first, rows, taps, centre):
    wide = jnp.concatenate(views(field, first, rows), axis=1)
    found = lax.dot_general(probe, wide, (((0,), (0,)), ((), ())), preferred_element_type=F32)
    group = group_of((CH, LANES))
    out = []
    for half in range(2):

        def piece(y, chunk):
            at = 2 * LANES * half + CH * y
            return found[at : at + CH, chunk * LANES : (chunk + 1) * LANES]

        plain = jnp.zeros((CH, LANES), F32)
        moved = jnp.zeros((CH, LANES), F32)
        for r in range(3):
            first_edge, last_edge = piece(0, 3 * r), piece(SEG - 1, 3 * r)
            edge = first_edge + last_edge
            for y in range(1, SEG - 1):
                edge = edge + piece(y, 3 * r)
            inside = edge[:, ROW : ROW + 1]
            counts = (
                inside + (first_edge[:, BEFORE : BEFORE + 1] - first_edge[:, ROW : ROW + 1]),
                inside,
                inside + (last_edge[:, AFTER : AFTER + 1] - last_edge[:, ROW : ROW + 1]),
            )
            for c in range(3):
                tap = tile4(low(taps[3 * (2 - r) + 2 - c]))
                val = jnp.zeros((CH, LANES), F32)
                for y in range(SEG):
                    d, a = spot_of(y + c - 1)
                    val = val + jnp.where(group == a, piece(y, 3 * r + d), 0.0)
                plain = plain + tap * counts[c]
                moved = moved + tap * val
        out += [plain, fold(moved) + centre * plain]
    return groups(*out)


def spot_of(x):
    if x < 0:
        return 0, 3
    if x == SEG:
        return 0, 0
    return 1 + x // GRP, x % GRP


def ahead_kernel(place, pay, sides, fields, lows, out, sums, below_x, xhat, shared, field, sems, *, spots, local_count):
    off = place[0]
    height = xhat.shape[0]
    own = pl.ds(off, height)
    fetched = copies(
        sems,
        (spots(fields, "xhat_zero").at[own], below_x),
        (spots(fields, "xhat_one").at[own], xhat),
        (spots(fields, "shared").at[own], shared),
        (spots(lows, "hidden_one").at[pl.ds(off, height + 2)], field),
    )
    wait(fetched[:1])
    at = pl.ds(0, height)
    low_x = jnp.concatenate([own_lanes(below_x, at), jnp.ones((height * field.shape[2], LANES), BF16)], axis=1)
    entries, alone = [], zero_row()
    lane = lane_of((1, LANES))
    for r in range(3):
        for tap, bare in pixel_taps(sides, off + r, height, low_x, (-1, 0, 1), True):
            for v, b in zip(tap, bare):
                alone = jnp.where(lane == ALONE + len(entries), b, alone)
                entries.append(v)
    wait(fetched[1:])
    centres = [fold(v) / local_count for v in row_sums(0, height, lambda at, k: (xhat[at, k], shared[at, k]))]
    probe = [flat(v[at, k] - c).astype(BF16) for v, c in zip((xhat, shared), centres) for k in range(2)]
    wide = jnp.concatenate(views(field, 0, height), axis=1)
    found = lax.dot_general(
        jnp.concatenate(probe, axis=1), wide, (((0,), (0,)), ((), ())), preferred_element_type=F32
    )
    ones = jnp.ones((8, wide.shape[0]), BF16)
    plain = jnp.dot(ones, wide, preferred_element_type=F32)[0:1]
    group = group_of((1, LANES))
    hidden = []
    for r in range(3):
        for s in range(3):
            val = zero_row()
            for y in range(SEG):
                d, a = spot_of(y + s - 1)
                spot = (3 * r + d) * LANES
                val = val + jnp.where(group == a, plain[:, spot : spot + LANES], 0.0)
            hidden.append(fold(val))
    packed = [groups(*hidden[0:4]), groups(*hidden[4:8]), hidden[8]]
    all_hidden = jnp.concatenate(packed, axis=0)
    last = [
        put_taps(
            found[2 * LANES * k : 2 * LANES * (k + 1)], out.at[:, 2 * k + 1 : 2 * k + 3, 0], (centres[k], all_hidden)
        )
        for k in range(2)
    ]
    entries += hidden
    entries.append(jnp.zeros((CH - len(entries), LANES), F32))
    out[:, 0, 0, :] = groups(jnp.concatenate(entries, axis=0), *last, jnp.zeros((CH, LANES), F32))
    notes(sums, *packed, alone)


def head_kernel(place, got, got_style, resid, sides, head_mat, w_head, below_x, ahead, image_sums, table, back, grad, xhat, pay, vec, decoded, slopes, grad_low, *, local_count, pixel_count, height):
    mean, inverse = merge_stats(row_of_each(got, 0), row_of_each(got, 1), local_count, pixel_count)
    notes(vec, inverse, mean)
    gain, bias = affine(table, 3)
    rows, segments = resid.shape[0], resid.shape[2]
    all_off, skipped, off = place[0], place[3], place[4]

    def norm_rows(i):
        at = pl.ds(4 * i, 4)
        for k in range(2):
            x = (resid[at, k] - mean) * inverse
            n = x * gain + bias
            s = sig_of(n)
            xhat[at, k] = x
            slopes[at, k] = slope(n, s)
            decoded[at, k] = (n * s).astype(BF16)

    loop(rows // 4, norm_rows, 10)
    head = head_mat[...]
    wide = jnp.concatenate([flat(decoded[:, 0]), flat(decoded[:, 1])], axis=1)
    bias_row = zero_row()
    for k in range(3):
        mine = (lane_of((1, LANES)) >> 3) == FLOW // 8 + k
        bias_row = jnp.where(mine, low(w_head[k : k + 1, CH : CH + 1]), bias_row)
    out = jnp.dot(wide, head, preferred_element_type=F32) + bias_row
    given = flat(sides[pl.ds(skipped + 1, rows)]).astype(F32)
    lane = lane_of(given.shape)
    is_flow = lane < LABEL
    near = [pltpu.roll(given, LANES - MASK + first, axis=1) for first in (FLOW, FLOW + 8, LABEL)]
    mask = jnp.where(lane < FLOW + 8, near[0], jnp.where(is_flow, near[1], near[2]))
    mask = jnp.where((lane >= FLOW) & (lane < LABEL + 8), mask, 0.0)
    count = jnp.sum(got_style[:, 2, 0, 3 * CH : 3 * CH + 1])
    diff = out - given / flow_scale
    hinge = jnp.maximum(out, 0.0) + jnp.log1p(jnp.exp(-jnp.abs(out)))
    loss = mask * jnp.where(is_flow, diff * diff, hinge - given * out)
    grad_out = (mask * jnp.where(is_flow, 2.0 * diff, sig_of(out) - given) / count).astype(BF16)
    at_row = lax.broadcasted_iota(jnp.int32, loss.shape, 0)
    inside = (at_row >= off * segments) & (at_row < (off + height) * segments)
    loss_sum = jnp.sum(jnp.where(inside, loss, 0.0))
    mine_out = jnp.where(inside, grad_out.astype(F32), 0.0).astype(BF16)
    outs = col_sum(mine_out.astype(F32))
    found = lax.dot_general(mine_out, wide, (((0,), (0,)), ((), ())), preferred_element_type=F32)
    shape = found.shape
    found = jnp.where((row_of(shape) & 7) == group_of(shape), found, 0.0)
    whole = [col_sum(found[FLOW + 8 * k : FLOW + 8 * k + 8]) for k in range(3)]
    whole = [fold(v[:, 0:LANES] + v[:, LANES:]) for v in whole]
    row = groups(*whole, zero_row())
    lane = lane_of((1, LANES))
    for k in range(3):
        row = jnp.where(lane == 3 * CH + k, jnp.sum(jnp.where((lane >> 3) == FLOW // 8 + k, outs, 0.0)), row)
    row = jnp.where(lane == 3 * CH + 3, loss_sum, row)
    y = lax.dot_general(grad_out, head, (((1,), (1,)), ((), ())), preferred_element_type=F32)
    for k, g in enumerate(blocks_of(y, rows)):
        grad[:, k] = g * slopes[:, k]
    factor = gain * inverse
    back_rows(grad_low, rows, lambda at, k: factor * grad[at, k], 10)
    shift_sum, scale_sum = own_sums(grad, xhat, off, height)
    y = conv(grad_low, back, off, height)
    slopes[0:height, 0], slopes[0:height, 1] = blocks_of(y, height)
    gain, bias = affine(table, 2)

    def links(at, k):
        x = below_x[pl.ds(all_off + at.start, at.size), k]
        g = slopes[at, k] * slope_at(x, gain, bias)
        return g, g * x

    below = [fold(v) for v in row_sums(0, height, links)]
    send(pay, groups(shift_sum, scale_sum, *below), row + image_sums[3:4], total_of(got, 2))
    send_parts(pay, 3, 5)
    pay[0:CH, 3:8] = ahead[...]


def own_sums(grad, xhat, first, rows):
    def both(at, k):
        g = grad[at, k]
        return g, g * xhat[at, k]

    return [fold(v) for v in row_sums(first, rows, both)]


def back_sums(got, pixel_count):
    whole = col_sum(got)
    return spread(whole, 0) / pixel_count, spread(whole, 1) / pixel_count


def low_sum(grad_low, first, rows):
    return fold(row_sums(first + 1, rows, lambda at, k: (grad_low[at, k].astype(F32),))[0])


def norm_back(grad, xhat, factor, shift, scale):
    return factor * (grad - (shift + xhat * scale))


def back_rows(grad_low, rows, value, unroll=5):
    def some(i):
        put_low(grad_low, 4 * i, *[value(pl.ds(4 * i, 4), k) for k in range(2)])

    blank(grad_low)
    loop(rows // 4, some, unroll)


def own_lanes(grad, at):
    return jnp.concatenate([flat(grad[at, k]).astype(BF16) for k in range(2)], axis=1)


def tap_sums(field, grad, first, rows, out, more=None):
    wide = jnp.concatenate(views(field, first, rows), axis=1)
    found = lax.dot_general(grad, wide, (((0,), (0,)), ((), ())), preferred_element_type=F32)
    return put_taps(found, out, more)


def put_taps(found, out, more=None):
    group = group_of((CH, LANES))
    taps = []
    for r in range(3):
        for s in range(3):
            val = jnp.zeros((CH, LANES), F32)
            for y in range(SEG):
                d, a = spot_of(y + s - 1)
                spot = (3 * r + d) * LANES
                val = val + jnp.where(group == a, found[CH * y : CH * y + CH, spot : spot + LANES], 0.0)
            taps.append(fold(val))
    for q in range(3):
        val = taps[4 * q]
        for b in range(1, min(4, 9 - 4 * q)):
            val = jnp.where(group == b, taps[4 * q + b], val)
        if more is not None:
            centre, sums = more
            val = val + column_of(centre) * sums[q : q + 1]
        if q == 2:
            return val
        out[:, q, :] = val


def column_of(v):
    shape = (CH, LANES)
    return jnp.sum(jnp.where(row_of(shape) == lane_of(shape), v, 0.0), axis=1, keepdims=True)


def at_lane(v, k):
    return jnp.sum(jnp.where(lane_of(v.shape) == k, v, 0.0), axis=1, keepdims=True)


def decoder_back_kernel(place, got, grad, xhat, mid_x, vec, vec_two, sums, table, back_two, weights, fields, lows, below, below_x, shared, pay, more, kept_grad, mid, low_two, low_one, field_two, field_one, field_zero, back_one, sems, *, spots, local_count, pixel_count):
    all_off, skipped, off = place[0], place[3], place[4]
    height = field_two.shape[0] - 2
    far_rows, near_rows = pl.ds(skipped, grad.shape[0]), pl.ds(all_off, height + 2)
    fetched = copies(
        sems,
        (back_at(weights), back_one),
        (spots(fields, "xhat_one").at[far_rows], below_x),
        (spots(fields, "shared").at[far_rows], shared),
        (spots(lows, "hidden_three").at[near_rows], field_two),
        (spots(lows, "merged").at[near_rows], field_one),
        (spots(lows, "hidden_one").at[near_rows], field_zero),
    )
    devices = got.shape[0]
    rows = grad.shape[0]
    total = total_of(got, 0)
    shift, scale = spread(total, 0) / pixel_count, spread(total, 1) / pixel_count
    inverse, mean = vec[0:1], vec[1:2]
    factor = affine(table, 3)[0] * inverse
    slant = scale * inverse
    held, carried = factor * (shift - slant * mean), factor * slant
    links = got[0:CH, 2, 0, :] * groups(held, carried, held, carried)
    group = group_of(links.shape)
    mine = (lane_of(links.shape) & 31) == row_of(links.shape)

    def across(pick):
        column = jnp.sum(jnp.where(pick, links, 0.0), axis=1, keepdims=True)
        return col_sum(jnp.where(mine, column, 0.0))

    shift_two = spread(total, 2) - across(group < 2)
    scale_two = spread(total, 3) - across(group >= 2)
    entry = total_of(got, 3)
    notes(more, scale_two, shift_two, total_of(got, 4), total_of(got, 5), spread(entry, 1))

    def value(at, k):
        g = norm_back(grad[at, k], xhat[at, k], factor, shift, scale)
        kept_grad[at, k] = g
        return g

    back_rows(low_two, rows, value)

    @pl.when(place[0] >= 0)
    def _():
        mid[:, 0], mid[:, 1] = blocks_of(conv(low_two, back_two, 0, rows), rows)

    gain, bias = affine(table, 2)
    factor = gain * vec_two[0:1]
    shift, scale = shift_two / pixel_count, scale_two / pixel_count

    def value_two(at, k):
        x = mid_x[pl.ds(skipped + at.start, at.size), k]
        return norm_back(mid[at, k] * slope_at(x, gain, bias), x, factor, shift, scale)

    back_rows(low_one, rows, value_two)
    wait(fetched)
    sum_two = low_sum(low_two, off, height)
    sum_one = low_sum(low_one, off, height)
    y = conv(low_one, back_one, 0, rows)
    gain, bias = affine(table, 1)
    for k, y in enumerate(blocks_of(y, rows)):
        g = (y + kept_grad[:, k]).reshape(rows // 2, 2, -1, LANES)
        both = flat(g[:, 0] + g[:, 1])
        both = (both + partner(both)).reshape(rows // 2, 1, -1, LANES)
        g = g * slope_at(below_x[:, k], gain, bias).reshape(g.shape) + both * shared[:, k].reshape(g.shape)
        below[:, k] = g.reshape(rows, -1, LANES)
    shift_sum, scale_sum = own_sums(below, below_x, off, height)
    send(pay, groups(shift_sum, scale_sum, sum_one, sum_two))
    entry = spread(entry, 0)
    pay[:, 1, 0, :] = jnp.broadcast_to(entry, (devices, LANES))
    at = pl.ds(off + 1, height)
    last_two = tap_sums(field_two, own_lanes(low_two, at), 0, height, send_parts(pay, 2, 2))
    last_one = tap_sums(field_one, own_lanes(low_one, at), 0, height, send_parts(pay, 4, 2))
    centre = shift_sum / local_count
    at = pl.ds(off, height)
    grad = jnp.concatenate([flat(below[at, k] - centre).astype(BF16) for k in range(2)], axis=1)
    last_zero = tap_sums(field_zero, grad, 0, height, send_parts(pay, 6, 2), (centre, sums))
    pay[0:CH, 1, 0, :] = groups(last_two, last_one, last_zero, jnp.broadcast_to(entry, (CH, LANES)))


def summed_kernel(place, got, got_style, got_head, grad, xhat, shared, vec, more_two, table, w_style, sides, back, fields, pay, more, below, below_x, grad_low, sems, *, spots, pixel_count, pool_cells, parts):
    off, mine = place[0], place[4]
    height = below.shape[0]
    fetched = copies(sems, (spots(fields, "xhat_zero").at[pl.ds(off, height)], below_x))
    devices = got.shape[0]
    rows = grad.shape[0]
    dims = (((1,), (1,)), ((), ()))
    first = row_of_each(got, 0)
    each = wide_dot(spread(first, 2), diagonal_blocks(w_style[0]), dims) + wide_dot(
        spread(first, 3), diagonal_blocks(w_style[1]), dims
    )
    each = each / pool_cells
    total = col_sum(first)
    shift = spread(total, 0) + col_sum(each * by_image(spread(row_of_each(got_style, 2), 1), parts))
    scale = spread(total, 1) + col_sum(each * by_image(spread(row_of_each(got_style, 2), 2), parts))
    style_grad = col_sum(jnp.where(row_of(each.shape) // parts == place[2] // parts, each, 0.0))
    factor = affine(table, 1)[0] * vec[0:1]
    shift_mean, scale_mean = shift / pixel_count, scale / pixel_count
    def value(at, k):
        return norm_back(grad[at, k] + shared[at, k] * style_grad, xhat[at, k], factor, shift_mean, scale_mean)

    back_rows(grad_low, rows, value)
    gain, bias = affine(table, 0)
    wait(fetched)
    for k, y in enumerate(blocks_of(conv(grad_low, back, mine, height), height)):
        below[:, k] = y * slope_at(below_x[:, k], gain, bias)
    me = place[2]
    weights = at_lane(by_image(each, parts), me)
    hidden = spread(got[0:CH, 1, 0, :], 3)
    hidden = [groups(*[hidden[18 + t : 19 + t] for t in range(4 * q, min(4 * q + 4, 9))]) for q in range(3)]
    last = total_of(got, 1)
    direct = [total_of(got, 6), total_of(got, 7), spread(last, 2)]
    shares = [row_of_each(got_head, 6), row_of_each(got_head, 7), spread(row_of_each(got_head, 3), 2)]
    shard = []
    for q in range(3):
        val = direct[q] + col_sum(weights * shares[q])
        val = val - at_lane(shift_mean, me) * hidden[q] - at_lane(scale_mean, me) * more_two[2 + q : 3 + q]
        shard.append(at_lane(factor, me) * val)
    at = pl.ds(mine + 1, height)
    side = pixel_taps(sides, off + 1, height, own_lanes(grad_low, at), (0,))[0]
    low_below = own_lanes(below, pl.ds(0, height))
    taps = []
    for r in range(3):
        for tap in pixel_taps(sides, off + r, height, low_below, (-1, 0, 1)):
            taps.extend(tap)
    taps = [shard[2]] + taps + side
    send(
        pay,
        groups(*own_sums(below, below_x, 0, height), spread(last, 0), spread(last, 1)),
        *[total_of(got, r) for r in range(2, 6)],
        *shard[0:2],
        *[groups(*(taps[4 * q : 4 * q + 4] + [zero_row()])[0:4]) for q in range(6)],
    )
    notes(more, scale, shift)


def pixel_taps(sides, row, rows, grad, shift, alone=False):
    x = flat(sides[pl.ds(row, rows)])
    found = lax.dot_general(x, grad, (((0,), (0,)), ((), ())), preferred_element_type=F32)
    inside, channel, column = image_lanes((LANES, 2 * LANES))
    here = column - group_of((LANES, 2 * LANES))
    out = []
    for s in shift:
        both, bare = [], []
        for c in range(2):
            v = col_sum(jnp.where(inside & (channel == c) & (here == s), found[:, 0 : 2 * LANES], 0.0))
            both.append(fold(v[:, 0:LANES] + v[:, LANES:]))
            if alone:
                cut = slice(0, LANES)
                hit = (inside & (channel == c) & (column >= s) & (column < s + SEG))[:, cut]
                bare.append(col_sum(jnp.where(hit, found[:, 2 * LANES :], 0.0)))
        out.append((both, bare) if alone else both)
    return out


def adamw(master, moment, square, grad, rate):
    new_moment = beta_one * moment + (1.0 - beta_one) * grad
    new_square = beta_two * square + (1.0 - beta_two) * grad * grad
    moment_hat = new_moment / (1.0 - beta_one**STEP)
    square_hat = new_square / (1.0 - beta_two**STEP)
    new_master = master - rate * (moment_hat / (jnp.sqrt(square_hat) + adam_eps) + weight_decay * master)
    return new_master, new_moment, new_square


def put(at, refs, grad, rate, outs):
    found = adamw(*[ref[at] for ref in refs], grad, rate)
    for out, value in zip(outs, found + (found[0].astype(BF16),)):
        out[at] = value


def update_early(
    got_one_back, got_head, got_style, pay, style, w_style, w_head, m_style, m_head, s_style, s_head,
    loss_out, count_out, style_master, style_moment, style_square, head_master, head_moment, head_square, head_copy,
):
    count_out[0, 0] = jnp.sum(got_style[:, 2, 0, 3 * CH : 3 * CH + 1])
    loss_out[0, 0] = jnp.sum(got_head[:, 1, 0, 99:100])
    dims = (((0,), (0,)), ((), ()))
    for i in range(2):
        sums = spread(row_of_each(got_one_back, 0), 2 + i)
        grad = lax.dot_general(style[...], sums, dims, precision=highest, preferred_element_type=F32)
        put(i, (w_style, m_style, s_style), grad[0:CH, 0:CH], rate_table[2], (style_master, style_moment, style_square))

    head = total_of(got_head, 1)
    lane = lane_of((1, LANES))
    rows = []
    for k in range(3):
        last = jnp.sum(jnp.where(lane == 3 * CH + k, head, 0.0), axis=1, keepdims=True)
        rows.append(jnp.where(lane < CH, spread(head, k), last))
    grad = jnp.concatenate(rows, axis=0)[:, 0 : CH + 1]
    put(slice(None), (w_head, m_head, s_head), grad, rate_table[3], (head_master, head_moment, head_square, head_copy))


def update_late(
    got, got_one_back, got_head, more, more_two, vec, w_first, w_convs, table, m_first, m_convs, m_norms, s_first, s_convs, s_norms,
    first_master, first_moment, first_square, first_copy,
    convs_master, convs_moment, convs_square, convs_copy,
    norms_master, norms_moment, norms_square, *, pixel_count
):
    refs = (w_convs, m_convs, s_convs)
    outs = (convs_master, convs_moment, convs_square, convs_copy)
    packs = [[got[0:CH, k, 0, :].T for k in ks] for ks in ((5, 6, 7), (3, 4, 0), (1, 2, 0))]
    for i, pack in enumerate(packs):
        for t in range(9):
            b = t % 4 if t < 8 else (0, 3, 2)[i]
            put((i, t), refs, pack[t // 4][CH * b : CH * b + CH], rate_table[1], outs)

    zero_sums = total_of(got, 0)
    totals = [total_of(got, r) for r in range(7, 13)]
    shift, scale = spread(zero_sums, 0), spread(zero_sums, 1)
    factor = affine(table, 0)[0] * vec[0:1]
    by_x = spread(got_one_back[0:CH, 1, 0, :], 3)
    alone = total_of(got_head, 1)
    refs = (w_first, m_first, s_first)
    outs = (first_master, first_moment, first_square, first_copy)
    for t in range(10):
        pair = []
        for e in (2 * t, 2 * t + 1):
            k, b = divmod(1 + e, 4)
            v = spread(totals[k], b)
            if t < 9:
                v = factor * (v - (at_lane(alone, ALONE + e) * shift + by_x[e : e + 1] * scale) / pixel_count)
            pair.append(v[:, 0:CH])
        put(t, refs, jnp.concatenate(pair, axis=0), rate_table[0], outs)

    three_sums = total_of(got_head, 0)
    scales = [scale, more[0:1], more_two[0:1], spread(three_sums, 1)]
    shifts = [shift, more[1:2], more_two[1:2], spread(three_sums, 0)]
    for i, rows in enumerate((scales, shifts)):
        grad = jnp.concatenate(rows, axis=0)[:, 0:CH]
        put(i, (table, m_norms, s_norms), grad, rate_table[4], (norms_master, norms_moment, norms_square))


def far(x):
    return ("far", x)


def call(kernel, outs, *operands, scalars=0, scratch=(), sems=0, scalar_outs=(), aliases=None, limit=VMEM_LIMIT, name):
    smem = pl.BlockSpec(memory_space=pltpu.SMEM)
    vmem = pl.BlockSpec(memory_space=pltpu.VMEM)
    hbm = pl.BlockSpec(memory_space=pltpu.HBM)
    is_far = lambda x: isinstance(x, tuple) and x[0] == "far"
    in_specs = [smem if i < scalars else hbm if is_far(x) else vmem for i, x in enumerate(operands)]
    out_specs = [smem if i in scalar_outs else hbm if is_far(x) else vmem for i, x in enumerate(outs)]
    plain = lambda x: x[1] if is_far(x) else x
    shapes = [pltpu.VMEM(shape, dtype) for shape, dtype in scratch]
    if sems:
        shapes.append(pltpu.SemaphoreType.DMA((sems,)))
    return pl.pallas_call(
        kernel,
        out_shape=[jax.ShapeDtypeStruct(*plain(x)) for x in outs],
        in_specs=in_specs,
        out_specs=out_specs,
        scratch_shapes=shapes,
        input_output_aliases=aliases or {},
        compiler_params=pltpu.CompilerParams(vmem_limit_bytes=limit),
        name=name,
    )(*[plain(x) for x in operands])


def exchange(pay):
    return lax.all_to_all(pay, ("row", "col"), 0, 0)


def local(
    image_batch, valid_mask, flow_target, cell_labels,
    w_first, w_convs, w_style, w_head, batch_norm_table,
    mom_first, mom_convs, mom_style, mom_head, mom_norms,
    sqr_first, sqr_convs, sqr_style, sqr_head, sqr_norms,
):
    images, block_rows, block_cols, _ = image_batch.shape
    row_count, col_count = lax.axis_size("row"), lax.axis_size("col")
    devices = row_count * col_count
    parts = devices // images
    image_rows, image_cols = row_count * block_rows, col_count * block_cols
    assert devices == parts * images and block_rows == RIM and block_cols == 2 * block_rows * 2
    assert image_rows % (parts * RIM) == 0 and devices >= CH
    height = image_rows // parts
    rows = min(image_rows, height + RIM * min(2, parts - 1))
    segments = image_cols // SEG
    local_count = float(height * image_cols)
    pixel_count = local_count * devices
    pool_cells = float(image_rows * image_cols // 4)
    part = functools.partial
    counts = dict(local_count=local_count, pixel_count=pixel_count, height=height)
    styled = dict(pool_cells=pool_cells, parts=parts)

    me = lax.axis_index("row") * col_count + lax.axis_index("col")
    first_row = (me % parts) * height
    start = jnp.clip(first_row - RIM, 0, image_rows - rows)
    off = first_row - start
    back_rim = RIM // 2
    rows_back = min(rows, height + back_rim * min(2, parts - 1))
    skipped = jnp.clip(off - back_rim, 0, rows - rows_back)
    place = jnp.stack([off, start // block_rows, me, skipped, off - skipped]).astype(jnp.int32)

    field = ((rows, 2, segments, LANES), F32)
    own_field = ((height,) + field[0][1:], F32)
    back_field = ((rows_back,) + field[0][1:], F32)
    low_field = ((rows + 2, 3, segments, LANES), BF16)
    own_low = ((height + 2,) + low_field[0][1:], BF16)
    back_low = ((rows_back + 2,) + low_field[0][1:], BF16)
    vec = ((8, LANES), F32)

    def payload(count):
        return ((devices, count, 1, LANES), F32)

    nine = ((BACK, 2 * LANES), BF16)
    ten = ((FORWARD, 2 * LANES), BF16)

    places = {
        name: i * count
        for count, names in (
            (rows, ("xhat_zero", "xhat_one", "shared")),
            (rows + 2, ("hidden_one", "hidden_three", "merged")),
        )
        for i, name in enumerate(names)
    }

    def spots(store, name):
        count = rows if name[0] in "xs" else rows + 2
        return store.at[places[name] : places[name] + count]

    def store_of(like):
        shape, dtype = like
        row_bytes = shape[1] * segments * LANES * jnp.dtype(dtype).itemsize
        return far(((-(-STORE_BYTES // row_bytes),) + shape[1:], dtype))

    inputs = (
        jnp.transpose(image_batch, (0, 1, 3, 2)), jnp.transpose(flow_target, (0, 1, 3, 2)), cell_labels, valid_mask
    )
    (pay,) = call(
        pack_kernel,
        [((devices, 16, LANES), BF16)],
        *[far(v) for v in inputs],
        scratch=[(v.shape, v.dtype) for v in inputs], sems=4, limit=WHOLE_VMEM, name="pack",
    )
    got_inputs = exchange(pay)
    head_rows = w_head.T
    weights, back_zero, back_two, head_mat = call(
        prepare,
        [far(((STORE_BYTES // (4 * LANES), 2 * LANES), BF16)), nine, nine, ((2 * LANES, LANES), BF16)],
        far(w_first), far(w_convs), far(head_rows),
        scratch=[
            (w_first.shape, F32), (w_convs.shape, F32), (head_rows.shape, F32), ((BACK_AT + BACK, 2 * LANES), BF16)
        ],
        sems=5, limit=WHOLE_VMEM, name="prepare",
    )

    sides, raw, pay, count, taps = call(
        part(start_kernel, local_count=local_count, height=height, sources=col_count),
        [((rows + 2, segments, LANES), BF16), field, payload(2), vec, ten],
        place, got_inputs, far(weights),
        scalars=1, scratch=[((3 * LANES, 2 * LANES), BF16)], sems=2, name="image_conv",
    )
    got_zero = exchange(pay)
    summed, pay, inv_zero, fields, lows = call(
        part(first_kernel, spots=spots, **counts),
        [field, payload(2), vec, store_of(field), store_of(low_field)],
        place, got_zero, raw, sides, batch_norm_table, taps,
        scalars=1, scratch=[low_field, field], sems=2, name="first_block",
    )
    got_one = exchange(pay)

    raw, pay, inv_one, merged, taps, fields, lows = call(
        part(pool_kernel, spots=spots, **counts),
        [field, payload(3), vec, low_field, nine, store_of(field), store_of(low_field)],
        place, got_one, summed, count, batch_norm_table, far(weights), far(fields), far(lows),
        scalars=1, scratch=[field, field, nine], sems=5,
        aliases={6: 5, 7: 6}, name="pool_and_merge",
    )
    got_style = exchange(pay)

    resid, pay, inv_two, style, xhat_two, lows = call(
        part(style_kernel, spots=spots, **styled, **counts),
        [back_field, payload(3), vec, ((devices, LANES), F32), field, store_of(low_field)],
        place, got_style, raw, merged, batch_norm_table, w_style, far(w_convs), taps, far(lows),
        scalars=1, scratch=[low_field, field, (w_convs.shape[1:], F32)], sems=2,
        aliases={8: 5}, name="decoder",
    )
    got_three = exchange(pay)
    ahead, hidden_sums = call(
        part(ahead_kernel, spots=spots, local_count=local_count),
        [((CH, 5, 1, LANES), F32), vec],
        place, far(pay), sides, far(fields), far(lows),
        scalars=1, scratch=[own_field, own_field, own_field, own_low], sems=4, name="ahead",
    )

    grad_three, xhat_three, pay, inv_three = call(
        part(head_kernel, **counts),
        [back_field, back_field, payload(8), vec],
        place, got_three, got_style, resid, sides, head_mat, head_rows, xhat_two, ahead, hidden_sums, batch_norm_table, back_two,
        scalars=1, scratch=[((rows_back, 2, segments, LANES), BF16), back_field, back_low], name="head",
    )
    got_head = exchange(pay)

    grad_one, xhat_one, shared, pay, more_two = call(
        part(decoder_back_kernel, spots=spots, local_count=local_count, pixel_count=pixel_count),
        [back_field, back_field, back_field, payload(8), vec],
        place, got_head, grad_three, xhat_three, xhat_two, inv_three, inv_two, hidden_sums, batch_norm_table, back_two, far(weights),
        far(fields), far(lows),
        scalars=1, scratch=[back_field, back_field, back_low, back_low, own_low, own_low, own_low, nine], sems=6,
        name="decoder_back",
    )
    got_one_back = exchange(pay)

    pay, more = call(
        part(summed_kernel, spots=spots, pixel_count=pixel_count, **styled),
        [payload(13), vec],
        place, got_one_back, got_style, got_head, grad_one, xhat_one, shared, inv_one, more_two, batch_norm_table, w_style,
        sides, back_zero, far(fields),
        scalars=1, scratch=[own_field, own_field, back_low], sems=1, name="summed_back",
    )
    got_last = exchange(pay)

    def results(param, copy):
        return [(param.shape, F32)] * 3 + [(param.shape, BF16)] * copy

    early = call(
        update_early,
        [((1, 1), F32), ((1, 1), F32)] + results(w_style, 0) + results(head_rows, 1),
        got_one_back, got_head, got_style, far(pay), style,
        w_style, head_rows, mom_style, mom_head.T, sqr_style, sqr_head.T,
        scalar_outs=(0, 1), name="update_early",
    )
    late = call(
        part(update_late, pixel_count=pixel_count),
        results(w_first, 1) + results(w_convs, 1) + results(batch_norm_table, 0),
        got_last, got_one_back, got_head, more, more_two, inv_zero,
        w_first, w_convs, batch_norm_table, mom_first, mom_convs, mom_norms, sqr_first, sqr_convs, sqr_norms,
        name="update_late",
    )
    loss, count = early[0].reshape(()), early[1].reshape(())
    head = tuple(value.T for value in early[5:9])
    return (loss, count, *late[0:8], *early[2:5], *head, *late[8:11])


def solution(mesh):
    field = P(None, "row", "col", None)
    plane = P(None, "row", "col")
    return jax.shard_map(
        local,
        mesh=mesh,
        in_specs=(field, plane, field, plane) + (P(),) * 15,
        out_specs=(P(),) * 20,
        check_vma=False,
    )
```

```python
import functools

import jax
import jax.numpy as jnp
from jax import lax
from jax.experimental import pallas as pl
from jax.experimental.pallas import tpu as pltpu
from jax.sharding import PartitionSpec as P

STEP = 5

highest = lax.Precision.HIGHEST
norm_eps = 1e-05
flow_scale = 32.0
adam_eps = 1e-08
weight_decay = 0.01
beta_one = 0.5
beta_two = 0.5
rate_table = (0.2, 0.05, 0.15, 0.15, 0.2)

CH = 32
GRP = 4
SEG = 8
LANES = 128
RIM = 8
FLOW, LABEL, MASK = 16, 32, 40
LEFT, RIGHT = 64, 96
ALONE = 100
AFTER, ROW, BEFORE = 32, 33, 64
F32 = jnp.float32
BF16 = jnp.bfloat16
VMEM_LIMIT = 36 * 1024 * 1024
WHOLE_VMEM = 56 * 1024 * 1024
STORE_BYTES = 32 * 1024 * 1024
FORWARD = 10 * LANES
BACK = 9 * LANES
IMAGE_AT = 3 * FORWARD
BACK_AT = IMAGE_AT + 3 * LANES


def lane_of(shape):
    return lax.broadcasted_iota(jnp.int32, shape, len(shape) - 1)


def row_of(shape):
    return lax.broadcasted_iota(jnp.int32, shape, 0)


def group_of(shape):
    return lane_of(shape) >> 5


def fold(v):
    return v + pltpu.roll(v, 32, axis=1) + (pltpu.roll(v, 64, axis=1) + pltpu.roll(v, 96, axis=1))


def spread(v, k):
    return fold(jnp.where(group_of(v.shape) == k, v, 0.0))


def partner(v):
    odd = (group_of(v.shape) & 1) == 1
    return jnp.where(odd, pltpu.roll(v, 32, axis=1), pltpu.roll(v, 96, axis=1))


def tile4(v):
    return jnp.concatenate([v, v, v, v], axis=1)


def col_sum(v):
    return jnp.sum(v, axis=0, keepdims=True)


def zero_row():
    return jnp.zeros((1, LANES), F32)


def groups(*values):
    group = group_of(values[0].shape)
    out = values[-1]
    for k in range(len(values) - 2, -1, -1):
        out = jnp.where(group == k, values[k], out)
    return out


def low(v):
    return v.astype(BF16).astype(F32)


def sig_of(v):
    return 0.5 + 0.5 * jnp.tanh(0.5 * v)


def slope(n, sig):
    return sig * (1.0 + n * (1.0 - sig))


def slope_at(x, gain, bias):
    n = x * gain + bias
    return slope(n, sig_of(n))


def flat(v):
    return v.reshape(-1, LANES)


def loop(count, body, unroll=5):
    def step(i, carry):
        body(i)
        return carry

    lax.fori_loop(0, count, step, 0, unroll=min(count, unroll))


def copies(sems, *pairs):
    found = []
    for i, (source, target) in enumerate(pairs):
        found.append(pltpu.make_async_copy(source, target, sems.at[i]))
        found[-1].start()
    return found


def wait(started):
    for copy in started:
        copy.wait()


def shift_segments(v, way):
    half = v.shape[1]
    at = lax.broadcasted_iota(jnp.int32, v.shape, 1)
    if way == 1:
        return jnp.where(at == 0, 0.0, pltpu.roll(v, 1, axis=1))
    return jnp.where(at == half - 1, 0.0, pltpu.roll(v, half - 1, axis=1))


def beside(first, second):
    half = first.shape[1] // 2
    left = jnp.concatenate([shift_segments(second[:, half:], 1), second[:, :half]], axis=1)
    right = jnp.concatenate([first[:, half:], shift_segments(first[:, :half], -1)], axis=1)
    return left, right


def put_low(ref, row, first, second, marked=False):
    left, right = beside(first, second)
    lane = lane_of(left.shape)
    edge = jnp.where(lane < 64, right, left)
    if marked:
        at = lax.broadcasted_iota(jnp.int32, left.shape, 1)
        edge = jnp.where(lane == ROW, 1.0, edge)
        edge = jnp.where(lane == AFTER, jnp.where(at == left.shape[1] - 1, 0.0, 1.0), edge)
        edge = jnp.where(lane == BEFORE, jnp.where(at == 0, 0.0, 1.0), edge)
    at = pl.ds(row + 1, first.shape[0])
    for k, v in enumerate((first, second, edge)):
        ref[at, k] = v.astype(BF16)


def blank(ref):
    zero = jnp.zeros((1,) + ref.shape[1:], ref.dtype)
    ref[0:1] = zero
    ref[ref.shape[0] - 1 : ref.shape[0]] = zero


def views(src, row, rows):
    return [flat(src[pl.ds(row + r, rows), k]) for r in range(3) for k in (2, 0, 1)]


def conv(src, mat, row, rows, *more):
    wide = jnp.concatenate(views(src, row, rows) + list(more), axis=1)
    return jnp.dot(wide, mat[...], preferred_element_type=F32)


def blocks_of(y, rows):
    return [y[:, k * LANES : (k + 1) * LANES].reshape(rows, -1, LANES) for k in range(2)]


def narrow(v):
    while v.shape[0] > 1:
        half = v.shape[0] // 2
        v = v[:half] + v[half:]
    return v[0]


def row_sums(first, rows, values):
    step = 4

    def add(i, carry):
        found = [values(pl.ds(first + step * i, step), k) for k in range(2)]
        return tuple(c + a + b for c, a, b in zip(carry, *found))

    shapes = jax.eval_shape(lambda: values(pl.ds(0, step), 0))
    zeros = tuple(jnp.zeros(v.shape, F32) for v in shapes)
    found = lax.fori_loop(0, rows // step, add, zeros, unroll=min(rows // step, 8))
    return [col_sum(narrow(v)) for v in found]


def local_stats(v, first, rows, count):
    count = count / GRP
    pivot = col_sum(v[first, 0] + v[first, 1]) / (2 * v.shape[2])

    def moments(at, k):
        away = v[at, k] - pivot
        return away, away * away

    total, square = row_sums(first, rows, moments)
    return pivot + total / count, square - total * (total / count)


def merge_stats(means, squares, local_count, pixel_count):
    mean = fold(col_sum(means)) / (GRP * means.shape[0])
    away = means - mean
    total = fold(col_sum(squares + (local_count / GRP) * (away * away)))
    return mean, lax.rsqrt(total / pixel_count + norm_eps)


def row_of_each(got, r):
    return got[:, r, 0, :]


def total_of(got, r):
    return col_sum(row_of_each(got, r))


def send(pay, *rows):
    for r, row in enumerate(rows):
        pay[:, r, 0, :] = jnp.broadcast_to(row, (pay.shape[0], LANES))


def send_parts(pay, first, count):
    devices = pay.shape[0]
    if devices > CH:
        for r in range(first, first + count):
            pay[CH:, r, 0, :] = jnp.zeros((devices - CH, LANES), F32)
    return pay.at[0:CH, first : first + count, 0]


def affine(table, q):
    return tile4(table[0, q : q + 1, :]), tile4(table[1, q : q + 1, :])


def diagonal_blocks(mat):
    wide = tile4(mat)
    group = group_of(wide.shape)
    return jnp.concatenate([jnp.where(group == b, wide, 0.0) for b in range(GRP)], axis=0)


def notes(ref, *rows):
    for i, row in enumerate(rows):
        ref[i : i + 1, :] = row


def taps_at(store, i):
    return store.at[FORWARD * i : FORWARD * i + (BACK if i else FORWARD)]


def image_at(store):
    return store.at[IMAGE_AT : IMAGE_AT + 3 * LANES]


def back_at(store):
    return store.at[BACK_AT : BACK_AT + BACK]


def pack_kernel(image_in, flow_in, labels_in, valid_in, out, image, flow, labels, valid, sems):
    fetched = copies(sems, (image_in, image), (flow_in, flow), (labels_in, labels), (valid_in, valid))
    images, height, _, width = image.shape
    parts = out.shape[0] // images
    wait(fetched)
    fields = [image[:, :, c, :].astype(F32) for c in range(2)]
    fields += [flow[:, :, c, :].astype(F32) for c in range(2)]
    fields += [labels[...].astype(F32), valid[...].astype(F32)]
    halves = width // 16
    shape = (width, halves * LANES)
    lane = lane_of(shape)
    column = (lane >> 7) * 16 + ((lane >> 6) & 1) * 8 + (lane & 7)
    hit = row_of(shape) == column
    which = (lane >> 3) & 7
    total = jnp.zeros((images * height, halves * LANES), F32)
    for k, v in enumerate(fields):
        x = v.reshape(images * height, width).astype(BF16)
        mat = jnp.where(hit & (which == k), 1.0, 0.0).astype(BF16)
        total = total + jnp.dot(x, mat, preferred_element_type=F32)
    for b in range(images):
        rows = total[b * height : (b + 1) * height]
        slot = jnp.concatenate([rows[:, h * LANES : (h + 1) * LANES] for h in range(halves)], axis=0).astype(BF16)
        for p in range(parts):
            out[b * parts + p] = slot


COLUMNS = ((8, None, None, -1), (0, 1, 2, 3), (4, 5, 6, 7))


def conv_matrix(taps, mats, base, back):
    out_at = group_of((CH, 2 * LANES))
    for r in range(3):
        wide = []
        for s in range(3):
            if back:
                k = taps[3 * (2 - r) + s]
                k = jnp.concatenate([k, k, k, k], axis=0).T
            else:
                k = tile4(taps[3 * r + s])
            wide.append(jnp.concatenate([k, k], axis=1))
        for d in range(3):
            for a in range(GRP):
                val = jnp.zeros((CH, 2 * LANES), F32)
                column = COLUMNS[d][a]
                if column is not None:
                    for s in range(3):
                        val = jnp.where(out_at == (column + s - 1 if back else column + 1 - s), wide[s], val)
                mats[pl.ds(base + (3 * r + d) * LANES + CH * a, CH), :] = val.astype(BF16)


def image_lanes(shape):
    at = row_of(shape)
    kind = at >> 5
    column = (at & 7) + jnp.where(kind == LEFT // 32, -SEG, jnp.where(kind == RIGHT // 32, SEG, 0))
    return (kind != 1) & ((at & 31) < 16), (at >> 3) & 1, column


def first_taps(w_first, t):
    found = [tile4(low(w_first[t][c : c + 1])) for c in range(2)]
    return [jnp.concatenate([v, v], axis=1) for v in found]


def image_matrix(w_first, r):
    shape = (LANES, 2 * LANES)
    inside, channel, here = image_lanes(shape)
    val = jnp.zeros(shape, F32)
    for s in range(3):
        for c, tap in enumerate(first_taps(w_first, 3 * r + s)):
            val = jnp.where(inside & (channel == c) & (here == group_of(shape) + s - 1), tap, val)
    return val.astype(BF16)


def prepare(w_first_in, w_convs_in, w_head_in, store, back_zero_out, back_two_out, head_out, w_first, w_convs, w_head, mats, back_zero, back_two, head_mat, sems):
    wait(copies(sems, (w_first_in, w_first), (w_convs_in, w_convs), (w_head_in, w_head)))
    stored = []

    def keep(source, target):
        stored.extend(copies(sems.at[len(stored) :], (source, target)))

    for i, back, out in ((2, back_two, back_two_out), (0, back_zero, back_zero_out)):
        conv_matrix(w_convs.at[i], back, 0, True)
        keep(back, out)
    conv_matrix(w_convs.at[1], mats, BACK_AT, True)
    keep(back_at(mats), back_at(store))
    shape = (LANES, 2 * LANES)
    inside, channel, here = image_lanes(shape)
    val = jnp.zeros(shape, F32)
    for c, tap in enumerate(first_taps(w_first, 9)):
        val = jnp.where((row_of(shape) < 16) & (channel == c) & (here == group_of(shape)), tap, val)
    mats[BACK:FORWARD, :] = val.astype(BF16)
    for i in range(3):
        conv_matrix(w_convs.at[i], mats, FORWARD * i, False)
        keep(taps_at(mats, i), taps_at(store, i))
    for r in range(3):
        mats[IMAGE_AT + LANES * r : IMAGE_AT + LANES * (r + 1), :] = image_matrix(w_first, r)
    keep(image_at(mats), image_at(store))
    lane = lane_of((CH, LANES))
    head = jnp.zeros((CH, LANES), F32)
    diagonal = row_of((CH, CH)) == lane_of((CH, CH))
    for k in range(3):
        column = jnp.sum(jnp.where(diagonal, low(w_head[k : k + 1, 0:CH]), 0.0), axis=1, keepdims=True)
        head = jnp.where((lane >> 3) == FLOW // 8 + k, column, head)
    for y in range(SEG):
        head_mat[CH * y : CH * (y + 1), :] = jnp.where((lane & 7) == y, head, 0.0).astype(BF16)
    keep(head_mat, head_out)
    wait(stored)


def start_kernel(place, got, weights, sides, raw, pay, vec, taps, first_mat, sems, *, local_count, height, sources):
    fetched = copies(sems, (image_at(weights), first_mat), (taps_at(weights, 0), taps))
    rows, segments = raw.shape[0], raw.shape[2]
    off, block = place[0], place[1]
    blank(sides)

    def eight(t):
        v = got[pl.ds((block + t) * sources, sources)].astype(F32)
        v = jnp.swapaxes(v.reshape(segments // 2, 8, LANES), 0, 1)
        near = lane_of(v.shape) < 64
        v = jnp.concatenate([jnp.where(near, v, 0.0), jnp.where(near, pltpu.roll(v, 64, axis=2), 0.0)], axis=1)
        pixels = jnp.where(lane_of(v.shape) < 16, v, 0.0)
        left, right = beside(pixels, pixels)
        v = v + pltpu.roll(left, LEFT, axis=2) + pltpu.roll(right, RIGHT, axis=2)
        sides[pl.ds(8 * t + 1, 8)] = v.astype(BF16)

    loop(rows // 8, eight)
    wait(fetched[:1])
    y = None
    for r in range(3):
        part = jnp.dot(flat(sides[r : r + rows]), first_mat[LANES * r : LANES * (r + 1)], preferred_element_type=F32)
        y = part if y is None else y + part
    raw[:, 0], raw[:, 1] = blocks_of(y, rows)
    mean, square = local_stats(raw, off, height, local_count)
    mask = jnp.zeros(sides.shape[1:], F32)
    for i in range(height):
        mask = mask + sides[off + 1 + i].astype(F32)
    lane = lane_of(mask.shape)
    count = jnp.sum(jnp.where((lane >= MASK) & (lane < MASK + 8), mask, 0.0))
    send(pay, mean, square)
    notes(vec, jnp.full((1, LANES), count, F32))
    wait(fetched[1:])


def first_kernel(place, got, raw, sides, table, taps, summed, pay, vec, fields, lows, hidden, xhat, sems, *, spots, local_count, pixel_count, height):
    mean, inverse = merge_stats(row_of_each(got, 0), row_of_each(got, 1), local_count, pixel_count)
    notes(vec, inverse)
    gain, bias = affine(table, 0)
    rows = raw.shape[0]

    def norm_rows(i):
        at = pl.ds(4 * i, 4)
        out = []
        for k in range(2):
            x = (raw[at, k] - mean) * inverse
            xhat[at, k] = x
            n = x * gain + bias
            out.append(n * sig_of(n))
        put_low(hidden, 4 * i, *out)

    blank(hidden)
    loop(rows // 4, norm_rows)
    stored = copies(sems, (xhat, spots(fields, "xhat_zero")), (hidden, spots(lows, "hidden_one")))

    @pl.when(place[0] >= 0)
    def _():
        y = conv(hidden, taps, 0, rows, flat(sides[1 : rows + 1]))
        summed[:, 0], summed[:, 1] = blocks_of(y, rows)

    send(pay, *local_stats(summed, place[0], height, local_count))
    wait(stored)


def pool_kernel(place, got, summed, count_in, table, weights, fields_in, lows_in, raw, pay, vec, merged, taps_next, fields, lows, xhat, shared, taps, sems, *, spots, local_count, pixel_count, height):
    fetched = copies(sems, (taps_at(weights, 1), taps), (taps_at(weights, 2), taps_next))
    mean, inverse = merge_stats(row_of_each(got, 0), row_of_each(got, 1), local_count, pixel_count)
    gain, bias = affine(table, 1)
    rows, segments = summed.shape[0], summed.shape[2]
    off = place[0]

    step = 4

    def some(i, carry):
        at = pl.ds(step * i, step)
        pairs = (step // 2, 2, segments, LANES)
        outs, sums = [], [jnp.zeros((step // 2 * segments, LANES), F32) for _ in range(3)]
        for k in range(2):
            x = (summed[at, k] - mean) * inverse
            n = x * gain + bias
            sig = sig_of(n)
            e = (n * sig).reshape(pairs)
            top = flat(jnp.maximum(e[:, 0], e[:, 1]))
            top = jnp.maximum(top, partner(top))
            wide_top = top.reshape(step // 2, 1, segments, LANES)
            exps = jnp.exp(e - wide_top)
            whole = flat(exps[:, 0] + exps[:, 1])
            whole = whole + partner(whole)
            pooled = top + jnp.log(whole)
            outs.append((e + pooled.reshape(wide_top.shape)).reshape(step, segments, LANES))
            share = exps * (1.0 / whole).reshape(wide_top.shape) * slope(n, sig).reshape(pairs)
            share_x = share * x.reshape(pairs)
            xhat[at, k] = x
            shared[at, k] = share.reshape(step, segments, LANES)
            sums[0] = sums[0] + pooled
            sums[1] = sums[1] + flat(share[:, 0] + share[:, 1])
            sums[2] = sums[2] + flat(share_x[:, 0] + share_x[:, 1])
        put_low(merged, step * i, *outs)
        mine = (step * i >= off) & (step * i < off + height)
        keep = jnp.where(mine, 1.0, 0.0)
        return tuple(a + keep * b for a, b in zip(carry, sums))

    blank(merged)
    zero = jnp.zeros((step // 2 * segments, LANES), F32)
    sums = lax.fori_loop(0, rows // step, some, (zero, zero, zero), unroll=min(rows // step, 5))
    pool_sum, share_sum, share_x = [fold(col_sum(v)) for v in sums]
    stored = copies(
        sems.at[2:],
        (xhat, spots(fields, "xhat_one")),
        (shared, spots(fields, "shared")),
        (merged, spots(lows, "merged")),
    )
    wait(fetched)
    raw[:, 0], raw[:, 1] = blocks_of(conv(merged, taps, 0, rows), rows)
    mean, square = local_stats(raw, place[0], height, local_count)
    send(pay, mean, square, groups(0.5 * pool_sum, share_sum, share_x, count_in[0:1]))
    notes(vec, inverse)
    wait(stored)


def by_image(v, parts):
    devices = v.shape[0]
    step = 1
    while step < parts:
        upper = (row_of(v.shape) // step) % 2 == 1
        v = v + jnp.where(upper, pltpu.roll(v, step, axis=0), pltpu.roll(v, devices - step, axis=0))
        step *= 2
    return v


def wide_dot(a, b, dims=(((1,), (0,)), ((), ()))):
    (a_high, a_low), (b_high, b_low) = [[v.astype(BF16) for v in in_parts(x, 2)] for x in (a, b)]
    axis_a, axis_b = dims[0][0][0], dims[0][1][0]
    left = jnp.concatenate([a_high, a_high, a_low], axis=axis_a)
    right = jnp.concatenate([b_high, b_low, b_high], axis=axis_b)
    return lax.dot_general(left, right, dims, preferred_element_type=F32)


def in_parts(v, count):
    out = []
    for _ in range(count):
        out.append(low(v))
        v = v - out[-1]
    return out


def mine_of(v, me):
    return col_sum(jnp.where(row_of(v.shape) == me, v, 0.0))


def style_kernel(place, got, raw, merged, table, w_style, w_convs_in, taps, lows_in, resid, pay, vec, style_out, xhat, lows, hidden, slopes, w_conv, sems, *, spots, local_count, pixel_count, pool_cells, height, parts):
    fetched = copies(sems, (w_convs_in.at[2], w_conv))
    style = by_image(spread(row_of_each(got, 2), 0), parts) / pool_cells
    style_out[...] = style
    one, two = [
        wide_dot(style, diagonal_blocks(w_style[i])) for i in range(2)
    ]
    mean, inverse = merge_stats(row_of_each(got, 0) + one, row_of_each(got, 1), local_count, pixel_count)
    notes(vec, inverse)
    gain, bias = affine(table, 2)
    rows, kept = raw.shape[0], resid.shape[0]
    off, skipped, mine = place[0], place[3], place[4]
    me = place[2]
    shift = mine_of(one, me) - mean
    two = mine_of(two, me)

    def norm_rows(i):
        at = pl.ds(4 * i, 4)
        out = []
        for k in range(2):
            x = (raw[at, k] + shift) * inverse
            xhat[at, k] = x
            n = x * gain + bias
            sig = sig_of(n)
            slopes[at, k] = slope(n, sig)
            out.append(n * sig)
        put_low(hidden, 4 * i, *out)

    blank(hidden)
    loop(rows // 4, norm_rows)
    stored = copies(sems.at[1:], (hidden, spots(lows, "hidden_three")))

    @pl.when(place[0] >= 0)
    def _():
        for k, y in enumerate(blocks_of(conv(hidden, taps, skipped, kept), kept)):
            resid[:, k] = y + two + merged[pl.ds(skipped + 1, kept), k].astype(F32)

    wait(fetched + stored)
    hidden[kept + 1 : kept + 2] = jnp.zeros((1,) + hidden.shape[1:], BF16)
    centre = fold(col_sum(resid[mine, 0] + resid[mine, 1])) / (SEG * raw.shape[2])
    at = pl.ds(off, height)
    probe = [slopes[at, k] for k in range(2)]
    probe += [slopes[at, k] * xhat[at, k] for k in range(2)]
    probe = jnp.concatenate([flat(v).astype(BF16) for v in probe], axis=1)

    def centred(i):
        at = pl.ds(4 * i, 4)
        put_low(hidden, 4 * i, resid[at, 0] - centre, resid[at, 1] - centre, True)

    loop(kept // 4, centred)
    links = norm_links(hidden, probe, mine, height, w_conv, centre)
    send(pay, *local_stats(resid, mine, height, local_count))
    send_parts(pay, 2, 1)[:, 0, :] = links


def norm_links(field, probe, first, rows, taps, centre):
    wide = jnp.concatenate(views(field, first, rows), axis=1)
    found = lax.dot_general(probe, wide, (((0,), (0,)), ((), ())), preferred_element_type=F32)
    group = group_of((CH, LANES))
    out = []
    for half in range(2):

        def piece(y, chunk):
            at = 2 * LANES * half + CH * y
            return found[at : at + CH, chunk * LANES : (chunk + 1) * LANES]

        plain = jnp.zeros((CH, LANES), F32)
        moved = jnp.zeros((CH, LANES), F32)
        for r in range(3):
            first_edge, last_edge = piece(0, 3 * r), piece(SEG - 1, 3 * r)
            edge = first_edge + last_edge
            for y in range(1, SEG - 1):
                edge = edge + piece(y, 3 * r)
            inside = edge[:, ROW : ROW + 1]
            counts = (
                inside + (first_edge[:, BEFORE : BEFORE + 1] - first_edge[:, ROW : ROW + 1]),
                inside,
                inside + (last_edge[:, AFTER : AFTER + 1] - last_edge[:, ROW : ROW + 1]),
            )
            for c in range(3):
                tap = tile4(low(taps[3 * (2 - r) + 2 - c]))
                val = jnp.zeros((CH, LANES), F32)
                for y in range(SEG):
                    d, a = spot_of(y + c - 1)
                    val = val + jnp.where(group == a, piece(y, 3 * r + d), 0.0)
                plain = plain + tap * counts[c]
                moved = moved + tap * val
        out += [plain, fold(moved) + centre * plain]
    return groups(*out)


def spot_of(x):
    if x < 0:
        return 0, 3
    if x == SEG:
        return 0, 0
    return 1 + x // GRP, x % GRP


def ahead_kernel(place, pay, sides, fields, lows, out, sums, below_x, xhat, shared, field, sems, *, spots, local_count):
    off = place[0]
    height = xhat.shape[0]
    own = pl.ds(off, height)
    fetched = copies(
        sems,
        (spots(fields, "xhat_zero").at[own], below_x),
        (spots(fields, "xhat_one").at[own], xhat),
        (spots(fields, "shared").at[own], shared),
        (spots(lows, "hidden_one").at[pl.ds(off, height + 2)], field),
    )
    wait(fetched[:1])
    at = pl.ds(0, height)
    low_x = jnp.concatenate([own_lanes(below_x, at), jnp.ones((height * field.shape[2], LANES), BF16)], axis=1)
    entries, alone = [], zero_row()
    lane = lane_of((1, LANES))
    for r in range(3):
        for tap, bare in pixel_taps(sides, off + r, height, low_x, (-1, 0, 1), True):
            for v, b in zip(tap, bare):
                alone = jnp.where(lane == ALONE + len(entries), b, alone)
                entries.append(v)
    wait(fetched[1:])
    centres = [fold(v) / local_count for v in row_sums(0, height, lambda at, k: (xhat[at, k], shared[at, k]))]
    probe = [flat(v[at, k] - c).astype(BF16) for v, c in zip((xhat, shared), centres) for k in range(2)]
    wide = jnp.concatenate(views(field, 0, height), axis=1)
    found = lax.dot_general(
        jnp.concatenate(probe, axis=1), wide, (((0,), (0,)), ((), ())), preferred_element_type=F32
    )
    ones = jnp.ones((8, wide.shape[0]), BF16)
    plain = jnp.dot(ones, wide, preferred_element_type=F32)[0:1]
    group = group_of((1, LANES))
    hidden = []
    for r in range(3):
        for s in range(3):
            val = zero_row()
            for y in range(SEG):
                d, a = spot_of(y + s - 1)
                spot = (3 * r + d) * LANES
                val = val + jnp.where(group == a, plain[:, spot : spot + LANES], 0.0)
            hidden.append(fold(val))
    packed = [groups(*hidden[0:4]), groups(*hidden[4:8]), hidden[8]]
    all_hidden = jnp.concatenate(packed, axis=0)
    last = [
        put_taps(
            found[2 * LANES * k : 2 * LANES * (k + 1)], out.at[:, 2 * k + 1 : 2 * k + 3, 0], (centres[k], all_hidden)
        )
        for k in range(2)
    ]
    entries += hidden
    entries.append(jnp.zeros((CH - len(entries), LANES), F32))
    out[:, 0, 0, :] = groups(jnp.concatenate(entries, axis=0), *last, jnp.zeros((CH, LANES), F32))
    notes(sums, *packed, alone)


def head_kernel(place, got, got_style, resid, sides, head_mat, w_head, below_x, ahead, image_sums, table, back, grad, xhat, pay, vec, decoded, slopes, grad_low, *, local_count, pixel_count, height):
    mean, inverse = merge_stats(row_of_each(got, 0), row_of_each(got, 1), local_count, pixel_count)
    notes(vec, inverse, mean)
    gain, bias = affine(table, 3)
    rows, segments = resid.shape[0], resid.shape[2]
    all_off, skipped, off = place[0], place[3], place[4]

    def norm_rows(i):
        at = pl.ds(4 * i, 4)
        for k in range(2):
            x = (resid[at, k] - mean) * inverse
            n = x * gain + bias
            s = sig_of(n)
            xhat[at, k] = x
            slopes[at, k] = slope(n, s)
            decoded[at, k] = (n * s).astype(BF16)

    loop(rows // 4, norm_rows, 10)
    head = head_mat[...]
    wide = jnp.concatenate([flat(decoded[:, 0]), flat(decoded[:, 1])], axis=1)
    bias_row = zero_row()
    for k in range(3):
        mine = (lane_of((1, LANES)) >> 3) == FLOW // 8 + k
        bias_row = jnp.where(mine, low(w_head[k : k + 1, CH : CH + 1]), bias_row)
    out = jnp.dot(wide, head, preferred_element_type=F32) + bias_row
    given = flat(sides[pl.ds(skipped + 1, rows)]).astype(F32)
    lane = lane_of(given.shape)
    is_flow = lane < LABEL
    near = [pltpu.roll(given, LANES - MASK + first, axis=1) for first in (FLOW, FLOW + 8, LABEL)]
    mask = jnp.where(lane < FLOW + 8, near[0], jnp.where(is_flow, near[1], near[2]))
    mask = jnp.where((lane >= FLOW) & (lane < LABEL + 8), mask, 0.0)
    count = jnp.sum(got_style[:, 2, 0, 3 * CH : 3 * CH + 1])
    diff = out - given / flow_scale
    hinge = jnp.maximum(out, 0.0) + jnp.log1p(jnp.exp(-jnp.abs(out)))
    loss = mask * jnp.where(is_flow, diff * diff, hinge - given * out)
    grad_out = (mask * jnp.where(is_flow, 2.0 * diff, sig_of(out) - given) / count).astype(BF16)
    at_row = lax.broadcasted_iota(jnp.int32, loss.shape, 0)
    inside = (at_row >= off * segments) & (at_row < (off + height) * segments)
    loss_sum = jnp.sum(jnp.where(inside, loss, 0.0))
    mine_out = jnp.where(inside, grad_out.astype(F32), 0.0).astype(BF16)
    outs = col_sum(mine_out.astype(F32))
    found = lax.dot_general(mine_out, wide, (((0,), (0,)), ((), ())), preferred_element_type=F32)
    shape = found.shape
    found = jnp.where((row_of(shape) & 7) == group_of(shape), found, 0.0)
    whole = [col_sum(found[FLOW + 8 * k : FLOW + 8 * k + 8]) for k in range(3)]
    whole = [fold(v[:, 0:LANES] + v[:, LANES:]) for v in whole]
    row = groups(*whole, zero_row())
    lane = lane_of((1, LANES))
    for k in range(3):
        row = jnp.where(lane == 3 * CH + k, jnp.sum(jnp.where((lane >> 3) == FLOW // 8 + k, outs, 0.0)), row)
    row = jnp.where(lane == 3 * CH + 3, loss_sum, row)
    y = lax.dot_general(grad_out, head, (((1,), (1,)), ((), ())), preferred_element_type=F32)
    for k, g in enumerate(blocks_of(y, rows)):
        grad[:, k] = g * slopes[:, k]
    factor = gain * inverse
    back_rows(grad_low, rows, lambda at, k: factor * grad[at, k], 10)
    shift_sum, scale_sum = own_sums(grad, xhat, off, height)
    y = conv(grad_low, back, off, height)
    slopes[0:height, 0], slopes[0:height, 1] = blocks_of(y, height)
    gain, bias = affine(table, 2)

    def links(at, k):
        x = below_x[pl.ds(all_off + at.start, at.size), k]
        g = slopes[at, k] * slope_at(x, gain, bias)
        return g, g * x

    below = [fold(v) for v in row_sums(0, height, links)]
    send(pay, groups(shift_sum, scale_sum, *below), row + image_sums[3:4], total_of(got, 2))
    send_parts(pay, 3, 5)
    pay[0:CH, 3:8] = ahead[...]


def own_sums(grad, xhat, first, rows):
    def both(at, k):
        g = grad[at, k]
        return g, g * xhat[at, k]

    return [fold(v) for v in row_sums(first, rows, both)]


def back_sums(got, pixel_count):
    whole = col_sum(got)
    return spread(whole, 0) / pixel_count, spread(whole, 1) / pixel_count


def low_sum(grad_low, first, rows):
    return fold(row_sums(first + 1, rows, lambda at, k: (grad_low[at, k].astype(F32),))[0])


def norm_back(grad, xhat, factor, shift, scale):
    return factor * (grad - (shift + xhat * scale))


def back_rows(grad_low, rows, value, unroll=5):
    def some(i):
        put_low(grad_low, 4 * i, *[value(pl.ds(4 * i, 4), k) for k in range(2)])

    blank(grad_low)
    loop(rows // 4, some, unroll)


def own_lanes(grad, at):
    return jnp.concatenate([flat(grad[at, k]).astype(BF16) for k in range(2)], axis=1)


def tap_sums(field, grad, first, rows, out, more=None):
    wide = jnp.concatenate(views(field, first, rows), axis=1)
    found = lax.dot_general(grad, wide, (((0,), (0,)), ((), ())), preferred_element_type=F32)
    return put_taps(found, out, more)


def put_taps(found, out, more=None):
    group = group_of((CH, LANES))
    taps = []
    for r in range(3):
        for s in range(3):
            val = jnp.zeros((CH, LANES), F32)
            for y in range(SEG):
                d, a = spot_of(y + s - 1)
                spot = (3 * r + d) * LANES
                val = val + jnp.where(group == a, found[CH * y : CH * y + CH, spot : spot + LANES], 0.0)
            taps.append(fold(val))
    for q in range(3):
        val = taps[4 * q]
        for b in range(1, min(4, 9 - 4 * q)):
            val = jnp.where(group == b, taps[4 * q + b], val)
        if more is not None:
            centre, sums = more
            val = val + column_of(centre) * sums[q : q + 1]
        if q == 2:
            return val
        out[:, q, :] = val


def column_of(v):
    shape = (CH, LANES)
    return jnp.sum(jnp.where(row_of(shape) == lane_of(shape), v, 0.0), axis=1, keepdims=True)


def at_lane(v, k):
    return jnp.sum(jnp.where(lane_of(v.shape) == k, v, 0.0), axis=1, keepdims=True)


def decoder_back_kernel(place, got, grad, xhat, mid_x, vec, vec_two, sums, table, back_two, weights, fields, lows, below, below_x, shared, pay, more, first_x, kept_grad, mid, low_two, low_one, field_two, field_one, field_zero, back_one, sems, *, spots, local_count, pixel_count):
    all_off, skipped, off = place[0], place[3], place[4]
    height = field_two.shape[0] - 2
    far_rows, near_rows = pl.ds(skipped, grad.shape[0]), pl.ds(all_off, height + 2)
    fetched = copies(
        sems,
        (back_at(weights), back_one),
        (spots(fields, "xhat_one").at[far_rows], below_x),
        (spots(fields, "shared").at[far_rows], shared),
        (spots(lows, "hidden_three").at[near_rows], field_two),
        (spots(lows, "merged").at[near_rows], field_one),
        (spots(lows, "hidden_one").at[near_rows], field_zero),
    )
    handed = copies(sems.at[6:], (spots(fields, "xhat_zero").at[pl.ds(all_off, height)], first_x))
    devices = got.shape[0]
    rows = grad.shape[0]
    total = total_of(got, 0)
    shift, scale = spread(total, 0) / pixel_count, spread(total, 1) / pixel_count
    inverse, mean = vec[0:1], vec[1:2]
    factor = affine(table, 3)[0] * inverse
    slant = scale * inverse
    held, carried = factor * (shift - slant * mean), factor * slant
    links = got[0:CH, 2, 0, :] * groups(held, carried, held, carried)
    group = group_of(links.shape)
    mine = (lane_of(links.shape) & 31) == row_of(links.shape)

    def across(pick):
        column = jnp.sum(jnp.where(pick, links, 0.0), axis=1, keepdims=True)
        return col_sum(jnp.where(mine, column, 0.0))

    shift_two = spread(total, 2) - across(group < 2)
    scale_two = spread(total, 3) - across(group >= 2)
    entry = total_of(got, 3)
    notes(more, scale_two, shift_two, total_of(got, 4), total_of(got, 5), spread(entry, 1))

    def value(at, k):
        g = norm_back(grad[at, k], xhat[at, k], factor, shift, scale)
        kept_grad[at, k] = g
        return g

    back_rows(low_two, rows, value)

    @pl.when(place[0] >= 0)
    def _():
        mid[:, 0], mid[:, 1] = blocks_of(conv(low_two, back_two, 0, rows), rows)

    gain, bias = affine(table, 2)
    factor = gain * vec_two[0:1]
    shift, scale = shift_two / pixel_count, scale_two / pixel_count

    def value_two(at, k):
        x = mid_x[pl.ds(skipped + at.start, at.size), k]
        return norm_back(mid[at, k] * slope_at(x, gain, bias), x, factor, shift, scale)

    back_rows(low_one, rows, value_two)
    wait(fetched)
    sum_two = low_sum(low_two, off, height)
    sum_one = low_sum(low_one, off, height)
    y = conv(low_one, back_one, 0, rows)
    gain, bias = affine(table, 1)
    for k, y in enumerate(blocks_of(y, rows)):
        g = (y + kept_grad[:, k]).reshape(rows // 2, 2, -1, LANES)
        both = flat(g[:, 0] + g[:, 1])
        both = (both + partner(both)).reshape(rows // 2, 1, -1, LANES)
        g = g * slope_at(below_x[:, k], gain, bias).reshape(g.shape) + both * shared[:, k].reshape(g.shape)
        below[:, k] = g.reshape(rows, -1, LANES)
    shift_sum, scale_sum = own_sums(below, below_x, off, height)
    send(pay, groups(shift_sum, scale_sum, sum_one, sum_two))
    entry = spread(entry, 0)
    pay[:, 1, 0, :] = jnp.broadcast_to(entry, (devices, LANES))
    at = pl.ds(off + 1, height)
    last_two = tap_sums(field_two, own_lanes(low_two, at), 0, height, send_parts(pay, 2, 2))
    last_one = tap_sums(field_one, own_lanes(low_one, at), 0, height, send_parts(pay, 4, 2))
    centre = shift_sum / local_count
    at = pl.ds(off, height)
    grad = jnp.concatenate([flat(below[at, k] - centre).astype(BF16) for k in range(2)], axis=1)
    last_zero = tap_sums(field_zero, grad, 0, height, send_parts(pay, 6, 2), (centre, sums))
    pay[0:CH, 1, 0, :] = groups(last_two, last_one, last_zero, jnp.broadcast_to(entry, (CH, LANES)))
    wait(handed)


def summed_kernel(place, got, got_style, got_head, grad, xhat, shared, vec, more_two, table, w_style, sides, back, below_x, pay, more, below, grad_low, *, pixel_count, pool_cells, parts):
    off, mine = place[0], place[4]
    height = below.shape[0]
    devices = got.shape[0]
    rows = grad.shape[0]
    dims = (((1,), (1,)), ((), ()))
    first = row_of_each(got, 0)
    each = wide_dot(spread(first, 2), diagonal_blocks(w_style[0]), dims) + wide_dot(
        spread(first, 3), diagonal_blocks(w_style[1]), dims
    )
    each = each / pool_cells
    total = col_sum(first)
    shift = spread(total, 0) + col_sum(each * by_image(spread(row_of_each(got_style, 2), 1), parts))
    scale = spread(total, 1) + col_sum(each * by_image(spread(row_of_each(got_style, 2), 2), parts))
    style_grad = col_sum(jnp.where(row_of(each.shape) // parts == place[2] // parts, each, 0.0))
    factor = affine(table, 1)[0] * vec[0:1]
    shift_mean, scale_mean = shift / pixel_count, scale / pixel_count
    def value(at, k):
        return norm_back(grad[at, k] + shared[at, k] * style_grad, xhat[at, k], factor, shift_mean, scale_mean)

    back_rows(grad_low, rows, value)
    gain, bias = affine(table, 0)
    for k, y in enumerate(blocks_of(conv(grad_low, back, mine, height), height)):
        below[:, k] = y * slope_at(below_x[:, k], gain, bias)
    me = place[2]
    weights = at_lane(by_image(each, parts), me)
    hidden = spread(got[0:CH, 1, 0, :], 3)
    hidden = [groups(*[hidden[18 + t : 19 + t] for t in range(4 * q, min(4 * q + 4, 9))]) for q in range(3)]
    last = total_of(got, 1)
    direct = [total_of(got, 6), total_of(got, 7), spread(last, 2)]
    shares = [row_of_each(got_head, 6), row_of_each(got_head, 7), spread(row_of_each(got_head, 3), 2)]
    shard = []
    for q in range(3):
        val = direct[q] + col_sum(weights * shares[q])
        val = val - at_lane(shift_mean, me) * hidden[q] - at_lane(scale_mean, me) * more_two[2 + q : 3 + q]
        shard.append(at_lane(factor, me) * val)
    at = pl.ds(mine + 1, height)
    side = pixel_taps(sides, off + 1, height, own_lanes(grad_low, at), (0,))[0]
    low_below = own_lanes(below, pl.ds(0, height))
    taps = []
    for r in range(3):
        for tap in pixel_taps(sides, off + r, height, low_below, (-1, 0, 1)):
            taps.extend(tap)
    taps = [shard[2]] + taps + side
    send(
        pay,
        groups(*own_sums(below, below_x, 0, height), spread(last, 0), spread(last, 1)),
        *[total_of(got, r) for r in range(2, 6)],
        *shard[0:2],
        *[groups(*(taps[4 * q : 4 * q + 4] + [zero_row()])[0:4]) for q in range(6)],
    )
    notes(more, scale, shift)


def pixel_taps(sides, row, rows, grad, shift, alone=False):
    x = flat(sides[pl.ds(row, rows)])
    found = lax.dot_general(x, grad, (((0,), (0,)), ((), ())), preferred_element_type=F32)
    inside, channel, column = image_lanes((LANES, 2 * LANES))
    here = column - group_of((LANES, 2 * LANES))
    out = []
    for s in shift:
        both, bare = [], []
        for c in range(2):
            v = col_sum(jnp.where(inside & (channel == c) & (here == s), found[:, 0 : 2 * LANES], 0.0))
            both.append(fold(v[:, 0:LANES] + v[:, LANES:]))
            if alone:
                cut = slice(0, LANES)
                hit = (inside & (channel == c) & (column >= s) & (column < s + SEG))[:, cut]
                bare.append(col_sum(jnp.where(hit, found[:, 2 * LANES :], 0.0)))
        out.append((both, bare) if alone else both)
    return out


def adamw(master, moment, square, grad, rate):
    new_moment = beta_one * moment + (1.0 - beta_one) * grad
    new_square = beta_two * square + (1.0 - beta_two) * grad * grad
    moment_hat = new_moment / (1.0 - beta_one**STEP)
    square_hat = new_square / (1.0 - beta_two**STEP)
    new_master = master - rate * (moment_hat / (jnp.sqrt(square_hat) + adam_eps) + weight_decay * master)
    return new_master, new_moment, new_square


def put(at, refs, grad, rate, outs):
    found = adamw(*[ref[at] for ref in refs], grad, rate)
    for out, value in zip(outs, found + (found[0].astype(BF16),)):
        out[at] = value


def update_early(
    got_one_back, got_head, got_style, pay, style, w_style, w_head, m_style, m_head, s_style, s_head,
    loss_out, count_out, style_master, style_moment, style_square, head_master, head_moment, head_square, head_copy,
):
    count_out[0, 0] = jnp.sum(got_style[:, 2, 0, 3 * CH : 3 * CH + 1])
    loss_out[0, 0] = jnp.sum(got_head[:, 1, 0, 99:100])
    dims = (((0,), (0,)), ((), ()))
    for i in range(2):
        sums = spread(row_of_each(got_one_back, 0), 2 + i)
        grad = lax.dot_general(style[...], sums, dims, precision=highest, preferred_element_type=F32)
        put(i, (w_style, m_style, s_style), grad[0:CH, 0:CH], rate_table[2], (style_master, style_moment, style_square))

    head = total_of(got_head, 1)
    lane = lane_of((1, LANES))
    rows = []
    for k in range(3):
        last = jnp.sum(jnp.where(lane == 3 * CH + k, head, 0.0), axis=1, keepdims=True)
        rows.append(jnp.where(lane < CH, spread(head, k), last))
    grad = jnp.concatenate(rows, axis=0)[:, 0 : CH + 1]
    put(slice(None), (w_head, m_head, s_head), grad, rate_table[3], (head_master, head_moment, head_square, head_copy))


def update_late(
    got, got_one_back, got_head, more, more_two, vec, w_first, w_convs, table, m_first, m_convs, m_norms, s_first, s_convs, s_norms,
    first_master, first_moment, first_square, first_copy,
    convs_master, convs_moment, convs_square, convs_copy,
    norms_master, norms_moment, norms_square, *, pixel_count
):
    refs = (w_convs, m_convs, s_convs)
    outs = (convs_master, convs_moment, convs_square, convs_copy)
    packs = [[got[0:CH, k, 0, :].T for k in ks] for ks in ((5, 6, 7), (3, 4, 0), (1, 2, 0))]
    for i, pack in enumerate(packs):
        for t in range(9):
            b = t % 4 if t < 8 else (0, 3, 2)[i]
            put((i, t), refs, pack[t // 4][CH * b : CH * b + CH], rate_table[1], outs)

    zero_sums = total_of(got, 0)
    totals = [total_of(got, r) for r in range(7, 13)]
    shift, scale = spread(zero_sums, 0), spread(zero_sums, 1)
    factor = affine(table, 0)[0] * vec[0:1]
    by_x = spread(got_one_back[0:CH, 1, 0, :], 3)
    alone = total_of(got_head, 1)
    refs = (w_first, m_first, s_first)
    outs = (first_master, first_moment, first_square, first_copy)
    for t in range(10):
        pair = []
        for e in (2 * t, 2 * t + 1):
            k, b = divmod(1 + e, 4)
            v = spread(totals[k], b)
            if t < 9:
                v = factor * (v - (at_lane(alone, ALONE + e) * shift + by_x[e : e + 1] * scale) / pixel_count)
            pair.append(v[:, 0:CH])
        put(t, refs, jnp.concatenate(pair, axis=0), rate_table[0], outs)

    three_sums = total_of(got_head, 0)
    scales = [scale, more[0:1], more_two[0:1], spread(three_sums, 1)]
    shifts = [shift, more[1:2], more_two[1:2], spread(three_sums, 0)]
    for i, rows in enumerate((scales, shifts)):
        grad = jnp.concatenate(rows, axis=0)[:, 0:CH]
        put(i, (table, m_norms, s_norms), grad, rate_table[4], (norms_master, norms_moment, norms_square))


def far(x):
    return ("far", x)


def call(kernel, outs, *operands, scalars=0, scratch=(), sems=0, scalar_outs=(), aliases=None, limit=VMEM_LIMIT, name):
    smem = pl.BlockSpec(memory_space=pltpu.SMEM)
    vmem = pl.BlockSpec(memory_space=pltpu.VMEM)
    hbm = pl.BlockSpec(memory_space=pltpu.HBM)
    is_far = lambda x: isinstance(x, tuple) and x[0] == "far"
    in_specs = [smem if i < scalars else hbm if is_far(x) else vmem for i, x in enumerate(operands)]
    out_specs = [smem if i in scalar_outs else hbm if is_far(x) else vmem for i, x in enumerate(outs)]
    plain = lambda x: x[1] if is_far(x) else x
    shapes = [pltpu.VMEM(shape, dtype) for shape, dtype in scratch]
    if sems:
        shapes.append(pltpu.SemaphoreType.DMA((sems,)))
    return pl.pallas_call(
        kernel,
        out_shape=[jax.ShapeDtypeStruct(*plain(x)) for x in outs],
        in_specs=in_specs,
        out_specs=out_specs,
        scratch_shapes=shapes,
        input_output_aliases=aliases or {},
        compiler_params=pltpu.CompilerParams(vmem_limit_bytes=limit),
        name=name,
    )(*[plain(x) for x in operands])


def exchange(pay):
    return lax.all_to_all(pay, ("row", "col"), 0, 0)


def local(
    image_batch, valid_mask, flow_target, cell_labels,
    w_first, w_convs, w_style, w_head, batch_norm_table,
    mom_first, mom_convs, mom_style, mom_head, mom_norms,
    sqr_first, sqr_convs, sqr_style, sqr_head, sqr_norms,
):
    images, block_rows, block_cols, _ = image_batch.shape
    row_count, col_count = lax.axis_size("row"), lax.axis_size("col")
    devices = row_count * col_count
    parts = devices // images
    image_rows, image_cols = row_count * block_rows, col_count * block_cols
    assert devices == parts * images and block_rows == RIM and block_cols == 2 * block_rows * 2
    assert image_rows % (parts * RIM) == 0 and devices >= CH
    height = image_rows // parts
    rows = min(image_rows, height + RIM * min(2, parts - 1))
    segments = image_cols // SEG
    local_count = float(height * image_cols)
    pixel_count = local_count * devices
    pool_cells = float(image_rows * image_cols // 4)
    part = functools.partial
    counts = dict(local_count=local_count, pixel_count=pixel_count, height=height)
    styled = dict(pool_cells=pool_cells, parts=parts)

    me = lax.axis_index("row") * col_count + lax.axis_index("col")
    first_row = (me % parts) * height
    start = jnp.clip(first_row - RIM, 0, image_rows - rows)
    off = first_row - start
    back_rim = RIM // 2
    rows_back = min(rows, height + back_rim * min(2, parts - 1))
    skipped = jnp.clip(off - back_rim, 0, rows - rows_back)
    place = jnp.stack([off, start // block_rows, me, skipped, off - skipped]).astype(jnp.int32)

    field = ((rows, 2, segments, LANES), F32)
    own_field = ((height,) + field[0][1:], F32)
    back_field = ((rows_back,) + field[0][1:], F32)
    low_field = ((rows + 2, 3, segments, LANES), BF16)
    own_low = ((height + 2,) + low_field[0][1:], BF16)
    back_low = ((rows_back + 2,) + low_field[0][1:], BF16)
    vec = ((8, LANES), F32)

    def payload(count):
        return ((devices, count, 1, LANES), F32)

    nine = ((BACK, 2 * LANES), BF16)
    ten = ((FORWARD, 2 * LANES), BF16)

    places = {
        name: i * count
        for count, names in (
            (rows, ("xhat_zero", "xhat_one", "shared")),
            (rows + 2, ("hidden_one", "hidden_three", "merged")),
        )
        for i, name in enumerate(names)
    }

    def spots(store, name):
        count = rows if name[0] in "xs" else rows + 2
        return store.at[places[name] : places[name] + count]

    def store_of(like):
        shape, dtype = like
        row_bytes = shape[1] * segments * LANES * jnp.dtype(dtype).itemsize
        return far(((-(-STORE_BYTES // row_bytes),) + shape[1:], dtype))

    inputs = (
        jnp.transpose(image_batch, (0, 1, 3, 2)), jnp.transpose(flow_target, (0, 1, 3, 2)), cell_labels, valid_mask
    )
    (pay,) = call(
        pack_kernel,
        [((devices, 16, LANES), BF16)],
        *[far(v) for v in inputs],
        scratch=[(v.shape, v.dtype) for v in inputs], sems=4, limit=WHOLE_VMEM, name="pack",
    )
    got_inputs = exchange(pay)
    head_rows = w_head.T
    weights, back_zero, back_two, head_mat = call(
        prepare,
        [far(((STORE_BYTES // (4 * LANES), 2 * LANES), BF16)), far(nine), far(nine), far(((2 * LANES, LANES), BF16))],
        far(w_first), far(w_convs), far(head_rows),
        scratch=[
            (w_first.shape, F32), (w_convs.shape, F32), (head_rows.shape, F32), ((BACK_AT + BACK, 2 * LANES), BF16),
            nine, nine, ((2 * LANES, LANES), BF16),
        ],
        sems=8, limit=WHOLE_VMEM, name="prepare",
    )

    sides, raw, pay, count, taps = call(
        part(start_kernel, local_count=local_count, height=height, sources=col_count),
        [((rows + 2, segments, LANES), BF16), field, payload(2), vec, ten],
        place, got_inputs, far(weights),
        scalars=1, scratch=[((3 * LANES, 2 * LANES), BF16)], sems=2, name="image_conv",
    )
    got_zero = exchange(pay)
    summed, pay, inv_zero, fields, lows = call(
        part(first_kernel, spots=spots, **counts),
        [field, payload(2), vec, store_of(field), store_of(low_field)],
        place, got_zero, raw, sides, batch_norm_table, taps,
        scalars=1, scratch=[low_field, field], sems=2, name="first_block",
    )
    got_one = exchange(pay)

    raw, pay, inv_one, merged, taps, fields, lows = call(
        part(pool_kernel, spots=spots, **counts),
        [field, payload(3), vec, low_field, nine, store_of(field), store_of(low_field)],
        place, got_one, summed, count, batch_norm_table, far(weights), far(fields), far(lows),
        scalars=1, scratch=[field, field, nine], sems=5,
        aliases={6: 5, 7: 6}, name="pool_and_merge",
    )
    got_style = exchange(pay)

    resid, pay, inv_two, style, xhat_two, lows = call(
        part(style_kernel, spots=spots, **styled, **counts),
        [back_field, payload(3), vec, ((devices, LANES), F32), field, store_of(low_field)],
        place, got_style, raw, merged, batch_norm_table, w_style, far(w_convs), taps, far(lows),
        scalars=1, scratch=[low_field, field, (w_convs.shape[1:], F32)], sems=2,
        aliases={8: 5}, name="decoder",
    )
    got_three = exchange(pay)
    ahead, hidden_sums = call(
        part(ahead_kernel, spots=spots, local_count=local_count),
        [((CH, 5, 1, LANES), F32), vec],
        place, far(pay), sides, far(fields), far(lows),
        scalars=1, scratch=[own_field, own_field, own_field, own_low], sems=4, name="ahead",
    )

    grad_three, xhat_three, pay, inv_three = call(
        part(head_kernel, **counts),
        [back_field, back_field, payload(8), vec],
        place, got_three, got_style, resid, sides, head_mat, head_rows, xhat_two, ahead, hidden_sums, batch_norm_table, back_two,
        scalars=1, scratch=[((rows_back, 2, segments, LANES), BF16), back_field, back_low], name="head",
    )
    got_head = exchange(pay)

    grad_one, xhat_one, shared, pay, more_two, xhat_zero = call(
        part(decoder_back_kernel, spots=spots, local_count=local_count, pixel_count=pixel_count),
        [back_field, back_field, back_field, payload(8), vec, own_field],
        place, got_head, grad_three, xhat_three, xhat_two, inv_three, inv_two, hidden_sums, batch_norm_table, back_two, far(weights),
        far(fields), far(lows),
        scalars=1, scratch=[back_field, back_field, back_low, back_low, own_low, own_low, own_low, nine], sems=7,
        name="decoder_back",
    )
    got_one_back = exchange(pay)

    pay, more = call(
        part(summed_kernel, pixel_count=pixel_count, **styled),
        [payload(13), vec],
        place, got_one_back, got_style, got_head, grad_one, xhat_one, shared, inv_one, more_two, batch_norm_table, w_style,
        sides, back_zero, xhat_zero,
        scalars=1, scratch=[own_field, back_low], name="summed_back",
    )
    got_last = exchange(pay)

    def results(param, copy):
        return [(param.shape, F32)] * 3 + [(param.shape, BF16)] * copy

    early = call(
        update_early,
        [((1, 1), F32), ((1, 1), F32)] + results(w_style, 0) + results(head_rows, 1),
        got_one_back, got_head, got_style, far(pay), style,
        w_style, head_rows, mom_style, mom_head.T, sqr_style, sqr_head.T,
        scalar_outs=(0, 1), name="update_early",
    )
    late = call(
        part(update_late, pixel_count=pixel_count),
        results(w_first, 1) + results(w_convs, 1) + results(batch_norm_table, 0),
        got_last, got_one_back, got_head, more, more_two, inv_zero,
        w_first, w_convs, batch_norm_table, mom_first, mom_convs, mom_norms, sqr_first, sqr_convs, sqr_norms,
        name="update_late",
    )
    loss, count = early[0].reshape(()), early[1].reshape(())
    head = tuple(value.T for value in early[5:9])
    return (loss, count, *late[0:8], *early[2:5], *head, *late[8:11])


def solution(mesh):
    field = P(None, "row", "col", None)
    plane = P(None, "row", "col")
    return jax.shard_map(
        local,
        mesh=mesh,
        in_specs=(field, plane, field, plane) + (P(),) * 15,
        out_specs=(P(),) * 20,
        check_vma=False,
    )
```

```python
import functools

import jax
import jax.numpy as jnp
from jax import lax
from jax.experimental import pallas as pl
from jax.experimental.pallas import tpu as pltpu
from jax.sharding import PartitionSpec as P

STEP = 5

highest = lax.Precision.HIGHEST
norm_eps = 1e-05
flow_scale = 32.0
adam_eps = 1e-08
weight_decay = 0.01
beta_one = 0.5
beta_two = 0.5
rate_table = (0.2, 0.05, 0.15, 0.15, 0.2)

CH = 32
GRP = 4
SEG = 8
LANES = 128
RIM = 8
FLOW, LABEL, MASK = 16, 32, 40
LEFT, RIGHT = 64, 96
ALONE = 100
AFTER, ROW, BEFORE = 32, 33, 64
F32 = jnp.float32
BF16 = jnp.bfloat16
VMEM_LIMIT = 36 * 1024 * 1024
WHOLE_VMEM = 56 * 1024 * 1024
STORE_BYTES = 32 * 1024 * 1024
FORWARD = 10 * LANES
BACK = 9 * LANES
IMAGE_AT = 3 * FORWARD
BACK_AT = IMAGE_AT + 3 * LANES


def lane_of(shape):
    return lax.broadcasted_iota(jnp.int32, shape, len(shape) - 1)


def row_of(shape):
    return lax.broadcasted_iota(jnp.int32, shape, 0)


def group_of(shape):
    return lane_of(shape) >> 5


def fold(v):
    return v + pltpu.roll(v, 32, axis=1) + (pltpu.roll(v, 64, axis=1) + pltpu.roll(v, 96, axis=1))


def spread(v, k):
    return fold(jnp.where(group_of(v.shape) == k, v, 0.0))


def partner(v):
    odd = (group_of(v.shape) & 1) == 1
    return jnp.where(odd, pltpu.roll(v, 32, axis=1), pltpu.roll(v, 96, axis=1))


def tile4(v):
    return jnp.concatenate([v, v, v, v], axis=1)


def col_sum(v):
    return jnp.sum(v, axis=0, keepdims=True)


def zero_row():
    return jnp.zeros((1, LANES), F32)


def groups(*values):
    group = group_of(values[0].shape)
    out = values[-1]
    for k in range(len(values) - 2, -1, -1):
        out = jnp.where(group == k, values[k], out)
    return out


def low(v):
    return v.astype(BF16).astype(F32)


def sig_of(v):
    return 0.5 + 0.5 * jnp.tanh(0.5 * v)


def slope(n, sig):
    return sig * (1.0 + n * (1.0 - sig))


def slope_at(x, gain, bias):
    n = x * gain + bias
    return slope(n, sig_of(n))


def flat(v):
    return v.reshape(-1, LANES)


def loop(count, body, unroll=5):
    def step(i, carry):
        body(i)
        return carry

    lax.fori_loop(0, count, step, 0, unroll=min(count, unroll))


def copies(sems, *pairs):
    found = []
    for i, (source, target) in enumerate(pairs):
        found.append(pltpu.make_async_copy(source, target, sems.at[i]))
        found[-1].start()
    return found


def wait(started):
    for copy in started:
        copy.wait()


def shift_segments(v, way):
    half = v.shape[1]
    at = lax.broadcasted_iota(jnp.int32, v.shape, 1)
    if way == 1:
        return jnp.where(at == 0, 0.0, pltpu.roll(v, 1, axis=1))
    return jnp.where(at == half - 1, 0.0, pltpu.roll(v, half - 1, axis=1))


def beside(first, second):
    half = first.shape[1] // 2
    left = jnp.concatenate([shift_segments(second[:, half:], 1), second[:, :half]], axis=1)
    right = jnp.concatenate([first[:, half:], shift_segments(first[:, :half], -1)], axis=1)
    return left, right


def put_low(ref, row, first, second, marked=False):
    left, right = beside(first, second)
    lane = lane_of(left.shape)
    edge = jnp.where(lane < 64, right, left)
    if marked:
        at = lax.broadcasted_iota(jnp.int32, left.shape, 1)
        edge = jnp.where(lane == ROW, 1.0, edge)
        edge = jnp.where(lane == AFTER, jnp.where(at == left.shape[1] - 1, 0.0, 1.0), edge)
        edge = jnp.where(lane == BEFORE, jnp.where(at == 0, 0.0, 1.0), edge)
    at = pl.ds(row + 1, first.shape[0])
    for k, v in enumerate((first, second, edge)):
        ref[at, k] = v.astype(BF16)


def blank(ref):
    zero = jnp.zeros((1,) + ref.shape[1:], ref.dtype)
    ref[0:1] = zero
    ref[ref.shape[0] - 1 : ref.shape[0]] = zero


def views(src, row, rows):
    return [flat(src[pl.ds(row + r, rows), k]) for r in range(3) for k in (2, 0, 1)]


def conv(src, mat, row, rows, *more):
    wide = jnp.concatenate(views(src, row, rows) + list(more), axis=1)
    return jnp.dot(wide, mat[...], preferred_element_type=F32)


def blocks_of(y, rows):
    return [y[:, k * LANES : (k + 1) * LANES].reshape(rows, -1, LANES) for k in range(2)]


def narrow(v):
    while v.shape[0] > 1:
        half = v.shape[0] // 2
        v = v[:half] + v[half:]
    return v[0]


def row_sums(first, rows, values):
    step = 4

    def add(i, carry):
        found = [values(pl.ds(first + step * i, step), k) for k in range(2)]
        return tuple(c + a + b for c, a, b in zip(carry, *found))

    shapes = jax.eval_shape(lambda: values(pl.ds(0, step), 0))
    zeros = tuple(jnp.zeros(v.shape, F32) for v in shapes)
    found = lax.fori_loop(0, rows // step, add, zeros, unroll=min(rows // step, 8))
    return [col_sum(narrow(v)) for v in found]


def local_stats(v, first, rows, count):
    count = count / GRP
    pivot = col_sum(v[first, 0] + v[first, 1]) / (2 * v.shape[2])

    def moments(at, k):
        away = v[at, k] - pivot
        return away, away * away

    total, square = row_sums(first, rows, moments)
    return pivot + total / count, square - total * (total / count)


def merge_stats(means, squares, local_count, pixel_count):
    mean = fold(col_sum(means)) / (GRP * means.shape[0])
    away = means - mean
    total = fold(col_sum(squares + (local_count / GRP) * (away * away)))
    return mean, lax.rsqrt(total / pixel_count + norm_eps)


def row_of_each(got, r):
    return got[:, r, 0, :]


def total_of(got, r):
    return col_sum(row_of_each(got, r))


def send(pay, *rows):
    for r, row in enumerate(rows):
        pay[:, r, 0, :] = jnp.broadcast_to(row, (pay.shape[0], LANES))


def send_parts(pay, first, count):
    devices = pay.shape[0]
    if devices > CH:
        for r in range(first, first + count):
            pay[CH:, r, 0, :] = jnp.zeros((devices - CH, LANES), F32)
    return pay.at[0:CH, first : first + count, 0]


def affine(table, q):
    return tile4(table[0, q : q + 1, :]), tile4(table[1, q : q + 1, :])


def diagonal_blocks(mat):
    wide = tile4(mat)
    group = group_of(wide.shape)
    return jnp.concatenate([jnp.where(group == b, wide, 0.0) for b in range(GRP)], axis=0)


def notes(ref, *rows):
    for i, row in enumerate(rows):
        ref[i : i + 1, :] = row


def taps_at(store, i):
    return store.at[FORWARD * i : FORWARD * i + (BACK if i else FORWARD)]


def image_at(store):
    return store.at[IMAGE_AT : IMAGE_AT + 3 * LANES]


def back_at(store):
    return store.at[BACK_AT : BACK_AT + BACK]


def pack_kernel(image_in, flow_in, labels_in, valid_in, out, image, flow, labels, valid, sems):
    fetched = copies(sems, (image_in, image), (flow_in, flow), (labels_in, labels), (valid_in, valid))
    images, height, _, width = image.shape
    parts = out.shape[0] // images
    wait(fetched)
    fields = [image[:, :, c, :].astype(F32) for c in range(2)]
    fields += [flow[:, :, c, :].astype(F32) for c in range(2)]
    fields += [labels[...].astype(F32), valid[...].astype(F32)]
    halves = width // 16
    shape = (width, halves * LANES)
    lane = lane_of(shape)
    column = (lane >> 7) * 16 + ((lane >> 6) & 1) * 8 + (lane & 7)
    hit = row_of(shape) == column
    which = (lane >> 3) & 7
    total = jnp.zeros((images * height, halves * LANES), F32)
    for k, v in enumerate(fields):
        x = v.reshape(images * height, width).astype(BF16)
        mat = jnp.where(hit & (which == k), 1.0, 0.0).astype(BF16)
        total = total + jnp.dot(x, mat, preferred_element_type=F32)
    for b in range(images):
        rows = total[b * height : (b + 1) * height]
        slot = jnp.concatenate([rows[:, h * LANES : (h + 1) * LANES] for h in range(halves)], axis=0).astype(BF16)
        for p in range(parts):
            out[b * parts + p] = slot


COLUMNS = ((8, None, None, -1), (0, 1, 2, 3), (4, 5, 6, 7))


def conv_matrix(taps, mats, base, back):
    out_at = group_of((CH, 2 * LANES))
    for r in range(3):
        wide = []
        for s in range(3):
            if back:
                k = taps[3 * (2 - r) + s]
                k = jnp.concatenate([k, k, k, k], axis=0).T
            else:
                k = tile4(taps[3 * r + s])
            wide.append(jnp.concatenate([k, k], axis=1))
        for d in range(3):
            for a in range(GRP):
                val = jnp.zeros((CH, 2 * LANES), F32)
                column = COLUMNS[d][a]
                if column is not None:
                    for s in range(3):
                        val = jnp.where(out_at == (column + s - 1 if back else column + 1 - s), wide[s], val)
                mats[pl.ds(base + (3 * r + d) * LANES + CH * a, CH), :] = val.astype(BF16)


def image_lanes(shape):
    at = row_of(shape)
    kind = at >> 5
    column = (at & 7) + jnp.where(kind == LEFT // 32, -SEG, jnp.where(kind == RIGHT // 32, SEG, 0))
    return (kind != 1) & ((at & 31) < 16), (at >> 3) & 1, column


def first_taps(w_first, t):
    found = [tile4(low(w_first[t][c : c + 1])) for c in range(2)]
    return [jnp.concatenate([v, v], axis=1) for v in found]


def image_matrix(w_first, r):
    shape = (LANES, 2 * LANES)
    inside, channel, here = image_lanes(shape)
    val = jnp.zeros(shape, F32)
    for s in range(3):
        for c, tap in enumerate(first_taps(w_first, 3 * r + s)):
            val = jnp.where(inside & (channel == c) & (here == group_of(shape) + s - 1), tap, val)
    return val.astype(BF16)


def prepare(w_first_in, w_convs_in, w_head_in, store, back_zero_out, back_two_out, head_out, w_first, w_convs, w_head, mats, back_zero, back_two, head_mat, sems):
    wait(copies(sems, (w_first_in, w_first), (w_convs_in, w_convs), (w_head_in, w_head)))
    stored = []

    def keep(source, target):
        stored.extend(copies(sems.at[len(stored) :], (source, target)))

    for i, back, out in ((2, back_two, back_two_out), (0, back_zero, back_zero_out)):
        conv_matrix(w_convs.at[i], back, 0, True)
        keep(back, out)
    conv_matrix(w_convs.at[1], mats, BACK_AT, True)
    keep(back_at(mats), back_at(store))
    shape = (LANES, 2 * LANES)
    inside, channel, here = image_lanes(shape)
    val = jnp.zeros(shape, F32)
    for c, tap in enumerate(first_taps(w_first, 9)):
        val = jnp.where((row_of(shape) < 16) & (channel == c) & (here == group_of(shape)), tap, val)
    mats[BACK:FORWARD, :] = val.astype(BF16)
    for i in range(3):
        conv_matrix(w_convs.at[i], mats, FORWARD * i, False)
        keep(taps_at(mats, i), taps_at(store, i))
    for r in range(3):
        mats[IMAGE_AT + LANES * r : IMAGE_AT + LANES * (r + 1), :] = image_matrix(w_first, r)
    keep(image_at(mats), image_at(store))
    lane = lane_of((CH, LANES))
    head = jnp.zeros((CH, LANES), F32)
    diagonal = row_of((CH, CH)) == lane_of((CH, CH))
    for k in range(3):
        column = jnp.sum(jnp.where(diagonal, low(w_head[k : k + 1, 0:CH]), 0.0), axis=1, keepdims=True)
        head = jnp.where((lane >> 3) == FLOW // 8 + k, column, head)
    for y in range(SEG):
        head_mat[CH * y : CH * (y + 1), :] = jnp.where((lane & 7) == y, head, 0.0).astype(BF16)
    keep(head_mat, head_out)
    wait(stored)


def start_kernel(place, got, weights, sides, raw, pay, vec, taps, first_mat, sems, *, local_count, height, sources):
    fetched = copies(sems, (image_at(weights), first_mat), (taps_at(weights, 0), taps))
    rows, segments = raw.shape[0], raw.shape[2]
    off, block = place[0], place[1]
    blank(sides)

    def eight(t):
        v = got[pl.ds((block + t) * sources, sources)].astype(F32)
        v = jnp.swapaxes(v.reshape(segments // 2, 8, LANES), 0, 1)
        near = lane_of(v.shape) < 64
        v = jnp.concatenate([jnp.where(near, v, 0.0), jnp.where(near, pltpu.roll(v, 64, axis=2), 0.0)], axis=1)
        pixels = jnp.where(lane_of(v.shape) < 16, v, 0.0)
        left, right = beside(pixels, pixels)
        v = v + pltpu.roll(left, LEFT, axis=2) + pltpu.roll(right, RIGHT, axis=2)
        sides[pl.ds(8 * t + 1, 8)] = v.astype(BF16)

    loop(rows // 8, eight)
    wait(fetched[:1])
    y = None
    for r in range(3):
        part = jnp.dot(flat(sides[r : r + rows]), first_mat[LANES * r : LANES * (r + 1)], preferred_element_type=F32)
        y = part if y is None else y + part
    raw[:, 0], raw[:, 1] = blocks_of(y, rows)
    mean, square = local_stats(raw, off, height, local_count)
    mask = jnp.zeros(sides.shape[1:], F32)
    for i in range(height):
        mask = mask + sides[off + 1 + i].astype(F32)
    lane = lane_of(mask.shape)
    count = jnp.sum(jnp.where((lane >= MASK) & (lane < MASK + 8), mask, 0.0))
    send(pay, mean, square)
    notes(vec, jnp.full((1, LANES), count, F32))
    wait(fetched[1:])


def first_kernel(place, got, raw, sides, table, taps, summed, pay, vec, fields, lows, hidden, xhat, sems, *, spots, local_count, pixel_count, height):
    mean, inverse = merge_stats(row_of_each(got, 0), row_of_each(got, 1), local_count, pixel_count)
    notes(vec, inverse)
    gain, bias = affine(table, 0)
    rows = raw.shape[0]

    def norm_rows(i):
        at = pl.ds(4 * i, 4)
        out = []
        for k in range(2):
            x = (raw[at, k] - mean) * inverse
            xhat[at, k] = x
            n = x * gain + bias
            out.append(n * sig_of(n))
        put_low(hidden, 4 * i, *out)

    blank(hidden)
    loop(rows // 4, norm_rows)
    stored = copies(sems, (xhat, spots(fields, "xhat_zero")), (hidden, spots(lows, "hidden_one")))

    @pl.when(place[0] >= 0)
    def _():
        y = conv(hidden, taps, 0, rows, flat(sides[1 : rows + 1]))
        summed[:, 0], summed[:, 1] = blocks_of(y, rows)

    send(pay, *local_stats(summed, place[0], height, local_count))
    wait(stored)


def pool_kernel(place, got, summed, count_in, table, weights, fields_in, lows_in, raw, pay, vec, merged, taps_next, fields, lows, xhat, shared, taps, sems, *, spots, local_count, pixel_count, height):
    fetched = copies(sems, (taps_at(weights, 1), taps), (taps_at(weights, 2), taps_next))
    mean, inverse = merge_stats(row_of_each(got, 0), row_of_each(got, 1), local_count, pixel_count)
    gain, bias = affine(table, 1)
    rows, segments = summed.shape[0], summed.shape[2]
    off = place[0]

    step = 4

    def some(i, carry):
        at = pl.ds(step * i, step)
        pairs = (step // 2, 2, segments, LANES)
        outs, sums = [], [jnp.zeros((step // 2 * segments, LANES), F32) for _ in range(3)]
        for k in range(2):
            x = (summed[at, k] - mean) * inverse
            n = x * gain + bias
            sig = sig_of(n)
            e = (n * sig).reshape(pairs)
            top = flat(jnp.maximum(e[:, 0], e[:, 1]))
            top = jnp.maximum(top, partner(top))
            wide_top = top.reshape(step // 2, 1, segments, LANES)
            exps = jnp.exp(e - wide_top)
            whole = flat(exps[:, 0] + exps[:, 1])
            whole = whole + partner(whole)
            pooled = top + jnp.log(whole)
            outs.append((e + pooled.reshape(wide_top.shape)).reshape(step, segments, LANES))
            share = exps * (1.0 / whole).reshape(wide_top.shape) * slope(n, sig).reshape(pairs)
            share_x = share * x.reshape(pairs)
            xhat[at, k] = x
            shared[at, k] = share.reshape(step, segments, LANES)
            sums[0] = sums[0] + pooled
            sums[1] = sums[1] + flat(share[:, 0] + share[:, 1])
            sums[2] = sums[2] + flat(share_x[:, 0] + share_x[:, 1])
        put_low(merged, step * i, *outs)
        mine = (step * i >= off) & (step * i < off + height)
        keep = jnp.where(mine, 1.0, 0.0)
        return tuple(a + keep * b for a, b in zip(carry, sums))

    blank(merged)
    zero = jnp.zeros((step // 2 * segments, LANES), F32)
    sums = lax.fori_loop(0, rows // step, some, (zero, zero, zero), unroll=min(rows // step, 5))
    pool_sum, share_sum, share_x = [fold(col_sum(v)) for v in sums]
    stored = copies(
        sems.at[2:],
        (xhat, spots(fields, "xhat_one")),
        (shared, spots(fields, "shared")),
        (merged, spots(lows, "merged")),
    )
    wait(fetched)
    raw[:, 0], raw[:, 1] = blocks_of(conv(merged, taps, 0, rows), rows)
    mean, square = local_stats(raw, place[0], height, local_count)
    send(pay, mean, square, groups(0.5 * pool_sum, share_sum, share_x, count_in[0:1]))
    notes(vec, inverse)
    wait(stored)


def by_image(v, parts):
    devices = v.shape[0]
    step = 1
    while step < parts:
        upper = (row_of(v.shape) // step) % 2 == 1
        v = v + jnp.where(upper, pltpu.roll(v, step, axis=0), pltpu.roll(v, devices - step, axis=0))
        step *= 2
    return v


def wide_dot(a, b, dims=(((1,), (0,)), ((), ()))):
    (a_high, a_low), (b_high, b_low) = [[v.astype(BF16) for v in in_parts(x, 2)] for x in (a, b)]
    axis_a, axis_b = dims[0][0][0], dims[0][1][0]
    left = jnp.concatenate([a_high, a_high, a_low], axis=axis_a)
    right = jnp.concatenate([b_high, b_low, b_high], axis=axis_b)
    return lax.dot_general(left, right, dims, preferred_element_type=F32)


def in_parts(v, count):
    out = []
    for _ in range(count):
        out.append(low(v))
        v = v - out[-1]
    return out


def mine_of(v, me):
    return col_sum(jnp.where(row_of(v.shape) == me, v, 0.0))


def style_kernel(place, got, raw, merged, table, w_style, w_convs_in, taps, sides, fields, lows_in, resid, pay, vec, style_out, xhat, ahead, sums, lows, hidden, slopes, w_conv, zero_x, one_x, shared, field, sems, *, spots, local_count, pixel_count, pool_cells, height, parts):
    own = pl.ds(place[0], height)
    fetched = copies(
        sems,
        (w_convs_in.at[2], w_conv),
        (spots(fields, "xhat_zero").at[own], zero_x),
        (spots(fields, "xhat_one").at[own], one_x),
        (spots(fields, "shared").at[own], shared),
        (spots(lows_in, "hidden_one").at[pl.ds(place[0], height + 2)], field),
    )
    style = by_image(spread(row_of_each(got, 2), 0), parts) / pool_cells
    style_out[...] = style
    one, two = [
        wide_dot(style, diagonal_blocks(w_style[i])) for i in range(2)
    ]
    mean, inverse = merge_stats(row_of_each(got, 0) + one, row_of_each(got, 1), local_count, pixel_count)
    notes(vec, inverse)
    gain, bias = affine(table, 2)
    rows, kept = raw.shape[0], resid.shape[0]
    off, skipped, mine = place[0], place[3], place[4]
    me = place[2]
    shift = mine_of(one, me) - mean
    two = mine_of(two, me)

    def norm_rows(i):
        at = pl.ds(4 * i, 4)
        out = []
        for k in range(2):
            x = (raw[at, k] + shift) * inverse
            xhat[at, k] = x
            n = x * gain + bias
            sig = sig_of(n)
            slopes[at, k] = slope(n, sig)
            out.append(n * sig)
        put_low(hidden, 4 * i, *out)

    blank(hidden)
    loop(rows // 4, norm_rows)
    stored = copies(sems.at[5:], (hidden, spots(lows, "hidden_three")))

    @pl.when(place[0] >= 0)
    def _():
        for k, y in enumerate(blocks_of(conv(hidden, taps, skipped, kept), kept)):
            resid[:, k] = y + two + merged[pl.ds(skipped + 1, kept), k].astype(F32)

    wait(fetched + stored)
    hidden[kept + 1 : kept + 2] = jnp.zeros((1,) + hidden.shape[1:], BF16)
    centre = fold(col_sum(resid[mine, 0] + resid[mine, 1])) / (SEG * raw.shape[2])
    at = pl.ds(off, height)
    probe = [slopes[at, k] for k in range(2)]
    probe += [slopes[at, k] * xhat[at, k] for k in range(2)]
    probe = jnp.concatenate([flat(v).astype(BF16) for v in probe], axis=1)

    def centred(i):
        at = pl.ds(4 * i, 4)
        put_low(hidden, 4 * i, resid[at, 0] - centre, resid[at, 1] - centre, True)

    loop(kept // 4, centred)
    links = norm_links(hidden, probe, mine, height, w_conv, centre)
    send(pay, *local_stats(resid, mine, height, local_count))
    send_parts(pay, 2, 1)[:, 0, :] = links
    put_ahead(off, sides, ahead, sums, zero_x, one_x, shared, field, local_count)


def norm_links(field, probe, first, rows, taps, centre):
    wide = jnp.concatenate(views(field, first, rows), axis=1)
    found = lax.dot_general(probe, wide, (((0,), (0,)), ((), ())), preferred_element_type=F32)
    group = group_of((CH, LANES))
    out = []
    for half in range(2):

        def piece(y, chunk):
            at = 2 * LANES * half + CH * y
            return found[at : at + CH, chunk * LANES : (chunk + 1) * LANES]

        plain = jnp.zeros((CH, LANES), F32)
        moved = jnp.zeros((CH, LANES), F32)
        for r in range(3):
            first_edge, last_edge = piece(0, 3 * r), piece(SEG - 1, 3 * r)
            edge = first_edge + last_edge
            for y in range(1, SEG - 1):
                edge = edge + piece(y, 3 * r)
            inside = edge[:, ROW : ROW + 1]
            counts = (
                inside + (first_edge[:, BEFORE : BEFORE + 1] - first_edge[:, ROW : ROW + 1]),
                inside,
                inside + (last_edge[:, AFTER : AFTER + 1] - last_edge[:, ROW : ROW + 1]),
            )
            for c in range(3):
                tap = tile4(low(taps[3 * (2 - r) + 2 - c]))
                val = jnp.zeros((CH, LANES), F32)
                for y in range(SEG):
                    d, a = spot_of(y + c - 1)
                    val = val + jnp.where(group == a, piece(y, 3 * r + d), 0.0)
                plain = plain + tap * counts[c]
                moved = moved + tap * val
        out += [plain, fold(moved) + centre * plain]
    return groups(*out)


def spot_of(x):
    if x < 0:
        return 0, 3
    if x == SEG:
        return 0, 0
    return 1 + x // GRP, x % GRP


def put_ahead(off, sides, out, sums, below_x, xhat, shared, field, local_count):
    height = xhat.shape[0]
    at = pl.ds(0, height)
    low_x = jnp.concatenate([own_lanes(below_x, at), jnp.ones((height * field.shape[2], LANES), BF16)], axis=1)
    entries, alone = [], zero_row()
    lane = lane_of((1, LANES))
    for r in range(3):
        for tap, bare in pixel_taps(sides, off + r, height, low_x, (-1, 0, 1), True):
            for v, b in zip(tap, bare):
                alone = jnp.where(lane == ALONE + len(entries), b, alone)
                entries.append(v)
    centres = [fold(v) / local_count for v in row_sums(0, height, lambda at, k: (xhat[at, k], shared[at, k]))]
    probe = [flat(v[at, k] - c).astype(BF16) for v, c in zip((xhat, shared), centres) for k in range(2)]
    wide = jnp.concatenate(views(field, 0, height), axis=1)
    found = lax.dot_general(
        jnp.concatenate(probe, axis=1), wide, (((0,), (0,)), ((), ())), preferred_element_type=F32
    )
    ones = jnp.ones((8, wide.shape[0]), BF16)
    plain = jnp.dot(ones, wide, preferred_element_type=F32)[0:1]
    group = group_of((1, LANES))
    hidden = []
    for r in range(3):
        for s in range(3):
            val = zero_row()
            for y in range(SEG):
                d, a = spot_of(y + s - 1)
                spot = (3 * r + d) * LANES
                val = val + jnp.where(group == a, plain[:, spot : spot + LANES], 0.0)
            hidden.append(fold(val))
    packed = [groups(*hidden[0:4]), groups(*hidden[4:8]), hidden[8]]
    all_hidden = jnp.concatenate(packed, axis=0)
    last = [
        put_taps(
            found[2 * LANES * k : 2 * LANES * (k + 1)], out.at[:, 2 * k + 1 : 2 * k + 3, 0], (centres[k], all_hidden)
        )
        for k in range(2)
    ]
    entries += hidden
    entries.append(jnp.zeros((CH - len(entries), LANES), F32))
    out[:, 0, 0, :] = groups(jnp.concatenate(entries, axis=0), *last, jnp.zeros((CH, LANES), F32))
    notes(sums, *packed, alone)


def head_kernel(place, got, got_style, resid, sides, head_mat, w_head, below_x, ahead, image_sums, table, back, grad, xhat, pay, vec, decoded, slopes, grad_low, *, local_count, pixel_count, height):
    mean, inverse = merge_stats(row_of_each(got, 0), row_of_each(got, 1), local_count, pixel_count)
    notes(vec, inverse, mean)
    gain, bias = affine(table, 3)
    rows, segments = resid.shape[0], resid.shape[2]
    all_off, skipped, off = place[0], place[3], place[4]

    def norm_rows(i):
        at = pl.ds(4 * i, 4)
        for k in range(2):
            x = (resid[at, k] - mean) * inverse
            n = x * gain + bias
            s = sig_of(n)
            xhat[at, k] = x
            slopes[at, k] = slope(n, s)
            decoded[at, k] = (n * s).astype(BF16)

    loop(rows // 4, norm_rows, 10)
    head = head_mat[...]
    wide = jnp.concatenate([flat(decoded[:, 0]), flat(decoded[:, 1])], axis=1)
    bias_row = zero_row()
    for k in range(3):
        mine = (lane_of((1, LANES)) >> 3) == FLOW // 8 + k
        bias_row = jnp.where(mine, low(w_head[k : k + 1, CH : CH + 1]), bias_row)
    out = jnp.dot(wide, head, preferred_element_type=F32) + bias_row
    given = flat(sides[pl.ds(skipped + 1, rows)]).astype(F32)
    lane = lane_of(given.shape)
    is_flow = lane < LABEL
    near = [pltpu.roll(given, LANES - MASK + first, axis=1) for first in (FLOW, FLOW + 8, LABEL)]
    mask = jnp.where(lane < FLOW + 8, near[0], jnp.where(is_flow, near[1], near[2]))
    mask = jnp.where((lane >= FLOW) & (lane < LABEL + 8), mask, 0.0)
    count = jnp.sum(got_style[:, 2, 0, 3 * CH : 3 * CH + 1])
    diff = out - given / flow_scale
    hinge = jnp.maximum(out, 0.0) + jnp.log1p(jnp.exp(-jnp.abs(out)))
    loss = mask * jnp.where(is_flow, diff * diff, hinge - given * out)
    grad_out = (mask * jnp.where(is_flow, 2.0 * diff, sig_of(out) - given) / count).astype(BF16)
    at_row = lax.broadcasted_iota(jnp.int32, loss.shape, 0)
    inside = (at_row >= off * segments) & (at_row < (off + height) * segments)
    loss_sum = jnp.sum(jnp.where(inside, loss, 0.0))
    mine_out = jnp.where(inside, grad_out.astype(F32), 0.0).astype(BF16)
    outs = col_sum(mine_out.astype(F32))
    found = lax.dot_general(mine_out, wide, (((0,), (0,)), ((), ())), preferred_element_type=F32)
    shape = found.shape
    found = jnp.where((row_of(shape) & 7) == group_of(shape), found, 0.0)
    whole = [col_sum(found[FLOW + 8 * k : FLOW + 8 * k + 8]) for k in range(3)]
    whole = [fold(v[:, 0:LANES] + v[:, LANES:]) for v in whole]
    row = groups(*whole, zero_row())
    lane = lane_of((1, LANES))
    for k in range(3):
        row = jnp.where(lane == 3 * CH + k, jnp.sum(jnp.where((lane >> 3) == FLOW // 8 + k, outs, 0.0)), row)
    row = jnp.where(lane == 3 * CH + 3, loss_sum, row)
    y = lax.dot_general(grad_out, head, (((1,), (1,)), ((), ())), preferred_element_type=F32)
    for k, g in enumerate(blocks_of(y, rows)):
        grad[:, k] = g * slopes[:, k]
    factor = gain * inverse
    back_rows(grad_low, rows, lambda at, k: factor * grad[at, k], 10)
    shift_sum, scale_sum = own_sums(grad, xhat, off, height)
    y = conv(grad_low, back, off, height)
    slopes[0:height, 0], slopes[0:height, 1] = blocks_of(y, height)
    gain, bias = affine(table, 2)

    def links(at, k):
        x = below_x[pl.ds(all_off + at.start, at.size), k]
        g = slopes[at, k] * slope_at(x, gain, bias)
        return g, g * x

    below = [fold(v) for v in row_sums(0, height, links)]
    send(pay, groups(shift_sum, scale_sum, *below), row + image_sums[3:4], total_of(got, 2))
    send_parts(pay, 3, 5)
    pay[0:CH, 3:8] = ahead[...]


def own_sums(grad, xhat, first, rows):
    def both(at, k):
        g = grad[at, k]
        return g, g * xhat[at, k]

    return [fold(v) for v in row_sums(first, rows, both)]


def back_sums(got, pixel_count):
    whole = col_sum(got)
    return spread(whole, 0) / pixel_count, spread(whole, 1) / pixel_count


def low_sum(grad_low, first, rows):
    return fold(row_sums(first + 1, rows, lambda at, k: (grad_low[at, k].astype(F32),))[0])


def norm_back(grad, xhat, factor, shift, scale):
    return factor * (grad - (shift + xhat * scale))


def back_rows(grad_low, rows, value, unroll=5):
    def some(i):
        put_low(grad_low, 4 * i, *[value(pl.ds(4 * i, 4), k) for k in range(2)])

    blank(grad_low)
    loop(rows // 4, some, unroll)


def own_lanes(grad, at):
    return jnp.concatenate([flat(grad[at, k]).astype(BF16) for k in range(2)], axis=1)


def tap_sums(field, grad, first, rows, out, more=None):
    wide = jnp.concatenate(views(field, first, rows), axis=1)
    found = lax.dot_general(grad, wide, (((0,), (0,)), ((), ())), preferred_element_type=F32)
    return put_taps(found, out, more)


def put_taps(found, out, more=None):
    group = group_of((CH, LANES))
    taps = []
    for r in range(3):
        for s in range(3):
            val = jnp.zeros((CH, LANES), F32)
            for y in range(SEG):
                d, a = spot_of(y + s - 1)
                spot = (3 * r + d) * LANES
                val = val + jnp.where(group == a, found[CH * y : CH * y + CH, spot : spot + LANES], 0.0)
            taps.append(fold(val))
    for q in range(3):
        val = taps[4 * q]
        for b in range(1, min(4, 9 - 4 * q)):
            val = jnp.where(group == b, taps[4 * q + b], val)
        if more is not None:
            centre, sums = more
            val = val + column_of(centre) * sums[q : q + 1]
        if q == 2:
            return val
        out[:, q, :] = val


def column_of(v):
    shape = (CH, LANES)
    return jnp.sum(jnp.where(row_of(shape) == lane_of(shape), v, 0.0), axis=1, keepdims=True)


def at_lane(v, k):
    return jnp.sum(jnp.where(lane_of(v.shape) == k, v, 0.0), axis=1, keepdims=True)


def decoder_back_kernel(place, got, grad, xhat, mid_x, vec, vec_two, sums, table, back_two, weights, fields, lows, below, below_x, shared, pay, more, first_x, kept_grad, mid, low_two, low_one, field_two, field_one, field_zero, back_one, sems, *, spots, local_count, pixel_count):
    all_off, skipped, off = place[0], place[3], place[4]
    height = field_two.shape[0] - 2
    far_rows, near_rows = pl.ds(skipped, grad.shape[0]), pl.ds(all_off, height + 2)
    fetched = copies(
        sems,
        (back_at(weights), back_one),
        (spots(fields, "xhat_one").at[far_rows], below_x),
        (spots(fields, "shared").at[far_rows], shared),
        (spots(lows, "hidden_three").at[near_rows], field_two),
        (spots(lows, "merged").at[near_rows], field_one),
        (spots(lows, "hidden_one").at[near_rows], field_zero),
    )
    handed = copies(sems.at[6:], (spots(fields, "xhat_zero").at[pl.ds(all_off, height)], first_x))
    devices = got.shape[0]
    rows = grad.shape[0]
    total = total_of(got, 0)
    shift, scale = spread(total, 0) / pixel_count, spread(total, 1) / pixel_count
    inverse, mean = vec[0:1], vec[1:2]
    factor = affine(table, 3)[0] * inverse
    slant = scale * inverse
    held, carried = factor * (shift - slant * mean), factor * slant
    links = got[0:CH, 2, 0, :] * groups(held, carried, held, carried)
    group = group_of(links.shape)
    mine = (lane_of(links.shape) & 31) == row_of(links.shape)

    def across(pick):
        column = jnp.sum(jnp.where(pick, links, 0.0), axis=1, keepdims=True)
        return col_sum(jnp.where(mine, column, 0.0))

    shift_two = spread(total, 2) - across(group < 2)
    scale_two = spread(total, 3) - across(group >= 2)
    entry = total_of(got, 3)
    notes(more, scale_two, shift_two, total_of(got, 4), total_of(got, 5), spread(entry, 1))

    def value(at, k):
        g = norm_back(grad[at, k], xhat[at, k], factor, shift, scale)
        kept_grad[at, k] = g
        return g

    back_rows(low_two, rows, value)

    @pl.when(place[0] >= 0)
    def _():
        mid[:, 0], mid[:, 1] = blocks_of(conv(low_two, back_two, 0, rows), rows)

    gain, bias = affine(table, 2)
    factor = gain * vec_two[0:1]
    shift, scale = shift_two / pixel_count, scale_two / pixel_count

    def value_two(at, k):
        x = mid_x[pl.ds(skipped + at.start, at.size), k]
        return norm_back(mid[at, k] * slope_at(x, gain, bias), x, factor, shift, scale)

    back_rows(low_one, rows, value_two)
    wait(fetched)
    sum_two = low_sum(low_two, off, height)
    sum_one = low_sum(low_one, off, height)
    y = conv(low_one, back_one, 0, rows)
    gain, bias = affine(table, 1)
    for k, y in enumerate(blocks_of(y, rows)):
        g = (y + kept_grad[:, k]).reshape(rows // 2, 2, -1, LANES)
        both = flat(g[:, 0] + g[:, 1])
        both = (both + partner(both)).reshape(rows // 2, 1, -1, LANES)
        g = g * slope_at(below_x[:, k], gain, bias).reshape(g.shape) + both * shared[:, k].reshape(g.shape)
        below[:, k] = g.reshape(rows, -1, LANES)
    shift_sum, scale_sum = own_sums(below, below_x, off, height)
    send(pay, groups(shift_sum, scale_sum, sum_one, sum_two))
    entry = spread(entry, 0)
    pay[:, 1, 0, :] = jnp.broadcast_to(entry, (devices, LANES))
    at = pl.ds(off + 1, height)
    last_two = tap_sums(field_two, own_lanes(low_two, at), 0, height, send_parts(pay, 2, 2))
    last_one = tap_sums(field_one, own_lanes(low_one, at), 0, height, send_parts(pay, 4, 2))
    centre = shift_sum / local_count
    at = pl.ds(off, height)
    grad = jnp.concatenate([flat(below[at, k] - centre).astype(BF16) for k in range(2)], axis=1)
    last_zero = tap_sums(field_zero, grad, 0, height, send_parts(pay, 6, 2), (centre, sums))
    pay[0:CH, 1, 0, :] = groups(last_two, last_one, last_zero, jnp.broadcast_to(entry, (CH, LANES)))
    wait(handed)


def summed_kernel(place, got, got_style, got_head, grad, xhat, shared, vec, more_two, table, w_style, sides, back, below_x, pay, more, below, grad_low, *, pixel_count, pool_cells, parts):
    off, mine = place[0], place[4]
    height = below.shape[0]
    devices = got.shape[0]
    rows = grad.shape[0]
    dims = (((1,), (1,)), ((), ()))
    first = row_of_each(got, 0)
    each = wide_dot(spread(first, 2), diagonal_blocks(w_style[0]), dims) + wide_dot(
        spread(first, 3), diagonal_blocks(w_style[1]), dims
    )
    each = each / pool_cells
    total = col_sum(first)
    shift = spread(total, 0) + col_sum(each * by_image(spread(row_of_each(got_style, 2), 1), parts))
    scale = spread(total, 1) + col_sum(each * by_image(spread(row_of_each(got_style, 2), 2), parts))
    style_grad = col_sum(jnp.where(row_of(each.shape) // parts == place[2] // parts, each, 0.0))
    factor = affine(table, 1)[0] * vec[0:1]
    shift_mean, scale_mean = shift / pixel_count, scale / pixel_count
    def value(at, k):
        return norm_back(grad[at, k] + shared[at, k] * style_grad, xhat[at, k], factor, shift_mean, scale_mean)

    back_rows(grad_low, rows, value)
    gain, bias = affine(table, 0)
    for k, y in enumerate(blocks_of(conv(grad_low, back, mine, height), height)):
        below[:, k] = y * slope_at(below_x[:, k], gain, bias)
    me = place[2]
    weights = at_lane(by_image(each, parts), me)
    hidden = spread(got[0:CH, 1, 0, :], 3)
    hidden = [groups(*[hidden[18 + t : 19 + t] for t in range(4 * q, min(4 * q + 4, 9))]) for q in range(3)]
    last = total_of(got, 1)
    direct = [total_of(got, 6), total_of(got, 7), spread(last, 2)]
    shares = [row_of_each(got_head, 6), row_of_each(got_head, 7), spread(row_of_each(got_head, 3), 2)]
    shard = []
    for q in range(3):
        val = direct[q] + col_sum(weights * shares[q])
        val = val - at_lane(shift_mean, me) * hidden[q] - at_lane(scale_mean, me) * more_two[2 + q : 3 + q]
        shard.append(at_lane(factor, me) * val)
    at = pl.ds(mine + 1, height)
    side = pixel_taps(sides, off + 1, height, own_lanes(grad_low, at), (0,))[0]
    low_below = own_lanes(below, pl.ds(0, height))
    taps = []
    for r in range(3):
        for tap in pixel_taps(sides, off + r, height, low_below, (-1, 0, 1)):
            taps.extend(tap)
    taps = [shard[2]] + taps + side
    send(
        pay,
        groups(*own_sums(below, below_x, 0, height), spread(last, 0), spread(last, 1)),
        *[total_of(got, r) for r in range(2, 6)],
        *shard[0:2],
        *[groups(*(taps[4 * q : 4 * q + 4] + [zero_row()])[0:4]) for q in range(6)],
    )
    notes(more, scale, shift)


def pixel_taps(sides, row, rows, grad, shift, alone=False):
    x = flat(sides[pl.ds(row, rows)])
    found = lax.dot_general(x, grad, (((0,), (0,)), ((), ())), preferred_element_type=F32)
    inside, channel, column = image_lanes((LANES, 2 * LANES))
    here = column - group_of((LANES, 2 * LANES))
    out = []
    for s in shift:
        both, bare = [], []
        for c in range(2):
            v = col_sum(jnp.where(inside & (channel == c) & (here == s), found[:, 0 : 2 * LANES], 0.0))
            both.append(fold(v[:, 0:LANES] + v[:, LANES:]))
            if alone:
                cut = slice(0, LANES)
                hit = (inside & (channel == c) & (column >= s) & (column < s + SEG))[:, cut]
                bare.append(col_sum(jnp.where(hit, found[:, 2 * LANES :], 0.0)))
        out.append((both, bare) if alone else both)
    return out


def adamw(master, moment, square, grad, rate):
    new_moment = beta_one * moment + (1.0 - beta_one) * grad
    new_square = beta_two * square + (1.0 - beta_two) * grad * grad
    moment_hat = new_moment / (1.0 - beta_one**STEP)
    square_hat = new_square / (1.0 - beta_two**STEP)
    new_master = master - rate * (moment_hat / (jnp.sqrt(square_hat) + adam_eps) + weight_decay * master)
    return new_master, new_moment, new_square


def put(at, refs, grad, rate, outs):
    found = adamw(*[ref[at] for ref in refs], grad, rate)
    for out, value in zip(outs, found + (found[0].astype(BF16),)):
        out[at] = value


def update_early(
    got_one_back, got_head, got_style, pay, style, w_style, w_head, m_style, m_head, s_style, s_head,
    loss_out, count_out, style_master, style_moment, style_square, head_master, head_moment, head_square, head_copy,
):
    count_out[0, 0] = jnp.sum(got_style[:, 2, 0, 3 * CH : 3 * CH + 1])
    loss_out[0, 0] = jnp.sum(got_head[:, 1, 0, 99:100])
    dims = (((0,), (0,)), ((), ()))
    for i in range(2):
        sums = spread(row_of_each(got_one_back, 0), 2 + i)
        grad = lax.dot_general(style[...], sums, dims, precision=highest, preferred_element_type=F32)
        put(i, (w_style, m_style, s_style), grad[0:CH, 0:CH], rate_table[2], (style_master, style_moment, style_square))

    head = total_of(got_head, 1)
    lane = lane_of((1, LANES))
    rows = []
    for k in range(3):
        last = jnp.sum(jnp.where(lane == 3 * CH + k, head, 0.0), axis=1, keepdims=True)
        rows.append(jnp.where(lane < CH, spread(head, k), last))
    grad = jnp.concatenate(rows, axis=0)[:, 0 : CH + 1]
    put(slice(None), (w_head, m_head, s_head), grad, rate_table[3], (head_master, head_moment, head_square, head_copy))


def update_late(
    got, got_one_back, got_head, more, more_two, vec, w_first, w_convs, table, m_first, m_convs, m_norms, s_first, s_convs, s_norms,
    first_master, first_moment, first_square, first_copy,
    convs_master, convs_moment, convs_square, convs_copy,
    norms_master, norms_moment, norms_square, *, pixel_count
):
    refs = (w_convs, m_convs, s_convs)
    outs = (convs_master, convs_moment, convs_square, convs_copy)
    packs = [[got[0:CH, k, 0, :].T for k in ks] for ks in ((5, 6, 7), (3, 4, 0), (1, 2, 0))]
    for i, pack in enumerate(packs):
        for t in range(9):
            b = t % 4 if t < 8 else (0, 3, 2)[i]
            put((i, t), refs, pack[t // 4][CH * b : CH * b + CH], rate_table[1], outs)

    zero_sums = total_of(got, 0)
    totals = [total_of(got, r) for r in range(7, 13)]
    shift, scale = spread(zero_sums, 0), spread(zero_sums, 1)
    factor = affine(table, 0)[0] * vec[0:1]
    by_x = spread(got_one_back[0:CH, 1, 0, :], 3)
    alone = total_of(got_head, 1)
    refs = (w_first, m_first, s_first)
    outs = (first_master, first_moment, first_square, first_copy)
    for t in range(10):
        pair = []
        for e in (2 * t, 2 * t + 1):
            k, b = divmod(1 + e, 4)
            v = spread(totals[k], b)
            if t < 9:
                v = factor * (v - (at_lane(alone, ALONE + e) * shift + by_x[e : e + 1] * scale) / pixel_count)
            pair.append(v[:, 0:CH])
        put(t, refs, jnp.concatenate(pair, axis=0), rate_table[0], outs)

    three_sums = total_of(got_head, 0)
    scales = [scale, more[0:1], more_two[0:1], spread(three_sums, 1)]
    shifts = [shift, more[1:2], more_two[1:2], spread(three_sums, 0)]
    for i, rows in enumerate((scales, shifts)):
        grad = jnp.concatenate(rows, axis=0)[:, 0:CH]
        put(i, (table, m_norms, s_norms), grad, rate_table[4], (norms_master, norms_moment, norms_square))


def update_kernel(*refs, pixel_count):
    ins, outs = refs[:23], refs[23:]
    late, early = ins[:15], ins[15:]
    update_late(*late, *outs[:11], pixel_count=pixel_count)
    update_early(late[1], late[2], early[0], None, *early[1:], *outs[11:])


def far(x):
    return ("far", x)


def call(kernel, outs, *operands, scalars=0, scratch=(), sems=0, scalar_outs=(), aliases=None, limit=VMEM_LIMIT, name):
    smem = pl.BlockSpec(memory_space=pltpu.SMEM)
    vmem = pl.BlockSpec(memory_space=pltpu.VMEM)
    hbm = pl.BlockSpec(memory_space=pltpu.HBM)
    is_far = lambda x: isinstance(x, tuple) and x[0] == "far"
    in_specs = [smem if i < scalars else hbm if is_far(x) else vmem for i, x in enumerate(operands)]
    out_specs = [smem if i in scalar_outs else hbm if is_far(x) else vmem for i, x in enumerate(outs)]
    plain = lambda x: x[1] if is_far(x) else x
    shapes = [pltpu.VMEM(shape, dtype) for shape, dtype in scratch]
    if sems:
        shapes.append(pltpu.SemaphoreType.DMA((sems,)))
    return pl.pallas_call(
        kernel,
        out_shape=[jax.ShapeDtypeStruct(*plain(x)) for x in outs],
        in_specs=in_specs,
        out_specs=out_specs,
        scratch_shapes=shapes,
        input_output_aliases=aliases or {},
        compiler_params=pltpu.CompilerParams(vmem_limit_bytes=limit),
        name=name,
    )(*[plain(x) for x in operands])


def exchange(pay):
    return lax.all_to_all(pay, ("row", "col"), 0, 0)


def local(
    image_batch, valid_mask, flow_target, cell_labels,
    w_first, w_convs, w_style, w_head, batch_norm_table,
    mom_first, mom_convs, mom_style, mom_head, mom_norms,
    sqr_first, sqr_convs, sqr_style, sqr_head, sqr_norms,
):
    images, block_rows, block_cols, _ = image_batch.shape
    row_count, col_count = lax.axis_size("row"), lax.axis_size("col")
    devices = row_count * col_count
    parts = devices // images
    image_rows, image_cols = row_count * block_rows, col_count * block_cols
    assert devices == parts * images and block_rows == RIM and block_cols == 2 * block_rows * 2
    assert image_rows % (parts * RIM) == 0 and devices >= CH
    height = image_rows // parts
    rows = min(image_rows, height + RIM * min(2, parts - 1))
    segments = image_cols // SEG
    local_count = float(height * image_cols)
    pixel_count = local_count * devices
    pool_cells = float(image_rows * image_cols // 4)
    part = functools.partial
    counts = dict(local_count=local_count, pixel_count=pixel_count, height=height)
    styled = dict(pool_cells=pool_cells, parts=parts)

    me = lax.axis_index("row") * col_count + lax.axis_index("col")
    first_row = (me % parts) * height
    start = jnp.clip(first_row - RIM, 0, image_rows - rows)
    off = first_row - start
    back_rim = RIM // 2
    rows_back = min(rows, height + back_rim * min(2, parts - 1))
    skipped = jnp.clip(off - back_rim, 0, rows - rows_back)
    place = jnp.stack([off, start // block_rows, me, skipped, off - skipped]).astype(jnp.int32)

    field = ((rows, 2, segments, LANES), F32)
    own_field = ((height,) + field[0][1:], F32)
    back_field = ((rows_back,) + field[0][1:], F32)
    low_field = ((rows + 2, 3, segments, LANES), BF16)
    own_low = ((height + 2,) + low_field[0][1:], BF16)
    back_low = ((rows_back + 2,) + low_field[0][1:], BF16)
    vec = ((8, LANES), F32)

    def payload(count):
        return ((devices, count, 1, LANES), F32)

    nine = ((BACK, 2 * LANES), BF16)
    ten = ((FORWARD, 2 * LANES), BF16)

    places = {
        name: i * count
        for count, names in (
            (rows, ("xhat_zero", "xhat_one", "shared")),
            (rows + 2, ("hidden_one", "hidden_three", "merged")),
        )
        for i, name in enumerate(names)
    }

    def spots(store, name):
        count = rows if name[0] in "xs" else rows + 2
        return store.at[places[name] : places[name] + count]

    def store_of(like):
        shape, dtype = like
        row_bytes = shape[1] * segments * LANES * jnp.dtype(dtype).itemsize
        return far(((-(-STORE_BYTES // row_bytes),) + shape[1:], dtype))

    inputs = (
        jnp.transpose(image_batch, (0, 1, 3, 2)), jnp.transpose(flow_target, (0, 1, 3, 2)), cell_labels, valid_mask
    )
    (pay,) = call(
        pack_kernel,
        [((devices, 16, LANES), BF16)],
        *[far(v) for v in inputs],
        scratch=[(v.shape, v.dtype) for v in inputs], sems=4, limit=WHOLE_VMEM, name="pack",
    )
    got_inputs = exchange(pay)
    head_rows = w_head.T
    weights, back_zero, back_two, head_mat = call(
        prepare,
        [far(((STORE_BYTES // (4 * LANES), 2 * LANES), BF16)), far(nine), far(nine), far(((2 * LANES, LANES), BF16))],
        far(w_first), far(w_convs), far(head_rows),
        scratch=[
            (w_first.shape, F32), (w_convs.shape, F32), (head_rows.shape, F32), ((BACK_AT + BACK, 2 * LANES), BF16),
            nine, nine, ((2 * LANES, LANES), BF16),
        ],
        sems=8, limit=WHOLE_VMEM, name="prepare",
    )

    sides, raw, pay, count, taps = call(
        part(start_kernel, local_count=local_count, height=height, sources=col_count),
        [((rows + 2, segments, LANES), BF16), field, payload(2), vec, ten],
        place, got_inputs, far(weights),
        scalars=1, scratch=[((3 * LANES, 2 * LANES), BF16)], sems=2, name="image_conv",
    )
    got_zero = exchange(pay)
    summed, pay, inv_zero, fields, lows = call(
        part(first_kernel, spots=spots, **counts),
        [field, payload(2), vec, store_of(field), store_of(low_field)],
        place, got_zero, raw, sides, batch_norm_table, taps,
        scalars=1, scratch=[low_field, field], sems=2, name="first_block",
    )
    got_one = exchange(pay)

    raw, pay, inv_one, merged, taps, fields, lows = call(
        part(pool_kernel, spots=spots, **counts),
        [field, payload(3), vec, low_field, nine, store_of(field), store_of(low_field)],
        place, got_one, summed, count, batch_norm_table, far(weights), far(fields), far(lows),
        scalars=1, scratch=[field, field, nine], sems=5,
        aliases={6: 5, 7: 6}, name="pool_and_merge",
    )
    got_style = exchange(pay)

    resid, pay, inv_two, style, xhat_two, ahead, hidden_sums, lows = call(
        part(style_kernel, spots=spots, **styled, **counts),
        [back_field, payload(3), vec, ((devices, LANES), F32), field, ((CH, 5, 1, LANES), F32), vec, store_of(low_field)],
        place, got_style, raw, merged, batch_norm_table, w_style, far(w_convs), taps, sides, far(fields),
        far(lows),
        scalars=1, scratch=[low_field, field, (w_convs.shape[1:], F32), own_field, own_field, own_field, own_low], sems=6,
        aliases={10: 7}, name="decoder",
    )
    got_three = exchange(pay)

    grad_three, xhat_three, pay, inv_three = call(
        part(head_kernel, **counts),
        [back_field, back_field, payload(8), vec],
        place, got_three, got_style, resid, sides, head_mat, head_rows, xhat_two, ahead, hidden_sums, batch_norm_table, back_two,
        scalars=1, scratch=[((rows_back, 2, segments, LANES), BF16), back_field, back_low], name="head",
    )
    got_head = exchange(pay)

    grad_one, xhat_one, shared, pay, more_two, xhat_zero = call(
        part(decoder_back_kernel, spots=spots, local_count=local_count, pixel_count=pixel_count),
        [back_field, back_field, back_field, payload(8), vec, own_field],
        place, got_head, grad_three, xhat_three, xhat_two, inv_three, inv_two, hidden_sums, batch_norm_table, back_two, far(weights),
        far(fields), far(lows),
        scalars=1, scratch=[back_field, back_field, back_low, back_low, own_low, own_low, own_low, nine], sems=7,
        name="decoder_back",
    )
    got_one_back = exchange(pay)

    pay, more = call(
        part(summed_kernel, pixel_count=pixel_count, **styled),
        [payload(13), vec],
        place, got_one_back, got_style, got_head, grad_one, xhat_one, shared, inv_one, more_two, batch_norm_table, w_style,
        sides, back_zero, xhat_zero,
        scalars=1, scratch=[own_field, back_low], name="summed_back",
    )
    got_last = exchange(pay)

    def results(param, copy):
        return [(param.shape, F32)] * 3 + [(param.shape, BF16)] * copy

    found = call(
        part(update_kernel, pixel_count=pixel_count),
        results(w_first, 1)
        + results(w_convs, 1)
        + results(batch_norm_table, 0)
        + [((1, 1), F32), ((1, 1), F32)]
        + results(w_style, 0)
        + results(head_rows, 1),
        got_last, got_one_back, got_head, more, more_two, inv_zero,
        w_first, w_convs, batch_norm_table, mom_first, mom_convs, mom_norms, sqr_first, sqr_convs, sqr_norms,
        got_style, style, w_style, head_rows, mom_style, mom_head.T, sqr_style, sqr_head.T,
        scalar_outs=(11, 12), name="update",
    )
    late, early = found[:11], found[11:]
    loss, count = early[0].reshape(()), early[1].reshape(())
    head = tuple(value.T for value in early[5:9])
    return (loss, count, *late[0:8], *early[2:5], *head, *late[8:11])


def solution(mesh):
    field = P(None, "row", "col", None)
    plane = P(None, "row", "col")
    return jax.shard_map(
        local,
        mesh=mesh,
        in_specs=(field, plane, field, plane) + (P(),) * 15,
        out_specs=(P(),) * 20,
        check_vma=False,
    )
```

```python
import functools

import jax
import jax.numpy as jnp
from jax import lax
from jax.experimental import pallas as pl
from jax.experimental.pallas import tpu as pltpu
from jax.sharding import PartitionSpec as P

STEP = 5

highest = lax.Precision.HIGHEST
norm_eps = 1e-05
flow_scale = 32.0
adam_eps = 1e-08
weight_decay = 0.01
beta_one = 0.5
beta_two = 0.5
rate_table = (0.2, 0.05, 0.15, 0.15, 0.2)

CH = 32
GRP = 4
SEG = 8
LANES = 128
RIM = 8
FLOW, LABEL, MASK = 16, 32, 40
LEFT, RIGHT = 64, 96
ALONE = 100
AFTER, ROW, BEFORE = 32, 33, 64
F32 = jnp.float32
BF16 = jnp.bfloat16
VMEM_LIMIT = 36 * 1024 * 1024
WHOLE_VMEM = 56 * 1024 * 1024
STORE_BYTES = 32 * 1024 * 1024
FORWARD = 10 * LANES
BACK = 9 * LANES
IMAGE_AT = 3 * FORWARD
BACK_AT = IMAGE_AT + 3 * LANES


def lane_of(shape):
    return lax.broadcasted_iota(jnp.int32, shape, len(shape) - 1)


def row_of(shape):
    return lax.broadcasted_iota(jnp.int32, shape, 0)


def group_of(shape):
    return lane_of(shape) >> 5


def fold(v):
    return v + pltpu.roll(v, 32, axis=1) + (pltpu.roll(v, 64, axis=1) + pltpu.roll(v, 96, axis=1))


def spread(v, k):
    return fold(jnp.where(group_of(v.shape) == k, v, 0.0))


def partner(v):
    odd = (group_of(v.shape) & 1) == 1
    return jnp.where(odd, pltpu.roll(v, 32, axis=1), pltpu.roll(v, 96, axis=1))


def tile4(v):
    return jnp.concatenate([v, v, v, v], axis=1)


def col_sum(v):
    return jnp.sum(v, axis=0, keepdims=True)


def zero_row():
    return jnp.zeros((1, LANES), F32)


def groups(*values):
    group = group_of(values[0].shape)
    out = values[-1]
    for k in range(len(values) - 2, -1, -1):
        out = jnp.where(group == k, values[k], out)
    return out


def low(v):
    return v.astype(BF16).astype(F32)


def sig_of(v):
    return 0.5 + 0.5 * jnp.tanh(0.5 * v)


def slope(n, sig):
    return sig * (1.0 + n * (1.0 - sig))


def slope_at(x, gain, bias):
    n = x * gain + bias
    return slope(n, sig_of(n))


def flat(v):
    return v.reshape(-1, LANES)


def loop(count, body, unroll=5):
    def step(i, carry):
        body(i)
        return carry

    lax.fori_loop(0, count, step, 0, unroll=min(count, unroll))


def copies(sems, *pairs):
    found = []
    for i, (source, target) in enumerate(pairs):
        found.append(pltpu.make_async_copy(source, target, sems.at[i]))
        found[-1].start()
    return found


def wait(started):
    for copy in started:
        copy.wait()


def shift_segments(v, way):
    half = v.shape[1]
    at = lax.broadcasted_iota(jnp.int32, v.shape, 1)
    if way == 1:
        return jnp.where(at == 0, 0.0, pltpu.roll(v, 1, axis=1))
    return jnp.where(at == half - 1, 0.0, pltpu.roll(v, half - 1, axis=1))


def beside(first, second):
    half = first.shape[1] // 2
    left = jnp.concatenate([shift_segments(second[:, half:], 1), second[:, :half]], axis=1)
    right = jnp.concatenate([first[:, half:], shift_segments(first[:, :half], -1)], axis=1)
    return left, right


def put_low(ref, row, first, second, marked=False):
    left, right = beside(first, second)
    lane = lane_of(left.shape)
    edge = jnp.where(lane < 64, right, left)
    if marked:
        at = lax.broadcasted_iota(jnp.int32, left.shape, 1)
        edge = jnp.where(lane == ROW, 1.0, edge)
        edge = jnp.where(lane == AFTER, jnp.where(at == left.shape[1] - 1, 0.0, 1.0), edge)
        edge = jnp.where(lane == BEFORE, jnp.where(at == 0, 0.0, 1.0), edge)
    at = pl.ds(row + 1, first.shape[0])
    for k, v in enumerate((first, second, edge)):
        ref[at, k] = v.astype(BF16)


def blank(ref):
    zero = jnp.zeros((1,) + ref.shape[1:], ref.dtype)
    ref[0:1] = zero
    ref[ref.shape[0] - 1 : ref.shape[0]] = zero


def views(src, row, rows):
    return [flat(src[pl.ds(row + r, rows), k]) for r in range(3) for k in (2, 0, 1)]


def conv(src, mat, row, rows, *more):
    wide = jnp.concatenate(views(src, row, rows) + list(more), axis=1)
    return jnp.dot(wide, mat[...], preferred_element_type=F32)


def blocks_of(y, rows):
    return [y[:, k * LANES : (k + 1) * LANES].reshape(rows, -1, LANES) for k in range(2)]


def narrow(v):
    while v.shape[0] > 1:
        half = v.shape[0] // 2
        v = v[:half] + v[half:]
    return v[0]


def row_sums(first, rows, values):
    step = 4

    def add(i, carry):
        found = [values(pl.ds(first + step * i, step), k) for k in range(2)]
        return tuple(c + a + b for c, a, b in zip(carry, *found))

    shapes = jax.eval_shape(lambda: values(pl.ds(0, step), 0))
    zeros = tuple(jnp.zeros(v.shape, F32) for v in shapes)
    found = lax.fori_loop(0, rows // step, add, zeros, unroll=min(rows // step, 8))
    return [col_sum(narrow(v)) for v in found]


def local_stats(v, first, rows, count):
    count = count / GRP
    pivot = col_sum(v[first, 0] + v[first, 1]) / (2 * v.shape[2])

    def moments(at, k):
        away = v[at, k] - pivot
        return away, away * away

    total, square = row_sums(first, rows, moments)
    return pivot + total / count, square - total * (total / count)


def merge_stats(means, squares, local_count, pixel_count):
    mean = fold(col_sum(means)) / (GRP * means.shape[0])
    away = means - mean
    total = fold(col_sum(squares + (local_count / GRP) * (away * away)))
    return mean, lax.rsqrt(total / pixel_count + norm_eps)


def row_of_each(got, r):
    return got[:, r, 0, :]


def total_of(got, r):
    return col_sum(row_of_each(got, r))


def send(pay, *rows):
    for r, row in enumerate(rows):
        pay[:, r, 0, :] = jnp.broadcast_to(row, (pay.shape[0], LANES))


def send_parts(pay, first, count):
    devices = pay.shape[0]
    if devices > CH:
        for r in range(first, first + count):
            pay[CH:, r, 0, :] = jnp.zeros((devices - CH, LANES), F32)
    return pay.at[0:CH, first : first + count, 0]


def affine(table, q):
    return tile4(table[0, q : q + 1, :]), tile4(table[1, q : q + 1, :])


def diagonal_blocks(mat):
    wide = tile4(mat)
    group = group_of(wide.shape)
    return jnp.concatenate([jnp.where(group == b, wide, 0.0) for b in range(GRP)], axis=0)


def notes(ref, *rows):
    for i, row in enumerate(rows):
        ref[i : i + 1, :] = row


def taps_at(store, i):
    return store.at[FORWARD * i : FORWARD * i + (BACK if i else FORWARD)]


def image_at(store):
    return store.at[IMAGE_AT : IMAGE_AT + 3 * LANES]


def back_at(store):
    return store.at[BACK_AT : BACK_AT + BACK]


def pack_kernel(image_in, flow_in, labels_in, valid_in, out, image, flow, labels, valid, sems):
    fetched = copies(sems, (image_in, image), (flow_in, flow), (labels_in, labels), (valid_in, valid))
    images, height, _, width = image.shape
    parts = out.shape[0] // images
    wait(fetched)
    fields = [image[:, :, c, :].astype(F32) for c in range(2)]
    fields += [flow[:, :, c, :].astype(F32) for c in range(2)]
    fields += [labels[...].astype(F32), valid[...].astype(F32)]
    halves = width // 16
    shape = (width, halves * LANES)
    lane = lane_of(shape)
    column = (lane >> 7) * 16 + ((lane >> 6) & 1) * 8 + (lane & 7)
    hit = row_of(shape) == column
    which = (lane >> 3) & 7
    total = jnp.zeros((images * height, halves * LANES), F32)
    for k, v in enumerate(fields):
        x = v.reshape(images * height, width).astype(BF16)
        mat = jnp.where(hit & (which == k), 1.0, 0.0).astype(BF16)
        total = total + jnp.dot(x, mat, preferred_element_type=F32)
    for b in range(images):
        rows = total[b * height : (b + 1) * height]
        slot = jnp.concatenate([rows[:, h * LANES : (h + 1) * LANES] for h in range(halves)], axis=0).astype(BF16)
        for p in range(parts):
            out[b * parts + p] = slot


COLUMNS = ((8, None, None, -1), (0, 1, 2, 3), (4, 5, 6, 7))


def conv_matrix(taps, mats, base, back):
    out_at = group_of((CH, 2 * LANES))
    for r in range(3):
        wide = []
        for s in range(3):
            if back:
                k = taps[3 * (2 - r) + s]
                k = jnp.concatenate([k, k, k, k], axis=0).T
            else:
                k = tile4(taps[3 * r + s])
            wide.append(jnp.concatenate([k, k], axis=1))
        for d in range(3):
            for a in range(GRP):
                val = jnp.zeros((CH, 2 * LANES), F32)
                column = COLUMNS[d][a]
                if column is not None:
                    for s in range(3):
                        val = jnp.where(out_at == (column + s - 1 if back else column + 1 - s), wide[s], val)
                mats[pl.ds(base + (3 * r + d) * LANES + CH * a, CH), :] = val.astype(BF16)


def image_lanes(shape):
    at = row_of(shape)
    kind = at >> 5
    column = (at & 7) + jnp.where(kind == LEFT // 32, -SEG, jnp.where(kind == RIGHT // 32, SEG, 0))
    return (kind != 1) & ((at & 31) < 16), (at >> 3) & 1, column


def first_taps(w_first, t):
    found = [tile4(low(w_first[t][c : c + 1])) for c in range(2)]
    return [jnp.concatenate([v, v], axis=1) for v in found]


def image_matrix(w_first, r):
    shape = (LANES, 2 * LANES)
    inside, channel, here = image_lanes(shape)
    val = jnp.zeros(shape, F32)
    for s in range(3):
        for c, tap in enumerate(first_taps(w_first, 3 * r + s)):
            val = jnp.where(inside & (channel == c) & (here == group_of(shape) + s - 1), tap, val)
    return val.astype(BF16)


def prepare(w_first_in, w_convs_in, w_head_in, store, back_zero_out, back_two_out, head_out, w_first, w_convs, w_head, mats, back_zero, back_two, head_mat, sems):
    wait(copies(sems, (w_first_in, w_first), (w_convs_in, w_convs), (w_head_in, w_head)))
    stored = []

    def keep(source, target):
        stored.extend(copies(sems.at[len(stored) :], (source, target)))

    for i, back, out in ((2, back_two, back_two_out), (0, back_zero, back_zero_out)):
        conv_matrix(w_convs.at[i], back, 0, True)
        keep(back, out)
    conv_matrix(w_convs.at[1], mats, BACK_AT, True)
    keep(back_at(mats), back_at(store))
    shape = (LANES, 2 * LANES)
    inside, channel, here = image_lanes(shape)
    val = jnp.zeros(shape, F32)
    for c, tap in enumerate(first_taps(w_first, 9)):
        val = jnp.where((row_of(shape) < 16) & (channel == c) & (here == group_of(shape)), tap, val)
    mats[BACK:FORWARD, :] = val.astype(BF16)
    for i in range(3):
        conv_matrix(w_convs.at[i], mats, FORWARD * i, False)
        keep(taps_at(mats, i), taps_at(store, i))
    for r in range(3):
        mats[IMAGE_AT + LANES * r : IMAGE_AT + LANES * (r + 1), :] = image_matrix(w_first, r)
    keep(image_at(mats), image_at(store))
    lane = lane_of((CH, LANES))
    head = jnp.zeros((CH, LANES), F32)
    diagonal = row_of((CH, CH)) == lane_of((CH, CH))
    for k in range(3):
        column = jnp.sum(jnp.where(diagonal, low(w_head[k : k + 1, 0:CH]), 0.0), axis=1, keepdims=True)
        head = jnp.where((lane >> 3) == FLOW // 8 + k, column, head)
    for y in range(SEG):
        head_mat[CH * y : CH * (y + 1), :] = jnp.where((lane & 7) == y, head, 0.0).astype(BF16)
    keep(head_mat, head_out)
    wait(stored)


def start_kernel(place, got, weights, sides, raw, pay, vec, taps, first_mat, sems, *, local_count, height, sources):
    fetched = copies(sems, (image_at(weights), first_mat), (taps_at(weights, 0), taps))
    rows, segments = raw.shape[0], raw.shape[2]
    off, block = place[0], place[1]
    blank(sides)

    def eight(t):
        v = got[pl.ds((block + t) * sources, sources)].astype(F32)
        v = jnp.swapaxes(v.reshape(segments // 2, 8, LANES), 0, 1)
        near = lane_of(v.shape) < 64
        v = jnp.concatenate([jnp.where(near, v, 0.0), jnp.where(near, pltpu.roll(v, 64, axis=2), 0.0)], axis=1)
        pixels = jnp.where(lane_of(v.shape) < 16, v, 0.0)
        left, right = beside(pixels, pixels)
        v = v + pltpu.roll(left, LEFT, axis=2) + pltpu.roll(right, RIGHT, axis=2)
        sides[pl.ds(8 * t + 1, 8)] = v.astype(BF16)

    loop(rows // 8, eight)
    wait(fetched[:1])
    y = None
    for r in range(3):
        part = jnp.dot(flat(sides[r : r + rows]), first_mat[LANES * r : LANES * (r + 1)], preferred_element_type=F32)
        y = part if y is None else y + part
    raw[:, 0], raw[:, 1] = blocks_of(y, rows)
    mean, square = local_stats(raw, off, height, local_count)
    mask = jnp.zeros(sides.shape[1:], F32)
    for i in range(height):
        mask = mask + sides[off + 1 + i].astype(F32)
    lane = lane_of(mask.shape)
    count = jnp.sum(jnp.where((lane >= MASK) & (lane < MASK + 8), mask, 0.0))
    send(pay, mean, square)
    notes(vec, jnp.full((1, LANES), count, F32))
    wait(fetched[1:])


def first_kernel(place, got, raw, sides, table, taps, summed, pay, vec, fields, lows, hidden, xhat, sems, *, spots, local_count, pixel_count, height):
    mean, inverse = merge_stats(row_of_each(got, 0), row_of_each(got, 1), local_count, pixel_count)
    notes(vec, inverse)
    gain, bias = affine(table, 0)
    rows = raw.shape[0]

    def norm_rows(i):
        at = pl.ds(4 * i, 4)
        out = []
        for k in range(2):
            x = (raw[at, k] - mean) * inverse
            xhat[at, k] = x
            n = x * gain + bias
            out.append(n * sig_of(n))
        put_low(hidden, 4 * i, *out)

    blank(hidden)
    loop(rows // 4, norm_rows)
    stored = copies(sems, (xhat, spots(fields, "xhat_zero")), (hidden, spots(lows, "hidden_one")))

    @pl.when(place[0] >= 0)
    def _():
        y = conv(hidden, taps, 0, rows, flat(sides[1 : rows + 1]))
        summed[:, 0], summed[:, 1] = blocks_of(y, rows)

    send(pay, *local_stats(summed, place[0], height, local_count))
    wait(stored)


def pool_kernel(place, got, summed, count_in, table, weights, fields_in, lows_in, raw, pay, vec, merged, taps_next, fields, lows, xhat, shared, taps, sems, *, spots, local_count, pixel_count, height):
    fetched = copies(sems, (taps_at(weights, 1), taps), (taps_at(weights, 2), taps_next))
    mean, inverse = merge_stats(row_of_each(got, 0), row_of_each(got, 1), local_count, pixel_count)
    gain, bias = affine(table, 1)
    rows, segments = summed.shape[0], summed.shape[2]
    off = place[0]

    step = 4

    def some(i, carry):
        at = pl.ds(step * i, step)
        pairs = (step // 2, 2, segments, LANES)
        outs, sums = [], [jnp.zeros((step // 2 * segments, LANES), F32) for _ in range(3)]
        for k in range(2):
            x = (summed[at, k] - mean) * inverse
            n = x * gain + bias
            sig = sig_of(n)
            e = (n * sig).reshape(pairs)
            top = flat(jnp.maximum(e[:, 0], e[:, 1]))
            top = jnp.maximum(top, partner(top))
            wide_top = top.reshape(step // 2, 1, segments, LANES)
            exps = jnp.exp(e - wide_top)
            whole = flat(exps[:, 0] + exps[:, 1])
            whole = whole + partner(whole)
            pooled = top + jnp.log(whole)
            outs.append((e + pooled.reshape(wide_top.shape)).reshape(step, segments, LANES))
            share = exps * (1.0 / whole).reshape(wide_top.shape) * slope(n, sig).reshape(pairs)
            share_x = share * x.reshape(pairs)
            xhat[at, k] = x
            shared[at, k] = share.reshape(step, segments, LANES)
            sums[0] = sums[0] + pooled
            sums[1] = sums[1] + flat(share[:, 0] + share[:, 1])
            sums[2] = sums[2] + flat(share_x[:, 0] + share_x[:, 1])
        put_low(merged, step * i, *outs)
        mine = (step * i >= off) & (step * i < off + height)
        keep = jnp.where(mine, 1.0, 0.0)
        return tuple(a + keep * b for a, b in zip(carry, sums))

    blank(merged)
    zero = jnp.zeros((step // 2 * segments, LANES), F32)
    sums = lax.fori_loop(0, rows // step, some, (zero, zero, zero), unroll=min(rows // step, 5))
    pool_sum, share_sum, share_x = [fold(col_sum(v)) for v in sums]
    stored = copies(
        sems.at[2:],
        (xhat, spots(fields, "xhat_one")),
        (shared, spots(fields, "shared")),
        (merged, spots(lows, "merged")),
    )
    wait(fetched)
    raw[:, 0], raw[:, 1] = blocks_of(conv(merged, taps, 0, rows), rows)
    mean, square = local_stats(raw, place[0], height, local_count)
    send(pay, mean, square, groups(0.5 * pool_sum, share_sum, share_x, count_in[0:1]))
    notes(vec, inverse)
    wait(stored)


def by_image(v, parts):
    devices = v.shape[0]
    step = 1
    while step < parts:
        upper = (row_of(v.shape) // step) % 2 == 1
        v = v + jnp.where(upper, pltpu.roll(v, step, axis=0), pltpu.roll(v, devices - step, axis=0))
        step *= 2
    return v


def wide_dot(a, b, dims=(((1,), (0,)), ((), ()))):
    (a_high, a_low), (b_high, b_low) = [[v.astype(BF16) for v in in_parts(x, 2)] for x in (a, b)]
    axis_a, axis_b = dims[0][0][0], dims[0][1][0]
    left = jnp.concatenate([a_high, a_high, a_low], axis=axis_a)
    right = jnp.concatenate([b_high, b_low, b_high], axis=axis_b)
    return lax.dot_general(left, right, dims, preferred_element_type=F32)


def in_parts(v, count):
    out = []
    for _ in range(count):
        out.append(low(v))
        v = v - out[-1]
    return out


def mine_of(v, me):
    return col_sum(jnp.where(row_of(v.shape) == me, v, 0.0))


def style_kernel(place, got, raw, merged, table, w_style, w_convs_in, taps, sides, fields, lows_in, resid, pay, vec, style_out, xhat, ahead, sums, lows, hidden, slopes, w_conv, zero_x, one_x, shared, field, sems, *, spots, local_count, pixel_count, pool_cells, height, parts):
    own = pl.ds(place[0], height)
    fetched = copies(
        sems,
        (w_convs_in.at[2], w_conv),
        (spots(fields, "xhat_zero").at[own], zero_x),
        (spots(fields, "xhat_one").at[own], one_x),
        (spots(fields, "shared").at[own], shared),
        (spots(lows_in, "hidden_one").at[pl.ds(place[0], height + 2)], field),
    )
    style = by_image(spread(row_of_each(got, 2), 0), parts) / pool_cells
    style_out[...] = style
    one, two = [
        wide_dot(style, diagonal_blocks(w_style[i])) for i in range(2)
    ]
    mean, inverse = merge_stats(row_of_each(got, 0) + one, row_of_each(got, 1), local_count, pixel_count)
    notes(vec, inverse)
    gain, bias = affine(table, 2)
    rows, kept = raw.shape[0], resid.shape[0]
    off, skipped, mine = place[0], place[3], place[4]
    me = place[2]
    shift = mine_of(one, me) - mean
    two = mine_of(two, me)

    def norm_rows(i):
        at = pl.ds(4 * i, 4)
        out = []
        for k in range(2):
            x = (raw[at, k] + shift) * inverse
            xhat[at, k] = x
            n = x * gain + bias
            sig = sig_of(n)
            slopes[at, k] = slope(n, sig)
            out.append(n * sig)
        put_low(hidden, 4 * i, *out)

    blank(hidden)
    loop(rows // 4, norm_rows)
    stored = copies(sems.at[5:], (hidden, spots(lows, "hidden_three")))

    @pl.when(place[0] >= 0)
    def _():
        for k, y in enumerate(blocks_of(conv(hidden, taps, skipped, kept), kept)):
            resid[:, k] = y + two + merged[pl.ds(skipped + 1, kept), k].astype(F32)

    wait(fetched + stored)
    hidden[kept + 1 : kept + 2] = jnp.zeros((1,) + hidden.shape[1:], BF16)
    centre = fold(col_sum(resid[mine, 0] + resid[mine, 1])) / (SEG * raw.shape[2])
    at = pl.ds(off, height)
    probe = [slopes[at, k] for k in range(2)]
    probe += [slopes[at, k] * xhat[at, k] for k in range(2)]
    probe = jnp.concatenate([flat(v).astype(BF16) for v in probe], axis=1)

    def centred(i):
        at = pl.ds(4 * i, 4)
        put_low(hidden, 4 * i, resid[at, 0] - centre, resid[at, 1] - centre, True)

    loop(kept // 4, centred)
    links = norm_links(hidden, probe, mine, height, w_conv, centre)
    send(pay, *local_stats(resid, mine, height, local_count))
    send_parts(pay, 2, 1)[:, 0, :] = links
    put_ahead(off, sides, ahead, sums, zero_x, one_x, shared, field, local_count)


def norm_links(field, probe, first, rows, taps, centre):
    wide = jnp.concatenate(views(field, first, rows), axis=1)
    found = lax.dot_general(probe, wide, (((0,), (0,)), ((), ())), preferred_element_type=F32)
    group = group_of((CH, LANES))
    out = []
    for half in range(2):

        def piece(y, chunk):
            at = 2 * LANES * half + CH * y
            return found[at : at + CH, chunk * LANES : (chunk + 1) * LANES]

        plain = jnp.zeros((CH, LANES), F32)
        moved = jnp.zeros((CH, LANES), F32)
        for r in range(3):
            first_edge, last_edge = piece(0, 3 * r), piece(SEG - 1, 3 * r)
            edge = first_edge + last_edge
            for y in range(1, SEG - 1):
                edge = edge + piece(y, 3 * r)
            inside = edge[:, ROW : ROW + 1]
            counts = (
                inside + (first_edge[:, BEFORE : BEFORE + 1] - first_edge[:, ROW : ROW + 1]),
                inside,
                inside + (last_edge[:, AFTER : AFTER + 1] - last_edge[:, ROW : ROW + 1]),
            )
            for c in range(3):
                tap = tile4(low(taps[3 * (2 - r) + 2 - c]))
                val = jnp.zeros((CH, LANES), F32)
                for y in range(SEG):
                    d, a = spot_of(y + c - 1)
                    val = val + jnp.where(group == a, piece(y, 3 * r + d), 0.0)
                plain = plain + tap * counts[c]
                moved = moved + tap * val
        out += [plain, fold(moved) + centre * plain]
    return groups(*out)


def spot_of(x):
    if x < 0:
        return 0, 3
    if x == SEG:
        return 0, 0
    return 1 + x // GRP, x % GRP


def put_ahead(off, sides, out, sums, below_x, xhat, shared, field, local_count):
    height = xhat.shape[0]
    at = pl.ds(0, height)
    low_x = jnp.concatenate([own_lanes(below_x, at), jnp.ones((height * field.shape[2], LANES), BF16)], axis=1)
    entries, alone = [], zero_row()
    lane = lane_of((1, LANES))
    for r in range(3):
        for tap, bare in pixel_taps(sides, off + r, height, low_x, (-1, 0, 1), True):
            for v, b in zip(tap, bare):
                alone = jnp.where(lane == ALONE + len(entries), b, alone)
                entries.append(v)
    centres = [fold(v) / local_count for v in row_sums(0, height, lambda at, k: (xhat[at, k], shared[at, k]))]
    probe = [flat(v[at, k] - c).astype(BF16) for v, c in zip((xhat, shared), centres) for k in range(2)]
    wide = jnp.concatenate(views(field, 0, height), axis=1)
    found = lax.dot_general(
        jnp.concatenate(probe, axis=1), wide, (((0,), (0,)), ((), ())), preferred_element_type=F32
    )
    ones = jnp.ones((8, wide.shape[0]), BF16)
    plain = jnp.dot(ones, wide, preferred_element_type=F32)[0:1]
    group = group_of((1, LANES))
    hidden = []
    for r in range(3):
        for s in range(3):
            val = zero_row()
            for y in range(SEG):
                d, a = spot_of(y + s - 1)
                spot = (3 * r + d) * LANES
                val = val + jnp.where(group == a, plain[:, spot : spot + LANES], 0.0)
            hidden.append(fold(val))
    packed = [groups(*hidden[0:4]), groups(*hidden[4:8]), hidden[8]]
    all_hidden = jnp.concatenate(packed, axis=0)
    last = [
        put_taps(
            found[2 * LANES * k : 2 * LANES * (k + 1)], out.at[:, 2 * k + 1 : 2 * k + 3, 0], (centres[k], all_hidden)
        )
        for k in range(2)
    ]
    entries += hidden
    entries.append(jnp.zeros((CH - len(entries), LANES), F32))
    out[:, 0, 0, :] = groups(jnp.concatenate(entries, axis=0), *last, jnp.zeros((CH, LANES), F32))
    notes(sums, *packed, alone)


def head_kernel(place, got, got_style, resid, sides, head_mat, w_head, below_x, ahead, image_sums, table, back, grad, xhat, pay, vec, decoded, slopes, grad_low, *, local_count, pixel_count, height):
    mean, inverse = merge_stats(row_of_each(got, 0), row_of_each(got, 1), local_count, pixel_count)
    notes(vec, inverse, mean)
    gain, bias = affine(table, 3)
    rows, segments = resid.shape[0], resid.shape[2]
    all_off, skipped, off = place[0], place[3], place[4]

    def norm_rows(i):
        at = pl.ds(4 * i, 4)
        for k in range(2):
            x = (resid[at, k] - mean) * inverse
            n = x * gain + bias
            s = sig_of(n)
            xhat[at, k] = x
            slopes[at, k] = slope(n, s)
            decoded[at, k] = (n * s).astype(BF16)

    loop(rows // 4, norm_rows, 10)
    head = head_mat[...]
    wide = jnp.concatenate([flat(decoded[:, 0]), flat(decoded[:, 1])], axis=1)
    bias_row = zero_row()
    for k in range(3):
        mine = (lane_of((1, LANES)) >> 3) == FLOW // 8 + k
        bias_row = jnp.where(mine, low(w_head[k : k + 1, CH : CH + 1]), bias_row)
    out = jnp.dot(wide, head, preferred_element_type=F32) + bias_row
    given = flat(sides[pl.ds(skipped + 1, rows)]).astype(F32)
    lane = lane_of(given.shape)
    is_flow = lane < LABEL
    near = [pltpu.roll(given, LANES - MASK + first, axis=1) for first in (FLOW, FLOW + 8, LABEL)]
    mask = jnp.where(lane < FLOW + 8, near[0], jnp.where(is_flow, near[1], near[2]))
    mask = jnp.where((lane >= FLOW) & (lane < LABEL + 8), mask, 0.0)
    count = jnp.sum(got_style[:, 2, 0, 3 * CH : 3 * CH + 1])
    diff = out - given / flow_scale
    hinge = jnp.maximum(out, 0.0) + jnp.log1p(jnp.exp(-jnp.abs(out)))
    loss = mask * jnp.where(is_flow, diff * diff, hinge - given * out)
    grad_out = (mask * jnp.where(is_flow, 2.0 * diff, sig_of(out) - given) / count).astype(BF16)
    at_row = lax.broadcasted_iota(jnp.int32, loss.shape, 0)
    inside = (at_row >= off * segments) & (at_row < (off + height) * segments)
    loss_sum = jnp.sum(jnp.where(inside, loss, 0.0))
    mine_out = jnp.where(inside, grad_out.astype(F32), 0.0).astype(BF16)
    outs = col_sum(mine_out.astype(F32))
    found = lax.dot_general(mine_out, wide, (((0,), (0,)), ((), ())), preferred_element_type=F32)
    shape = found.shape
    found = jnp.where((row_of(shape) & 7) == group_of(shape), found, 0.0)
    whole = [col_sum(found[FLOW + 8 * k : FLOW + 8 * k + 8]) for k in range(3)]
    whole = [fold(v[:, 0:LANES] + v[:, LANES:]) for v in whole]
    row = groups(*whole, zero_row())
    lane = lane_of((1, LANES))
    for k in range(3):
        row = jnp.where(lane == 3 * CH + k, jnp.sum(jnp.where((lane >> 3) == FLOW // 8 + k, outs, 0.0)), row)
    row = jnp.where(lane == 3 * CH + 3, loss_sum, row)
    y = lax.dot_general(grad_out, head, (((1,), (1,)), ((), ())), preferred_element_type=F32)
    for k, g in enumerate(blocks_of(y, rows)):
        grad[:, k] = g * slopes[:, k]
    factor = gain * inverse
    back_rows(grad_low, rows, lambda at, k: factor * grad[at, k], 10)
    shift_sum, scale_sum = own_sums(grad, xhat, off, height)
    y = conv(grad_low, back, off, height)
    slopes[0:height, 0], slopes[0:height, 1] = blocks_of(y, height)
    gain, bias = affine(table, 2)

    def links(at, k):
        x = below_x[pl.ds(all_off + at.start, at.size), k]
        g = slopes[at, k] * slope_at(x, gain, bias)
        return g, g * x

    below = [fold(v) for v in row_sums(0, height, links)]
    send(pay, groups(shift_sum, scale_sum, *below), row + image_sums[3:4], total_of(got, 2))
    send_parts(pay, 3, 5)
    pay[0:CH, 3:8] = ahead[...]


def own_sums(grad, xhat, first, rows):
    def both(at, k):
        g = grad[at, k]
        return g, g * xhat[at, k]

    return [fold(v) for v in row_sums(first, rows, both)]


def back_sums(got, pixel_count):
    whole = col_sum(got)
    return spread(whole, 0) / pixel_count, spread(whole, 1) / pixel_count


def low_sum(grad_low, first, rows):
    return fold(row_sums(first + 1, rows, lambda at, k: (grad_low[at, k].astype(F32),))[0])


def norm_back(grad, xhat, factor, shift, scale):
    return factor * (grad - (shift + xhat * scale))


def back_rows(grad_low, rows, value, unroll=5):
    def some(i):
        put_low(grad_low, 4 * i, *[value(pl.ds(4 * i, 4), k) for k in range(2)])

    blank(grad_low)
    loop(rows // 4, some, unroll)


def own_lanes(grad, at):
    return jnp.concatenate([flat(grad[at, k]).astype(BF16) for k in range(2)], axis=1)


def tap_sums(field, grad, first, rows, out, more=None):
    wide = jnp.concatenate(views(field, first, rows), axis=1)
    found = lax.dot_general(grad, wide, (((0,), (0,)), ((), ())), preferred_element_type=F32)
    return put_taps(found, out, more)


def put_taps(found, out, more=None):
    group = group_of((CH, LANES))
    taps = []
    for r in range(3):
        for s in range(3):
            val = jnp.zeros((CH, LANES), F32)
            for y in range(SEG):
                d, a = spot_of(y + s - 1)
                spot = (3 * r + d) * LANES
                val = val + jnp.where(group == a, found[CH * y : CH * y + CH, spot : spot + LANES], 0.0)
            taps.append(fold(val))
    for q in range(3):
        val = taps[4 * q]
        for b in range(1, min(4, 9 - 4 * q)):
            val = jnp.where(group == b, taps[4 * q + b], val)
        if more is not None:
            centre, sums = more
            val = val + column_of(centre) * sums[q : q + 1]
        if q == 2:
            return val
        out[:, q, :] = val


def column_of(v):
    shape = (CH, LANES)
    return jnp.sum(jnp.where(row_of(shape) == lane_of(shape), v, 0.0), axis=1, keepdims=True)


def at_lane(v, k):
    return jnp.sum(jnp.where(lane_of(v.shape) == k, v, 0.0), axis=1, keepdims=True)


def decoder_back_kernel(place, got, grad, xhat, mid_x, vec, vec_two, sums, table, back_two, weights, fields, lows, below, below_x, shared, pay, more, first_x, kept_grad, mid, low_two, low_one, field_two, field_one, field_zero, back_one, sems, *, spots, local_count, pixel_count):
    all_off, skipped, off = place[0], place[3], place[4]
    height = field_two.shape[0] - 2
    far_rows, near_rows = pl.ds(skipped, grad.shape[0]), pl.ds(all_off, height + 2)
    fetched = copies(
        sems,
        (back_at(weights), back_one),
        (spots(fields, "xhat_one").at[far_rows], below_x),
        (spots(fields, "shared").at[far_rows], shared),
        (spots(lows, "hidden_three").at[near_rows], field_two),
        (spots(lows, "merged").at[near_rows], field_one),
        (spots(lows, "hidden_one").at[near_rows], field_zero),
    )
    handed = copies(sems.at[6:], (spots(fields, "xhat_zero").at[pl.ds(all_off, height)], first_x))
    devices = got.shape[0]
    rows = grad.shape[0]
    total = total_of(got, 0)
    shift, scale = spread(total, 0) / pixel_count, spread(total, 1) / pixel_count
    inverse, mean = vec[0:1], vec[1:2]
    factor = affine(table, 3)[0] * inverse
    slant = scale * inverse
    held, carried = factor * (shift - slant * mean), factor * slant
    links = got[0:CH, 2, 0, :] * groups(held, carried, held, carried)
    group = group_of(links.shape)
    mine = (lane_of(links.shape) & 31) == row_of(links.shape)

    def across(pick):
        column = jnp.sum(jnp.where(pick, links, 0.0), axis=1, keepdims=True)
        return col_sum(jnp.where(mine, column, 0.0))

    shift_two = spread(total, 2) - across(group < 2)
    scale_two = spread(total, 3) - across(group >= 2)
    entry = total_of(got, 3)
    notes(more, scale_two, shift_two, total_of(got, 4), total_of(got, 5), spread(entry, 1))

    def value(at, k):
        g = norm_back(grad[at, k], xhat[at, k], factor, shift, scale)
        kept_grad[at, k] = g
        return g

    back_rows(low_two, rows, value)

    @pl.when(place[0] >= 0)
    def _():
        mid[:, 0], mid[:, 1] = blocks_of(conv(low_two, back_two, 0, rows), rows)

    gain, bias = affine(table, 2)
    factor = gain * vec_two[0:1]
    shift, scale = shift_two / pixel_count, scale_two / pixel_count

    def value_two(at, k):
        x = mid_x[pl.ds(skipped + at.start, at.size), k]
        return norm_back(mid[at, k] * slope_at(x, gain, bias), x, factor, shift, scale)

    back_rows(low_one, rows, value_two)
    wait(fetched)
    sum_two = low_sum(low_two, off, height)
    sum_one = low_sum(low_one, off, height)
    y = conv(low_one, back_one, 0, rows)
    gain, bias = affine(table, 1)
    for k, y in enumerate(blocks_of(y, rows)):
        g = (y + kept_grad[:, k]).reshape(rows // 2, 2, -1, LANES)
        both = flat(g[:, 0] + g[:, 1])
        both = (both + partner(both)).reshape(rows // 2, 1, -1, LANES)
        g = g * slope_at(below_x[:, k], gain, bias).reshape(g.shape) + both * shared[:, k].reshape(g.shape)
        below[:, k] = g.reshape(rows, -1, LANES)
    shift_sum, scale_sum = own_sums(below, below_x, off, height)
    send(pay, groups(shift_sum, scale_sum, sum_one, sum_two))
    entry = spread(entry, 0)
    pay[:, 1, 0, :] = jnp.broadcast_to(entry, (devices, LANES))
    at = pl.ds(off + 1, height)
    last_two = tap_sums(field_two, own_lanes(low_two, at), 0, height, send_parts(pay, 2, 2))
    last_one = tap_sums(field_one, own_lanes(low_one, at), 0, height, send_parts(pay, 4, 2))
    centre = shift_sum / local_count
    at = pl.ds(off, height)
    grad = jnp.concatenate([flat(below[at, k] - centre).astype(BF16) for k in range(2)], axis=1)
    last_zero = tap_sums(field_zero, grad, 0, height, send_parts(pay, 6, 2), (centre, sums))
    pay[0:CH, 1, 0, :] = groups(last_two, last_one, last_zero, jnp.broadcast_to(entry, (CH, LANES)))
    wait(handed)


def summed_kernel(place, got, got_style, got_head, grad, xhat, shared, vec, more_two, table, w_style, sides, back, below_x, pay, more, below, grad_low, *, pixel_count, pool_cells, parts):
    off, mine = place[0], place[4]
    height = below.shape[0]
    devices = got.shape[0]
    rows = grad.shape[0]
    dims = (((1,), (1,)), ((), ()))
    first = row_of_each(got, 0)
    each = wide_dot(spread(first, 2), diagonal_blocks(w_style[0]), dims) + wide_dot(
        spread(first, 3), diagonal_blocks(w_style[1]), dims
    )
    each = each / pool_cells
    total = col_sum(first)
    shift = spread(total, 0) + col_sum(each * by_image(spread(row_of_each(got_style, 2), 1), parts))
    scale = spread(total, 1) + col_sum(each * by_image(spread(row_of_each(got_style, 2), 2), parts))
    style_grad = col_sum(jnp.where(row_of(each.shape) // parts == place[2] // parts, each, 0.0))
    factor = affine(table, 1)[0] * vec[0:1]
    shift_mean, scale_mean = shift / pixel_count, scale / pixel_count
    def value(at, k):
        return norm_back(grad[at, k] + shared[at, k] * style_grad, xhat[at, k], factor, shift_mean, scale_mean)

    back_rows(grad_low, rows, value)
    gain, bias = affine(table, 0)
    for k, y in enumerate(blocks_of(conv(grad_low, back, mine, height), height)):
        below[:, k] = y * slope_at(below_x[:, k], gain, bias)
    me = place[2]
    weights = at_lane(by_image(each, parts), me)
    hidden = spread(got[0:CH, 1, 0, :], 3)
    hidden = [groups(*[hidden[18 + t : 19 + t] for t in range(4 * q, min(4 * q + 4, 9))]) for q in range(3)]
    last = total_of(got, 1)
    direct = [total_of(got, 6), total_of(got, 7), spread(last, 2)]
    shares = [row_of_each(got_head, 6), row_of_each(got_head, 7), spread(row_of_each(got_head, 3), 2)]
    shard = []
    for q in range(3):
        val = direct[q] + col_sum(weights * shares[q])
        val = val - at_lane(shift_mean, me) * hidden[q] - at_lane(scale_mean, me) * more_two[2 + q : 3 + q]
        shard.append(at_lane(factor, me) * val)
    at = pl.ds(mine + 1, height)
    side = pixel_taps(sides, off + 1, height, own_lanes(grad_low, at), (0,))[0]
    low_below = own_lanes(below, pl.ds(0, height))
    taps = []
    for r in range(3):
        for tap in pixel_taps(sides, off + r, height, low_below, (-1, 0, 1)):
            taps.extend(tap)
    sums = [in_parts(v, 3) for v in own_sums(below, below_x, 0, height)]
    entries = [in_parts(v, 2) for v in taps + side]
    tail = [shard[2]] + [v[0] for v in entries] + [v[1] for v in entries]
    tail += [zero_row()] * (-len(tail) % 4)
    values = [
        groups(sums[0][0], sums[1][0], sums[0][1], sums[1][1]),
        groups(sums[0][2], sums[1][2], spread(last, 0), spread(last, 1)),
        *[total_of(got, r) for r in range(2, 6)],
        *shard[0:2],
        *[groups(*tail[k : k + 4]) for k in range(0, len(tail), 4)],
    ]
    values += [zero_row()] * (len(values) % 2)
    for k in range(len(values) // 2):
        pair = jnp.concatenate(values[2 * k : 2 * k + 2], axis=0).astype(BF16)
        pay[:, k] = jnp.broadcast_to(pair[None], (devices, 2, LANES))
    notes(more, scale, shift)


def pixel_taps(sides, row, rows, grad, shift, alone=False):
    x = flat(sides[pl.ds(row, rows)])
    found = lax.dot_general(x, grad, (((0,), (0,)), ((), ())), preferred_element_type=F32)
    inside, channel, column = image_lanes((LANES, 2 * LANES))
    here = column - group_of((LANES, 2 * LANES))
    out = []
    for s in shift:
        both, bare = [], []
        for c in range(2):
            v = col_sum(jnp.where(inside & (channel == c) & (here == s), found[:, 0 : 2 * LANES], 0.0))
            both.append(fold(v[:, 0:LANES] + v[:, LANES:]))
            if alone:
                cut = slice(0, LANES)
                hit = (inside & (channel == c) & (column >= s) & (column < s + SEG))[:, cut]
                bare.append(col_sum(jnp.where(hit, found[:, 2 * LANES :], 0.0)))
        out.append((both, bare) if alone else both)
    return out


def adamw(master, moment, square, grad, rate):
    new_moment = beta_one * moment + (1.0 - beta_one) * grad
    new_square = beta_two * square + (1.0 - beta_two) * grad * grad
    moment_hat = new_moment / (1.0 - beta_one**STEP)
    square_hat = new_square / (1.0 - beta_two**STEP)
    new_master = master - rate * (moment_hat / (jnp.sqrt(square_hat) + adam_eps) + weight_decay * master)
    return new_master, new_moment, new_square


def put(at, refs, grad, rate, outs):
    found = adamw(*[ref[at] for ref in refs], grad, rate)
    for out, value in zip(outs, found + (found[0].astype(BF16),)):
        out[at] = value


def update_early(
    got_one_back, got_head, got_style, pay, style, w_style, w_head, m_style, m_head, s_style, s_head,
    loss_out, count_out, style_master, style_moment, style_square, head_master, head_moment, head_square, head_copy,
):
    count_out[0, 0] = jnp.sum(got_style[:, 2, 0, 3 * CH : 3 * CH + 1])
    loss_out[0, 0] = jnp.sum(got_head[:, 1, 0, 99:100])
    dims = (((0,), (0,)), ((), ()))
    for i in range(2):
        sums = spread(row_of_each(got_one_back, 0), 2 + i)
        grad = lax.dot_general(style[...], sums, dims, precision=highest, preferred_element_type=F32)
        put(i, (w_style, m_style, s_style), grad[0:CH, 0:CH], rate_table[2], (style_master, style_moment, style_square))

    head = total_of(got_head, 1)
    lane = lane_of((1, LANES))
    rows = []
    for k in range(3):
        last = jnp.sum(jnp.where(lane == 3 * CH + k, head, 0.0), axis=1, keepdims=True)
        rows.append(jnp.where(lane < CH, spread(head, k), last))
    grad = jnp.concatenate(rows, axis=0)[:, 0 : CH + 1]
    put(slice(None), (w_head, m_head, s_head), grad, rate_table[3], (head_master, head_moment, head_square, head_copy))


def update_late(
    got, got_one_back, got_head, more, more_two, vec, w_first, w_convs, table, m_first, m_convs, m_norms, s_first, s_convs, s_norms,
    first_master, first_moment, first_square, first_copy,
    convs_master, convs_moment, convs_square, convs_copy,
    norms_master, norms_moment, norms_square, *, pixel_count
):
    refs = (w_convs, m_convs, s_convs)
    outs = (convs_master, convs_moment, convs_square, convs_copy)
    pairs = [got[:, k].astype(F32) for k in range(got.shape[1])]
    packs = [[pairs[k // 2][0:CH, k % 2, :].T for k in ks] for ks in ((6, 7, 8), (4, 5, 1), (2, 3, 1))]
    for i, pack in enumerate(packs):
        for t in range(9):
            b = t % 4 if t < 8 else (0, 3, 2)[i]
            put((i, t), refs, pack[t // 4][CH * b : CH * b + CH], rate_table[1], outs)

    totals = [jnp.sum(pair, axis=0) for pair in pairs]
    totals = [pair[h : h + 1] for pair in totals for h in range(2)]
    shift, scale = [spread(totals[0], k) + (spread(totals[0], 2 + k) + spread(totals[1], k)) for k in range(2)]
    factor = affine(table, 0)[0] * vec[0:1]
    by_x = spread(got_one_back[0:CH, 1, 0, :], 3)
    alone = total_of(got_head, 1)
    refs = (w_first, m_first, s_first)
    outs = (first_master, first_moment, first_square, first_copy)
    for t in range(10):
        pair = []
        for e in (2 * t, 2 * t + 1):
            k, b = divmod(1 + e, 4)
            v = spread(totals[8 + k], b)
            k, b = divmod(21 + e, 4)
            v = v + spread(totals[8 + k], b)
            if t < 9:
                v = factor * (v - (at_lane(alone, ALONE + e) * shift + by_x[e : e + 1] * scale) / pixel_count)
            pair.append(v[:, 0:CH])
        put(t, refs, jnp.concatenate(pair, axis=0), rate_table[0], outs)

    three_sums = total_of(got_head, 0)
    scales = [scale, more[0:1], more_two[0:1], spread(three_sums, 1)]
    shifts = [shift, more[1:2], more_two[1:2], spread(three_sums, 0)]
    for i, rows in enumerate((scales, shifts)):
        grad = jnp.concatenate(rows, axis=0)[:, 0:CH]
        put(i, (table, m_norms, s_norms), grad, rate_table[4], (norms_master, norms_moment, norms_square))


def update_kernel(*refs, pixel_count):
    ins, outs = refs[:23], refs[23:]
    late, early = ins[:15], ins[15:]
    update_late(*late, *outs[:11], pixel_count=pixel_count)
    update_early(late[1], late[2], early[0], None, *early[1:], *outs[11:])


def far(x):
    return ("far", x)


def call(kernel, outs, *operands, scalars=0, scratch=(), sems=0, scalar_outs=(), aliases=None, limit=VMEM_LIMIT, name):
    smem = pl.BlockSpec(memory_space=pltpu.SMEM)
    vmem = pl.BlockSpec(memory_space=pltpu.VMEM)
    hbm = pl.BlockSpec(memory_space=pltpu.HBM)
    is_far = lambda x: isinstance(x, tuple) and x[0] == "far"
    in_specs = [smem if i < scalars else hbm if is_far(x) else vmem for i, x in enumerate(operands)]
    out_specs = [smem if i in scalar_outs else hbm if is_far(x) else vmem for i, x in enumerate(outs)]
    plain = lambda x: x[1] if is_far(x) else x
    shapes = [pltpu.VMEM(shape, dtype) for shape, dtype in scratch]
    if sems:
        shapes.append(pltpu.SemaphoreType.DMA((sems,)))
    return pl.pallas_call(
        kernel,
        out_shape=[jax.ShapeDtypeStruct(*plain(x)) for x in outs],
        in_specs=in_specs,
        out_specs=out_specs,
        scratch_shapes=shapes,
        input_output_aliases=aliases or {},
        compiler_params=pltpu.CompilerParams(vmem_limit_bytes=limit),
        name=name,
    )(*[plain(x) for x in operands])


def exchange(pay):
    return lax.all_to_all(pay, ("row", "col"), 0, 0)


def local(
    image_batch, valid_mask, flow_target, cell_labels,
    w_first, w_convs, w_style, w_head, batch_norm_table,
    mom_first, mom_convs, mom_style, mom_head, mom_norms,
    sqr_first, sqr_convs, sqr_style, sqr_head, sqr_norms,
):
    images, block_rows, block_cols, _ = image_batch.shape
    row_count, col_count = lax.axis_size("row"), lax.axis_size("col")
    devices = row_count * col_count
    parts = devices // images
    image_rows, image_cols = row_count * block_rows, col_count * block_cols
    assert devices == parts * images and block_rows == RIM and block_cols == 2 * block_rows * 2
    assert image_rows % (parts * RIM) == 0 and devices >= CH
    height = image_rows // parts
    rows = min(image_rows, height + RIM * min(2, parts - 1))
    segments = image_cols // SEG
    local_count = float(height * image_cols)
    pixel_count = local_count * devices
    pool_cells = float(image_rows * image_cols // 4)
    part = functools.partial
    counts = dict(local_count=local_count, pixel_count=pixel_count, height=height)
    styled = dict(pool_cells=pool_cells, parts=parts)

    me = lax.axis_index("row") * col_count + lax.axis_index("col")
    first_row = (me % parts) * height
    start = jnp.clip(first_row - RIM, 0, image_rows - rows)
    off = first_row - start
    back_rim = RIM // 2
    rows_back = min(rows, height + back_rim * min(2, parts - 1))
    skipped = jnp.clip(off - back_rim, 0, rows - rows_back)
    place = jnp.stack([off, start // block_rows, me, skipped, off - skipped]).astype(jnp.int32)

    field = ((rows, 2, segments, LANES), F32)
    own_field = ((height,) + field[0][1:], F32)
    back_field = ((rows_back,) + field[0][1:], F32)
    low_field = ((rows + 2, 3, segments, LANES), BF16)
    own_low = ((height + 2,) + low_field[0][1:], BF16)
    back_low = ((rows_back + 2,) + low_field[0][1:], BF16)
    vec = ((8, LANES), F32)

    def payload(count):
        return ((devices, count, 1, LANES), F32)

    nine = ((BACK, 2 * LANES), BF16)
    ten = ((FORWARD, 2 * LANES), BF16)

    places = {
        name: i * count
        for count, names in (
            (rows, ("xhat_zero", "xhat_one", "shared")),
            (rows + 2, ("hidden_one", "hidden_three", "merged")),
        )
        for i, name in enumerate(names)
    }

    def spots(store, name):
        count = rows if name[0] in "xs" else rows + 2
        return store.at[places[name] : places[name] + count]

    def store_of(like):
        shape, dtype = like
        row_bytes = shape[1] * segments * LANES * jnp.dtype(dtype).itemsize
        return far(((-(-STORE_BYTES // row_bytes),) + shape[1:], dtype))

    inputs = (
        jnp.transpose(image_batch, (0, 1, 3, 2)), jnp.transpose(flow_target, (0, 1, 3, 2)), cell_labels, valid_mask
    )
    (pay,) = call(
        pack_kernel,
        [((devices, 16, LANES), BF16)],
        *[far(v) for v in inputs],
        scratch=[(v.shape, v.dtype) for v in inputs], sems=4, limit=WHOLE_VMEM, name="pack",
    )
    got_inputs = exchange(pay)
    head_rows = w_head.T
    weights, back_zero, back_two, head_mat = call(
        prepare,
        [far(((STORE_BYTES // (4 * LANES), 2 * LANES), BF16)), far(nine), far(nine), far(((2 * LANES, LANES), BF16))],
        far(w_first), far(w_convs), far(head_rows),
        scratch=[
            (w_first.shape, F32), (w_convs.shape, F32), (head_rows.shape, F32), ((BACK_AT + BACK, 2 * LANES), BF16),
            nine, nine, ((2 * LANES, LANES), BF16),
        ],
        sems=8, limit=WHOLE_VMEM, name="prepare",
    )

    sides, raw, pay, count, taps = call(
        part(start_kernel, local_count=local_count, height=height, sources=col_count),
        [((rows + 2, segments, LANES), BF16), field, payload(2), vec, ten],
        place, got_inputs, far(weights),
        scalars=1, scratch=[((3 * LANES, 2 * LANES), BF16)], sems=2, name="image_conv",
    )
    got_zero = exchange(pay)
    summed, pay, inv_zero, fields, lows = call(
        part(first_kernel, spots=spots, **counts),
        [field, payload(2), vec, store_of(field), store_of(low_field)],
        place, got_zero, raw, sides, batch_norm_table, taps,
        scalars=1, scratch=[low_field, field], sems=2, name="first_block",
    )
    got_one = exchange(pay)

    raw, pay, inv_one, merged, taps, fields, lows = call(
        part(pool_kernel, spots=spots, **counts),
        [field, payload(3), vec, low_field, nine, store_of(field), store_of(low_field)],
        place, got_one, summed, count, batch_norm_table, far(weights), far(fields), far(lows),
        scalars=1, scratch=[field, field, nine], sems=5,
        aliases={6: 5, 7: 6}, name="pool_and_merge",
    )
    got_style = exchange(pay)

    resid, pay, inv_two, style, xhat_two, ahead, hidden_sums, lows = call(
        part(style_kernel, spots=spots, **styled, **counts),
        [back_field, payload(3), vec, ((devices, LANES), F32), field, ((CH, 5, 1, LANES), F32), vec, store_of(low_field)],
        place, got_style, raw, merged, batch_norm_table, w_style, far(w_convs), taps, sides, far(fields),
        far(lows),
        scalars=1, scratch=[low_field, field, (w_convs.shape[1:], F32), own_field, own_field, own_field, own_low], sems=6,
        aliases={10: 7}, name="decoder",
    )
    got_three = exchange(pay)

    grad_three, xhat_three, pay, inv_three = call(
        part(head_kernel, **counts),
        [back_field, back_field, payload(8), vec],
        place, got_three, got_style, resid, sides, head_mat, head_rows, xhat_two, ahead, hidden_sums, batch_norm_table, back_two,
        scalars=1, scratch=[((rows_back, 2, segments, LANES), BF16), back_field, back_low], name="head",
    )
    got_head = exchange(pay)

    grad_one, xhat_one, shared, pay, more_two, xhat_zero = call(
        part(decoder_back_kernel, spots=spots, local_count=local_count, pixel_count=pixel_count),
        [back_field, back_field, back_field, payload(8), vec, own_field],
        place, got_head, grad_three, xhat_three, xhat_two, inv_three, inv_two, hidden_sums, batch_norm_table, back_two, far(weights),
        far(fields), far(lows),
        scalars=1, scratch=[back_field, back_field, back_low, back_low, own_low, own_low, own_low, nine], sems=7,
        name="decoder_back",
    )
    got_one_back = exchange(pay)

    pay, more = call(
        part(summed_kernel, pixel_count=pixel_count, **styled),
        [((devices, 10, 2, LANES), BF16), vec],
        place, got_one_back, got_style, got_head, grad_one, xhat_one, shared, inv_one, more_two, batch_norm_table, w_style,
        sides, back_zero, xhat_zero,
        scalars=1, scratch=[own_field, back_low], name="summed_back",
    )
    got_last = exchange(pay)

    def results(param, copy):
        return [(param.shape, F32)] * 3 + [(param.shape, BF16)] * copy

    found = call(
        part(update_kernel, pixel_count=pixel_count),
        results(w_first, 1)
        + results(w_convs, 1)
        + results(batch_norm_table, 0)
        + [((1, 1), F32), ((1, 1), F32)]
        + results(w_style, 0)
        + results(head_rows, 1),
        got_last, got_one_back, got_head, more, more_two, inv_zero,
        w_first, w_convs, batch_norm_table, mom_first, mom_convs, mom_norms, sqr_first, sqr_convs, sqr_norms,
        got_style, style, w_style, head_rows, mom_style, mom_head.T, sqr_style, sqr_head.T,
        scalar_outs=(11, 12), name="update",
    )
    late, early = found[:11], found[11:]
    loss, count = early[0].reshape(()), early[1].reshape(())
    head = tuple(value.T for value in early[5:9])
    return (loss, count, *late[0:8], *early[2:5], *head, *late[8:11])


def solution(mesh):
    field = P(None, "row", "col", None)
    plane = P(None, "row", "col")
    return jax.shard_map(
        local,
        mesh=mesh,
        in_specs=(field, plane, field, plane) + (P(),) * 15,
        out_specs=(P(),) * 20,
        check_vma=False,
    )
```

```python
import functools

import jax
import jax.numpy as jnp
from jax import lax
from jax.experimental import pallas as pl
from jax.experimental.pallas import tpu as pltpu
from jax.sharding import PartitionSpec as P

STEP = 5

highest = lax.Precision.HIGHEST
norm_eps = 1e-05
flow_scale = 32.0
adam_eps = 1e-08
weight_decay = 0.01
beta_one = 0.5
beta_two = 0.5
rate_table = (0.2, 0.05, 0.15, 0.15, 0.2)

CH = 32
GRP = 4
SEG = 8
LANES = 128
RIM = 8
FLOW, LABEL, MASK = 16, 32, 40
LEFT, RIGHT = 64, 96
ALONE = 100
AFTER, ROW, BEFORE = 32, 33, 64
F32 = jnp.float32
BF16 = jnp.bfloat16
VMEM_LIMIT = 36 * 1024 * 1024
WHOLE_VMEM = 56 * 1024 * 1024
STORE_BYTES = 32 * 1024 * 1024
FORWARD = 10 * LANES
BACK = 9 * LANES
IMAGE_AT = 3 * FORWARD
BACK_AT = IMAGE_AT + 3 * LANES


def lane_of(shape):
    return lax.broadcasted_iota(jnp.int32, shape, len(shape) - 1)


def row_of(shape):
    return lax.broadcasted_iota(jnp.int32, shape, 0)


def group_of(shape):
    return lane_of(shape) >> 5


def fold(v):
    return v + pltpu.roll(v, 32, axis=1) + (pltpu.roll(v, 64, axis=1) + pltpu.roll(v, 96, axis=1))


def spread(v, k):
    return fold(jnp.where(group_of(v.shape) == k, v, 0.0))


def partner(v):
    odd = (group_of(v.shape) & 1) == 1
    return jnp.where(odd, pltpu.roll(v, 32, axis=1), pltpu.roll(v, 96, axis=1))


def tile4(v):
    return jnp.concatenate([v, v, v, v], axis=1)


def col_sum(v):
    return jnp.sum(v, axis=0, keepdims=True)


def zero_row():
    return jnp.zeros((1, LANES), F32)


def groups(*values):
    group = group_of(values[0].shape)
    out = values[-1]
    for k in range(len(values) - 2, -1, -1):
        out = jnp.where(group == k, values[k], out)
    return out


def low(v):
    return v.astype(BF16).astype(F32)


def sig_of(v):
    return 0.5 + 0.5 * jnp.tanh(0.5 * v)


def slope(n, sig):
    return sig * (1.0 + n * (1.0 - sig))


def slope_at(x, gain, bias):
    n = x * gain + bias
    return slope(n, sig_of(n))


def flat(v):
    return v.reshape(-1, LANES)


def loop(count, body, unroll=5):
    def step(i, carry):
        body(i)
        return carry

    lax.fori_loop(0, count, step, 0, unroll=min(count, unroll))


def copies(sems, *pairs):
    found = []
    for i, (source, target) in enumerate(pairs):
        found.append(pltpu.make_async_copy(source, target, sems.at[i]))
        found[-1].start()
    return found


def wait(started):
    for copy in started:
        copy.wait()


def shift_segments(v, way):
    half = v.shape[1]
    at = lax.broadcasted_iota(jnp.int32, v.shape, 1)
    if way == 1:
        return jnp.where(at == 0, 0.0, pltpu.roll(v, 1, axis=1))
    return jnp.where(at == half - 1, 0.0, pltpu.roll(v, half - 1, axis=1))


def beside(first, second):
    half = first.shape[1] // 2
    left = jnp.concatenate([shift_segments(second[:, half:], 1), second[:, :half]], axis=1)
    right = jnp.concatenate([first[:, half:], shift_segments(first[:, :half], -1)], axis=1)
    return left, right


def put_low(ref, row, first, second, marked=False):
    left, right = beside(first, second)
    lane = lane_of(left.shape)
    edge = jnp.where(lane < 64, right, left)
    if marked:
        at = lax.broadcasted_iota(jnp.int32, left.shape, 1)
        edge = jnp.where(lane == ROW, 1.0, edge)
        edge = jnp.where(lane == AFTER, jnp.where(at == left.shape[1] - 1, 0.0, 1.0), edge)
        edge = jnp.where(lane == BEFORE, jnp.where(at == 0, 0.0, 1.0), edge)
    at = pl.ds(row + 1, first.shape[0])
    for k, v in enumerate((first, second, edge)):
        ref[at, k] = v.astype(BF16)


def blank(ref):
    zero = jnp.zeros((1,) + ref.shape[1:], ref.dtype)
    ref[0:1] = zero
    ref[ref.shape[0] - 1 : ref.shape[0]] = zero


def views(src, row, rows):
    return [flat(src[pl.ds(row + r, rows), k]) for r in range(3) for k in (2, 0, 1)]


def conv(src, mat, row, rows, *more):
    wide = jnp.concatenate(views(src, row, rows) + list(more), axis=1)
    return jnp.dot(wide, mat[...], preferred_element_type=F32)


def blocks_of(y, rows):
    return [y[:, k * LANES : (k + 1) * LANES].reshape(rows, -1, LANES) for k in range(2)]


def narrow(v):
    while v.shape[0] > 1:
        half = v.shape[0] // 2
        v = v[:half] + v[half:]
    return v[0]


def row_sums(first, rows, values):
    step = 4

    def add(i, carry):
        found = [values(pl.ds(first + step * i, step), k) for k in range(2)]
        return tuple(c + a + b for c, a, b in zip(carry, *found))

    shapes = jax.eval_shape(lambda: values(pl.ds(0, step), 0))
    zeros = tuple(jnp.zeros(v.shape, F32) for v in shapes)
    found = lax.fori_loop(0, rows // step, add, zeros, unroll=min(rows // step, 8))
    return [col_sum(narrow(v)) for v in found]


def local_stats(v, first, rows, count):
    count = count / GRP
    pivot = col_sum(v[first, 0] + v[first, 1]) / (2 * v.shape[2])

    def moments(at, k):
        away = v[at, k] - pivot
        return away, away * away

    total, square = row_sums(first, rows, moments)
    return pivot + total / count, square - total * (total / count)


def merge_stats(means, squares, local_count, pixel_count):
    mean = fold(col_sum(means)) / (GRP * means.shape[0])
    away = means - mean
    total = fold(col_sum(squares + (local_count / GRP) * (away * away)))
    return mean, lax.rsqrt(total / pixel_count + norm_eps)


def row_of_each(got, r):
    return got[:, r, 0, :]


def total_of(got, r):
    return col_sum(row_of_each(got, r))


def send(pay, *rows):
    for r, row in enumerate(rows):
        pay[:, r, 0, :] = jnp.broadcast_to(row, (pay.shape[0], LANES))


def send_parts(pay, first, count):
    devices = pay.shape[0]
    if devices > CH:
        for r in range(first, first + count):
            pay[CH:, r, 0, :] = jnp.zeros((devices - CH, LANES), F32)
    return pay.at[0:CH, first : first + count, 0]


def affine(table, q):
    return tile4(table[0, q : q + 1, :]), tile4(table[1, q : q + 1, :])


def diagonal_blocks(mat):
    wide = tile4(mat)
    group = group_of(wide.shape)
    return jnp.concatenate([jnp.where(group == b, wide, 0.0) for b in range(GRP)], axis=0)


def notes(ref, *rows):
    for i, row in enumerate(rows):
        ref[i : i + 1, :] = row


def taps_at(store, i):
    return store.at[FORWARD * i : FORWARD * i + (BACK if i else FORWARD)]


def image_at(store):
    return store.at[IMAGE_AT : IMAGE_AT + 3 * LANES]


def back_at(store):
    return store.at[BACK_AT : BACK_AT + BACK]


def pack_kernel(image_in, flow_in, labels_in, valid_in, out, image, flow, labels, valid, sems):
    fetched = copies(sems, (image_in, image), (flow_in, flow), (labels_in, labels), (valid_in, valid))
    images, height, _, width = image.shape
    parts = out.shape[0] // images
    wait(fetched)
    fields = [image[:, :, c, :].astype(F32) for c in range(2)]
    fields += [flow[:, :, c, :].astype(F32) for c in range(2)]
    fields += [labels[...].astype(F32), valid[...].astype(F32)]
    halves = width // 16
    shape = (width, halves * LANES)
    lane = lane_of(shape)
    column = (lane >> 7) * 16 + ((lane >> 6) & 1) * 8 + (lane & 7)
    hit = row_of(shape) == column
    which = (lane >> 3) & 7
    total = jnp.zeros((images * height, halves * LANES), F32)
    for k, v in enumerate(fields):
        x = v.reshape(images * height, width).astype(BF16)
        mat = jnp.where(hit & (which == k), 1.0, 0.0).astype(BF16)
        total = total + jnp.dot(x, mat, preferred_element_type=F32)
    for b in range(images):
        rows = total[b * height : (b + 1) * height]
        slot = jnp.concatenate([rows[:, h * LANES : (h + 1) * LANES] for h in range(halves)], axis=0).astype(BF16)
        for p in range(parts):
            out[b * parts + p] = slot


COLUMNS = ((8, None, None, -1), (0, 1, 2, 3), (4, 5, 6, 7))


def conv_matrix(taps, mats, base, back):
    out_at = group_of((CH, 2 * LANES))
    for r in range(3):
        wide = []
        for s in range(3):
            if back:
                k = taps[3 * (2 - r) + s]
                k = jnp.concatenate([k, k, k, k], axis=0).T
            else:
                k = tile4(taps[3 * r + s])
            wide.append(jnp.concatenate([k, k], axis=1))
        for d in range(3):
            for a in range(GRP):
                val = jnp.zeros((CH, 2 * LANES), F32)
                column = COLUMNS[d][a]
                if column is not None:
                    for s in range(3):
                        val = jnp.where(out_at == (column + s - 1 if back else column + 1 - s), wide[s], val)
                mats[pl.ds(base + (3 * r + d) * LANES + CH * a, CH), :] = val.astype(BF16)


def image_lanes(shape):
    at = row_of(shape)
    kind = at >> 5
    column = (at & 7) + jnp.where(kind == LEFT // 32, -SEG, jnp.where(kind == RIGHT // 32, SEG, 0))
    return (kind != 1) & ((at & 31) < 16), (at >> 3) & 1, column


def first_taps(w_first, t):
    found = [tile4(low(w_first[t][c : c + 1])) for c in range(2)]
    return [jnp.concatenate([v, v], axis=1) for v in found]


def image_matrix(w_first, r):
    shape = (LANES, 2 * LANES)
    inside, channel, here = image_lanes(shape)
    val = jnp.zeros(shape, F32)
    for s in range(3):
        for c, tap in enumerate(first_taps(w_first, 3 * r + s)):
            val = jnp.where(inside & (channel == c) & (here == group_of(shape) + s - 1), tap, val)
    return val.astype(BF16)


def prepare(w_first_in, w_convs_in, w_head_in, store, back_zero_out, back_two_out, head_out, w_first, w_convs, w_head, mats, back_zero, back_two, head_mat, sems):
    wait(copies(sems, (w_first_in, w_first), (w_convs_in, w_convs), (w_head_in, w_head)))
    stored = []

    def keep(source, target):
        stored.extend(copies(sems.at[len(stored) :], (source, target)))

    for i, back, out in ((2, back_two, back_two_out), (0, back_zero, back_zero_out)):
        conv_matrix(w_convs.at[i], back, 0, True)
        keep(back, out)
    conv_matrix(w_convs.at[1], mats, BACK_AT, True)
    keep(back_at(mats), back_at(store))
    shape = (LANES, 2 * LANES)
    inside, channel, here = image_lanes(shape)
    val = jnp.zeros(shape, F32)
    for c, tap in enumerate(first_taps(w_first, 9)):
        val = jnp.where((row_of(shape) < 16) & (channel == c) & (here == group_of(shape)), tap, val)
    mats[BACK:FORWARD, :] = val.astype(BF16)
    for i in range(3):
        conv_matrix(w_convs.at[i], mats, FORWARD * i, False)
        keep(taps_at(mats, i), taps_at(store, i))
    for r in range(3):
        mats[IMAGE_AT + LANES * r : IMAGE_AT + LANES * (r + 1), :] = image_matrix(w_first, r)
    keep(image_at(mats), image_at(store))
    lane = lane_of((CH, LANES))
    head = jnp.zeros((CH, LANES), F32)
    diagonal = row_of((CH, CH)) == lane_of((CH, CH))
    for k in range(3):
        column = jnp.sum(jnp.where(diagonal, low(w_head[k : k + 1, 0:CH]), 0.0), axis=1, keepdims=True)
        head = jnp.where((lane >> 3) == FLOW // 8 + k, column, head)
    for y in range(SEG):
        head_mat[CH * y : CH * (y + 1), :] = jnp.where((lane & 7) == y, head, 0.0).astype(BF16)
    keep(head_mat, head_out)
    wait(stored)


def hand_kernel(weights, first_mat, taps, sems):
    wait(copies(sems, (image_at(weights), first_mat), (taps_at(weights, 0), taps)))


def start_kernel(place, got, first_mat, sides, raw, pay, vec, *, local_count, height, sources):
    rows, segments = raw.shape[0], raw.shape[2]
    off, block = place[0], place[1]
    blank(sides)

    def eight(t):
        v = got[pl.ds((block + t) * sources, sources)].astype(F32)
        v = jnp.swapaxes(v.reshape(segments // 2, 8, LANES), 0, 1)
        near = lane_of(v.shape) < 64
        v = jnp.concatenate([jnp.where(near, v, 0.0), jnp.where(near, pltpu.roll(v, 64, axis=2), 0.0)], axis=1)
        pixels = jnp.where(lane_of(v.shape) < 16, v, 0.0)
        left, right = beside(pixels, pixels)
        v = v + pltpu.roll(left, LEFT, axis=2) + pltpu.roll(right, RIGHT, axis=2)
        sides[pl.ds(8 * t + 1, 8)] = v.astype(BF16)

    loop(rows // 8, eight)
    y = None
    for r in range(3):
        part = jnp.dot(flat(sides[r : r + rows]), first_mat[LANES * r : LANES * (r + 1)], preferred_element_type=F32)
        y = part if y is None else y + part
    raw[:, 0], raw[:, 1] = blocks_of(y, rows)
    mean, square = local_stats(raw, off, height, local_count)
    mask = jnp.zeros(sides.shape[1:], F32)
    for i in range(height):
        mask = mask + sides[off + 1 + i].astype(F32)
    lane = lane_of(mask.shape)
    count = jnp.sum(jnp.where((lane >= MASK) & (lane < MASK + 8), mask, 0.0))
    send(pay, mean, square)
    notes(vec, jnp.full((1, LANES), count, F32))


def first_kernel(place, got, raw, sides, table, taps, summed, pay, vec, fields, lows, hidden, xhat, sems, *, spots, local_count, pixel_count, height):
    mean, inverse = merge_stats(row_of_each(got, 0), row_of_each(got, 1), local_count, pixel_count)
    notes(vec, inverse)
    gain, bias = affine(table, 0)
    rows = raw.shape[0]

    def norm_rows(i):
        at = pl.ds(4 * i, 4)
        out = []
        for k in range(2):
            x = (raw[at, k] - mean) * inverse
            xhat[at, k] = x
            n = x * gain + bias
            out.append(n * sig_of(n))
        put_low(hidden, 4 * i, *out)

    blank(hidden)
    loop(rows // 4, norm_rows)
    stored = copies(sems, (xhat, spots(fields, "xhat_zero")), (hidden, spots(lows, "hidden_one")))

    @pl.when(place[0] >= 0)
    def _():
        y = conv(hidden, taps, 0, rows, flat(sides[1 : rows + 1]))
        summed[:, 0], summed[:, 1] = blocks_of(y, rows)

    send(pay, *local_stats(summed, place[0], height, local_count))
    wait(stored)


def pool_kernel(place, got, summed, count_in, table, weights, fields_in, lows_in, raw, pay, vec, merged, taps_next, fields, lows, xhat, shared, taps, sems, *, spots, local_count, pixel_count, height):
    fetched = copies(sems, (taps_at(weights, 1), taps), (taps_at(weights, 2), taps_next))
    mean, inverse = merge_stats(row_of_each(got, 0), row_of_each(got, 1), local_count, pixel_count)
    gain, bias = affine(table, 1)
    rows, segments = summed.shape[0], summed.shape[2]
    off = place[0]

    step = 4

    def some(i, carry):
        at = pl.ds(step * i, step)
        pairs = (step // 2, 2, segments, LANES)
        outs, sums = [], [jnp.zeros((step // 2 * segments, LANES), F32) for _ in range(3)]
        for k in range(2):
            x = (summed[at, k] - mean) * inverse
            n = x * gain + bias
            sig = sig_of(n)
            e = (n * sig).reshape(pairs)
            top = flat(jnp.maximum(e[:, 0], e[:, 1]))
            top = jnp.maximum(top, partner(top))
            wide_top = top.reshape(step // 2, 1, segments, LANES)
            exps = jnp.exp(e - wide_top)
            whole = flat(exps[:, 0] + exps[:, 1])
            whole = whole + partner(whole)
            pooled = top + jnp.log(whole)
            outs.append((e + pooled.reshape(wide_top.shape)).reshape(step, segments, LANES))
            share = exps * (1.0 / whole).reshape(wide_top.shape) * slope(n, sig).reshape(pairs)
            share_x = share * x.reshape(pairs)
            xhat[at, k] = x
            shared[at, k] = share.reshape(step, segments, LANES)
            sums[0] = sums[0] + pooled
            sums[1] = sums[1] + flat(share[:, 0] + share[:, 1])
            sums[2] = sums[2] + flat(share_x[:, 0] + share_x[:, 1])
        put_low(merged, step * i, *outs)
        mine = (step * i >= off) & (step * i < off + height)
        keep = jnp.where(mine, 1.0, 0.0)
        return tuple(a + keep * b for a, b in zip(carry, sums))

    blank(merged)
    zero = jnp.zeros((step // 2 * segments, LANES), F32)
    sums = lax.fori_loop(0, rows // step, some, (zero, zero, zero), unroll=min(rows // step, 5))
    pool_sum, share_sum, share_x = [fold(col_sum(v)) for v in sums]
    stored = copies(
        sems.at[2:],
        (xhat, spots(fields, "xhat_one")),
        (shared, spots(fields, "shared")),
        (merged, spots(lows, "merged")),
    )
    wait(fetched)
    raw[:, 0], raw[:, 1] = blocks_of(conv(merged, taps, 0, rows), rows)
    mean, square = local_stats(raw, place[0], height, local_count)
    send(pay, mean, square, groups(0.5 * pool_sum, share_sum, share_x, count_in[0:1]))
    notes(vec, inverse)
    wait(stored)


def by_image(v, parts):
    devices = v.shape[0]
    step = 1
    while step < parts:
        upper = (row_of(v.shape) // step) % 2 == 1
        v = v + jnp.where(upper, pltpu.roll(v, step, axis=0), pltpu.roll(v, devices - step, axis=0))
        step *= 2
    return v


def wide_dot(a, b, dims=(((1,), (0,)), ((), ()))):
    (a_high, a_low), (b_high, b_low) = [[v.astype(BF16) for v in in_parts(x, 2)] for x in (a, b)]
    axis_a, axis_b = dims[0][0][0], dims[0][1][0]
    left = jnp.concatenate([a_high, a_high, a_low], axis=axis_a)
    right = jnp.concatenate([b_high, b_low, b_high], axis=axis_b)
    return lax.dot_general(left, right, dims, preferred_element_type=F32)


def in_parts(v, count):
    out = []
    for _ in range(count):
        out.append(low(v))
        v = v - out[-1]
    return out


def mine_of(v, me):
    return col_sum(jnp.where(row_of(v.shape) == me, v, 0.0))


def style_kernel(place, got, raw, merged, table, w_style, w_convs_in, taps, sides, fields, lows_in, resid, pay, vec, style_out, xhat, ahead, sums, lows, hidden, slopes, w_conv, zero_x, one_x, shared, field, sems, *, spots, local_count, pixel_count, pool_cells, height, parts):
    own = pl.ds(place[0], height)
    fetched = copies(
        sems,
        (w_convs_in.at[2], w_conv),
        (spots(fields, "xhat_zero").at[own], zero_x),
        (spots(fields, "xhat_one").at[own], one_x),
        (spots(fields, "shared").at[own], shared),
        (spots(lows_in, "hidden_one").at[pl.ds(place[0], height + 2)], field),
    )
    style = by_image(spread(row_of_each(got, 2), 0), parts) / pool_cells
    style_out[...] = style
    one, two = [
        wide_dot(style, diagonal_blocks(w_style[i])) for i in range(2)
    ]
    mean, inverse = merge_stats(row_of_each(got, 0) + one, row_of_each(got, 1), local_count, pixel_count)
    notes(vec, inverse)
    gain, bias = affine(table, 2)
    rows, kept = raw.shape[0], resid.shape[0]
    off, skipped, mine = place[0], place[3], place[4]
    me = place[2]
    shift = mine_of(one, me) - mean
    two = mine_of(two, me)

    def norm_rows(i):
        at = pl.ds(4 * i, 4)
        out = []
        for k in range(2):
            x = (raw[at, k] + shift) * inverse
            xhat[at, k] = x
            n = x * gain + bias
            sig = sig_of(n)
            slopes[at, k] = slope(n, sig)
            out.append(n * sig)
        put_low(hidden, 4 * i, *out)

    blank(hidden)
    loop(rows // 4, norm_rows)
    stored = copies(sems.at[5:], (hidden, spots(lows, "hidden_three")))

    @pl.when(place[0] >= 0)
    def _():
        for k, y in enumerate(blocks_of(conv(hidden, taps, skipped, kept), kept)):
            resid[:, k] = y + two + merged[pl.ds(skipped + 1, kept), k].astype(F32)

    wait(fetched + stored)
    hidden[kept + 1 : kept + 2] = jnp.zeros((1,) + hidden.shape[1:], BF16)
    centre = fold(col_sum(resid[mine, 0] + resid[mine, 1])) / (SEG * raw.shape[2])
    at = pl.ds(off, height)
    probe = [slopes[at, k] for k in range(2)]
    probe += [slopes[at, k] * xhat[at, k] for k in range(2)]
    probe = jnp.concatenate([flat(v).astype(BF16) for v in probe], axis=1)

    def centred(i):
        at = pl.ds(4 * i, 4)
        put_low(hidden, 4 * i, resid[at, 0] - centre, resid[at, 1] - centre, True)

    loop(kept // 4, centred)
    links = norm_links(hidden, probe, mine, height, w_conv, centre)
    send(pay, *local_stats(resid, mine, height, local_count))
    send_parts(pay, 2, 1)[:, 0, :] = links
    put_ahead(off, sides, ahead, sums, zero_x, one_x, shared, field, local_count)


def norm_links(field, probe, first, rows, taps, centre):
    wide = jnp.concatenate(views(field, first, rows), axis=1)
    found = lax.dot_general(probe, wide, (((0,), (0,)), ((), ())), preferred_element_type=F32)
    group = group_of((CH, LANES))
    out = []
    for half in range(2):

        def piece(y, chunk):
            at = 2 * LANES * half + CH * y
            return found[at : at + CH, chunk * LANES : (chunk + 1) * LANES]

        plain = jnp.zeros((CH, LANES), F32)
        moved = jnp.zeros((CH, LANES), F32)
        for r in range(3):
            first_edge, last_edge = piece(0, 3 * r), piece(SEG - 1, 3 * r)
            edge = first_edge + last_edge
            for y in range(1, SEG - 1):
                edge = edge + piece(y, 3 * r)
            inside = edge[:, ROW : ROW + 1]
            counts = (
                inside + (first_edge[:, BEFORE : BEFORE + 1] - first_edge[:, ROW : ROW + 1]),
                inside,
                inside + (last_edge[:, AFTER : AFTER + 1] - last_edge[:, ROW : ROW + 1]),
            )
            for c in range(3):
                tap = tile4(low(taps[3 * (2 - r) + 2 - c]))
                val = jnp.zeros((CH, LANES), F32)
                for y in range(SEG):
                    d, a = spot_of(y + c - 1)
                    val = val + jnp.where(group == a, piece(y, 3 * r + d), 0.0)
                plain = plain + tap * counts[c]
                moved = moved + tap * val
        out += [plain, fold(moved) + centre * plain]
    return groups(*out)


def spot_of(x):
    if x < 0:
        return 0, 3
    if x == SEG:
        return 0, 0
    return 1 + x // GRP, x % GRP


def put_ahead(off, sides, out, sums, below_x, xhat, shared, field, local_count):
    height = xhat.shape[0]
    at = pl.ds(0, height)
    low_x = jnp.concatenate([own_lanes(below_x, at), jnp.ones((height * field.shape[2], LANES), BF16)], axis=1)
    entries, alone = [], zero_row()
    lane = lane_of((1, LANES))
    for r in range(3):
        for tap, bare in pixel_taps(sides, off + r, height, low_x, (-1, 0, 1), True):
            for v, b in zip(tap, bare):
                alone = jnp.where(lane == ALONE + len(entries), b, alone)
                entries.append(v)
    centres = [fold(v) / local_count for v in row_sums(0, height, lambda at, k: (xhat[at, k], shared[at, k]))]
    probe = [flat(v[at, k] - c).astype(BF16) for v, c in zip((xhat, shared), centres) for k in range(2)]
    wide = jnp.concatenate(views(field, 0, height), axis=1)
    found = lax.dot_general(
        jnp.concatenate(probe, axis=1), wide, (((0,), (0,)), ((), ())), preferred_element_type=F32
    )
    ones = jnp.ones((8, wide.shape[0]), BF16)
    plain = jnp.dot(ones, wide, preferred_element_type=F32)[0:1]
    group = group_of((1, LANES))
    hidden = []
    for r in range(3):
        for s in range(3):
            val = zero_row()
            for y in range(SEG):
                d, a = spot_of(y + s - 1)
                spot = (3 * r + d) * LANES
                val = val + jnp.where(group == a, plain[:, spot : spot + LANES], 0.0)
            hidden.append(fold(val))
    packed = [groups(*hidden[0:4]), groups(*hidden[4:8]), hidden[8]]
    all_hidden = jnp.concatenate(packed, axis=0)
    last = [
        put_taps(
            found[2 * LANES * k : 2 * LANES * (k + 1)], out.at[:, 2 * k + 1 : 2 * k + 3, 0], (centres[k], all_hidden)
        )
        for k in range(2)
    ]
    entries += hidden
    entries.append(jnp.zeros((CH - len(entries), LANES), F32))
    out[:, 0, 0, :] = groups(jnp.concatenate(entries, axis=0), *last, jnp.zeros((CH, LANES), F32))
    notes(sums, *packed, alone)


def head_kernel(place, got, got_style, resid, sides, head_mat, w_head, below_x, ahead, image_sums, table, back, grad, xhat, pay, vec, decoded, slopes, grad_low, *, local_count, pixel_count, height):
    mean, inverse = merge_stats(row_of_each(got, 0), row_of_each(got, 1), local_count, pixel_count)
    notes(vec, inverse, mean)
    gain, bias = affine(table, 3)
    rows, segments = resid.shape[0], resid.shape[2]
    all_off, skipped, off = place[0], place[3], place[4]

    def norm_rows(i):
        at = pl.ds(4 * i, 4)
        for k in range(2):
            x = (resid[at, k] - mean) * inverse
            n = x * gain + bias
            s = sig_of(n)
            xhat[at, k] = x
            slopes[at, k] = slope(n, s)
            decoded[at, k] = (n * s).astype(BF16)

    loop(rows // 4, norm_rows, 10)
    head = head_mat[...]
    wide = jnp.concatenate([flat(decoded[:, 0]), flat(decoded[:, 1])], axis=1)
    bias_row = zero_row()
    for k in range(3):
        mine = (lane_of((1, LANES)) >> 3) == FLOW // 8 + k
        bias_row = jnp.where(mine, low(w_head[k : k + 1, CH : CH + 1]), bias_row)
    out = jnp.dot(wide, head, preferred_element_type=F32) + bias_row
    given = flat(sides[pl.ds(skipped + 1, rows)]).astype(F32)
    lane = lane_of(given.shape)
    is_flow = lane < LABEL
    near = [pltpu.roll(given, LANES - MASK + first, axis=1) for first in (FLOW, FLOW + 8, LABEL)]
    mask = jnp.where(lane < FLOW + 8, near[0], jnp.where(is_flow, near[1], near[2]))
    mask = jnp.where((lane >= FLOW) & (lane < LABEL + 8), mask, 0.0)
    count = jnp.sum(got_style[:, 2, 0, 3 * CH : 3 * CH + 1])
    diff = out - given / flow_scale
    hinge = jnp.maximum(out, 0.0) + jnp.log1p(jnp.exp(-jnp.abs(out)))
    loss = mask * jnp.where(is_flow, diff * diff, hinge - given * out)
    grad_out = (mask * jnp.where(is_flow, 2.0 * diff, sig_of(out) - given) / count).astype(BF16)
    at_row = lax.broadcasted_iota(jnp.int32, loss.shape, 0)
    inside = (at_row >= off * segments) & (at_row < (off + height) * segments)
    loss_sum = jnp.sum(jnp.where(inside, loss, 0.0))
    mine_out = jnp.where(inside, grad_out.astype(F32), 0.0).astype(BF16)
    outs = col_sum(mine_out.astype(F32))
    found = lax.dot_general(mine_out, wide, (((0,), (0,)), ((), ())), preferred_element_type=F32)
    shape = found.shape
    found = jnp.where((row_of(shape) & 7) == group_of(shape), found, 0.0)
    whole = [col_sum(found[FLOW + 8 * k : FLOW + 8 * k + 8]) for k in range(3)]
    whole = [fold(v[:, 0:LANES] + v[:, LANES:]) for v in whole]
    row = groups(*whole, zero_row())
    lane = lane_of((1, LANES))
    for k in range(3):
        row = jnp.where(lane == 3 * CH + k, jnp.sum(jnp.where((lane >> 3) == FLOW // 8 + k, outs, 0.0)), row)
    row = jnp.where(lane == 3 * CH + 3, loss_sum, row)
    y = lax.dot_general(grad_out, head, (((1,), (1,)), ((), ())), preferred_element_type=F32)
    for k, g in enumerate(blocks_of(y, rows)):
        grad[:, k] = g * slopes[:, k]
    factor = gain * inverse
    back_rows(grad_low, rows, lambda at, k: factor * grad[at, k], 10)
    shift_sum, scale_sum = own_sums(grad, xhat, off, height)
    y = conv(grad_low, back, off, height)
    slopes[0:height, 0], slopes[0:height, 1] = blocks_of(y, height)
    gain, bias = affine(table, 2)

    def links(at, k):
        x = below_x[pl.ds(all_off + at.start, at.size), k]
        g = slopes[at, k] * slope_at(x, gain, bias)
        return g, g * x

    below = [fold(v) for v in row_sums(0, height, links)]
    send(pay, groups(shift_sum, scale_sum, *below), row + image_sums[3:4], total_of(got, 2))
    send_parts(pay, 3, 5)
    pay[0:CH, 3:8] = ahead[...]


def own_sums(grad, xhat, first, rows):
    def both(at, k):
        g = grad[at, k]
        return g, g * xhat[at, k]

    return [fold(v) for v in row_sums(first, rows, both)]


def back_sums(got, pixel_count):
    whole = col_sum(got)
    return spread(whole, 0) / pixel_count, spread(whole, 1) / pixel_count


def low_sum(grad_low, first, rows):
    return fold(row_sums(first + 1, rows, lambda at, k: (grad_low[at, k].astype(F32),))[0])


def norm_back(grad, xhat, factor, shift, scale):
    return factor * (grad - (shift + xhat * scale))


def back_rows(grad_low, rows, value, unroll=5):
    def some(i):
        put_low(grad_low, 4 * i, *[value(pl.ds(4 * i, 4), k) for k in range(2)])

    blank(grad_low)
    loop(rows // 4, some, unroll)


def own_lanes(grad, at):
    return jnp.concatenate([flat(grad[at, k]).astype(BF16) for k in range(2)], axis=1)


def tap_sums(field, grad, first, rows, out, more=None):
    wide = jnp.concatenate(views(field, first, rows), axis=1)
    found = lax.dot_general(grad, wide, (((0,), (0,)), ((), ())), preferred_element_type=F32)
    return put_taps(found, out, more)


def put_taps(found, out, more=None):
    group = group_of((CH, LANES))
    taps = []
    for r in range(3):
        for s in range(3):
            val = jnp.zeros((CH, LANES), F32)
            for y in range(SEG):
                d, a = spot_of(y + s - 1)
                spot = (3 * r + d) * LANES
                val = val + jnp.where(group == a, found[CH * y : CH * y + CH, spot : spot + LANES], 0.0)
            taps.append(fold(val))
    for q in range(3):
        val = taps[4 * q]
        for b in range(1, min(4, 9 - 4 * q)):
            val = jnp.where(group == b, taps[4 * q + b], val)
        if more is not None:
            centre, sums = more
            val = val + column_of(centre) * sums[q : q + 1]
        if q == 2:
            return val
        out[:, q, :] = val


def column_of(v):
    shape = (CH, LANES)
    return jnp.sum(jnp.where(row_of(shape) == lane_of(shape), v, 0.0), axis=1, keepdims=True)


def at_lane(v, k):
    return jnp.sum(jnp.where(lane_of(v.shape) == k, v, 0.0), axis=1, keepdims=True)


def decoder_back_kernel(place, got, grad, xhat, mid_x, vec, vec_two, sums, table, back_two, weights, fields, lows, below, below_x, shared, pay, more, first_x, kept_grad, mid, low_two, low_one, field_two, field_one, field_zero, back_one, sems, *, spots, local_count, pixel_count):
    all_off, skipped, off = place[0], place[3], place[4]
    height = field_two.shape[0] - 2
    far_rows, near_rows = pl.ds(skipped, grad.shape[0]), pl.ds(all_off, height + 2)
    fetched = copies(
        sems,
        (back_at(weights), back_one),
        (spots(fields, "xhat_one").at[far_rows], below_x),
        (spots(fields, "shared").at[far_rows], shared),
        (spots(lows, "hidden_three").at[near_rows], field_two),
        (spots(lows, "merged").at[near_rows], field_one),
        (spots(lows, "hidden_one").at[near_rows], field_zero),
    )
    handed = copies(sems.at[6:], (spots(fields, "xhat_zero").at[pl.ds(all_off, height)], first_x))
    devices = got.shape[0]
    rows = grad.shape[0]
    total = total_of(got, 0)
    shift, scale = spread(total, 0) / pixel_count, spread(total, 1) / pixel_count
    inverse, mean = vec[0:1], vec[1:2]
    factor = affine(table, 3)[0] * inverse
    slant = scale * inverse
    held, carried = factor * (shift - slant * mean), factor * slant
    links = got[0:CH, 2, 0, :] * groups(held, carried, held, carried)
    group = group_of(links.shape)
    mine = (lane_of(links.shape) & 31) == row_of(links.shape)

    def across(pick):
        column = jnp.sum(jnp.where(pick, links, 0.0), axis=1, keepdims=True)
        return col_sum(jnp.where(mine, column, 0.0))

    shift_two = spread(total, 2) - across(group < 2)
    scale_two = spread(total, 3) - across(group >= 2)
    entry = total_of(got, 3)
    notes(more, scale_two, shift_two, total_of(got, 4), total_of(got, 5), spread(entry, 1))

    def value(at, k):
        g = norm_back(grad[at, k], xhat[at, k], factor, shift, scale)
        kept_grad[at, k] = g
        return g

    back_rows(low_two, rows, value)

    @pl.when(place[0] >= 0)
    def _():
        mid[:, 0], mid[:, 1] = blocks_of(conv(low_two, back_two, 0, rows), rows)

    gain, bias = affine(table, 2)
    factor = gain * vec_two[0:1]
    shift, scale = shift_two / pixel_count, scale_two / pixel_count

    def value_two(at, k):
        x = mid_x[pl.ds(skipped + at.start, at.size), k]
        return norm_back(mid[at, k] * slope_at(x, gain, bias), x, factor, shift, scale)

    back_rows(low_one, rows, value_two)
    wait(fetched)
    sum_two = low_sum(low_two, off, height)
    sum_one = low_sum(low_one, off, height)
    y = conv(low_one, back_one, 0, rows)
    gain, bias = affine(table, 1)
    for k, y in enumerate(blocks_of(y, rows)):
        g = (y + kept_grad[:, k]).reshape(rows // 2, 2, -1, LANES)
        both = flat(g[:, 0] + g[:, 1])
        both = (both + partner(both)).reshape(rows // 2, 1, -1, LANES)
        g = g * slope_at(below_x[:, k], gain, bias).reshape(g.shape) + both * shared[:, k].reshape(g.shape)
        below[:, k] = g.reshape(rows, -1, LANES)
    shift_sum, scale_sum = own_sums(below, below_x, off, height)
    send(pay, groups(shift_sum, scale_sum, sum_one, sum_two))
    entry = spread(entry, 0)
    pay[:, 1, 0, :] = jnp.broadcast_to(entry, (devices, LANES))
    at = pl.ds(off + 1, height)
    last_two = tap_sums(field_two, own_lanes(low_two, at), 0, height, send_parts(pay, 2, 2))
    last_one = tap_sums(field_one, own_lanes(low_one, at), 0, height, send_parts(pay, 4, 2))
    centre = shift_sum / local_count
    at = pl.ds(off, height)
    grad = jnp.concatenate([flat(below[at, k] - centre).astype(BF16) for k in range(2)], axis=1)
    last_zero = tap_sums(field_zero, grad, 0, height, send_parts(pay, 6, 2), (centre, sums))
    pay[0:CH, 1, 0, :] = groups(last_two, last_one, last_zero, jnp.broadcast_to(entry, (CH, LANES)))
    wait(handed)


def summed_kernel(place, got, got_style, got_head, grad, xhat, shared, vec, more_two, table, w_style, sides, back, below_x, pay, more, below, grad_low, *, pixel_count, pool_cells, parts):
    off, mine = place[0], place[4]
    height = below.shape[0]
    devices = got.shape[0]
    rows = grad.shape[0]
    dims = (((1,), (1,)), ((), ()))
    first = row_of_each(got, 0)
    each = wide_dot(spread(first, 2), diagonal_blocks(w_style[0]), dims) + wide_dot(
        spread(first, 3), diagonal_blocks(w_style[1]), dims
    )
    each = each / pool_cells
    total = col_sum(first)
    shift = spread(total, 0) + col_sum(each * by_image(spread(row_of_each(got_style, 2), 1), parts))
    scale = spread(total, 1) + col_sum(each * by_image(spread(row_of_each(got_style, 2), 2), parts))
    style_grad = col_sum(jnp.where(row_of(each.shape) // parts == place[2] // parts, each, 0.0))
    factor = affine(table, 1)[0] * vec[0:1]
    shift_mean, scale_mean = shift / pixel_count, scale / pixel_count
    def value(at, k):
        return norm_back(grad[at, k] + shared[at, k] * style_grad, xhat[at, k], factor, shift_mean, scale_mean)

    back_rows(grad_low, rows, value)
    gain, bias = affine(table, 0)
    for k, y in enumerate(blocks_of(conv(grad_low, back, mine, height), height)):
        below[:, k] = y * slope_at(below_x[:, k], gain, bias)
    me = place[2]
    weights = at_lane(by_image(each, parts), me)
    hidden = spread(got[0:CH, 1, 0, :], 3)
    hidden = [groups(*[hidden[18 + t : 19 + t] for t in range(4 * q, min(4 * q + 4, 9))]) for q in range(3)]
    last = total_of(got, 1)
    direct = [total_of(got, 6), total_of(got, 7), spread(last, 2)]
    shares = [row_of_each(got_head, 6), row_of_each(got_head, 7), spread(row_of_each(got_head, 3), 2)]
    shard = []
    for q in range(3):
        val = direct[q] + col_sum(weights * shares[q])
        val = val - at_lane(shift_mean, me) * hidden[q] - at_lane(scale_mean, me) * more_two[2 + q : 3 + q]
        shard.append(at_lane(factor, me) * val)
    at = pl.ds(mine + 1, height)
    side = pixel_taps(sides, off + 1, height, own_lanes(grad_low, at), (0,))[0]
    low_below = own_lanes(below, pl.ds(0, height))
    taps = []
    for r in range(3):
        for tap in pixel_taps(sides, off + r, height, low_below, (-1, 0, 1)):
            taps.extend(tap)
    sums = [in_parts(v, 3) for v in own_sums(below, below_x, 0, height)]
    entries = [in_parts(v, 2) for v in taps + side]
    tail = [shard[2]] + [v[0] for v in entries] + [v[1] for v in entries]
    tail += [zero_row()] * (-len(tail) % 4)
    values = [
        groups(sums[0][0], sums[1][0], sums[0][1], sums[1][1]),
        groups(sums[0][2], sums[1][2], spread(last, 0), spread(last, 1)),
        *[total_of(got, r) for r in range(2, 6)],
        *shard[0:2],
        *[groups(*tail[k : k + 4]) for k in range(0, len(tail), 4)],
    ]
    values += [zero_row()] * (len(values) % 2)
    for k in range(len(values) // 2):
        pair = jnp.concatenate(values[2 * k : 2 * k + 2], axis=0).astype(BF16)
        pay[:, k] = jnp.broadcast_to(pair[None], (devices, 2, LANES))
    notes(more, scale, shift)


def pixel_taps(sides, row, rows, grad, shift, alone=False):
    x = flat(sides[pl.ds(row, rows)])
    found = lax.dot_general(x, grad, (((0,), (0,)), ((), ())), preferred_element_type=F32)
    inside, channel, column = image_lanes((LANES, 2 * LANES))
    here = column - group_of((LANES, 2 * LANES))
    out = []
    for s in shift:
        both, bare = [], []
        for c in range(2):
            v = col_sum(jnp.where(inside & (channel == c) & (here == s), found[:, 0 : 2 * LANES], 0.0))
            both.append(fold(v[:, 0:LANES] + v[:, LANES:]))
            if alone:
                cut = slice(0, LANES)
                hit = (inside & (channel == c) & (column >= s) & (column < s + SEG))[:, cut]
                bare.append(col_sum(jnp.where(hit, found[:, 2 * LANES :], 0.0)))
        out.append((both, bare) if alone else both)
    return out


def adamw(master, moment, square, grad, rate):
    new_moment = beta_one * moment + (1.0 - beta_one) * grad
    new_square = beta_two * square + (1.0 - beta_two) * grad * grad
    moment_hat = new_moment / (1.0 - beta_one**STEP)
    square_hat = new_square / (1.0 - beta_two**STEP)
    new_master = master - rate * (moment_hat / (jnp.sqrt(square_hat) + adam_eps) + weight_decay * master)
    return new_master, new_moment, new_square


def put(at, refs, grad, rate, outs):
    found = adamw(*[ref[at] for ref in refs], grad, rate)
    for out, value in zip(outs, found + (found[0].astype(BF16),)):
        out[at] = value


def update_early(
    got_one_back, got_head, got_style, pay, style, w_style, w_head, m_style, m_head, s_style, s_head,
    loss_out, count_out, style_master, style_moment, style_square, head_master, head_moment, head_square, head_copy,
):
    count_out[0, 0] = jnp.sum(got_style[:, 2, 0, 3 * CH : 3 * CH + 1])
    loss_out[0, 0] = jnp.sum(got_head[:, 1, 0, 99:100])
    dims = (((0,), (0,)), ((), ()))
    for i in range(2):
        sums = spread(row_of_each(got_one_back, 0), 2 + i)
        grad = lax.dot_general(style[...], sums, dims, precision=highest, preferred_element_type=F32)
        put(i, (w_style, m_style, s_style), grad[0:CH, 0:CH], rate_table[2], (style_master, style_moment, style_square))

    head = total_of(got_head, 1)
    lane = lane_of((1, LANES))
    rows = []
    for k in range(3):
        last = jnp.sum(jnp.where(lane == 3 * CH + k, head, 0.0), axis=1, keepdims=True)
        rows.append(jnp.where(lane < CH, spread(head, k), last))
    grad = jnp.concatenate(rows, axis=0)[:, 0 : CH + 1]
    put(slice(None), (w_head, m_head, s_head), grad, rate_table[3], (head_master, head_moment, head_square, head_copy))


def update_late(
    got, got_one_back, got_head, more, more_two, vec, w_first, w_convs, table, m_first, m_convs, m_norms, s_first, s_convs, s_norms,
    first_master, first_moment, first_square, first_copy,
    convs_master, convs_moment, convs_square, convs_copy,
    norms_master, norms_moment, norms_square, *, pixel_count
):
    refs = (w_convs, m_convs, s_convs)
    outs = (convs_master, convs_moment, convs_square, convs_copy)
    pairs = [got[:, k].astype(F32) for k in range(got.shape[1])]
    packs = [[pairs[k // 2][0:CH, k % 2, :].T for k in ks] for ks in ((6, 7, 8), (4, 5, 1), (2, 3, 1))]
    for i, pack in enumerate(packs):
        for t in range(9):
            b = t % 4 if t < 8 else (0, 3, 2)[i]
            put((i, t), refs, pack[t // 4][CH * b : CH * b + CH], rate_table[1], outs)

    totals = [jnp.sum(pair, axis=0) for pair in pairs]
    totals = [pair[h : h + 1] for pair in totals for h in range(2)]
    shift, scale = [spread(totals[0], k) + (spread(totals[0], 2 + k) + spread(totals[1], k)) for k in range(2)]
    factor = affine(table, 0)[0] * vec[0:1]
    by_x = spread(got_one_back[0:CH, 1, 0, :], 3)
    alone = total_of(got_head, 1)
    refs = (w_first, m_first, s_first)
    outs = (first_master, first_moment, first_square, first_copy)
    for t in range(10):
        pair = []
        for e in (2 * t, 2 * t + 1):
            k, b = divmod(1 + e, 4)
            v = spread(totals[8 + k], b)
            k, b = divmod(21 + e, 4)
            v = v + spread(totals[8 + k], b)
            if t < 9:
                v = factor * (v - (at_lane(alone, ALONE + e) * shift + by_x[e : e + 1] * scale) / pixel_count)
            pair.append(v[:, 0:CH])
        put(t, refs, jnp.concatenate(pair, axis=0), rate_table[0], outs)

    three_sums = total_of(got_head, 0)
    scales = [scale, more[0:1], more_two[0:1], spread(three_sums, 1)]
    shifts = [shift, more[1:2], more_two[1:2], spread(three_sums, 0)]
    for i, rows in enumerate((scales, shifts)):
        grad = jnp.concatenate(rows, axis=0)[:, 0:CH]
        put(i, (table, m_norms, s_norms), grad, rate_table[4], (norms_master, norms_moment, norms_square))


def update_kernel(*refs, pixel_count):
    ins, outs = refs[:23], refs[23:]
    late, early = ins[:15], ins[15:]
    update_late(*late, *outs[:11], pixel_count=pixel_count)
    update_early(late[1], late[2], early[0], None, *early[1:], *outs[11:])


def far(x):
    return ("far", x)


def call(kernel, outs, *operands, scalars=0, scratch=(), sems=0, scalar_outs=(), aliases=None, limit=VMEM_LIMIT, name):
    smem = pl.BlockSpec(memory_space=pltpu.SMEM)
    vmem = pl.BlockSpec(memory_space=pltpu.VMEM)
    hbm = pl.BlockSpec(memory_space=pltpu.HBM)
    is_far = lambda x: isinstance(x, tuple) and x[0] == "far"
    in_specs = [smem if i < scalars else hbm if is_far(x) else vmem for i, x in enumerate(operands)]
    out_specs = [smem if i in scalar_outs else hbm if is_far(x) else vmem for i, x in enumerate(outs)]
    plain = lambda x: x[1] if is_far(x) else x
    shapes = [pltpu.VMEM(shape, dtype) for shape, dtype in scratch]
    if sems:
        shapes.append(pltpu.SemaphoreType.DMA((sems,)))
    return pl.pallas_call(
        kernel,
        out_shape=[jax.ShapeDtypeStruct(*plain(x)) for x in outs],
        in_specs=in_specs,
        out_specs=out_specs,
        scratch_shapes=shapes,
        input_output_aliases=aliases or {},
        compiler_params=pltpu.CompilerParams(vmem_limit_bytes=limit),
        name=name,
    )(*[plain(x) for x in operands])


def exchange(pay):
    return lax.all_to_all(pay, ("row", "col"), 0, 0)


def local(
    image_batch, valid_mask, flow_target, cell_labels,
    w_first, w_convs, w_style, w_head, batch_norm_table,
    mom_first, mom_convs, mom_style, mom_head, mom_norms,
    sqr_first, sqr_convs, sqr_style, sqr_head, sqr_norms,
):
    images, block_rows, block_cols, _ = image_batch.shape
    row_count, col_count = lax.axis_size("row"), lax.axis_size("col")
    devices = row_count * col_count
    parts = devices // images
    image_rows, image_cols = row_count * block_rows, col_count * block_cols
    assert devices == parts * images and block_rows == RIM and block_cols == 2 * block_rows * 2
    assert image_rows % (parts * RIM) == 0 and devices >= CH
    height = image_rows // parts
    rows = min(image_rows, height + RIM * min(2, parts - 1))
    segments = image_cols // SEG
    local_count = float(height * image_cols)
    pixel_count = local_count * devices
    pool_cells = float(image_rows * image_cols // 4)
    part = functools.partial
    counts = dict(local_count=local_count, pixel_count=pixel_count, height=height)
    styled = dict(pool_cells=pool_cells, parts=parts)

    me = lax.axis_index("row") * col_count + lax.axis_index("col")
    first_row = (me % parts) * height
    start = jnp.clip(first_row - RIM, 0, image_rows - rows)
    off = first_row - start
    back_rim = RIM // 2
    rows_back = min(rows, height + back_rim * min(2, parts - 1))
    skipped = jnp.clip(off - back_rim, 0, rows - rows_back)
    place = jnp.stack([off, start // block_rows, me, skipped, off - skipped]).astype(jnp.int32)

    field = ((rows, 2, segments, LANES), F32)
    own_field = ((height,) + field[0][1:], F32)
    back_field = ((rows_back,) + field[0][1:], F32)
    low_field = ((rows + 2, 3, segments, LANES), BF16)
    own_low = ((height + 2,) + low_field[0][1:], BF16)
    back_low = ((rows_back + 2,) + low_field[0][1:], BF16)
    vec = ((8, LANES), F32)

    def payload(count):
        return ((devices, count, 1, LANES), F32)

    nine = ((BACK, 2 * LANES), BF16)
    ten = ((FORWARD, 2 * LANES), BF16)

    places = {
        name: i * count
        for count, names in (
            (rows, ("xhat_zero", "xhat_one", "shared")),
            (rows + 2, ("hidden_one", "hidden_three", "merged")),
        )
        for i, name in enumerate(names)
    }

    def spots(store, name):
        count = rows if name[0] in "xs" else rows + 2
        return store.at[places[name] : places[name] + count]

    def store_of(like):
        shape, dtype = like
        row_bytes = shape[1] * segments * LANES * jnp.dtype(dtype).itemsize
        return far(((-(-STORE_BYTES // row_bytes),) + shape[1:], dtype))

    inputs = (
        jnp.transpose(image_batch, (0, 1, 3, 2)), jnp.transpose(flow_target, (0, 1, 3, 2)), cell_labels, valid_mask
    )
    (pay,) = call(
        pack_kernel,
        [((devices, 16, LANES), BF16)],
        *[far(v) for v in inputs],
        scratch=[(v.shape, v.dtype) for v in inputs], sems=4, limit=WHOLE_VMEM, name="pack",
    )
    got_inputs = exchange(pay)
    head_rows = w_head.T
    weights, back_zero, back_two, head_mat = call(
        prepare,
        [far(((STORE_BYTES // (4 * LANES), 2 * LANES), BF16)), far(nine), far(nine), far(((2 * LANES, LANES), BF16))],
        far(w_first), far(w_convs), far(head_rows),
        scratch=[
            (w_first.shape, F32), (w_convs.shape, F32), (head_rows.shape, F32), ((BACK_AT + BACK, 2 * LANES), BF16),
            nine, nine, ((2 * LANES, LANES), BF16),
        ],
        sems=8, limit=WHOLE_VMEM, name="prepare",
    )

    first_mat, taps = call(
        hand_kernel, [((3 * LANES, 2 * LANES), BF16), ten], far(weights), sems=2, name="hand"
    )
    sides, raw, pay, count = call(
        part(start_kernel, local_count=local_count, height=height, sources=col_count),
        [((rows + 2, segments, LANES), BF16), field, payload(2), vec],
        place, got_inputs, first_mat,
        scalars=1, name="image_conv",
    )
    got_zero = exchange(pay)
    summed, pay, inv_zero, fields, lows = call(
        part(first_kernel, spots=spots, **counts),
        [field, payload(2), vec, store_of(field), store_of(low_field)],
        place, got_zero, raw, sides, batch_norm_table, taps,
        scalars=1, scratch=[low_field, field], sems=2, name="first_block",
    )
    got_one = exchange(pay)

    raw, pay, inv_one, merged, taps, fields, lows = call(
        part(pool_kernel, spots=spots, **counts),
        [field, payload(3), vec, low_field, nine, store_of(field), store_of(low_field)],
        place, got_one, summed, count, batch_norm_table, far(weights), far(fields), far(lows),
        scalars=1, scratch=[field, field, nine], sems=5,
        aliases={6: 5, 7: 6}, name="pool_and_merge",
    )
    got_style = exchange(pay)

    resid, pay, inv_two, style, xhat_two, ahead, hidden_sums, lows = call(
        part(style_kernel, spots=spots, **styled, **counts),
        [back_field, payload(3), vec, ((devices, LANES), F32), field, ((CH, 5, 1, LANES), F32), vec, store_of(low_field)],
        place, got_style, raw, merged, batch_norm_table, w_style, far(w_convs), taps, sides, far(fields),
        far(lows),
        scalars=1, scratch=[low_field, field, (w_convs.shape[1:], F32), own_field, own_field, own_field, own_low], sems=6,
        aliases={10: 7}, name="decoder",
    )
    got_three = exchange(pay)

    grad_three, xhat_three, pay, inv_three = call(
        part(head_kernel, **counts),
        [back_field, back_field, payload(8), vec],
        place, got_three, got_style, resid, sides, head_mat, head_rows, xhat_two, ahead, hidden_sums, batch_norm_table, back_two,
        scalars=1, scratch=[((rows_back, 2, segments, LANES), BF16), back_field, back_low], name="head",
    )
    got_head = exchange(pay)

    grad_one, xhat_one, shared, pay, more_two, xhat_zero = call(
        part(decoder_back_kernel, spots=spots, local_count=local_count, pixel_count=pixel_count),
        [back_field, back_field, back_field, payload(8), vec, own_field],
        place, got_head, grad_three, xhat_three, xhat_two, inv_three, inv_two, hidden_sums, batch_norm_table, back_two, far(weights),
        far(fields), far(lows),
        scalars=1, scratch=[back_field, back_field, back_low, back_low, own_low, own_low, own_low, nine], sems=7,
        name="decoder_back",
    )
    got_one_back = exchange(pay)

    pay, more = call(
        part(summed_kernel, pixel_count=pixel_count, **styled),
        [((devices, 10, 2, LANES), BF16), vec],
        place, got_one_back, got_style, got_head, grad_one, xhat_one, shared, inv_one, more_two, batch_norm_table, w_style,
        sides, back_zero, xhat_zero,
        scalars=1, scratch=[own_field, back_low], name="summed_back",
    )
    got_last = exchange(pay)

    def results(param, copy):
        return [(param.shape, F32)] * 3 + [(param.shape, BF16)] * copy

    found = call(
        part(update_kernel, pixel_count=pixel_count),
        results(w_first, 1)
        + results(w_convs, 1)
        + results(batch_norm_table, 0)
        + [((1, 1), F32), ((1, 1), F32)]
        + results(w_style, 0)
        + results(head_rows, 1),
        got_last, got_one_back, got_head, more, more_two, inv_zero,
        w_first, w_convs, batch_norm_table, mom_first, mom_convs, mom_norms, sqr_first, sqr_convs, sqr_norms,
        got_style, style, w_style, head_rows, mom_style, mom_head.T, sqr_style, sqr_head.T,
        scalar_outs=(11, 12), name="update",
    )
    late, early = found[:11], found[11:]
    loss, count = early[0].reshape(()), early[1].reshape(())
    head = tuple(value.T for value in early[5:9])
    return (loss, count, *late[0:8], *early[2:5], *head, *late[8:11])


def solution(mesh):
    field = P(None, "row", "col", None)
    plane = P(None, "row", "col")
    return jax.shard_map(
        local,
        mesh=mesh,
        in_specs=(field, plane, field, plane) + (P(),) * 15,
        out_specs=(P(),) * 20,
        check_vma=False,
    )
```

```python
import functools

import jax
import jax.numpy as jnp
from jax import lax
from jax.experimental import pallas as pl
from jax.experimental.pallas import tpu as pltpu
from jax.sharding import PartitionSpec as P

STEP = 5

highest = lax.Precision.HIGHEST
norm_eps = 1e-05
flow_scale = 32.0
adam_eps = 1e-08
weight_decay = 0.01
beta_one = 0.5
beta_two = 0.5
rate_table = (0.2, 0.05, 0.15, 0.15, 0.2)

CH = 32
GRP = 4
SEG = 8
LANES = 128
RIM = 8
FLOW, LABEL, MASK = 16, 32, 40
LEFT, RIGHT = 64, 96
ALONE = 100
AFTER, ROW, BEFORE = 32, 33, 64
F32 = jnp.float32
BF16 = jnp.bfloat16
VMEM_LIMIT = 36 * 1024 * 1024
WHOLE_VMEM = 56 * 1024 * 1024
STORE_BYTES = 32 * 1024 * 1024
FORWARD = 10 * LANES
BACK = 9 * LANES
IMAGE_AT = 3 * FORWARD
BACK_AT = IMAGE_AT + 3 * LANES


def lane_of(shape):
    return lax.broadcasted_iota(jnp.int32, shape, len(shape) - 1)


def row_of(shape):
    return lax.broadcasted_iota(jnp.int32, shape, 0)


def group_of(shape):
    return lane_of(shape) >> 5


def fold(v):
    return v + pltpu.roll(v, 32, axis=1) + (pltpu.roll(v, 64, axis=1) + pltpu.roll(v, 96, axis=1))


def spread(v, k):
    return fold(jnp.where(group_of(v.shape) == k, v, 0.0))


def partner(v):
    odd = (group_of(v.shape) & 1) == 1
    return jnp.where(odd, pltpu.roll(v, 32, axis=1), pltpu.roll(v, 96, axis=1))


def tile4(v):
    return jnp.concatenate([v, v, v, v], axis=1)


def col_sum(v):
    return jnp.sum(v, axis=0, keepdims=True)


def zero_row():
    return jnp.zeros((1, LANES), F32)


def groups(*values):
    group = group_of(values[0].shape)
    out = values[-1]
    for k in range(len(values) - 2, -1, -1):
        out = jnp.where(group == k, values[k], out)
    return out


def low(v):
    return v.astype(BF16).astype(F32)


def sig_of(v):
    return 0.5 + 0.5 * jnp.tanh(0.5 * v)


def slope(n, sig):
    return sig * (1.0 + n * (1.0 - sig))


def slope_at(x, gain, bias):
    n = x * gain + bias
    return slope(n, sig_of(n))


def flat(v):
    return v.reshape(-1, LANES)


def loop(count, body, unroll=5):
    def step(i, carry):
        body(i)
        return carry

    lax.fori_loop(0, count, step, 0, unroll=min(count, unroll))


def copies(sems, *pairs):
    found = []
    for i, (source, target) in enumerate(pairs):
        found.append(pltpu.make_async_copy(source, target, sems.at[i]))
        found[-1].start()
    return found


def wait(started):
    for copy in started:
        copy.wait()


def shift_segments(v, way):
    half = v.shape[1]
    at = lax.broadcasted_iota(jnp.int32, v.shape, 1)
    if way == 1:
        return jnp.where(at == 0, 0.0, pltpu.roll(v, 1, axis=1))
    return jnp.where(at == half - 1, 0.0, pltpu.roll(v, half - 1, axis=1))


def beside(first, second):
    half = first.shape[1] // 2
    left = jnp.concatenate([shift_segments(second[:, half:], 1), second[:, :half]], axis=1)
    right = jnp.concatenate([first[:, half:], shift_segments(first[:, :half], -1)], axis=1)
    return left, right


def put_low(ref, row, first, second, marked=False):
    left, right = beside(first, second)
    lane = lane_of(left.shape)
    edge = jnp.where(lane < 64, right, left)
    if marked:
        at = lax.broadcasted_iota(jnp.int32, left.shape, 1)
        edge = jnp.where(lane == ROW, 1.0, edge)
        edge = jnp.where(lane == AFTER, jnp.where(at == left.shape[1] - 1, 0.0, 1.0), edge)
        edge = jnp.where(lane == BEFORE, jnp.where(at == 0, 0.0, 1.0), edge)
    at = pl.ds(row + 1, first.shape[0])
    for k, v in enumerate((first, second, edge)):
        ref[at, k] = v.astype(BF16)


def blank(ref):
    zero = jnp.zeros((1,) + ref.shape[1:], ref.dtype)
    ref[0:1] = zero
    ref[ref.shape[0] - 1 : ref.shape[0]] = zero


def views(src, row, rows):
    return [flat(src[pl.ds(row + r, rows), k]) for r in range(3) for k in (2, 0, 1)]


def conv(src, mat, row, rows, *more):
    wide = jnp.concatenate(views(src, row, rows) + list(more), axis=1)
    return jnp.dot(wide, mat[...], preferred_element_type=F32)


def blocks_of(y, rows):
    return [y[:, k * LANES : (k + 1) * LANES].reshape(rows, -1, LANES) for k in range(2)]


def narrow(v):
    while v.shape[0] > 1:
        half = v.shape[0] // 2
        v = v[:half] + v[half:]
    return v[0]


def row_sums(first, rows, values):
    step = 4

    def add(i, carry):
        found = [values(pl.ds(first + step * i, step), k) for k in range(2)]
        return tuple(c + a + b for c, a, b in zip(carry, *found))

    shapes = jax.eval_shape(lambda: values(pl.ds(0, step), 0))
    zeros = tuple(jnp.zeros(v.shape, F32) for v in shapes)
    found = lax.fori_loop(0, rows // step, add, zeros, unroll=min(rows // step, 8))
    return [col_sum(narrow(v)) for v in found]


def local_stats(v, first, rows, count):
    count = count / GRP
    pivot = col_sum(v[first, 0] + v[first, 1]) / (2 * v.shape[2])

    def moments(at, k):
        away = v[at, k] - pivot
        return away, away * away

    total, square = row_sums(first, rows, moments)
    return pivot + total / count, square - total * (total / count)


def merge_stats(means, squares, local_count, pixel_count):
    mean = fold(col_sum(means)) / (GRP * means.shape[0])
    away = means - mean
    total = fold(col_sum(squares + (local_count / GRP) * (away * away)))
    return mean, lax.rsqrt(total / pixel_count + norm_eps)


def row_of_each(got, r):
    return got[:, r, 0, :]


def total_of(got, r):
    return col_sum(row_of_each(got, r))


def send(pay, *rows):
    for r, row in enumerate(rows):
        pay[:, r, 0, :] = jnp.broadcast_to(row, (pay.shape[0], LANES))


def send_parts(pay, first, count):
    devices = pay.shape[0]
    if devices > CH:
        for r in range(first, first + count):
            pay[CH:, r, 0, :] = jnp.zeros((devices - CH, LANES), F32)
    return pay.at[0:CH, first : first + count, 0]


def affine(table, q):
    return tile4(table[0, q : q + 1, :]), tile4(table[1, q : q + 1, :])


def diagonal_blocks(mat):
    wide = tile4(mat)
    group = group_of(wide.shape)
    return jnp.concatenate([jnp.where(group == b, wide, 0.0) for b in range(GRP)], axis=0)


def notes(ref, *rows):
    for i, row in enumerate(rows):
        ref[i : i + 1, :] = row


def taps_at(store, i):
    return store.at[FORWARD * i : FORWARD * i + (BACK if i else FORWARD)]


def image_at(store):
    return store.at[IMAGE_AT : IMAGE_AT + 3 * LANES]


def back_at(store):
    return store.at[BACK_AT : BACK_AT + BACK]


def pack_kernel(image_in, flow_in, labels_in, valid_in, out, image, flow, labels, valid, sems):
    fetched = copies(sems, (image_in, image), (flow_in, flow), (labels_in, labels), (valid_in, valid))
    images, height, _, width = image.shape
    parts = out.shape[0] // images
    wait(fetched)
    fields = [image[:, :, c, :].astype(F32) for c in range(2)]
    fields += [flow[:, :, c, :].astype(F32) for c in range(2)]
    fields += [labels[...].astype(F32), valid[...].astype(F32)]
    halves = width // 16
    shape = (width, halves * LANES)
    lane = lane_of(shape)
    column = (lane >> 7) * 16 + ((lane >> 6) & 1) * 8 + (lane & 7)
    hit = row_of(shape) == column
    which = (lane >> 3) & 7
    total = jnp.zeros((images * height, halves * LANES), F32)
    for k, v in enumerate(fields):
        x = v.reshape(images * height, width).astype(BF16)
        mat = jnp.where(hit & (which == k), 1.0, 0.0).astype(BF16)
        total = total + jnp.dot(x, mat, preferred_element_type=F32)
    for b in range(images):
        rows = total[b * height : (b + 1) * height]
        slot = jnp.concatenate([rows[:, h * LANES : (h + 1) * LANES] for h in range(halves)], axis=0).astype(BF16)
        for p in range(parts):
            out[b * parts + p] = slot


COLUMNS = ((8, None, None, -1), (0, 1, 2, 3), (4, 5, 6, 7))


def conv_matrix(taps, mats, base, back):
    out_at = group_of((CH, 2 * LANES))
    for r in range(3):
        wide = []
        for s in range(3):
            if back:
                k = taps[3 * (2 - r) + s]
                k = jnp.concatenate([k, k, k, k], axis=0).T
            else:
                k = tile4(taps[3 * r + s])
            wide.append(jnp.concatenate([k, k], axis=1))
        for d in range(3):
            for a in range(GRP):
                val = jnp.zeros((CH, 2 * LANES), F32)
                column = COLUMNS[d][a]
                if column is not None:
                    for s in range(3):
                        val = jnp.where(out_at == (column + s - 1 if back else column + 1 - s), wide[s], val)
                mats[pl.ds(base + (3 * r + d) * LANES + CH * a, CH), :] = val.astype(BF16)


def image_lanes(shape):
    at = row_of(shape)
    kind = at >> 5
    column = (at & 7) + jnp.where(kind == LEFT // 32, -SEG, jnp.where(kind == RIGHT // 32, SEG, 0))
    return (kind != 1) & ((at & 31) < 16), (at >> 3) & 1, column


def first_taps(w_first, t):
    found = [tile4(low(w_first[t][c : c + 1])) for c in range(2)]
    return [jnp.concatenate([v, v], axis=1) for v in found]


def image_matrix(w_first, r):
    shape = (LANES, 2 * LANES)
    inside, channel, here = image_lanes(shape)
    val = jnp.zeros(shape, F32)
    for s in range(3):
        for c, tap in enumerate(first_taps(w_first, 3 * r + s)):
            val = jnp.where(inside & (channel == c) & (here == group_of(shape) + s - 1), tap, val)
    return val.astype(BF16)


def prepare(w_first_in, w_convs_in, w_head_in, store, back_zero_out, back_two_out, head_out, w_first, w_convs, w_head, mats, back_zero, back_two, head_mat, sems):
    wait(copies(sems, (w_first_in, w_first), (w_convs_in, w_convs), (w_head_in, w_head)))
    stored = []

    def keep(source, target):
        stored.extend(copies(sems.at[len(stored) :], (source, target)))

    for i, back, out in ((2, back_two, back_two_out), (0, back_zero, back_zero_out)):
        conv_matrix(w_convs.at[i], back, 0, True)
        keep(back, out)
    conv_matrix(w_convs.at[1], mats, BACK_AT, True)
    keep(back_at(mats), back_at(store))
    shape = (LANES, 2 * LANES)
    inside, channel, here = image_lanes(shape)
    val = jnp.zeros(shape, F32)
    for c, tap in enumerate(first_taps(w_first, 9)):
        val = jnp.where((row_of(shape) < 16) & (channel == c) & (here == group_of(shape)), tap, val)
    mats[BACK:FORWARD, :] = val.astype(BF16)
    for i in range(3):
        conv_matrix(w_convs.at[i], mats, FORWARD * i, False)
        keep(taps_at(mats, i), taps_at(store, i))
    for r in range(3):
        mats[IMAGE_AT + LANES * r : IMAGE_AT + LANES * (r + 1), :] = image_matrix(w_first, r)
    keep(image_at(mats), image_at(store))
    lane = lane_of((CH, LANES))
    head = jnp.zeros((CH, LANES), F32)
    diagonal = row_of((CH, CH)) == lane_of((CH, CH))
    for k in range(3):
        column = jnp.sum(jnp.where(diagonal, low(w_head[k : k + 1, 0:CH]), 0.0), axis=1, keepdims=True)
        head = jnp.where((lane >> 3) == FLOW // 8 + k, column, head)
    for y in range(SEG):
        head_mat[CH * y : CH * (y + 1), :] = jnp.where((lane & 7) == y, head, 0.0).astype(BF16)
    keep(head_mat, head_out)
    wait(stored)


def hand_kernel(weights, first_mat, sems):
    wait(copies(sems, (image_at(weights), first_mat)))


def start_kernel(place, got, first_mat, weights, sides, raw, pay, vec, taps, sems, *, local_count, height, sources):
    fetched = copies(sems, (taps_at(weights, 0), taps))
    rows, segments = raw.shape[0], raw.shape[2]
    off, block = place[0], place[1]
    blank(sides)

    def eight(t):
        v = got[pl.ds((block + t) * sources, sources)].astype(F32)
        v = jnp.swapaxes(v.reshape(segments // 2, 8, LANES), 0, 1)
        near = lane_of(v.shape) < 64
        v = jnp.concatenate([jnp.where(near, v, 0.0), jnp.where(near, pltpu.roll(v, 64, axis=2), 0.0)], axis=1)
        pixels = jnp.where(lane_of(v.shape) < 16, v, 0.0)
        left, right = beside(pixels, pixels)
        v = v + pltpu.roll(left, LEFT, axis=2) + pltpu.roll(right, RIGHT, axis=2)
        sides[pl.ds(8 * t + 1, 8)] = v.astype(BF16)

    loop(rows // 8, eight)
    y = None
    for r in range(3):
        part = jnp.dot(flat(sides[r : r + rows]), first_mat[LANES * r : LANES * (r + 1)], preferred_element_type=F32)
        y = part if y is None else y + part
    raw[:, 0], raw[:, 1] = blocks_of(y, rows)
    mean, square = local_stats(raw, off, height, local_count)
    mask = jnp.zeros(sides.shape[1:], F32)
    for i in range(height):
        mask = mask + sides[off + 1 + i].astype(F32)
    lane = lane_of(mask.shape)
    count = jnp.sum(jnp.where((lane >= MASK) & (lane < MASK + 8), mask, 0.0))
    send(pay, mean, square)
    notes(vec, jnp.full((1, LANES), count, F32))
    wait(fetched)


def first_kernel(place, got, raw, sides, table, taps, summed, pay, vec, fields, lows, hidden, xhat, sems, *, spots, local_count, pixel_count, height):
    mean, inverse = merge_stats(row_of_each(got, 0), row_of_each(got, 1), local_count, pixel_count)
    notes(vec, inverse)
    gain, bias = affine(table, 0)
    rows = raw.shape[0]

    def norm_rows(i):
        at = pl.ds(4 * i, 4)
        out = []
        for k in range(2):
            x = (raw[at, k] - mean) * inverse
            xhat[at, k] = x
            n = x * gain + bias
            out.append(n * sig_of(n))
        put_low(hidden, 4 * i, *out)

    blank(hidden)
    loop(rows // 4, norm_rows)
    stored = copies(sems, (xhat, spots(fields, "xhat_zero")), (hidden, spots(lows, "hidden_one")))

    @pl.when(place[0] >= 0)
    def _():
        y = conv(hidden, taps, 0, rows, flat(sides[1 : rows + 1]))
        summed[:, 0], summed[:, 1] = blocks_of(y, rows)

    send(pay, *local_stats(summed, place[0], height, local_count))
    wait(stored)


def pool_kernel(place, got, summed, count_in, table, weights, fields_in, lows_in, raw, pay, vec, merged, taps_next, fields, lows, xhat, shared, taps, sems, *, spots, local_count, pixel_count, height):
    fetched = copies(sems, (taps_at(weights, 1), taps), (taps_at(weights, 2), taps_next))
    mean, inverse = merge_stats(row_of_each(got, 0), row_of_each(got, 1), local_count, pixel_count)
    gain, bias = affine(table, 1)
    rows, segments = summed.shape[0], summed.shape[2]
    off = place[0]

    step = 4

    def some(i, carry):
        at = pl.ds(step * i, step)
        pairs = (step // 2, 2, segments, LANES)
        outs, sums = [], [jnp.zeros((step // 2 * segments, LANES), F32) for _ in range(3)]
        for k in range(2):
            x = (summed[at, k] - mean) * inverse
            n = x * gain + bias
            sig = sig_of(n)
            e = (n * sig).reshape(pairs)
            top = flat(jnp.maximum(e[:, 0], e[:, 1]))
            top = jnp.maximum(top, partner(top))
            wide_top = top.reshape(step // 2, 1, segments, LANES)
            exps = jnp.exp(e - wide_top)
            whole = flat(exps[:, 0] + exps[:, 1])
            whole = whole + partner(whole)
            pooled = top + jnp.log(whole)
            outs.append((e + pooled.reshape(wide_top.shape)).reshape(step, segments, LANES))
            share = exps * (1.0 / whole).reshape(wide_top.shape) * slope(n, sig).reshape(pairs)
            share_x = share * x.reshape(pairs)
            xhat[at, k] = x
            shared[at, k] = share.reshape(step, segments, LANES)
            sums[0] = sums[0] + pooled
            sums[1] = sums[1] + flat(share[:, 0] + share[:, 1])
            sums[2] = sums[2] + flat(share_x[:, 0] + share_x[:, 1])
        put_low(merged, step * i, *outs)
        mine = (step * i >= off) & (step * i < off + height)
        keep = jnp.where(mine, 1.0, 0.0)
        return tuple(a + keep * b for a, b in zip(carry, sums))

    blank(merged)
    zero = jnp.zeros((step // 2 * segments, LANES), F32)
    sums = lax.fori_loop(0, rows // step, some, (zero, zero, zero), unroll=min(rows // step, 5))
    pool_sum, share_sum, share_x = [fold(col_sum(v)) for v in sums]
    stored = copies(
        sems.at[2:],
        (xhat, spots(fields, "xhat_one")),
        (shared, spots(fields, "shared")),
        (merged, spots(lows, "merged")),
    )
    wait(fetched)
    raw[:, 0], raw[:, 1] = blocks_of(conv(merged, taps, 0, rows), rows)
    mean, square = local_stats(raw, place[0], height, local_count)
    send(pay, mean, square, groups(0.5 * pool_sum, share_sum, share_x, count_in[0:1]))
    notes(vec, inverse)
    wait(stored)


def by_image(v, parts):
    devices = v.shape[0]
    step = 1
    while step < parts:
        upper = (row_of(v.shape) // step) % 2 == 1
        v = v + jnp.where(upper, pltpu.roll(v, step, axis=0), pltpu.roll(v, devices - step, axis=0))
        step *= 2
    return v


def wide_dot(a, b, dims=(((1,), (0,)), ((), ()))):
    (a_high, a_low), (b_high, b_low) = [[v.astype(BF16) for v in in_parts(x, 2)] for x in (a, b)]
    axis_a, axis_b = dims[0][0][0], dims[0][1][0]
    left = jnp.concatenate([a_high, a_high, a_low], axis=axis_a)
    right = jnp.concatenate([b_high, b_low, b_high], axis=axis_b)
    return lax.dot_general(left, right, dims, preferred_element_type=F32)


def in_parts(v, count):
    out = []
    for _ in range(count):
        out.append(low(v))
        v = v - out[-1]
    return out


def mine_of(v, me):
    return col_sum(jnp.where(row_of(v.shape) == me, v, 0.0))


def style_kernel(place, got, raw, merged, table, w_style, w_convs_in, taps, sides, fields, lows_in, resid, pay, vec, style_out, xhat, ahead, sums, lows, hidden, slopes, w_conv, zero_x, one_x, shared, field, sems, *, spots, local_count, pixel_count, pool_cells, height, parts):
    own = pl.ds(place[0], height)
    fetched = copies(
        sems,
        (w_convs_in.at[2], w_conv),
        (spots(fields, "xhat_zero").at[own], zero_x),
        (spots(fields, "xhat_one").at[own], one_x),
        (spots(fields, "shared").at[own], shared),
        (spots(lows_in, "hidden_one").at[pl.ds(place[0], height + 2)], field),
    )
    style = by_image(spread(row_of_each(got, 2), 0), parts) / pool_cells
    style_out[...] = style
    one, two = [
        wide_dot(style, diagonal_blocks(w_style[i])) for i in range(2)
    ]
    mean, inverse = merge_stats(row_of_each(got, 0) + one, row_of_each(got, 1), local_count, pixel_count)
    notes(vec, inverse)
    gain, bias = affine(table, 2)
    rows, kept = raw.shape[0], resid.shape[0]
    off, skipped, mine = place[0], place[3], place[4]
    me = place[2]
    shift = mine_of(one, me) - mean
    two = mine_of(two, me)

    def norm_rows(i):
        at = pl.ds(4 * i, 4)
        out = []
        for k in range(2):
            x = (raw[at, k] + shift) * inverse
            xhat[at, k] = x
            n = x * gain + bias
            sig = sig_of(n)
            slopes[at, k] = slope(n, sig)
            out.append(n * sig)
        put_low(hidden, 4 * i, *out)

    blank(hidden)
    loop(rows // 4, norm_rows)
    stored = copies(sems.at[5:], (hidden, spots(lows, "hidden_three")))

    @pl.when(place[0] >= 0)
    def _():
        for k, y in enumerate(blocks_of(conv(hidden, taps, skipped, kept), kept)):
            resid[:, k] = y + two + merged[pl.ds(skipped + 1, kept), k].astype(F32)

    wait(fetched + stored)
    hidden[kept + 1 : kept + 2] = jnp.zeros((1,) + hidden.shape[1:], BF16)
    centre = fold(col_sum(resid[mine, 0] + resid[mine, 1])) / (SEG * raw.shape[2])
    at = pl.ds(off, height)
    probe = [slopes[at, k] for k in range(2)]
    probe += [slopes[at, k] * xhat[at, k] for k in range(2)]
    probe = jnp.concatenate([flat(v).astype(BF16) for v in probe], axis=1)

    def centred(i):
        at = pl.ds(4 * i, 4)
        put_low(hidden, 4 * i, resid[at, 0] - centre, resid[at, 1] - centre, True)

    loop(kept // 4, centred)
    links = norm_links(hidden, probe, mine, height, w_conv, centre)
    send(pay, *local_stats(resid, mine, height, local_count))
    send_parts(pay, 2, 1)[:, 0, :] = links
    put_ahead(off, sides, ahead, sums, zero_x, one_x, shared, field, local_count)


def norm_links(field, probe, first, rows, taps, centre):
    wide = jnp.concatenate(views(field, first, rows), axis=1)
    found = lax.dot_general(probe, wide, (((0,), (0,)), ((), ())), preferred_element_type=F32)
    group = group_of((CH, LANES))
    out = []
    for half in range(2):

        def piece(y, chunk):
            at = 2 * LANES * half + CH * y
            return found[at : at + CH, chunk * LANES : (chunk + 1) * LANES]

        plain = jnp.zeros((CH, LANES), F32)
        moved = jnp.zeros((CH, LANES), F32)
        for r in range(3):
            first_edge, last_edge = piece(0, 3 * r), piece(SEG - 1, 3 * r)
            edge = first_edge + last_edge
            for y in range(1, SEG - 1):
                edge = edge + piece(y, 3 * r)
            inside = edge[:, ROW : ROW + 1]
            counts = (
                inside + (first_edge[:, BEFORE : BEFORE + 1] - first_edge[:, ROW : ROW + 1]),
                inside,
                inside + (last_edge[:, AFTER : AFTER + 1] - last_edge[:, ROW : ROW + 1]),
            )
            for c in range(3):
                tap = tile4(low(taps[3 * (2 - r) + 2 - c]))
                val = jnp.zeros((CH, LANES), F32)
                for y in range(SEG):
                    d, a = spot_of(y + c - 1)
                    val = val + jnp.where(group == a, piece(y, 3 * r + d), 0.0)
                plain = plain + tap * counts[c]
                moved = moved + tap * val
        out += [plain, fold(moved) + centre * plain]
    return groups(*out)


def spot_of(x):
    if x < 0:
        return 0, 3
    if x == SEG:
        return 0, 0
    return 1 + x // GRP, x % GRP


def put_ahead(off, sides, out, sums, below_x, xhat, shared, field, local_count):
    height = xhat.shape[0]
    at = pl.ds(0, height)
    low_x = jnp.concatenate([own_lanes(below_x, at), jnp.ones((height * field.shape[2], LANES), BF16)], axis=1)
    entries, alone = [], zero_row()
    lane = lane_of((1, LANES))
    for r in range(3):
        for tap, bare in pixel_taps(sides, off + r, height, low_x, (-1, 0, 1), True):
            for v, b in zip(tap, bare):
                alone = jnp.where(lane == ALONE + len(entries), b, alone)
                entries.append(v)
    centres = [fold(v) / local_count for v in row_sums(0, height, lambda at, k: (xhat[at, k], shared[at, k]))]
    probe = [flat(v[at, k] - c).astype(BF16) for v, c in zip((xhat, shared), centres) for k in range(2)]
    wide = jnp.concatenate(views(field, 0, height), axis=1)
    found = lax.dot_general(
        jnp.concatenate(probe, axis=1), wide, (((0,), (0,)), ((), ())), preferred_element_type=F32
    )
    ones = jnp.ones((8, wide.shape[0]), BF16)
    plain = jnp.dot(ones, wide, preferred_element_type=F32)[0:1]
    group = group_of((1, LANES))
    hidden = []
    for r in range(3):
        for s in range(3):
            val = zero_row()
            for y in range(SEG):
                d, a = spot_of(y + s - 1)
                spot = (3 * r + d) * LANES
                val = val + jnp.where(group == a, plain[:, spot : spot + LANES], 0.0)
            hidden.append(fold(val))
    packed = [groups(*hidden[0:4]), groups(*hidden[4:8]), hidden[8]]
    all_hidden = jnp.concatenate(packed, axis=0)
    last = [
        put_taps(
            found[2 * LANES * k : 2 * LANES * (k + 1)], out.at[:, 2 * k + 1 : 2 * k + 3, 0], (centres[k], all_hidden)
        )
        for k in range(2)
    ]
    entries += hidden
    entries.append(jnp.zeros((CH - len(entries), LANES), F32))
    out[:, 0, 0, :] = groups(jnp.concatenate(entries, axis=0), *last, jnp.zeros((CH, LANES), F32))
    notes(sums, *packed, alone)


def head_kernel(place, got, got_style, resid, sides, head_mat, w_head, below_x, ahead, image_sums, table, back, grad, xhat, pay, vec, decoded, slopes, grad_low, *, local_count, pixel_count, height):
    mean, inverse = merge_stats(row_of_each(got, 0), row_of_each(got, 1), local_count, pixel_count)
    notes(vec, inverse, mean)
    gain, bias = affine(table, 3)
    rows, segments = resid.shape[0], resid.shape[2]
    all_off, skipped, off = place[0], place[3], place[4]

    def norm_rows(i):
        at = pl.ds(4 * i, 4)
        for k in range(2):
            x = (resid[at, k] - mean) * inverse
            n = x * gain + bias
            s = sig_of(n)
            xhat[at, k] = x
            slopes[at, k] = slope(n, s)
            decoded[at, k] = (n * s).astype(BF16)

    loop(rows // 4, norm_rows, 10)
    head = head_mat[...]
    wide = jnp.concatenate([flat(decoded[:, 0]), flat(decoded[:, 1])], axis=1)
    bias_row = zero_row()
    for k in range(3):
        mine = (lane_of((1, LANES)) >> 3) == FLOW // 8 + k
        bias_row = jnp.where(mine, low(w_head[k : k + 1, CH : CH + 1]), bias_row)
    out = jnp.dot(wide, head, preferred_element_type=F32) + bias_row
    given = flat(sides[pl.ds(skipped + 1, rows)]).astype(F32)
    lane = lane_of(given.shape)
    is_flow = lane < LABEL
    near = [pltpu.roll(given, LANES - MASK + first, axis=1) for first in (FLOW, FLOW + 8, LABEL)]
    mask = jnp.where(lane < FLOW + 8, near[0], jnp.where(is_flow, near[1], near[2]))
    mask = jnp.where((lane >= FLOW) & (lane < LABEL + 8), mask, 0.0)
    count = jnp.sum(got_style[:, 2, 0, 3 * CH : 3 * CH + 1])
    diff = out - given / flow_scale
    hinge = jnp.maximum(out, 0.0) + jnp.log1p(jnp.exp(-jnp.abs(out)))
    loss = mask * jnp.where(is_flow, diff * diff, hinge - given * out)
    grad_out = (mask * jnp.where(is_flow, 2.0 * diff, sig_of(out) - given) / count).astype(BF16)
    at_row = lax.broadcasted_iota(jnp.int32, loss.shape, 0)
    inside = (at_row >= off * segments) & (at_row < (off + height) * segments)
    loss_sum = jnp.sum(jnp.where(inside, loss, 0.0))
    mine_out = jnp.where(inside, grad_out.astype(F32), 0.0).astype(BF16)
    outs = col_sum(mine_out.astype(F32))
    found = lax.dot_general(mine_out, wide, (((0,), (0,)), ((), ())), preferred_element_type=F32)
    shape = found.shape
    found = jnp.where((row_of(shape) & 7) == group_of(shape), found, 0.0)
    whole = [col_sum(found[FLOW + 8 * k : FLOW + 8 * k + 8]) for k in range(3)]
    whole = [fold(v[:, 0:LANES] + v[:, LANES:]) for v in whole]
    row = groups(*whole, zero_row())
    lane = lane_of((1, LANES))
    for k in range(3):
        row = jnp.where(lane == 3 * CH + k, jnp.sum(jnp.where((lane >> 3) == FLOW // 8 + k, outs, 0.0)), row)
    row = jnp.where(lane == 3 * CH + 3, loss_sum, row)
    y = lax.dot_general(grad_out, head, (((1,), (1,)), ((), ())), preferred_element_type=F32)
    for k, g in enumerate(blocks_of(y, rows)):
        grad[:, k] = g * slopes[:, k]
    factor = gain * inverse
    back_rows(grad_low, rows, lambda at, k: factor * grad[at, k], 10)
    shift_sum, scale_sum = own_sums(grad, xhat, off, height)
    y = conv(grad_low, back, off, height)
    slopes[0:height, 0], slopes[0:height, 1] = blocks_of(y, height)
    gain, bias = affine(table, 2)

    def links(at, k):
        x = below_x[pl.ds(all_off + at.start, at.size), k]
        g = slopes[at, k] * slope_at(x, gain, bias)
        return g, g * x

    below = [fold(v) for v in row_sums(0, height, links)]
    send(pay, groups(shift_sum, scale_sum, *below), row + image_sums[3:4], total_of(got, 2))
    send_parts(pay, 3, 5)
    pay[0:CH, 3:8] = ahead[...]


def own_sums(grad, xhat, first, rows):
    def both(at, k):
        g = grad[at, k]
        return g, g * xhat[at, k]

    return [fold(v) for v in row_sums(first, rows, both)]


def back_sums(got, pixel_count):
    whole = col_sum(got)
    return spread(whole, 0) / pixel_count, spread(whole, 1) / pixel_count


def low_sum(grad_low, first, rows):
    return fold(row_sums(first + 1, rows, lambda at, k: (grad_low[at, k].astype(F32),))[0])


def norm_back(grad, xhat, factor, shift, scale):
    return factor * (grad - (shift + xhat * scale))


def back_rows(grad_low, rows, value, unroll=5):
    def some(i):
        put_low(grad_low, 4 * i, *[value(pl.ds(4 * i, 4), k) for k in range(2)])

    blank(grad_low)
    loop(rows // 4, some, unroll)


def own_lanes(grad, at):
    return jnp.concatenate([flat(grad[at, k]).astype(BF16) for k in range(2)], axis=1)


def tap_sums(field, grad, first, rows, out, more=None):
    wide = jnp.concatenate(views(field, first, rows), axis=1)
    found = lax.dot_general(grad, wide, (((0,), (0,)), ((), ())), preferred_element_type=F32)
    return put_taps(found, out, more)


def put_taps(found, out, more=None):
    group = group_of((CH, LANES))
    taps = []
    for r in range(3):
        for s in range(3):
            val = jnp.zeros((CH, LANES), F32)
            for y in range(SEG):
                d, a = spot_of(y + s - 1)
                spot = (3 * r + d) * LANES
                val = val + jnp.where(group == a, found[CH * y : CH * y + CH, spot : spot + LANES], 0.0)
            taps.append(fold(val))
    for q in range(3):
        val = taps[4 * q]
        for b in range(1, min(4, 9 - 4 * q)):
            val = jnp.where(group == b, taps[4 * q + b], val)
        if more is not None:
            centre, sums = more
            val = val + column_of(centre) * sums[q : q + 1]
        if q == 2:
            return val
        out[:, q, :] = val


def column_of(v):
    shape = (CH, LANES)
    return jnp.sum(jnp.where(row_of(shape) == lane_of(shape), v, 0.0), axis=1, keepdims=True)


def at_lane(v, k):
    return jnp.sum(jnp.where(lane_of(v.shape) == k, v, 0.0), axis=1, keepdims=True)


def decoder_back_kernel(place, got, grad, xhat, mid_x, vec, vec_two, sums, table, back_two, weights, fields, lows, below, below_x, shared, pay, more, first_x, kept_grad, mid, low_two, low_one, field_two, field_one, field_zero, back_one, sems, *, spots, local_count, pixel_count):
    all_off, skipped, off = place[0], place[3], place[4]
    height = field_two.shape[0] - 2
    far_rows, near_rows = pl.ds(skipped, grad.shape[0]), pl.ds(all_off, height + 2)
    fetched = copies(
        sems,
        (back_at(weights), back_one),
        (spots(fields, "xhat_one").at[far_rows], below_x),
        (spots(fields, "shared").at[far_rows], shared),
        (spots(lows, "hidden_three").at[near_rows], field_two),
        (spots(lows, "merged").at[near_rows], field_one),
        (spots(lows, "hidden_one").at[near_rows], field_zero),
    )
    handed = copies(sems.at[6:], (spots(fields, "xhat_zero").at[pl.ds(all_off, height)], first_x))
    devices = got.shape[0]
    rows = grad.shape[0]
    total = total_of(got, 0)
    shift, scale = spread(total, 0) / pixel_count, spread(total, 1) / pixel_count
    inverse, mean = vec[0:1], vec[1:2]
    factor = affine(table, 3)[0] * inverse
    slant = scale * inverse
    held, carried = factor * (shift - slant * mean), factor * slant
    links = got[0:CH, 2, 0, :] * groups(held, carried, held, carried)
    group = group_of(links.shape)
    mine = (lane_of(links.shape) & 31) == row_of(links.shape)

    def across(pick):
        column = jnp.sum(jnp.where(pick, links, 0.0), axis=1, keepdims=True)
        return col_sum(jnp.where(mine, column, 0.0))

    shift_two = spread(total, 2) - across(group < 2)
    scale_two = spread(total, 3) - across(group >= 2)
    entry = total_of(got, 3)
    notes(more, scale_two, shift_two, total_of(got, 4), total_of(got, 5), spread(entry, 1))

    def value(at, k):
        g = norm_back(grad[at, k], xhat[at, k], factor, shift, scale)
        kept_grad[at, k] = g
        return g

    back_rows(low_two, rows, value)

    @pl.when(place[0] >= 0)
    def _():
        mid[:, 0], mid[:, 1] = blocks_of(conv(low_two, back_two, 0, rows), rows)

    gain, bias = affine(table, 2)
    factor = gain * vec_two[0:1]
    shift, scale = shift_two / pixel_count, scale_two / pixel_count

    def value_two(at, k):
        x = mid_x[pl.ds(skipped + at.start, at.size), k]
        return norm_back(mid[at, k] * slope_at(x, gain, bias), x, factor, shift, scale)

    back_rows(low_one, rows, value_two)
    wait(fetched)
    sum_two = low_sum(low_two, off, height)
    sum_one = low_sum(low_one, off, height)
    y = conv(low_one, back_one, 0, rows)
    gain, bias = affine(table, 1)
    for k, y in enumerate(blocks_of(y, rows)):
        g = (y + kept_grad[:, k]).reshape(rows // 2, 2, -1, LANES)
        both = flat(g[:, 0] + g[:, 1])
        both = (both + partner(both)).reshape(rows // 2, 1, -1, LANES)
        g = g * slope_at(below_x[:, k], gain, bias).reshape(g.shape) + both * shared[:, k].reshape(g.shape)
        below[:, k] = g.reshape(rows, -1, LANES)
    shift_sum, scale_sum = own_sums(below, below_x, off, height)
    send(pay, groups(shift_sum, scale_sum, sum_one, sum_two))
    entry = spread(entry, 0)
    pay[:, 1, 0, :] = jnp.broadcast_to(entry, (devices, LANES))
    at = pl.ds(off + 1, height)
    last_two = tap_sums(field_two, own_lanes(low_two, at), 0, height, send_parts(pay, 2, 2))
    last_one = tap_sums(field_one, own_lanes(low_one, at), 0, height, send_parts(pay, 4, 2))
    centre = shift_sum / local_count
    at = pl.ds(off, height)
    grad = jnp.concatenate([flat(below[at, k] - centre).astype(BF16) for k in range(2)], axis=1)
    last_zero = tap_sums(field_zero, grad, 0, height, send_parts(pay, 6, 2), (centre, sums))
    pay[0:CH, 1, 0, :] = groups(last_two, last_one, last_zero, jnp.broadcast_to(entry, (CH, LANES)))
    wait(handed)


def summed_kernel(place, got, got_style, got_head, grad, xhat, shared, vec, more_two, table, w_style, sides, back, below_x, pay, more, below, grad_low, *, pixel_count, pool_cells, parts):
    off, mine = place[0], place[4]
    height = below.shape[0]
    devices = got.shape[0]
    rows = grad.shape[0]
    dims = (((1,), (1,)), ((), ()))
    first = row_of_each(got, 0)
    each = wide_dot(spread(first, 2), diagonal_blocks(w_style[0]), dims) + wide_dot(
        spread(first, 3), diagonal_blocks(w_style[1]), dims
    )
    each = each / pool_cells
    total = col_sum(first)
    shift = spread(total, 0) + col_sum(each * by_image(spread(row_of_each(got_style, 2), 1), parts))
    scale = spread(total, 1) + col_sum(each * by_image(spread(row_of_each(got_style, 2), 2), parts))
    style_grad = col_sum(jnp.where(row_of(each.shape) // parts == place[2] // parts, each, 0.0))
    factor = affine(table, 1)[0] * vec[0:1]
    shift_mean, scale_mean = shift / pixel_count, scale / pixel_count
    def value(at, k):
        return norm_back(grad[at, k] + shared[at, k] * style_grad, xhat[at, k], factor, shift_mean, scale_mean)

    back_rows(grad_low, rows, value)
    gain, bias = affine(table, 0)
    for k, y in enumerate(blocks_of(conv(grad_low, back, mine, height), height)):
        below[:, k] = y * slope_at(below_x[:, k], gain, bias)
    me = place[2]
    weights = at_lane(by_image(each, parts), me)
    hidden = spread(got[0:CH, 1, 0, :], 3)
    hidden = [groups(*[hidden[18 + t : 19 + t] for t in range(4 * q, min(4 * q + 4, 9))]) for q in range(3)]
    last = total_of(got, 1)
    direct = [total_of(got, 6), total_of(got, 7), spread(last, 2)]
    shares = [row_of_each(got_head, 6), row_of_each(got_head, 7), spread(row_of_each(got_head, 3), 2)]
    shard = []
    for q in range(3):
        val = direct[q] + col_sum(weights * shares[q])
        val = val - at_lane(shift_mean, me) * hidden[q] - at_lane(scale_mean, me) * more_two[2 + q : 3 + q]
        shard.append(at_lane(factor, me) * val)
    at = pl.ds(mine + 1, height)
    side = pixel_taps(sides, off + 1, height, own_lanes(grad_low, at), (0,))[0]
    low_below = own_lanes(below, pl.ds(0, height))
    taps = []
    for r in range(3):
        for tap in pixel_taps(sides, off + r, height, low_below, (-1, 0, 1)):
            taps.extend(tap)
    sums = [in_parts(v, 3) for v in own_sums(below, below_x, 0, height)]
    entries = [in_parts(v, 2) for v in taps + side]
    tail = [shard[2]] + [v[0] for v in entries] + [v[1] for v in entries]
    tail += [zero_row()] * (-len(tail) % 4)
    values = [
        groups(sums[0][0], sums[1][0], sums[0][1], sums[1][1]),
        groups(sums[0][2], sums[1][2], spread(last, 0), spread(last, 1)),
        *[total_of(got, r) for r in range(2, 6)],
        *shard[0:2],
        *[groups(*tail[k : k + 4]) for k in range(0, len(tail), 4)],
    ]
    values += [zero_row()] * (len(values) % 2)
    for k in range(len(values) // 2):
        pair = jnp.concatenate(values[2 * k : 2 * k + 2], axis=0).astype(BF16)
        pay[:, k] = jnp.broadcast_to(pair[None], (devices, 2, LANES))
    notes(more, scale, shift)


def pixel_taps(sides, row, rows, grad, shift, alone=False):
    x = flat(sides[pl.ds(row, rows)])
    found = lax.dot_general(x, grad, (((0,), (0,)), ((), ())), preferred_element_type=F32)
    inside, channel, column = image_lanes((LANES, 2 * LANES))
    here = column - group_of((LANES, 2 * LANES))
    out = []
    for s in shift:
        both, bare = [], []
        for c in range(2):
            v = col_sum(jnp.where(inside & (channel == c) & (here == s), found[:, 0 : 2 * LANES], 0.0))
            both.append(fold(v[:, 0:LANES] + v[:, LANES:]))
            if alone:
                cut = slice(0, LANES)
                hit = (inside & (channel == c) & (column >= s) & (column < s + SEG))[:, cut]
                bare.append(col_sum(jnp.where(hit, found[:, 2 * LANES :], 0.0)))
        out.append((both, bare) if alone else both)
    return out


def adamw(master, moment, square, grad, rate):
    new_moment = beta_one * moment + (1.0 - beta_one) * grad
    new_square = beta_two * square + (1.0 - beta_two) * grad * grad
    moment_hat = new_moment / (1.0 - beta_one**STEP)
    square_hat = new_square / (1.0 - beta_two**STEP)
    new_master = master - rate * (moment_hat / (jnp.sqrt(square_hat) + adam_eps) + weight_decay * master)
    return new_master, new_moment, new_square


def put(at, refs, grad, rate, outs):
    found = adamw(*[ref[at] for ref in refs], grad, rate)
    for out, value in zip(outs, found + (found[0].astype(BF16),)):
        out[at] = value


def update_early(
    got_one_back, got_head, got_style, pay, style, w_style, w_head, m_style, m_head, s_style, s_head,
    loss_out, count_out, style_master, style_moment, style_square, head_master, head_moment, head_square, head_copy,
):
    count_out[0, 0] = jnp.sum(got_style[:, 2, 0, 3 * CH : 3 * CH + 1])
    loss_out[0, 0] = jnp.sum(got_head[:, 1, 0, 99:100])
    dims = (((0,), (0,)), ((), ()))
    for i in range(2):
        sums = spread(row_of_each(got_one_back, 0), 2 + i)
        grad = lax.dot_general(style[...], sums, dims, precision=highest, preferred_element_type=F32)
        put(i, (w_style, m_style, s_style), grad[0:CH, 0:CH], rate_table[2], (style_master, style_moment, style_square))

    head = total_of(got_head, 1)
    lane = lane_of((1, LANES))
    rows = []
    for k in range(3):
        last = jnp.sum(jnp.where(lane == 3 * CH + k, head, 0.0), axis=1, keepdims=True)
        rows.append(jnp.where(lane < CH, spread(head, k), last))
    grad = jnp.concatenate(rows, axis=0)[:, 0 : CH + 1]
    put(slice(None), (w_head, m_head, s_head), grad, rate_table[3], (head_master, head_moment, head_square, head_copy))


def update_late(
    got, got_one_back, got_head, more, more_two, vec, w_first, w_convs, table, m_first, m_convs, m_norms, s_first, s_convs, s_norms,
    first_master, first_moment, first_square, first_copy,
    convs_master, convs_moment, convs_square, convs_copy,
    norms_master, norms_moment, norms_square, *, pixel_count
):
    refs = (w_convs, m_convs, s_convs)
    outs = (convs_master, convs_moment, convs_square, convs_copy)
    pairs = [got[:, k].astype(F32) for k in range(got.shape[1])]
    packs = [[pairs[k // 2][0:CH, k % 2, :].T for k in ks] for ks in ((6, 7, 8), (4, 5, 1), (2, 3, 1))]
    for i, pack in enumerate(packs):
        for t in range(9):
            b = t % 4 if t < 8 else (0, 3, 2)[i]
            put((i, t), refs, pack[t // 4][CH * b : CH * b + CH], rate_table[1], outs)

    totals = [jnp.sum(pair, axis=0) for pair in pairs]
    totals = [pair[h : h + 1] for pair in totals for h in range(2)]
    shift, scale = [spread(totals[0], k) + (spread(totals[0], 2 + k) + spread(totals[1], k)) for k in range(2)]
    factor = affine(table, 0)[0] * vec[0:1]
    by_x = spread(got_one_back[0:CH, 1, 0, :], 3)
    alone = total_of(got_head, 1)
    refs = (w_first, m_first, s_first)
    outs = (first_master, first_moment, first_square, first_copy)
    for t in range(10):
        pair = []
        for e in (2 * t, 2 * t + 1):
            k, b = divmod(1 + e, 4)
            v = spread(totals[8 + k], b)
            k, b = divmod(21 + e, 4)
            v = v + spread(totals[8 + k], b)
            if t < 9:
                v = factor * (v - (at_lane(alone, ALONE + e) * shift + by_x[e : e + 1] * scale) / pixel_count)
            pair.append(v[:, 0:CH])
        put(t, refs, jnp.concatenate(pair, axis=0), rate_table[0], outs)

    three_sums = total_of(got_head, 0)
    scales = [scale, more[0:1], more_two[0:1], spread(three_sums, 1)]
    shifts = [shift, more[1:2], more_two[1:2], spread(three_sums, 0)]
    for i, rows in enumerate((scales, shifts)):
        grad = jnp.concatenate(rows, axis=0)[:, 0:CH]
        put(i, (table, m_norms, s_norms), grad, rate_table[4], (norms_master, norms_moment, norms_square))


def update_kernel(*refs, pixel_count):
    ins, outs = refs[:23], refs[23:]
    late, early = ins[:15], ins[15:]
    update_late(*late, *outs[:11], pixel_count=pixel_count)
    update_early(late[1], late[2], early[0], None, *early[1:], *outs[11:])


def far(x):
    return ("far", x)


def call(kernel, outs, *operands, scalars=0, scratch=(), sems=0, scalar_outs=(), aliases=None, limit=VMEM_LIMIT, name):
    smem = pl.BlockSpec(memory_space=pltpu.SMEM)
    vmem = pl.BlockSpec(memory_space=pltpu.VMEM)
    hbm = pl.BlockSpec(memory_space=pltpu.HBM)
    is_far = lambda x: isinstance(x, tuple) and x[0] == "far"
    in_specs = [smem if i < scalars else hbm if is_far(x) else vmem for i, x in enumerate(operands)]
    out_specs = [smem if i in scalar_outs else hbm if is_far(x) else vmem for i, x in enumerate(outs)]
    plain = lambda x: x[1] if is_far(x) else x
    shapes = [pltpu.VMEM(shape, dtype) for shape, dtype in scratch]
    if sems:
        shapes.append(pltpu.SemaphoreType.DMA((sems,)))
    return pl.pallas_call(
        kernel,
        out_shape=[jax.ShapeDtypeStruct(*plain(x)) for x in outs],
        in_specs=in_specs,
        out_specs=out_specs,
        scratch_shapes=shapes,
        input_output_aliases=aliases or {},
        compiler_params=pltpu.CompilerParams(vmem_limit_bytes=limit),
        name=name,
    )(*[plain(x) for x in operands])


def exchange(pay):
    return lax.all_to_all(pay, ("row", "col"), 0, 0)


def local(
    image_batch, valid_mask, flow_target, cell_labels,
    w_first, w_convs, w_style, w_head, batch_norm_table,
    mom_first, mom_convs, mom_style, mom_head, mom_norms,
    sqr_first, sqr_convs, sqr_style, sqr_head, sqr_norms,
):
    images, block_rows, block_cols, _ = image_batch.shape
    row_count, col_count = lax.axis_size("row"), lax.axis_size("col")
    devices = row_count * col_count
    parts = devices // images
    image_rows, image_cols = row_count * block_rows, col_count * block_cols
    assert devices == parts * images and block_rows == RIM and block_cols == 2 * block_rows * 2
    assert image_rows % (parts * RIM) == 0 and devices >= CH
    height = image_rows // parts
    rows = min(image_rows, height + RIM * min(2, parts - 1))
    segments = image_cols // SEG
    local_count = float(height * image_cols)
    pixel_count = local_count * devices
    pool_cells = float(image_rows * image_cols // 4)
    part = functools.partial
    counts = dict(local_count=local_count, pixel_count=pixel_count, height=height)
    styled = dict(pool_cells=pool_cells, parts=parts)

    me = lax.axis_index("row") * col_count + lax.axis_index("col")
    first_row = (me % parts) * height
    start = jnp.clip(first_row - RIM, 0, image_rows - rows)
    off = first_row - start
    back_rim = RIM // 2
    rows_back = min(rows, height + back_rim * min(2, parts - 1))
    skipped = jnp.clip(off - back_rim, 0, rows - rows_back)
    place = jnp.stack([off, start // block_rows, me, skipped, off - skipped]).astype(jnp.int32)

    field = ((rows, 2, segments, LANES), F32)
    own_field = ((height,) + field[0][1:], F32)
    back_field = ((rows_back,) + field[0][1:], F32)
    low_field = ((rows + 2, 3, segments, LANES), BF16)
    own_low = ((height + 2,) + low_field[0][1:], BF16)
    back_low = ((rows_back + 2,) + low_field[0][1:], BF16)
    vec = ((8, LANES), F32)

    def payload(count):
        return ((devices, count, 1, LANES), F32)

    nine = ((BACK, 2 * LANES), BF16)
    ten = ((FORWARD, 2 * LANES), BF16)

    places = {
        name: i * count
        for count, names in (
            (rows, ("xhat_zero", "xhat_one", "shared")),
            (rows + 2, ("hidden_one", "hidden_three", "merged")),
        )
        for i, name in enumerate(names)
    }

    def spots(store, name):
        count = rows if name[0] in "xs" else rows + 2
        return store.at[places[name] : places[name] + count]

    def store_of(like):
        shape, dtype = like
        row_bytes = shape[1] * segments * LANES * jnp.dtype(dtype).itemsize
        return far(((-(-STORE_BYTES // row_bytes),) + shape[1:], dtype))

    inputs = (
        jnp.transpose(image_batch, (0, 1, 3, 2)), jnp.transpose(flow_target, (0, 1, 3, 2)), cell_labels, valid_mask
    )
    (pay,) = call(
        pack_kernel,
        [((devices, 16, LANES), BF16)],
        *[far(v) for v in inputs],
        scratch=[(v.shape, v.dtype) for v in inputs], sems=4, limit=WHOLE_VMEM, name="pack",
    )
    got_inputs = exchange(pay)
    head_rows = w_head.T
    weights, back_zero, back_two, head_mat = call(
        prepare,
        [far(((STORE_BYTES // (4 * LANES), 2 * LANES), BF16)), far(nine), far(nine), far(((2 * LANES, LANES), BF16))],
        far(w_first), far(w_convs), far(head_rows),
        scratch=[
            (w_first.shape, F32), (w_convs.shape, F32), (head_rows.shape, F32), ((BACK_AT + BACK, 2 * LANES), BF16),
            nine, nine, ((2 * LANES, LANES), BF16),
        ],
        sems=8, limit=WHOLE_VMEM, name="prepare",
    )

    (first_mat,) = call(hand_kernel, [((3 * LANES, 2 * LANES), BF16)], far(weights), sems=1, name="hand")
    sides, raw, pay, count, taps = call(
        part(start_kernel, local_count=local_count, height=height, sources=col_count),
        [((rows + 2, segments, LANES), BF16), field, payload(2), vec, ten],
        place, got_inputs, first_mat, far(weights),
        scalars=1, sems=1, name="image_conv",
    )
    got_zero = exchange(pay)
    summed, pay, inv_zero, fields, lows = call(
        part(first_kernel, spots=spots, **counts),
        [field, payload(2), vec, store_of(field), store_of(low_field)],
        place, got_zero, raw, sides, batch_norm_table, taps,
        scalars=1, scratch=[low_field, field], sems=2, name="first_block",
    )
    got_one = exchange(pay)

    raw, pay, inv_one, merged, taps, fields, lows = call(
        part(pool_kernel, spots=spots, **counts),
        [field, payload(3), vec, low_field, nine, store_of(field), store_of(low_field)],
        place, got_one, summed, count, batch_norm_table, far(weights), far(fields), far(lows),
        scalars=1, scratch=[field, field, nine], sems=5,
        aliases={6: 5, 7: 6}, name="pool_and_merge",
    )
    got_style = exchange(pay)

    resid, pay, inv_two, style, xhat_two, ahead, hidden_sums, lows = call(
        part(style_kernel, spots=spots, **styled, **counts),
        [back_field, payload(3), vec, ((devices, LANES), F32), field, ((CH, 5, 1, LANES), F32), vec, store_of(low_field)],
        place, got_style, raw, merged, batch_norm_table, w_style, far(w_convs), taps, sides, far(fields),
        far(lows),
        scalars=1, scratch=[low_field, field, (w_convs.shape[1:], F32), own_field, own_field, own_field, own_low], sems=6,
        aliases={10: 7}, name="decoder",
    )
    got_three = exchange(pay)

    grad_three, xhat_three, pay, inv_three = call(
        part(head_kernel, **counts),
        [back_field, back_field, payload(8), vec],
        place, got_three, got_style, resid, sides, head_mat, head_rows, xhat_two, ahead, hidden_sums, batch_norm_table, back_two,
        scalars=1, scratch=[((rows_back, 2, segments, LANES), BF16), back_field, back_low], name="head",
    )
    got_head = exchange(pay)

    grad_one, xhat_one, shared, pay, more_two, xhat_zero = call(
        part(decoder_back_kernel, spots=spots, local_count=local_count, pixel_count=pixel_count),
        [back_field, back_field, back_field, payload(8), vec, own_field],
        place, got_head, grad_three, xhat_three, xhat_two, inv_three, inv_two, hidden_sums, batch_norm_table, back_two, far(weights),
        far(fields), far(lows),
        scalars=1, scratch=[back_field, back_field, back_low, back_low, own_low, own_low, own_low, nine], sems=7,
        name="decoder_back",
    )
    got_one_back = exchange(pay)

    pay, more = call(
        part(summed_kernel, pixel_count=pixel_count, **styled),
        [((devices, 10, 2, LANES), BF16), vec],
        place, got_one_back, got_style, got_head, grad_one, xhat_one, shared, inv_one, more_two, batch_norm_table, w_style,
        sides, back_zero, xhat_zero,
        scalars=1, scratch=[own_field, back_low], name="summed_back",
    )
    got_last = exchange(pay)

    def results(param, copy):
        return [(param.shape, F32)] * 3 + [(param.shape, BF16)] * copy

    found = call(
        part(update_kernel, pixel_count=pixel_count),
        results(w_first, 1)
        + results(w_convs, 1)
        + results(batch_norm_table, 0)
        + [((1, 1), F32), ((1, 1), F32)]
        + results(w_style, 0)
        + results(head_rows, 1),
        got_last, got_one_back, got_head, more, more_two, inv_zero,
        w_first, w_convs, batch_norm_table, mom_first, mom_convs, mom_norms, sqr_first, sqr_convs, sqr_norms,
        got_style, style, w_style, head_rows, mom_style, mom_head.T, sqr_style, sqr_head.T,
        scalar_outs=(11, 12), name="update",
    )
    late, early = found[:11], found[11:]
    loss, count = early[0].reshape(()), early[1].reshape(())
    head = tuple(value.T for value in early[5:9])
    return (loss, count, *late[0:8], *early[2:5], *head, *late[8:11])


def solution(mesh):
    field = P(None, "row", "col", None)
    plane = P(None, "row", "col")
    return jax.shard_map(
        local,
        mesh=mesh,
        in_specs=(field, plane, field, plane) + (P(),) * 15,
        out_specs=(P(),) * 20,
        check_vma=False,
    )
```
